32 devices in a mesh: dp: 16 (over z, y, core), blk: 2 (over x).
Axes of the slice: x: 2, y: 2, z: 4, core: 2. Of those that a mesh axis runs over, the one named last changes fastest.
Arguments:
- frames: bfloat16 [8192, 768], P(('dp', 'blk')), may hold values from -6 to 6
- cotangent: bfloat16 [8192, 768], P(('dp', 'blk')), may hold values from -6 to 6
- seq_lengths: int32 [16, 4], P('dp'), may hold values from 32 to 257, as said below
- key_mask: int32 [8192], P(('dp', 'blk')), may hold values 0 or 1
- qkv_weight: bfloat16 [768, 2304], P(None, ('dp', 'blk')), may hold values from -0.21875 to 0.21875
- query_value_bias: bfloat16 [1536], P(('dp', 'blk')), may hold values from -3 to 3
- out_weight: bfloat16 [768, 768], P(None, ('dp', 'blk')), may hold values from -0.875 to 0.875
- out_bias: bfloat16 [768], P(('dp', 'blk')), may hold values from -3 to 3
- up_weight: bfloat16 [768, 3072], P(None, ('dp', 'blk')), may hold values from -0.21875 to 0.21875
- up_bias: bfloat16 [3072], P(('dp', 'blk')), may hold values from -3 to 3
- down_weight: bfloat16 [3072, 768], P(None, ('dp', 'blk')), may hold values from -0.109375 to 0.109375
- down_bias: bfloat16 [768], P(('dp', 'blk')), may hold values from -3 to 3
- first_gain: bfloat16 [768], P(('dp', 'blk')), may hold values from 0.5 to 1.5
- first_shift: bfloat16 [768], P(('dp', 'blk')), may hold values from -3 to 3
- second_gain: bfloat16 [768], P(('dp', 'blk')), may hold values from 0.5 to 1.5
- second_shift: bfloat16 [768], P(('dp', 'blk')), may hold values from -3 to 3
- rel_bias: bfloat16 [321, 12], replicated, may hold values from -4 to 4
Outputs:
- layer_out: float32 [8192, 768], P(('dp', 'blk'))
- frames_grad: float32 [8192, 768], P(('dp', 'blk'))
- qkv_weight_grad: float32 [768, 2304], P(None, ('dp', 'blk'))
- query_value_bias_grad: float32 [1536], P(('dp', 'blk'))
- out_weight_grad: float32 [768, 768], P(None, ('dp', 'blk'))
- out_bias_grad: float32 [768], P(('dp', 'blk'))
- up_weight_grad: float32 [768, 3072], P(None, ('dp', 'blk'))
- up_bias_grad: float32 [3072], P(('dp', 'blk'))
- down_weight_grad: float32 [3072, 768], P(None, ('dp', 'blk'))
- down_bias_grad: float32 [768], P(('dp', 'blk'))
- first_gain_grad: float32 [768], P(('dp', 'blk'))
- first_shift_grad: float32 [768], P(('dp', 'blk'))
- second_gain_grad: float32 [768], P(('dp', 'blk'))
- second_shift_grad: float32 [768], P(('dp', 'blk'))
- rel_bias_grad: float32 [321, 12], replicated
The draws below stay inside these ranges and needn't reach their ends.
Inputs may be any that keep to these rules, and one draw needn't show every extreme that they name: `seq_lengths`: in each row, the 4 lengths sum to 256 * 2; each row holds one sequence of exactly the largest length.
All inputs are finite; a program needn't handle non-finite values. No bound on the sum of `key_mask` on one device may be relied on, other than what follows from the above.
Results may differ from the reference program's by a relative error of at most 0.014.
Values may be sent and summed in bfloat16 or wider, within the bound.
No kernel may reach another device: no remote copies, remote signals or barrier semaphores. Data moves between devices by JAX's collectives and lax.ppermute only.
A program may use at most 192 MiB of HBM per device.

```python
import math
import jax
import jax.numpy as jnp
from jax import lax

D = 768
H = 12
HD = 64
FF = 3072
MAXREL = 160
TOK_DEV = 256
BLOCK = 256
NSEQ = 4
BUCKETS = 321
TOKENS = 8192
N_DP = 16
N_BLK = 2


def draw_seq_lengths(key, part):
    key = jax.random.fold_in(key, 11)
    low_len = max(1, TOK_DEV // 8)
    mean_len = TOK_DEV // 3
    swing = mean_len - low_len
    short_key, place_key = jax.random.split(key, 2)
    moved = jax.random.randint(short_key, (N_DP, 1), -swing, swing + 1)
    slots_short = jnp.arange(NSEQ - 1)[None, :]
    shorts = jnp.full((N_DP, NSEQ - 1), mean_len, jnp.int32)
    shorts = jnp.where(slots_short == 0, low_len, shorts)
    shorts = jnp.where(slots_short == 1, mean_len + moved, shorts)
    shorts = jnp.where(slots_short == NSEQ - 2, mean_len + swing - moved, shorts)
    longest = TOK_DEV * N_BLK - (NSEQ - 1) * mean_len
    place = jax.random.randint(place_key, (N_DP, 1), 0, NSEQ)
    slots = jnp.arange(NSEQ)[None, :]
    index = jnp.clip(slots - (slots > place).astype(jnp.int32), 0, NSEQ - 2)
    picked = jnp.take_along_axis(shorts, jnp.broadcast_to(index, (N_DP, NSEQ)), axis=1)
    return jnp.where(slots == place, longest, picked).astype(jnp.int32)


def plant(values, key, least, top_value):
    longest = values.shape.index(max(values.shape))
    spots = []
    for shift in (0, 1):
        where = [jax.random.randint(jax.random.fold_in(key, axis), (), 0, length) for axis, length in enumerate(values.shape)]
        where[longest] = (where[longest] + shift) % values.shape[longest]
        spots.append(tuple(where))
    return values.at[spots[0]].set(least).at[spots[1]].set(top_value)


def with_spikes(values, key, source, target, blocks, factor):
    def block_of(dim):
        return (jnp.arange(values.shape[dim]) // (values.shape[dim] // blocks)).reshape((-1,) + (1,) * (values.ndim - 1 - dim))

    one_side = jax.random.permutation(key, blocks)[block_of(target)]
    second = (block_of(target) + blocks // 2) % blocks
    return jnp.where((block_of(source) == one_side) | (block_of(source) == second), factor * values, values)


def level_of(key, extent, cuts, least, largest):
    level, own = 1.0, jax.random.fold_in(key, 6)
    for dim, parts in cuts:
        heights = jnp.exp(jax.random.uniform(jax.random.fold_in(own, dim), (parts,), jnp.float32, least / len(cuts), largest / len(cuts)))
        level = level * jnp.repeat(heights, extent[dim] // parts).reshape([-1 if axis == dim else 1 for axis in range(len(extent))])
    return level


def bell_draw(own_key, extent, scale, bound, cuts=(), kind=jnp.bfloat16):
    values = jax.random.normal(own_key, extent, jnp.float32) * scale
    if len(cuts) > 0:
        values = level_of(own_key, extent, cuts, -0.22, 0.18) * values
    return jnp.clip(values, min=-bound, max=bound).astype(kind)


def heavy_noise(stream_key, extent, scale, most, pieces, heavy, kind=jnp.bfloat16):
    values = scale * jax.random.normal(stream_key, extent, jnp.float32)
    if pieces:
        values = values * level_of(stream_key, extent, pieces, -0.22, 0.18)
    return jnp.clip(with_spikes(values, jax.random.fold_in(stream_key, 3), *heavy), -most, most).astype(kind)


def setup_inputs(seed: int = 0) -> dict:
    arg_keys = jax.random.split(jax.random.key(seed), 18)
    return {
        "frames": bell_draw(arg_keys[0], (TOKENS, D), 1.0, 6.0, ((0, 32),)),
        "cotangent": heavy_noise(arg_keys[1], (TOKENS, D), 1.0, 6.0, ((0, 32),), (0, 1, 32, 2.75)),
        "seq_lengths": draw_seq_lengths(jax.random.fold_in(arg_keys[17], 71), 0),
        "key_mask": plant((jax.random.randint(arg_keys[3], (TOKENS,), 0, 4) < 3).astype(jnp.int32), jax.random.fold_in(arg_keys[3], 1), 0, 1),
        "qkv_weight": bell_draw(arg_keys[4], (D, 3 * D), D ** -0.5, 0.21875, ((1, 32),)),
        "query_value_bias": bell_draw(arg_keys[5], (2 * D,), 0.5, 3.0, ((0, 32),)),
        "out_weight": bell_draw(arg_keys[6], (D, D), (D // 16) ** -0.5, 0.875, ((1, 32),)),
        "out_bias": bell_draw(arg_keys[7], (D,), 0.5, 3.0, ((0, 32),)),
        "up_weight": bell_draw(arg_keys[8], (D, FF), D ** -0.5, 0.21875, ((1, 32),)),
        "up_bias": bell_draw(arg_keys[9], (FF,), 0.5, 3.0, ((0, 32),)),
        "down_weight": bell_draw(arg_keys[10], (FF, D), FF ** -0.5, 0.109375, ((1, 32),)),
        "down_bias": bell_draw(arg_keys[11], (D,), 0.5, 3.0, ((0, 32),)),
        "first_gain": jnp.clip(1.0 + 0.1 * jax.random.normal(arg_keys[12], (D,), jnp.float32), 0.5, 1.5).astype(jnp.bfloat16),
        "first_shift": bell_draw(arg_keys[13], (D,), 0.5, 3.0, ((0, 32),)),
        "second_gain": jnp.clip(1.0 + 0.1 * jax.random.normal(arg_keys[14], (D,), jnp.float32), 0.5, 1.5).astype(jnp.bfloat16),
        "second_shift": bell_draw(arg_keys[15], (D,), 0.5, 3.0, ((0, 32),)),
        "rel_bias": bell_draw(arg_keys[16], (BUCKETS, H), 1.0, 4.0),
    }


@jax.custom_vjp
def low(v):
    return lax.optimization_barrier(v.astype(jnp.bfloat16)).astype(jnp.float32)

@jax.custom_vjp
def low_back(v):
    return v

def low_keep(v):
    return (low(v), None)

def low_pass(kept, grad):
    return (grad,)

def back_keep(v):
    return (v, None)

def back_low(kept, grad):
    return (low(grad),)
low.defvjp(low_keep, low_pass)
low_back.defvjp(back_keep, back_low)
EPSILON = 1e-05
MASKED = -2e+30
HIGHEST = lax.Precision.HIGHEST

def layer_norm(values, gain_vec, shift_vec):
    center = values - lax.optimization_barrier(jnp.mean(values, axis=-1, keepdims=True))
    spread = lax.optimization_barrier(jnp.mean(center * center, axis=-1, keepdims=True))
    return center * lax.rsqrt(spread + EPSILON) * gain_vec + shift_vec

def gelu_exact(values):
    return 0.5 * values * (1.0 + lax.erf(values * 0.7071067811865476))

def doc_numbers(seq_ends, positions):
    return lax.optimization_barrier(jnp.sum((positions[:, None] >= seq_ends[None, :]).astype(jnp.int32), axis=1)).astype(jnp.int32)

def layer(params, group_frames, group_docs, group_live):
    qkv_weight, query_value_bias, out_weight, out_bias, up_weight, up_bias, down_weight, down_bias, first_gain, first_shift, second_gain, second_shift, rel_bias = params
    width = group_frames.shape[1]
    length = group_frames.shape[0]
    positions = jnp.arange(length, dtype=jnp.int32)
    score_scale = 1.0 / math.sqrt(HD)
    normed = low(layer_norm(group_frames, first_gain, first_shift))
    projected = jnp.dot(normed, qkv_weight, precision=HIGHEST)
    queries = low(low_back(projected[:, :width] + query_value_bias[:width]))
    key_rows = low(low_back(projected[:, width:2 * width]))
    value_rows = low(low_back(projected[:, 2 * width:] + query_value_bias[width:]))
    key_heads = key_rows.reshape(length, H, HD)
    value_heads = value_rows.reshape(length, H, HD)

    def attend(block_start, query_all, key_all, value_all, table):
        query_block = lax.dynamic_slice_in_dim(query_all, block_start, BLOCK, 0).reshape(BLOCK, H, HD)
        query_pos = block_start + jnp.arange(BLOCK, dtype=jnp.int32)
        raw = jnp.einsum('qhd,khd->hqk', query_block, key_all, precision=HIGHEST)
        relative = jnp.clip(positions[None, :] - query_pos[:, None], -MAXREL, MAXREL) + MAXREL
        bias = jnp.transpose(table[relative], (2, 0, 1))
        query_doc = lax.dynamic_slice_in_dim(group_docs, block_start, BLOCK, 0)
        allowed = (query_doc[:, None] == group_docs[None, :]) & ((group_live[None, :] == 1) | (query_pos[:, None] == positions[None, :]))
        logits = jnp.where(allowed[None], low_back(raw) * score_scale + bias, MASKED)
        row_peak = lax.optimization_barrier(jnp.max(logits, axis=2, keepdims=True))
        exponent = jnp.exp(logits - row_peak)
        attn_prob = exponent / lax.optimization_barrier(jnp.sum(exponent, axis=2, keepdims=True))
        mixed = jnp.einsum('hqk,khd->qhd', low(attn_prob), value_all, precision=HIGHEST)
        return mixed.reshape(BLOCK, H * HD)
    checked = jax.checkpoint(attend)
    starts = jnp.arange(length // BLOCK, dtype=jnp.int32) * BLOCK
    attended = lax.map(lambda block_start: checked(block_start, queries, key_heads, value_heads, rel_bias), starts)
    context = low(low_back(attended.reshape(length, width)))
    branch = low_back(jnp.dot(context, out_weight, precision=HIGHEST) + out_bias)
    middle = group_frames + branch
    second = low(layer_norm(middle, second_gain, second_shift))
    hidden = low_back(jnp.dot(second, up_weight, precision=HIGHEST) + up_bias)
    active = low(gelu_exact(hidden))
    return middle + jnp.dot(active, down_weight, precision=HIGHEST) + down_bias

def reference(frames, cotangent, seq_lengths, key_mask, qkv_weight, query_value_bias, out_weight, out_bias, up_weight, up_bias, down_weight, down_bias, first_gain, first_shift, second_gain, second_shift, rel_bias):
    params = tuple((tensor.astype(jnp.float32) for tensor in (qkv_weight, query_value_bias, out_weight, out_bias, up_weight, up_bias, down_weight, down_bias, first_gain, first_shift, second_gain, second_shift, rel_bias)))
    group_size = TOK_DEV * N_BLK
    groups = frames.shape[0] // group_size
    width = frames.shape[1]
    frames_all = frames.astype(jnp.float32).reshape(groups, group_size, width)
    cotangents = cotangent.astype(jnp.float32).reshape(groups, group_size, width)
    live_all = key_mask.reshape(groups, group_size)
    ends_all = jnp.cumsum(seq_lengths, axis=1).astype(jnp.int32)
    positions = jnp.arange(group_size, dtype=jnp.int32)

    def one_group(totals, inputs):
        group_frames, group_cot, group_ends, group_live = inputs
        group_docs = doc_numbers(group_ends, positions)
        outputs, pullback = jax.vjp(lambda weights, values: layer(weights, values, group_docs, group_live), params, group_frames)
        weight_grads, frame_grads = pullback(group_cot)
        totals = jax.tree.map(lambda running, adding: running + adding, totals, weight_grads)
        return (totals, (outputs, frame_grads))
    zero_grads = jax.tree.map(jnp.zeros_like, params)
    totals, (outputs, frame_grads) = lax.scan(one_group, zero_grads, (frames_all, cotangents, ends_all, live_all))
    return (outputs.reshape(-1, width), frame_grads.reshape(-1, width), totals[0], totals[1], totals[2], totals[3], totals[4], totals[5], totals[6], totals[7], totals[8], totals[9], totals[10], totals[11], totals[12])
```

```python
import math

import jax
import jax.numpy as jnp
import numpy as np
from jax import lax
from jax.experimental import pallas as pl
from jax.experimental.pallas import tpu as pltpu
from jax.sharding import PartitionSpec as P

H = 12
HD = 64
MAXREL = 160
BLOCK = 256
BUCKETS = 321


EPSILON = 1e-05
MASKED = -2e30
START_PEAK = -1e30
HIGHEST = lax.Precision.HIGHEST


def from_behind(block, axis, distance):
    devices = range(lax.axis_size(axis))
    route = [((i - distance) % len(devices), i) for i in devices]
    return lax.ppermute(block, axis, route)


def layer_norm(values, gain_vec, shift_vec):
    center = values - jnp.mean(values, axis=-1, keepdims=True)
    inv_std = lax.rsqrt(jnp.mean(center * center, axis=-1, keepdims=True) + EPSILON)
    normed = center * inv_std
    return (normed * gain_vec + shift_vec, normed, inv_std)


def norm_back(gradient, normed, inv_std, gain_vec):
    scaled = gradient * gain_vec
    inner = (
        scaled
        - jnp.mean(scaled, axis=-1, keepdims=True)
        - normed * jnp.mean(scaled * normed, axis=-1, keepdims=True)
    )
    return (inner * inv_std, jnp.sum(gradient * normed, axis=0), jnp.sum(gradient, axis=0))


def gelu_parts(values):
    normal_cdf = 0.5 * (1.0 + lax.erf(values * 0.7071067811865476))
    density = jnp.exp(-0.5 * values * values) * 0.3989422804014327
    return (values * normal_cdf, normal_cdf + values * density)


def doc_numbers(seq_ends, positions):
    return jnp.sum((positions[:, None] >= seq_ends[None, :]).astype(jnp.int32), axis=1)


def pair_logits(
    query_block, key_block, query_pos, key_pos, query_doc, key_doc, key_live, table_heads
):
    block_len = query_block.shape[0]
    raw = jnp.einsum(
        "qhd,khd->hqk",
        query_block.reshape(block_len, H, HD),
        key_block.reshape(-1, H, HD),
        preferred_element_type=jnp.float32,
    )
    relative = jnp.clip(key_pos[None, :] - query_pos[:, None], -MAXREL, MAXREL) + MAXREL
    bias = jnp.take(table_heads, relative, axis=1)
    allowed = (query_doc[:, None] == key_doc[None, :]) & (
        (key_live[None, :] > 0.5) | (query_pos[:, None] == key_pos[None, :])
    )
    return jnp.where(allowed[None], raw * (1.0 / math.sqrt(HD)) + bias, MASKED)


def diagonal_sums(gradient, offset):
    heads, block_len, _ = gradient.shape
    flipped = gradient[:, ::-1, :]
    padded = jnp.pad(flipped, ((0, 0), (0, 0), (0, block_len)))
    sheared = padded.reshape(heads, 2 * block_len * block_len)[:, : block_len * (2 * block_len - 1)]
    sheared = sheared.reshape(heads, block_len, 2 * block_len - 1)
    diag_sums = jnp.sum(sheared, axis=1)
    distance = offset + jnp.arange(2 * block_len - 1, dtype=jnp.int32) - (block_len - 1)
    bucket = jnp.clip(distance, -MAXREL, MAXREL) + MAXREL
    onehot = (bucket[:, None] == jnp.arange(BUCKETS, dtype=jnp.int32)[None, :]).astype(jnp.float32)
    return jnp.dot(diag_sums, onehot, precision=HIGHEST)


def body(
    frames,
    cotangent,
    seq_lengths,
    key_mask,
    qkv_weight,
    query_value_bias,
    out_weight,
    out_bias,
    up_weight,
    up_bias,
    down_weight,
    down_bias,
    first_gain,
    first_shift,
    second_gain,
    second_shift,
    rel_bias,
):
    cycle_size = lax.axis_size("blk")
    cycle_place = lax.axis_index("blk")
    shard_len = frames.shape[0]
    width = frames.shape[1]
    block_count = shard_len // BLOCK
    score_scale = 1.0 / math.sqrt(HD)
    seq_ends = jnp.cumsum(seq_lengths[0])
    local_pos = jnp.arange(shard_len, dtype=jnp.int32)
    positions = cycle_place * shard_len + local_pos
    own_docs = doc_numbers(seq_ends, positions)
    table_heads = rel_bias.astype(jnp.float32).T

    def blocked(array):
        return array.reshape((block_count, BLOCK) + array.shape[1:])

    def key_meta(turn):
        source = (cycle_place - turn) % cycle_size
        key_pos = source * shard_len + local_pos
        return (key_pos, doc_numbers(seq_ends, key_pos))

    gathered = (
        lax.all_gather(qkv_weight, ("dp", "blk"), axis=1, tiled=True),
        lax.all_gather(query_value_bias, ("dp", "blk"), axis=0, tiled=True),
        lax.all_gather(out_weight, ("dp", "blk"), axis=1, tiled=True),
        lax.all_gather(out_bias, ("dp", "blk"), axis=0, tiled=True),
        lax.all_gather(up_weight, ("dp", "blk"), axis=1, tiled=True),
        lax.all_gather(up_bias, ("dp", "blk"), axis=0, tiled=True),
        lax.all_gather(down_weight, ("dp", "blk"), axis=1, tiled=True),
        lax.all_gather(down_bias, ("dp", "blk"), axis=0, tiled=True),
        lax.all_gather(first_gain, ("dp", "blk"), axis=0, tiled=True),
        lax.all_gather(first_shift, ("dp", "blk"), axis=0, tiled=True),
        lax.all_gather(second_gain, ("dp", "blk"), axis=0, tiled=True),
        lax.all_gather(second_shift, ("dp", "blk"), axis=0, tiled=True),
    )
    (
        qkv_full,
        qv_bias_full,
        out_full,
        out_bias_full,
        up_full,
        up_bias_full,
        down_full,
        down_bias_full,
        gain_one,
        shift_one,
        gain_two,
        shift_two,
    ) = gathered
    frames_wide = frames.astype(jnp.float32)
    first_out, first_normed, first_inv = layer_norm(
        frames_wide, gain_one.astype(jnp.float32), shift_one.astype(jnp.float32)
    )
    first_low = first_out.astype(jnp.bfloat16)
    projected = jnp.dot(first_low, qkv_full, preferred_element_type=jnp.float32)
    bias_vec = qv_bias_full.astype(jnp.float32)
    queries = (projected[:, :width] + bias_vec[:width]).astype(jnp.bfloat16)
    key_rows = projected[:, width : 2 * width].astype(jnp.bfloat16)
    value_rows = (projected[:, 2 * width :] + bias_vec[width:]).astype(jnp.bfloat16)
    live_rows = key_mask.astype(jnp.bfloat16)
    query_blocks = (blocked(queries), blocked(positions), blocked(own_docs))

    def forward_hop(turn, online_state, key_part, value_part, live_part):
        key_pos, key_doc = key_meta(turn)
        key_items = (
            blocked(key_part),
            blocked(value_part),
            blocked(key_pos),
            blocked(key_doc),
            blocked(live_part),
        )

        def forward_per_query(query_items):
            query_block, query_pos, query_doc, row_peak, row_total, accum = query_items

            def online(carried, key_block_items):
                row_peak, row_total, accum = carried
                key_block, value_block, key_bpos, key_bdoc, key_blive = key_block_items
                logits = pair_logits(
                    query_block,
                    key_block,
                    query_pos,
                    key_bpos,
                    query_doc,
                    key_bdoc,
                    key_blive,
                    table_heads,
                )
                new_peak = jnp.maximum(row_peak, jnp.max(logits, axis=2))
                decay = jnp.exp(row_peak - new_peak)
                weights = jnp.exp(logits - new_peak[:, :, None])
                row_total = row_total * decay + jnp.sum(weights, axis=2)
                accum = accum * decay.T[:, :, None] + jnp.einsum(
                    "hqk,khd->qhd",
                    weights.astype(jnp.bfloat16),
                    value_block.reshape(-1, H, HD),
                    preferred_element_type=jnp.float32,
                )
                return ((new_peak, row_total, accum), None)

            result, unused = lax.scan(online, (row_peak, row_total, accum), key_items)
            return result

        return lax.map(forward_per_query, query_blocks + online_state)

    def cycle_turn(turn, carried):
        online_state, key_part, value_part, live_part = carried
        online_state = forward_hop(turn, online_state, key_part, value_part, live_part)
        key_part, value_part, live_part = from_behind((key_part, value_part, live_part), "blk", 1)
        return (online_state, key_part, value_part, live_part)

    start_state = (
        jnp.full((block_count, H, BLOCK), START_PEAK, jnp.float32),
        jnp.zeros((block_count, H, BLOCK), jnp.float32),
        jnp.zeros((block_count, BLOCK, H, HD), jnp.float32),
    )
    carried = lax.fori_loop(
        0, cycle_size - 1, cycle_turn, (start_state, key_rows, value_rows, live_rows)
    )
    row_peak, row_total, accum = forward_hop(
        cycle_size - 1, carried[0], carried[1], carried[2], carried[3]
    )
    mixed = accum / jnp.transpose(row_total, (0, 2, 1))[:, :, :, None]
    mixed_flat = mixed.reshape(shard_len, width)
    context = mixed_flat.astype(jnp.bfloat16)
    branch = jnp.dot(context, out_full, preferred_element_type=jnp.float32) + out_bias_full.astype(
        jnp.float32
    )
    middle = frames_wide + branch
    second_out, second_normed, second_inv = layer_norm(
        middle, gain_two.astype(jnp.float32), shift_two.astype(jnp.float32)
    )
    second_low = second_out.astype(jnp.bfloat16)
    hidden = jnp.dot(second_low, up_full, preferred_element_type=jnp.float32) + up_bias_full.astype(
        jnp.float32
    )
    active, slope = gelu_parts(hidden)
    active_low = active.astype(jnp.bfloat16)
    layer_out = (
        middle
        + jnp.dot(active_low, down_full, preferred_element_type=jnp.float32)
        + down_bias_full.astype(jnp.float32)
    )
    weights_back = (
        lax.all_gather(qkv_weight, ("dp", "blk"), axis=1, tiled=True),
        lax.all_gather(query_value_bias, ("dp", "blk"), axis=0, tiled=True),
        lax.all_gather(out_weight, ("dp", "blk"), axis=1, tiled=True),
        lax.all_gather(out_bias, ("dp", "blk"), axis=0, tiled=True),
        lax.all_gather(up_weight, ("dp", "blk"), axis=1, tiled=True),
        lax.all_gather(up_bias, ("dp", "blk"), axis=0, tiled=True),
        lax.all_gather(down_weight, ("dp", "blk"), axis=1, tiled=True),
        lax.all_gather(down_bias, ("dp", "blk"), axis=0, tiled=True),
        lax.all_gather(first_gain, ("dp", "blk"), axis=0, tiled=True),
        lax.all_gather(first_shift, ("dp", "blk"), axis=0, tiled=True),
        lax.all_gather(second_gain, ("dp", "blk"), axis=0, tiled=True),
        lax.all_gather(second_shift, ("dp", "blk"), axis=0, tiled=True),
    )
    qkv_back = weights_back[0]
    out_back = weights_back[2]
    up_back = weights_back[4]
    down_back = weights_back[6]
    gain_one_back = weights_back[8].astype(jnp.float32)
    gain_two_back = weights_back[10].astype(jnp.float32)
    grad_wide = cotangent.astype(jnp.float32)
    down_grad = jnp.einsum("tf,td->fd", active_low, cotangent, preferred_element_type=jnp.float32)
    down_bias_grad = jnp.sum(grad_wide, axis=0)
    active_grad = jnp.einsum("td,fd->tf", cotangent, down_back, preferred_element_type=jnp.float32)
    hidden_low = (active_grad * slope).astype(jnp.bfloat16)
    up_grad = jnp.einsum("td,tf->df", second_low, hidden_low, preferred_element_type=jnp.float32)
    up_bias_grad = jnp.sum(hidden_low.astype(jnp.float32), axis=0)
    second_grad = jnp.einsum("tf,df->td", hidden_low, up_back, preferred_element_type=jnp.float32)
    middle_norm, gain_two_grad, shift_two_grad = norm_back(
        second_grad, second_normed, second_inv, gain_two_back
    )
    middle_grad = grad_wide + middle_norm
    branch_low = middle_grad.astype(jnp.bfloat16)
    out_grad = jnp.einsum("td,te->de", context, branch_low, preferred_element_type=jnp.float32)
    out_bias_grad = jnp.sum(branch_low.astype(jnp.float32), axis=0)
    context_low = jnp.einsum(
        "te,de->td", branch_low, out_back, preferred_element_type=jnp.float32
    ).astype(jnp.bfloat16)
    delta = jnp.sum(
        (context_low.astype(jnp.float32) * mixed_flat).reshape(shard_len, H, HD), axis=2
    )
    delta_blocks = jnp.transpose(blocked(delta), (0, 2, 1))
    query_back = (
        blocked(queries),
        blocked(context_low),
        blocked(positions),
        blocked(own_docs),
        row_peak,
        row_total,
        delta_blocks,
    )

    def backward_hop(
        turn, query_grad, table_grad, key_part, value_part, live_part, key_grad, value_grad
    ):
        key_pos, key_doc = key_meta(turn)

        def per_key(carried, key_block_items):
            query_grad, table_grad = carried
            key_block, value_block, key_bpos, key_bdoc, key_blive, key_bgrad, value_bgrad = (
                key_block_items
            )
            key_heads = key_block.reshape(-1, H, HD)
            value_heads = value_block.reshape(-1, H, HD)

            def per_per_query(inner, query_items):
                key_bgrad, value_bgrad, table_grad = inner
                (
                    query_block,
                    dout_block,
                    query_pos,
                    query_doc,
                    peak_block,
                    total_block,
                    delta_block,
                ) = query_items
                logits = pair_logits(
                    query_block,
                    key_block,
                    query_pos,
                    key_bpos,
                    query_doc,
                    key_bdoc,
                    key_blive,
                    table_heads,
                )
                attn_prob = jnp.exp(logits - peak_block[:, :, None]) / total_block[:, :, None]
                dout_heads = dout_block.reshape(-1, H, HD)
                prob_grad = jnp.einsum(
                    "qhd,khd->hqk", dout_heads, value_heads, preferred_element_type=jnp.float32
                )
                logit_grad = attn_prob * (prob_grad - delta_block[:, :, None])
                raw_low = (logit_grad * score_scale).astype(jnp.bfloat16)
                query_part = jnp.einsum(
                    "hqk,khd->qhd", raw_low, key_heads, preferred_element_type=jnp.float32
                ).reshape(-1, width)
                key_bgrad = key_bgrad + jnp.einsum(
                    "hqk,qhd->khd",
                    raw_low,
                    query_block.reshape(-1, H, HD),
                    preferred_element_type=jnp.float32,
                ).reshape(-1, width)
                value_bgrad = value_bgrad + jnp.einsum(
                    "hqk,qhd->khd",
                    attn_prob.astype(jnp.bfloat16),
                    dout_heads,
                    preferred_element_type=jnp.float32,
                ).reshape(-1, width)
                table_grad = table_grad + diagonal_sums(logit_grad, key_bpos[0] - query_pos[0])
                return ((key_bgrad, value_bgrad, table_grad), query_part)

            (key_bgrad, value_bgrad, table_grad), query_parts = lax.scan(
                per_per_query, (key_bgrad, value_bgrad, table_grad), query_back
            )
            return ((query_grad + query_parts, table_grad), (key_bgrad, value_bgrad))

        (query_grad, table_grad), (key_new, value_new) = lax.scan(
            per_key,
            (query_grad, table_grad),
            (
                blocked(key_part),
                blocked(value_part),
                blocked(key_pos),
                blocked(key_doc),
                blocked(live_part),
                blocked(key_grad),
                blocked(value_grad),
            ),
        )
        return (
            query_grad,
            table_grad,
            key_new.reshape(shard_len, width),
            value_new.reshape(shard_len, width),
        )

    def pass_grads(key_grad, value_grad):
        return (
            from_behind(key_grad.astype(jnp.bfloat16), "blk", 1).astype(key_grad.dtype),
            from_behind(value_grad.astype(jnp.bfloat16), "blk", 1).astype(value_grad.dtype),
        )

    def back_turn(turn, carried):
        query_grad, table_grad, key_part, value_part, live_part, key_grad, value_grad = carried
        query_grad, table_grad, key_grad, value_grad = backward_hop(
            turn, query_grad, table_grad, key_part, value_part, live_part, key_grad, value_grad
        )
        key_part, value_part, live_part = from_behind((key_part, value_part, live_part), "blk", 1)
        key_grad, value_grad = pass_grads(key_grad, value_grad)
        return (query_grad, table_grad, key_part, value_part, live_part, key_grad, value_grad)

    zero_rows = jnp.zeros((shard_len, width), jnp.float32)
    back_start = (
        jnp.zeros((block_count, BLOCK, width), jnp.float32),
        jnp.zeros((H, BUCKETS), jnp.float32),
        key_rows,
        value_rows,
        live_rows,
        zero_rows,
        zero_rows,
    )
    carried = lax.fori_loop(0, cycle_size - 1, back_turn, back_start)
    query_grad, table_grad, key_grad, value_grad = backward_hop(
        cycle_size - 1,
        carried[0],
        carried[1],
        carried[2],
        carried[3],
        carried[4],
        carried[5],
        carried[6],
    )
    key_grad, value_grad = pass_grads(key_grad, value_grad)
    query_low = query_grad.reshape(shard_len, width).astype(jnp.bfloat16)
    key_low = key_grad.astype(jnp.bfloat16)
    value_low = value_grad.astype(jnp.bfloat16)
    qkv_low = jnp.concatenate([query_low, key_low, value_low], axis=1)
    qkv_grad = jnp.einsum("td,te->de", first_low, qkv_low, preferred_element_type=jnp.float32)
    query_value_grad = jnp.concatenate(
        [
            jnp.sum(query_low.astype(jnp.float32), axis=0),
            jnp.sum(value_low.astype(jnp.float32), axis=0),
        ]
    )
    first_grad = jnp.einsum("te,de->td", qkv_low, qkv_back, preferred_element_type=jnp.float32)
    frames_norm, gain_one_grad, shift_one_grad = norm_back(
        first_grad, first_normed, first_inv, gain_one_back
    )
    frames_grad = middle_grad + frames_norm
    summed = (
        lax.psum_scatter(qkv_grad, ("dp", "blk"), scatter_dimension=1, tiled=True),
        lax.psum_scatter(query_value_grad, ("dp", "blk"), scatter_dimension=0, tiled=True),
        lax.psum_scatter(out_grad, ("dp", "blk"), scatter_dimension=1, tiled=True),
        lax.psum_scatter(out_bias_grad, ("dp", "blk"), scatter_dimension=0, tiled=True),
        lax.psum_scatter(up_grad, ("dp", "blk"), scatter_dimension=1, tiled=True),
        lax.psum_scatter(up_bias_grad, ("dp", "blk"), scatter_dimension=0, tiled=True),
        lax.psum_scatter(down_grad, ("dp", "blk"), scatter_dimension=1, tiled=True),
        lax.psum_scatter(down_bias_grad, ("dp", "blk"), scatter_dimension=0, tiled=True),
        lax.psum_scatter(gain_one_grad, ("dp", "blk"), scatter_dimension=0, tiled=True),
        lax.psum_scatter(shift_one_grad, ("dp", "blk"), scatter_dimension=0, tiled=True),
        lax.psum_scatter(gain_two_grad, ("dp", "blk"), scatter_dimension=0, tiled=True),
        lax.psum_scatter(shift_two_grad, ("dp", "blk"), scatter_dimension=0, tiled=True),
    )
    table_sum = lax.psum(table_grad, ("dp", "blk"))
    return (
        layer_out,
        frames_grad,
        summed[0],
        summed[1],
        summed[2],
        summed[3],
        summed[4],
        summed[5],
        summed[6],
        summed[7],
        summed[8],
        summed[9],
        summed[10],
        summed[11],
        table_sum.T,
    )


AXES = ("dp", "blk")
VMEM_BYTES = 56 * 1024 * 1024
F32 = jnp.float32
LOW = jnp.bfloat16
LANES = 128
NARROW = 6
PAD = 8


def route(move):
    n_dp, n_blk = lax.axis_size("dp"), lax.axis_size("blk")
    pairs = []
    for d in range(n_dp):
        d_bits, b_bits = move[d % 2]
        for b in range(n_blk):
            pairs.append((d * n_blk + b, (d ^ d_bits) * n_blk + (b ^ b_bits)))
    return pairs


def shift(array, move):
    return lax.ppermute(array, AXES, route(move))


CORE = ((1, 0), (1, 0))
SIDE = ((0, 1), (2, 0))
OTHER_SIDE = ((2, 0), (0, 1))
PACK = ((0, 1), (0, 1))
NEAR_Z = ((4, 0), (8, 0))
FAR_Z = ((12, 0), (12, 0))


def gather_units(unit, core):
    first = core == 0
    twin = shift(unit, CORE)
    far = shift(unit, FAR_Z)
    both = jnp.where(first, jnp.stack([unit, twin]), jnp.stack([twin, unit]))
    near = shift(both, NEAR_Z)
    far_twin = shift(far, CORE)
    near_twin = shift(near, CORE)
    column = jnp.where(
        first,
        jnp.stack([both, near, near_twin, jnp.stack([far, far_twin])], axis=1),
        jnp.stack([both, near_twin, near, jnp.stack([far_twin, far])], axis=1),
    )
    side = shift(column, SIDE)
    corner = shift(lax.dynamic_index_in_dim(side, core, 0, keepdims=False), OTHER_SIDE)
    return (column, side, shift(side, CORE), corner, shift(corner, CORE))


def scatter_units(parts, core):
    corner_send, corner_keep, side_send, side_keep, own = parts
    corner_got = shift(corner_send, CORE)
    side_got = shift(side_send, CORE)
    corner = (corner_keep.astype(F32) + corner_got.astype(F32)).astype(LOW)
    turned = shift(corner, OTHER_SIDE)
    plane = (jnp.arange(2) == core)[:, None, None, None]
    side = (
        side_keep.astype(F32)
        + side_got.astype(F32)
        + jnp.where(plane, turned[None].astype(F32), 0.0)
    ).astype(LOW)
    column = (own.astype(F32) + shift(side, SIDE).astype(F32)).astype(LOW)
    of_first = jnp.stack([column[0, 1], column[1, 1], column[0, 3], column[0, 0]])
    of_second = jnp.stack([column[0, 2], column[1, 2], column[1, 3], column[1, 0]])
    first = core == 0
    got = shift(jnp.where(first, of_second, of_first), CORE)
    total = jnp.where(first, of_first, of_second).astype(F32) + got.astype(F32)
    total_low = total.astype(LOW)
    near = shift(total_low[:2], NEAR_Z)
    far = shift(total_low[2], FAR_Z)
    near_twin = shift(lax.dynamic_index_in_dim(near, 1 - core, 0, keepdims=False), CORE)
    near_own = lax.dynamic_index_in_dim(near, core, 0, keepdims=False)
    return total[3] + near_own.astype(F32) + far.astype(F32) + near_twin.astype(F32)


def unit_of(place, x_turn, y_turn, z_turn, c):
    x, y, z = place[0] ^ x_turn, place[1] ^ y_turn, place[2] ^ z_turn
    return ((z * 2 + y) * 2 + c) * 2 + x


def gathered_copies(place, pieces):
    column, side, side_twin, corner, corner_twin = pieces
    c0 = place[3]
    found = []
    for z in range(4):
        for c in range(2):
            found.append((column.at[c, z], unit_of(place, 0, 0, z, c)))
            found.append((side.at[c, z], unit_of(place, 1 - c0, c0, z, c)))
            found.append((side_twin.at[c, z], unit_of(place, c0, 1 - c0, z, c)))
        found.append((corner.at[z], unit_of(place, 1, 1, z, c0)))
        found.append((corner_twin.at[z], unit_of(place, 1, 1, z, 1 - c0)))
    return found


def scattered_copies(place, parts):
    corner_send, corner_keep, side_send, side_keep, own = parts
    c0 = place[3]
    found = []
    for z in range(4):
        for c in range(2):
            found.append((own.at[c, z], unit_of(place, 0, 0, z, c)))
            found.append((side_keep.at[c, z], unit_of(place, 1 - c0, c0, z, c)))
            found.append((side_send.at[c, z], unit_of(place, c0, 1 - c0, z, c)))
        found.append((corner_keep.at[z], unit_of(place, 1, 1, z, c0)))
        found.append((corner_send.at[z], unit_of(place, 1, 1, z, 1 - c0)))
    return found


def load_units(place, pieces, stage, sems):
    copies = [
        pltpu.make_async_copy(ref, stage.at[unit], sems.at[n])
        for n, (ref, unit) in enumerate(gathered_copies(place, pieces))
    ]
    for copy in copies:
        copy.start()
    return copies


def store_units(place, stage, parts, sems):
    copies = [
        pltpu.make_async_copy(stage.at[unit], ref, sems.at[n])
        for n, (ref, unit) in enumerate(scattered_copies(place, parts))
    ]
    for copy in copies:
        copy.start()
    for copy in copies:
        copy.wait()


def part_shapes(rows, width):
    quarter = jax.ShapeDtypeStruct((4, rows, width), LOW)
    half = jax.ShapeDtypeStruct((2, 4, rows, width), LOW)
    return [quarter, quarter, half, half, half]


def dot_nn(a, b):
    return lax.dot_general(a, b, (((1,), (0,)), ((), ())), preferred_element_type=F32)


def dot_nt(a, b):
    return lax.dot_general(a, b, (((1,), (1,)), ((), ())), preferred_element_type=F32)


def dot_tn(a, b):
    return lax.dot_general(a, b, (((0,), (0,)), ((), ())), preferred_element_type=F32)


ANY = pl.BlockSpec(memory_space=pl.ANY)
SMEM = pl.BlockSpec(memory_space=pltpu.SMEM)
VMEM = pl.BlockSpec(memory_space=pltpu.VMEM)


def call(kernel, in_specs, outs, out_specs, scratch, args, flops, **kwargs):
    moved = sum(math.prod(a.shape) * a.dtype.itemsize for a in list(args) + list(outs))
    return pl.pallas_call(
        kernel,
        out_shape=outs,
        in_specs=in_specs,
        out_specs=out_specs,
        scratch_shapes=scratch,
        compiler_params=pltpu.CompilerParams(vmem_limit_bytes=VMEM_BYTES),
        cost_estimate=pl.CostEstimate(flops=flops, bytes_accessed=moved, transcendentals=0),
        **kwargs,
    )(*args)


def spread_tables(units, width):
    tables = []
    for n in (width // units, 2 * width // units, 4 * width // units):
        lane = np.arange(units * n)
        keep = lane[None, :] // n == np.arange(units)[:, None]
        pick = lane[None, :] % n == np.arange(LANES)[:, None]
        tables.append(jnp.asarray(np.concatenate([keep, pick]), LOW))
    return tables


def project_kernel(
    place, own, mate, column, side, side_twin, corner, corner_twin, wide_one, wide_two, wide_four,
    first, queries, keys, values, weight, vectors, up_bias, stage, small, sems,
):
    units = stage.shape[0]
    width = own.shape[1]
    rows = stage.shape[1] - PAD
    shard_len = own.shape[0]
    copies = load_units(place, (column, side, side_twin, corner, corner_twin), stage, sems)

    def normed(frames):
        wide = frames.astype(F32)
        center = wide - jnp.mean(wide, axis=1, keepdims=True)
        return center * lax.rsqrt(jnp.mean(center * center, axis=1, keepdims=True) + EPSILON)

    own_normed, mate_normed = normed(own[...]), normed(mate[...])
    for copy in copies:
        copy.wait()
    for unit in range(units):
        top = stage[unit, rows : rows + PAD, :].astype(F32)
        small[0, unit : unit + 1, :] = top[0:1]
        small[1, unit : unit + 1, :] = top[1:2]

    def spread(row, slot, table):
        held = small[row, :, slot * LANES : (slot + 1) * LANES].astype(LOW)
        laid = dot_nn(held, table[units:, :]) * table[:units, :].astype(F32)
        return jnp.sum(laid, axis=0, keepdims=True)

    for n in range(NARROW):
        vectors[n : n + 1, :] = spread(0, n, wide_one)
    qv_bias = spread(1, 0, wide_two)
    up_bias[...] = jnp.broadcast_to(spread(1, 1, wide_four), up_bias.shape)
    vectors[NARROW : NARROW + 1, :] = qv_bias[:, :width]
    vectors[NARROW + 1 : NARROW + 2, :] = qv_bias[:, width:]
    for pair in range(units // 2):
        joined = jnp.concatenate(
            [stage[2 * pair, :rows, :].astype(F32), stage[2 * pair + 1, :rows, :].astype(F32)], axis=0
        )
        weight[2 * rows * pair : 2 * rows * (pair + 1), :] = joined.astype(LOW)
    gain, offset = vectors[0:1, :], vectors[1:2, :]
    x = place[0]
    own_at = pl.multiple_of(x * shard_len, shard_len)
    mate_at = pl.multiple_of((1 - x) * shard_len, shard_len)
    first[pl.ds(own_at, shard_len), :] = (own_normed * gain + offset).astype(LOW)
    first[pl.ds(mate_at, shard_len), :] = (mate_normed * gain + offset).astype(LOW)
    mine = first[pl.ds(own_at, shard_len), :]
    queries[...] = (dot_nt(mine, weight[:width, :]) + vectors[NARROW : NARROW + 1, :]).astype(LOW)
    keys[...] = dot_nt(first[...], weight[width : 2 * width, :]).astype(LOW)
    values[...] = (
        dot_nt(first[...], weight[2 * width :, :]) + vectors[NARROW + 1 : NARROW + 2, :]
    ).astype(LOW)


def half_mask(shape, head):
    return (lax.broadcasted_iota(jnp.int32, shape, 1) // HD) == head


def attend_kernel(place, queries, keys, values, curve, hidden_pairs, probs, mixed):
    q, k, v = queries[...], keys[...], values[...]
    block_len, span = hidden_pairs.shape
    total = jnp.zeros(q.shape, F32)
    for head in range(2):
        q_head = jnp.where(half_mask(q.shape, head), q, 0) * (1.0 / math.sqrt(HD))
        bias = pltpu.roll(
            jnp.broadcast_to(curve[0, head : head + 1, :], (block_len, block_len + span)),
            span + 1, 1, stride=1, stride_axis=0,
        )[:, :span]
        logits = dot_nt(q_head.astype(LOW), k) + bias + hidden_pairs[...]
        weights = jnp.exp(logits - jnp.max(logits, axis=1, keepdims=True))
        prob = (weights * (1.0 / jnp.sum(weights, axis=1, keepdims=True))).astype(LOW)
        probs[head] = prob
        total = total + dot_nn(prob, jnp.where(half_mask(v.shape, head), v, 0))
    mixed[...] = total


def expand_kernel(
    place, frames, mixed, vectors, up_bias, column, side, side_twin, corner, corner_twin,
    middle, second, active, slope, context, up, out, stage, sems, out_sems,
):
    units, kept, width = stage.shape
    rows = column.shape[2] - kept
    found = gathered_copies(place, (column, side, side_twin, corner, corner_twin))
    copies = []
    for n, (ref, unit) in enumerate(found):
        at = pl.multiple_of(unit * rows, rows)
        copies.append(pltpu.make_async_copy(ref.at[:rows], up.at[pl.ds(at, rows)], sems.at[n]))
        copies.append(pltpu.make_async_copy(ref.at[rows:], stage.at[unit], out_sems.at[n]))
    for copy in copies:
        copy.start()
    for copy in copies:
        copy.wait()
    each = width // units
    for pair in range(units // 2):
        joined = jnp.concatenate(
            [stage[2 * pair].astype(F32)[:each], stage[2 * pair + 1].astype(F32)[:each]], axis=0
        )
        out[2 * each * pair : 2 * each * (pair + 1), :] = joined.astype(LOW)
    context[...] = mixed[...].astype(LOW)
    mid = frames[...].astype(F32) + (dot_nt(context[...], out[...]) + vectors[4:5, :])
    middle[...] = mid
    center = mid - jnp.mean(mid, axis=1, keepdims=True)
    normed = center * lax.rsqrt(jnp.mean(center * center, axis=1, keepdims=True) + EPSILON)
    second[...] = (normed * vectors[2:3, :] + vectors[3:4, :]).astype(LOW)
    tile = 2 * LANES

    @pl.loop(0, up.shape[0] // tile)
    def _(n):
        at = pl.multiple_of(n * tile, tile)
        hidden = dot_nt(second[...], up[pl.ds(at, tile), :]) + up_bias[0:1, pl.ds(at, tile)]
        cdf = 0.5 * (1.0 + lax.erf(hidden * 0.7071067811865476))
        density = jnp.exp(-0.5 * hidden * hidden) * 0.3989422804014327
        active[:, pl.ds(at, tile)] = (hidden * cdf).astype(LOW)
        slope[:, pl.ds(at, tile)] = cdf + hidden * density


def down_grad_kernel(
    place, active, cotangent, corner_send, corner_keep, side_send, side_keep, own, bias_grad, stage, sems
):
    units, rows, width = stage.shape
    each = width // units
    folds = rows // each
    dy = cotangent[...]
    bias_grad[...] = jnp.broadcast_to(
        jnp.sum(dy.astype(F32), axis=0, keepdims=True), bias_grad.shape
    )
    group = 2 * LANES // each if 2 * LANES % each == 0 else 8
    for start in range(0, units, group):
        lane = slice(start * each, (start + group) * each)
        grads = [
            dot_tn(dy[:, lane], active[:, fold * width : (fold + 1) * width]) for fold in range(folds)
        ]
        for n in range(group):
            stage[start + n] = jnp.concatenate(
                [grad[n * each : (n + 1) * each] for grad in grads], axis=0
            ).astype(LOW)
    store_units(place, stage, (corner_send, corner_keep, side_send, side_keep, own), sems)


def back_kernel(
    place, cotangent, slope, second, middle, context, vectors, up, out,
    column, side, side_twin, corner, corner_twin,
    corner_send, corner_keep, side_send, side_keep, own,
    down, middle_grad, context_grad, vector_grads, up_bias_grad,
    stage, hidden_grad, out_stage, up_stage, sems,
):
    units, rows, width = stage.shape
    each = width // units
    folds = rows // each
    shard_len = cotangent.shape[0]
    copies = load_units(place, (column, side, side_twin, corner, corner_twin), stage, sems)
    for copy in copies:
        copy.wait()
    for pair in range(units // 2):
        one, two = stage[2 * pair].astype(F32), stage[2 * pair + 1].astype(F32)
        for fold in range(folds):
            joined = jnp.concatenate(
                [one[fold * each : (fold + 1) * each], two[fold * each : (fold + 1) * each]], axis=0
            )
            down[2 * each * pair : 2 * each * (pair + 1), fold * width : (fold + 1) * width] = (
                joined.astype(LOW)
            )
    dy = cotangent[...]
    tile = 2 * LANES
    up_rows = up.shape[0] // units
    second_grad = jnp.zeros((shard_len, width), F32)
    for n in range(up.shape[0] // tile):
        at = slice(n * tile, (n + 1) * tile)
        grad = (dot_nn(dy, down[:, at]) * slope[:, at]).astype(LOW)
        hidden_grad[:, at] = grad
        up_bias_grad[:, at] = jnp.broadcast_to(
            jnp.sum(grad.astype(F32), axis=0, keepdims=True), (up_bias_grad.shape[0], tile)
        )
        second_grad = second_grad + dot_nn(grad, up[at, :])
    mid = middle[...]
    center = mid - jnp.mean(mid, axis=1, keepdims=True)
    inv_std = lax.rsqrt(jnp.mean(center * center, axis=1, keepdims=True) + EPSILON)
    normed = center * inv_std
    scaled = second_grad * vectors[2:3, :]
    inner = (
        scaled
        - jnp.mean(scaled, axis=1, keepdims=True)
        - normed * jnp.mean(scaled * normed, axis=1, keepdims=True)
    )
    mid_grad = dy.astype(F32) + inner * inv_std
    middle_grad[...] = mid_grad
    branch = mid_grad.astype(LOW)
    vector_grads[...] = jnp.concatenate(
        [
            jnp.sum(second_grad * normed, axis=0, keepdims=True),
            jnp.sum(second_grad, axis=0, keepdims=True),
            jnp.sum(branch.astype(F32), axis=0, keepdims=True),
            jnp.zeros((5, width), F32),
        ],
        axis=0,
    )
    context_grad[...] = dot_nn(branch, out[...]).astype(LOW)
    out_grad = dot_tn(branch, context[...])
    blank = jnp.zeros((rows_left(each), width), F32)
    for unit in range(units):
        out_stage[unit] = jnp.concatenate(
            [out_grad[unit * each : (unit + 1) * each], blank], axis=0
        ).astype(LOW)
    batch = 8
    for start in range(0, units, batch):
        at = slice(start * up_rows, (start + batch) * up_rows)
        grad = dot_tn(hidden_grad[:, at], second[...]).astype(LOW)
        for n in range(batch):
            up_stage[start + n, :up_rows] = grad[n * up_rows : (n + 1) * up_rows]
            up_stage[start + n, up_rows:] = out_stage[start + n]
    store_units(place, up_stage, (corner_send, corner_keep, side_send, side_keep, own), sems)


def rows_left(each):
    return -each % 16


def finish_kernel(active, down, middle, vectors, layer_out):
    layer_out[...] = middle[...] + dot_nt(active[...], down[...]) + vectors[5:6, :]


def attend_back_kernel(
    queries, keys, values, context_grad, mixed, probs, query_grad, key_grad, value_grad, diagonals
):
    q, k, v, dout = queries[...], keys[...], values[...], context_grad[...]
    block_len, span = probs.shape[1:]
    weighted = dout.astype(F32) * mixed[...]
    row = lax.broadcasted_iota(jnp.int32, (block_len, block_len), 0)
    lane = lax.broadcasted_iota(jnp.int32, (block_len, block_len), 1)
    turn = (row + lane == block_len - 1).astype(LOW)
    blank = jnp.zeros((block_len, block_len), F32)
    dq, dk, dv = jnp.zeros(q.shape, F32), jnp.zeros(k.shape, F32), jnp.zeros(v.shape, F32)
    for head in range(2):
        mine = half_mask(q.shape, head)
        dout_head = jnp.where(mine, dout, 0)
        delta = jnp.sum(jnp.where(mine, weighted, 0.0), axis=1, keepdims=True)
        prob = probs[head]
        grad = prob.astype(F32) * (dot_nt(dout_head, v) - delta)
        raw = (grad * (1.0 / math.sqrt(HD))).astype(LOW)
        dq = dq + dot_nn(raw, jnp.where(half_mask(k.shape, head), k, 0))
        dk = dk + dot_tn(raw, jnp.where(mine, q, 0))
        dv = dv + dot_tn(prob, dout_head)
        turned = jnp.concatenate([dot_nn(turn, raw), blank], axis=1)
        sheared = pltpu.roll(turned, 0, 1, stride=1, stride_axis=0)
        diagonals[0, head : head + 1, :] = jnp.sum(sheared, axis=0, keepdims=True) * math.sqrt(HD)
    query_grad[...] = dq.astype(LOW)
    key_grad[...] = dk.astype(LOW)
    value_grad[...] = dv.astype(LOW)


def qkv_grad_kernel(
    place, own_frames, mate_frames, first, query_grad, key_grad, value_grad, weight, vectors,
    diagonals, buckets, vector_grads, down_bias_grad, up_bias_grad, wide_one, wide_two, wide_four,
    corner_send, corner_keep, side_send, side_keep, own, own_grad, mate_grad, grads, small, stage, sems,
):
    units, full, width = stage.shape
    rows = full - PAD
    shard_len = own_frames.shape[0]
    x = place[0]
    own_at = pl.multiple_of(x * shard_len, shard_len)
    mate_at = pl.multiple_of((1 - x) * shard_len, shard_len)
    dq, dk, dv = query_grad[...], key_grad[...], value_grad[...]
    grads[:width, :] = dot_tn(dq, first[pl.ds(own_at, shard_len), :])
    grads[width : 2 * width, :] = dot_tn(dk, first[...])
    grads[2 * width :, :] = dot_tn(dv, first[...])

    def first_grad(at):
        return dot_nn(key_grad[pl.ds(at, shard_len), :], weight[width : 2 * width, :]) + dot_nn(
            value_grad[pl.ds(at, shard_len), :], weight[2 * width :, :]
        )

    def normed(frames):
        wide = frames.astype(F32)
        center = wide - jnp.mean(wide, axis=1, keepdims=True)
        return center * lax.rsqrt(jnp.mean(center * center, axis=1, keepdims=True) + EPSILON)

    of_own = first_grad(own_at) + dot_nn(dq, weight[:width, :])
    of_mate = first_grad(mate_at)
    own_grad[...] = of_own
    mate_grad[...] = of_mate.astype(LOW)

    def total(array):
        return jnp.sum(array, axis=0, keepdims=True)

    gain_grad = total(of_own * normed(own_frames[...])) + total(of_mate * normed(mate_frames[...]))
    shift_grad = total(of_own) + total(of_mate)
    narrow = (
        gain_grad, shift_grad, vector_grads[0:1, :], vector_grads[1:2, :], vector_grads[2:3, :],
        down_bias_grad[0:1, :],
    )

    def fold(vector, table):
        kept = (vector * table[:units, :].astype(F32)).astype(LOW)
        return dot_nt(kept, table[units:, :])

    for n, vector in enumerate(narrow):
        small[0, :, n * LANES : (n + 1) * LANES] = fold(vector, wide_one)
    small[1, :, :] = jnp.zeros((units, width), F32)
    both = jnp.concatenate([total(dq.astype(F32)), total(dv.astype(F32))], axis=1)
    small[1, :, :LANES] = fold(both, wide_two)
    small[1, :, LANES : 2 * LANES] = fold(up_bias_grad[0:1, :], wide_four)
    table = lax.dot_general(
        diagonals[...], buckets[...], (((1,), (0,)), ((), ())), precision=HIGHEST, preferred_element_type=F32
    )
    table = jnp.concatenate([table[: H // 2], table[H // 2 :]], axis=1)
    for unit in range(units):
        stage[unit] = jnp.concatenate(
            [
                grads[unit * rows : (unit + 1) * rows, :],
                small[0, unit : unit + 1, :],
                small[1, unit : unit + 1, :],
                table,
            ],
            axis=0,
        ).astype(LOW)
    store_units(place, stage, (corner_send, corner_keep, side_send, side_keep, own), sems)


def input_grad_kernel(frames, own_grad, mate_part, middle_grad, vectors, frames_grad):
    wide = frames[...].astype(F32)
    center = wide - jnp.mean(wide, axis=1, keepdims=True)
    inv_std = lax.rsqrt(jnp.mean(center * center, axis=1, keepdims=True) + EPSILON)
    normed = center * inv_std
    scaled = (own_grad[...] + mate_part[...].astype(F32)) * vectors[0:1, :]
    inner = (
        scaled
        - jnp.mean(scaled, axis=1, keepdims=True)
        - normed * jnp.mean(scaled * normed, axis=1, keepdims=True)
    )
    frames_grad[...] = middle_grad[...] + inner * inv_std


def paired_body(
    frames, cotangent, seq_lengths, key_mask, qkv_weight, query_value_bias, out_weight, out_bias,
    up_weight, up_bias, down_weight, down_bias, first_gain, first_shift, second_gain, second_shift,
    rel_bias,
):
    shard_len, width = frames.shape
    x = lax.axis_index("blk")
    d = lax.axis_index("dp")
    core = d % 2
    units = lax.axis_size("dp") * lax.axis_size("blk")
    span = shard_len * lax.axis_size("blk")
    place = jnp.stack([x, (d // 2) % 2, d // 4, core]).astype(jnp.int32)
    each = width // units
    ff = up_weight.shape[1] * units
    qkv_rows, up_rows = qkv_weight.shape[1], up_weight.shape[1]
    folds = ff // width
    down_rows = each * folds
    out_rows = each + rows_left(each)

    def slot(vector):
        return jnp.pad(vector, (0, LANES - vector.shape[0]))

    narrow_row = jnp.concatenate(
        [slot(v) for v in (first_gain, first_shift, second_gain, second_shift, out_bias, down_bias)]
    )
    wide_row = jnp.pad(
        jnp.concatenate([slot(query_value_bias), slot(up_bias)]), (0, width - 2 * LANES)
    )
    small_rows = jnp.pad(jnp.stack([narrow_row, wide_row]), ((0, PAD - 2), (0, 0)))
    qkv_unit = jnp.concatenate([qkv_weight.T, small_rows])
    out_unit = jnp.concatenate(
        [up_weight.T, out_weight.T, jnp.zeros((out_rows - each, width), LOW)]
    )
    down_unit = jnp.concatenate(
        [down_weight.T[:, fold * width : (fold + 1) * width] for fold in range(folds)]
    )
    live_row = jnp.pad(key_mask.astype(LOW), (0, width - shard_len))
    sent = jnp.concatenate([frames, jnp.pad(live_row[None], ((0, 15), (0, 0)))])
    got = shift(sent, PACK)
    mate_frames, mate_live = got[:shard_len], got[shard_len, :shard_len]
    qkv_pieces = gather_units(qkv_unit, core)
    up_pieces = gather_units(out_unit, core)
    down_pieces = gather_units(down_unit, core)

    seq_ends = jnp.cumsum(seq_lengths[0])
    key_pos = jnp.arange(span, dtype=jnp.int32)
    key_doc = doc_numbers(seq_ends, key_pos)
    query_pos = x * shard_len + jnp.arange(shard_len, dtype=jnp.int32)
    query_doc = doc_numbers(seq_ends, query_pos)
    own_live = key_mask.astype(LOW)
    live = jnp.where(
        x == 0, jnp.concatenate([own_live, mate_live]), jnp.concatenate([mate_live, own_live])
    )
    allowed = (query_doc[:, None] == key_doc[None, :]) & (
        (live[None, :] > 0.5) | (query_pos[:, None] == key_pos[None, :])
    )
    hidden_pairs = jnp.where(allowed, 0.0, MASKED).astype(F32)
    distance = jnp.arange(span + shard_len, dtype=jnp.int32) - (shard_len - 1) - x * shard_len
    bucket = jnp.clip(distance, -MAXREL, MAXREL) + MAXREL
    bucket_lanes = 3 * LANES
    buckets = (bucket[:, None] == jnp.arange(bucket_lanes, dtype=jnp.int32)[None, :]).astype(LOW)
    curve = jnp.dot(buckets[:, :BUCKETS], rel_bias, preferred_element_type=F32).T
    curve = curve.reshape(H // 2, 2, span + shard_len)
    spreads = spread_tables(units, width)

    def shape(*dims, kind=LOW):
        return jax.ShapeDtypeStruct(dims, kind)

    unit_sems = pltpu.SemaphoreType.DMA((units,))
    first, queries, keys, values, weight, vectors, up_bias_all = call(
        project_kernel,
        [SMEM, VMEM, VMEM] + [ANY] * 5 + [VMEM] * 3,
        [
            shape(span, width), shape(shard_len, width), shape(span, width), shape(span, width),
            shape(3 * width, width), shape(8, width, kind=F32), shape(8, ff, kind=F32),
        ],
        [VMEM] * 7,
        [
            pltpu.VMEM((units, qkv_rows + PAD, width), LOW), pltpu.VMEM((2, units, width), F32), unit_sems,
        ],
        (place, frames, mate_frames) + qkv_pieces + tuple(spreads),
        2 * shard_len * width * 5 * width,
        name="project",
    )
    pairs = H // 2
    pair_lanes = 2 * HD

    def lanes_of(rows):
        return pl.BlockSpec((rows, pair_lanes), lambda n: (0, n))

    def heads_of(*dims):
        return pl.BlockSpec(dims, lambda n: (n,) + (0,) * (len(dims) - 1))

    probs, mixed = call(
        attend_kernel,
        [
            SMEM, lanes_of(shard_len), lanes_of(span), lanes_of(span), heads_of(1, 2, span + shard_len),
            pl.BlockSpec((shard_len, span), lambda n: (0, 0)),
        ],
        [shape(H, shard_len, span), shape(shard_len, width, kind=F32)],
        [heads_of(2, shard_len, span), lanes_of(shard_len)],
        [],
        (place, queries, keys, values, curve, hidden_pairs),
        8 * shard_len * span * width,
        grid=(pairs,),
        name="attend",
    )
    middle, second, active, slope, context, up, out = call(
        expand_kernel,
        [SMEM] + [VMEM] * 4 + [ANY] * 5,
        [
            shape(shard_len, width, kind=F32), shape(shard_len, width), shape(shard_len, ff),
            shape(shard_len, ff, kind=F32), shape(shard_len, width), shape(ff, width), shape(width, width),
        ],
        [VMEM] * 7,
        [pltpu.VMEM((units, out_rows, width), LOW), unit_sems, unit_sems],
        (place, frames, mixed, vectors, up_bias_all) + up_pieces,
        2 * shard_len * width * (width + ff),
        name="expand",
    )
    down_parts = call(
        down_grad_kernel,
        [SMEM, VMEM, VMEM],
        part_shapes(down_rows, width) + [shape(8, width, kind=F32)],
        [ANY] * 5 + [VMEM],
        [pltpu.VMEM((units, down_rows, width), LOW), unit_sems],
        (place, active, cotangent),
        2 * shard_len * width * ff,
        name="down_grad",
    )
    down_bias_grad = down_parts[5]
    down_sum = scatter_units(down_parts[:5], core)
    back = call(
        back_kernel,
        [SMEM] + [VMEM] * 8 + [ANY] * 5,
        part_shapes(up_rows + out_rows, width)
        + [
            shape(width, ff), shape(shard_len, width, kind=F32), shape(shard_len, width),
            shape(8, width, kind=F32), shape(8, ff, kind=F32),
        ],
        [ANY] * 5 + [VMEM] * 5,
        [
            pltpu.VMEM((units, down_rows, width), LOW), pltpu.VMEM((shard_len, ff), LOW),
            pltpu.VMEM((units, out_rows, width), LOW),
            pltpu.VMEM((units, up_rows + out_rows, width), LOW), unit_sems,
        ],
        (place, cotangent, slope, second, middle, context, vectors, up, out) + down_pieces,
        2 * shard_len * width * (3 * ff + 2 * width),
        name="back",
    )
    down, middle_grad, context_grad, vector_grads, up_bias_grad = back[5:]
    up_sum = scatter_units(back[:5], core)
    layer_out = call(
        finish_kernel, [VMEM] * 4, shape(shard_len, width, kind=F32), VMEM, [],
        (active, down, middle, vectors), 2 * shard_len * width * ff, name="finish",
    ) if False else pl.pallas_call(
        finish_kernel,
        out_shape=shape(shard_len, width, kind=F32),
        compiler_params=pltpu.CompilerParams(vmem_limit_bytes=VMEM_BYTES),
        cost_estimate=pl.CostEstimate(
            flops=2 * shard_len * width * ff, bytes_accessed=8 * shard_len * ff, transcendentals=0
        ),
        name="finish",
    )(active, down, middle, vectors)
    query_grad, key_grad, value_grad, diagonals = call(
        attend_back_kernel,
        [
            lanes_of(shard_len), lanes_of(span), lanes_of(span), lanes_of(shard_len), lanes_of(shard_len),
            heads_of(2, shard_len, span),
        ],
        [
            shape(shard_len, width), shape(span, width), shape(span, width),
            shape(pairs, 2, span + shard_len, kind=F32),
        ],
        [lanes_of(shard_len), lanes_of(span), lanes_of(span), heads_of(1, 2, span + shard_len)],
        [],
        (queries, keys, values, context_grad, mixed, probs),
        16 * shard_len * span * width,
        grid=(pairs,),
        name="attend_back",
    )
    qkv_parts = call(
        qkv_grad_kernel,
        [SMEM] + [VMEM] * 16,
        part_shapes(qkv_rows + PAD, width) + [shape(shard_len, width, kind=F32), shape(shard_len, width)],
        [ANY] * 5 + [VMEM] * 2,
        [
            pltpu.VMEM((3 * width, width), F32), pltpu.VMEM((2, units, width), F32),
            pltpu.VMEM((units, qkv_rows + PAD, width), LOW), unit_sems,
        ],
        (
            place, frames, mate_frames, first, query_grad, key_grad, value_grad, weight, vectors,
            diagonals.reshape(H, span + shard_len), buckets.astype(F32), vector_grads, down_bias_grad,
            up_bias_grad,
        ) + tuple(spreads),
        2 * shard_len * width * 10 * width,
        name="qkv_grad",
    )
    own_grad, mate_grad = qkv_parts[5:]
    mate_part = shift(mate_grad, PACK)
    qkv_sum = scatter_units(qkv_parts[:5], core)
    frames_grad = pl.pallas_call(
        input_grad_kernel,
        out_shape=shape(shard_len, width, kind=F32),
        compiler_params=pltpu.CompilerParams(vmem_limit_bytes=VMEM_BYTES),
        name="input_grad",
    )(frames, own_grad, mate_part, middle_grad, vectors)

    down_grad = jnp.concatenate(
        [down_sum[fold * each : (fold + 1) * each] for fold in range(folds)], axis=1
    )
    narrow_sum, wide_sum, table_sum = (
        qkv_sum[qkv_rows], qkv_sum[qkv_rows + 1], qkv_sum[qkv_rows + 2 :],
    )
    table = jnp.concatenate([table_sum[:, :BUCKETS], table_sum[:, bucket_lanes : bucket_lanes + BUCKETS]])
    pieces = [narrow_sum[n * LANES : n * LANES + each] for n in range(NARROW)]
    return (
        layer_out, frames_grad, qkv_sum[:qkv_rows].T, wide_sum[: 2 * each],
        up_sum[up_rows : up_rows + each].T, pieces[4], up_sum[:up_rows].T,
        wide_sum[LANES : LANES + up_rows], down_grad.T, pieces[5], pieces[0], pieces[1], pieces[2],
        pieces[3], table.T,
    )


def paired(mesh):
    return mesh.shape["blk"] == 2 and mesh.shape["dp"] == 16


def solution(mesh):
    placed = (
        P(("dp", "blk"), None),
        P(("dp", "blk"), None),
        P("dp", None),
        P(("dp", "blk")),
        P(None, ("dp", "blk")),
        P(("dp", "blk")),
        P(None, ("dp", "blk")),
        P(("dp", "blk")),
        P(None, ("dp", "blk")),
        P(("dp", "blk")),
        P(None, ("dp", "blk")),
        P(("dp", "blk")),
        P(("dp", "blk")),
        P(("dp", "blk")),
        P(("dp", "blk")),
        P(("dp", "blk")),
        P(),
    )
    return jax.shard_map(
        paired_body if paired(mesh) else body,
        mesh=mesh,
        in_specs=placed,
        out_specs=(
            P(("dp", "blk"), None),
            P(("dp", "blk"), None),
            P(None, ("dp", "blk")),
            P(("dp", "blk")),
            P(None, ("dp", "blk")),
            P(("dp", "blk")),
            P(None, ("dp", "blk")),
            P(("dp", "blk")),
            P(None, ("dp", "blk")),
            P(("dp", "blk")),
            P(("dp", "blk")),
            P(("dp", "blk")),
            P(("dp", "blk")),
            P(("dp", "blk")),
            P(),
        ),
        check_vma=False,
    )
```

```python
import math

import jax
import jax.numpy as jnp
import numpy as np
from jax import lax
from jax.experimental import pallas as pl
from jax.experimental.pallas import tpu as pltpu
from jax.sharding import PartitionSpec as P

H = 12
HD = 64
MAXREL = 160
BLOCK = 256
BUCKETS = 321


EPSILON = 1e-05
MASKED = -2e30
START_PEAK = -1e30
HIGHEST = lax.Precision.HIGHEST


def from_behind(block, axis, distance):
    devices = range(lax.axis_size(axis))
    route = [((i - distance) % len(devices), i) for i in devices]
    return lax.ppermute(block, axis, route)


def layer_norm(values, gain_vec, shift_vec):
    center = values - jnp.mean(values, axis=-1, keepdims=True)
    inv_std = lax.rsqrt(jnp.mean(center * center, axis=-1, keepdims=True) + EPSILON)
    normed = center * inv_std
    return (normed * gain_vec + shift_vec, normed, inv_std)


def norm_back(gradient, normed, inv_std, gain_vec):
    scaled = gradient * gain_vec
    inner = (
        scaled
        - jnp.mean(scaled, axis=-1, keepdims=True)
        - normed * jnp.mean(scaled * normed, axis=-1, keepdims=True)
    )
    return (inner * inv_std, jnp.sum(gradient * normed, axis=0), jnp.sum(gradient, axis=0))


def gelu_parts(values):
    normal_cdf = 0.5 * (1.0 + lax.erf(values * 0.7071067811865476))
    density = jnp.exp(-0.5 * values * values) * 0.3989422804014327
    return (values * normal_cdf, normal_cdf + values * density)


def doc_numbers(seq_ends, positions):
    return jnp.sum((positions[:, None] >= seq_ends[None, :]).astype(jnp.int32), axis=1)


def pair_logits(
    query_block, key_block, query_pos, key_pos, query_doc, key_doc, key_live, table_heads
):
    block_len = query_block.shape[0]
    raw = jnp.einsum(
        "qhd,khd->hqk",
        query_block.reshape(block_len, H, HD),
        key_block.reshape(-1, H, HD),
        preferred_element_type=jnp.float32,
    )
    relative = jnp.clip(key_pos[None, :] - query_pos[:, None], -MAXREL, MAXREL) + MAXREL
    bias = jnp.take(table_heads, relative, axis=1)
    allowed = (query_doc[:, None] == key_doc[None, :]) & (
        (key_live[None, :] > 0.5) | (query_pos[:, None] == key_pos[None, :])
    )
    return jnp.where(allowed[None], raw * (1.0 / math.sqrt(HD)) + bias, MASKED)


def diagonal_sums(gradient, offset):
    heads, block_len, _ = gradient.shape
    flipped = gradient[:, ::-1, :]
    padded = jnp.pad(flipped, ((0, 0), (0, 0), (0, block_len)))
    sheared = padded.reshape(heads, 2 * block_len * block_len)[:, : block_len * (2 * block_len - 1)]
    sheared = sheared.reshape(heads, block_len, 2 * block_len - 1)
    diag_sums = jnp.sum(sheared, axis=1)
    distance = offset + jnp.arange(2 * block_len - 1, dtype=jnp.int32) - (block_len - 1)
    bucket = jnp.clip(distance, -MAXREL, MAXREL) + MAXREL
    onehot = (bucket[:, None] == jnp.arange(BUCKETS, dtype=jnp.int32)[None, :]).astype(jnp.float32)
    return jnp.dot(diag_sums, onehot, precision=HIGHEST)


def body(
    frames,
    cotangent,
    seq_lengths,
    key_mask,
    qkv_weight,
    query_value_bias,
    out_weight,
    out_bias,
    up_weight,
    up_bias,
    down_weight,
    down_bias,
    first_gain,
    first_shift,
    second_gain,
    second_shift,
    rel_bias,
):
    cycle_size = lax.axis_size("blk")
    cycle_place = lax.axis_index("blk")
    shard_len = frames.shape[0]
    width = frames.shape[1]
    block_count = shard_len // BLOCK
    score_scale = 1.0 / math.sqrt(HD)
    seq_ends = jnp.cumsum(seq_lengths[0])
    local_pos = jnp.arange(shard_len, dtype=jnp.int32)
    positions = cycle_place * shard_len + local_pos
    own_docs = doc_numbers(seq_ends, positions)
    table_heads = rel_bias.astype(jnp.float32).T

    def blocked(array):
        return array.reshape((block_count, BLOCK) + array.shape[1:])

    def key_meta(turn):
        source = (cycle_place - turn) % cycle_size
        key_pos = source * shard_len + local_pos
        return (key_pos, doc_numbers(seq_ends, key_pos))

    gathered = (
        lax.all_gather(qkv_weight, ("dp", "blk"), axis=1, tiled=True),
        lax.all_gather(query_value_bias, ("dp", "blk"), axis=0, tiled=True),
        lax.all_gather(out_weight, ("dp", "blk"), axis=1, tiled=True),
        lax.all_gather(out_bias, ("dp", "blk"), axis=0, tiled=True),
        lax.all_gather(up_weight, ("dp", "blk"), axis=1, tiled=True),
        lax.all_gather(up_bias, ("dp", "blk"), axis=0, tiled=True),
        lax.all_gather(down_weight, ("dp", "blk"), axis=1, tiled=True),
        lax.all_gather(down_bias, ("dp", "blk"), axis=0, tiled=True),
        lax.all_gather(first_gain, ("dp", "blk"), axis=0, tiled=True),
        lax.all_gather(first_shift, ("dp", "blk"), axis=0, tiled=True),
        lax.all_gather(second_gain, ("dp", "blk"), axis=0, tiled=True),
        lax.all_gather(second_shift, ("dp", "blk"), axis=0, tiled=True),
    )
    (
        qkv_full,
        qv_bias_full,
        out_full,
        out_bias_full,
        up_full,
        up_bias_full,
        down_full,
        down_bias_full,
        gain_one,
        shift_one,
        gain_two,
        shift_two,
    ) = gathered
    frames_wide = frames.astype(jnp.float32)
    first_out, first_normed, first_inv = layer_norm(
        frames_wide, gain_one.astype(jnp.float32), shift_one.astype(jnp.float32)
    )
    first_low = first_out.astype(jnp.bfloat16)
    projected = jnp.dot(first_low, qkv_full, preferred_element_type=jnp.float32)
    bias_vec = qv_bias_full.astype(jnp.float32)
    queries = (projected[:, :width] + bias_vec[:width]).astype(jnp.bfloat16)
    key_rows = projected[:, width : 2 * width].astype(jnp.bfloat16)
    value_rows = (projected[:, 2 * width :] + bias_vec[width:]).astype(jnp.bfloat16)
    live_rows = key_mask.astype(jnp.bfloat16)
    query_blocks = (blocked(queries), blocked(positions), blocked(own_docs))

    def forward_hop(turn, online_state, key_part, value_part, live_part):
        key_pos, key_doc = key_meta(turn)
        key_items = (
            blocked(key_part),
            blocked(value_part),
            blocked(key_pos),
            blocked(key_doc),
            blocked(live_part),
        )

        def forward_per_query(query_items):
            query_block, query_pos, query_doc, row_peak, row_total, accum = query_items

            def online(carried, key_block_items):
                row_peak, row_total, accum = carried
                key_block, value_block, key_bpos, key_bdoc, key_blive = key_block_items
                logits = pair_logits(
                    query_block,
                    key_block,
                    query_pos,
                    key_bpos,
                    query_doc,
                    key_bdoc,
                    key_blive,
                    table_heads,
                )
                new_peak = jnp.maximum(row_peak, jnp.max(logits, axis=2))
                decay = jnp.exp(row_peak - new_peak)
                weights = jnp.exp(logits - new_peak[:, :, None])
                row_total = row_total * decay + jnp.sum(weights, axis=2)
                accum = accum * decay.T[:, :, None] + jnp.einsum(
                    "hqk,khd->qhd",
                    weights.astype(jnp.bfloat16),
                    value_block.reshape(-1, H, HD),
                    preferred_element_type=jnp.float32,
                )
                return ((new_peak, row_total, accum), None)

            result, unused = lax.scan(online, (row_peak, row_total, accum), key_items)
            return result

        return lax.map(forward_per_query, query_blocks + online_state)

    def cycle_turn(turn, carried):
        online_state, key_part, value_part, live_part = carried
        online_state = forward_hop(turn, online_state, key_part, value_part, live_part)
        key_part, value_part, live_part = from_behind((key_part, value_part, live_part), "blk", 1)
        return (online_state, key_part, value_part, live_part)

    start_state = (
        jnp.full((block_count, H, BLOCK), START_PEAK, jnp.float32),
        jnp.zeros((block_count, H, BLOCK), jnp.float32),
        jnp.zeros((block_count, BLOCK, H, HD), jnp.float32),
    )
    carried = lax.fori_loop(
        0, cycle_size - 1, cycle_turn, (start_state, key_rows, value_rows, live_rows)
    )
    row_peak, row_total, accum = forward_hop(
        cycle_size - 1, carried[0], carried[1], carried[2], carried[3]
    )
    mixed = accum / jnp.transpose(row_total, (0, 2, 1))[:, :, :, None]
    mixed_flat = mixed.reshape(shard_len, width)
    context = mixed_flat.astype(jnp.bfloat16)
    branch = jnp.dot(context, out_full, preferred_element_type=jnp.float32) + out_bias_full.astype(
        jnp.float32
    )
    middle = frames_wide + branch
    second_out, second_normed, second_inv = layer_norm(
        middle, gain_two.astype(jnp.float32), shift_two.astype(jnp.float32)
    )
    second_low = second_out.astype(jnp.bfloat16)
    hidden = jnp.dot(second_low, up_full, preferred_element_type=jnp.float32) + up_bias_full.astype(
        jnp.float32
    )
    active, slope = gelu_parts(hidden)
    active_low = active.astype(jnp.bfloat16)
    layer_out = (
        middle
        + jnp.dot(active_low, down_full, preferred_element_type=jnp.float32)
        + down_bias_full.astype(jnp.float32)
    )
    weights_back = (
        lax.all_gather(qkv_weight, ("dp", "blk"), axis=1, tiled=True),
        lax.all_gather(query_value_bias, ("dp", "blk"), axis=0, tiled=True),
        lax.all_gather(out_weight, ("dp", "blk"), axis=1, tiled=True),
        lax.all_gather(out_bias, ("dp", "blk"), axis=0, tiled=True),
        lax.all_gather(up_weight, ("dp", "blk"), axis=1, tiled=True),
        lax.all_gather(up_bias, ("dp", "blk"), axis=0, tiled=True),
        lax.all_gather(down_weight, ("dp", "blk"), axis=1, tiled=True),
        lax.all_gather(down_bias, ("dp", "blk"), axis=0, tiled=True),
        lax.all_gather(first_gain, ("dp", "blk"), axis=0, tiled=True),
        lax.all_gather(first_shift, ("dp", "blk"), axis=0, tiled=True),
        lax.all_gather(second_gain, ("dp", "blk"), axis=0, tiled=True),
        lax.all_gather(second_shift, ("dp", "blk"), axis=0, tiled=True),
    )
    qkv_back = weights_back[0]
    out_back = weights_back[2]
    up_back = weights_back[4]
    down_back = weights_back[6]
    gain_one_back = weights_back[8].astype(jnp.float32)
    gain_two_back = weights_back[10].astype(jnp.float32)
    grad_wide = cotangent.astype(jnp.float32)
    down_grad = jnp.einsum("tf,td->fd", active_low, cotangent, preferred_element_type=jnp.float32)
    down_bias_grad = jnp.sum(grad_wide, axis=0)
    active_grad = jnp.einsum("td,fd->tf", cotangent, down_back, preferred_element_type=jnp.float32)
    hidden_low = (active_grad * slope).astype(jnp.bfloat16)
    up_grad = jnp.einsum("td,tf->df", second_low, hidden_low, preferred_element_type=jnp.float32)
    up_bias_grad = jnp.sum(hidden_low.astype(jnp.float32), axis=0)
    second_grad = jnp.einsum("tf,df->td", hidden_low, up_back, preferred_element_type=jnp.float32)
    middle_norm, gain_two_grad, shift_two_grad = norm_back(
        second_grad, second_normed, second_inv, gain_two_back
    )
    middle_grad = grad_wide + middle_norm
    branch_low = middle_grad.astype(jnp.bfloat16)
    out_grad = jnp.einsum("td,te->de", context, branch_low, preferred_element_type=jnp.float32)
    out_bias_grad = jnp.sum(branch_low.astype(jnp.float32), axis=0)
    context_low = jnp.einsum(
        "te,de->td", branch_low, out_back, preferred_element_type=jnp.float32
    ).astype(jnp.bfloat16)
    delta = jnp.sum(
        (context_low.astype(jnp.float32) * mixed_flat).reshape(shard_len, H, HD), axis=2
    )
    delta_blocks = jnp.transpose(blocked(delta), (0, 2, 1))
    query_back = (
        blocked(queries),
        blocked(context_low),
        blocked(positions),
        blocked(own_docs),
        row_peak,
        row_total,
        delta_blocks,
    )

    def backward_hop(
        turn, query_grad, table_grad, key_part, value_part, live_part, key_grad, value_grad
    ):
        key_pos, key_doc = key_meta(turn)

        def per_key(carried, key_block_items):
            query_grad, table_grad = carried
            key_block, value_block, key_bpos, key_bdoc, key_blive, key_bgrad, value_bgrad = (
                key_block_items
            )
            key_heads = key_block.reshape(-1, H, HD)
            value_heads = value_block.reshape(-1, H, HD)

            def per_per_query(inner, query_items):
                key_bgrad, value_bgrad, table_grad = inner
                (
                    query_block,
                    dout_block,
                    query_pos,
                    query_doc,
                    peak_block,
                    total_block,
                    delta_block,
                ) = query_items
                logits = pair_logits(
                    query_block,
                    key_block,
                    query_pos,
                    key_bpos,
                    query_doc,
                    key_bdoc,
                    key_blive,
                    table_heads,
                )
                attn_prob = jnp.exp(logits - peak_block[:, :, None]) / total_block[:, :, None]
                dout_heads = dout_block.reshape(-1, H, HD)
                prob_grad = jnp.einsum(
                    "qhd,khd->hqk", dout_heads, value_heads, preferred_element_type=jnp.float32
                )
                logit_grad = attn_prob * (prob_grad - delta_block[:, :, None])
                raw_low = (logit_grad * score_scale).astype(jnp.bfloat16)
                query_part = jnp.einsum(
                    "hqk,khd->qhd", raw_low, key_heads, preferred_element_type=jnp.float32
                ).reshape(-1, width)
                key_bgrad = key_bgrad + jnp.einsum(
                    "hqk,qhd->khd",
                    raw_low,
                    query_block.reshape(-1, H, HD),
                    preferred_element_type=jnp.float32,
                ).reshape(-1, width)
                value_bgrad = value_bgrad + jnp.einsum(
                    "hqk,qhd->khd",
                    attn_prob.astype(jnp.bfloat16),
                    dout_heads,
                    preferred_element_type=jnp.float32,
                ).reshape(-1, width)
                table_grad = table_grad + diagonal_sums(logit_grad, key_bpos[0] - query_pos[0])
                return ((key_bgrad, value_bgrad, table_grad), query_part)

            (key_bgrad, value_bgrad, table_grad), query_parts = lax.scan(
                per_per_query, (key_bgrad, value_bgrad, table_grad), query_back
            )
            return ((query_grad + query_parts, table_grad), (key_bgrad, value_bgrad))

        (query_grad, table_grad), (key_new, value_new) = lax.scan(
            per_key,
            (query_grad, table_grad),
            (
                blocked(key_part),
                blocked(value_part),
                blocked(key_pos),
                blocked(key_doc),
                blocked(live_part),
                blocked(key_grad),
                blocked(value_grad),
            ),
        )
        return (
            query_grad,
            table_grad,
            key_new.reshape(shard_len, width),
            value_new.reshape(shard_len, width),
        )

    def pass_grads(key_grad, value_grad):
        return (
            from_behind(key_grad.astype(jnp.bfloat16), "blk", 1).astype(key_grad.dtype),
            from_behind(value_grad.astype(jnp.bfloat16), "blk", 1).astype(value_grad.dtype),
        )

    def back_turn(turn, carried):
        query_grad, table_grad, key_part, value_part, live_part, key_grad, value_grad = carried
        query_grad, table_grad, key_grad, value_grad = backward_hop(
            turn, query_grad, table_grad, key_part, value_part, live_part, key_grad, value_grad
        )
        key_part, value_part, live_part = from_behind((key_part, value_part, live_part), "blk", 1)
        key_grad, value_grad = pass_grads(key_grad, value_grad)
        return (query_grad, table_grad, key_part, value_part, live_part, key_grad, value_grad)

    zero_rows = jnp.zeros((shard_len, width), jnp.float32)
    back_start = (
        jnp.zeros((block_count, BLOCK, width), jnp.float32),
        jnp.zeros((H, BUCKETS), jnp.float32),
        key_rows,
        value_rows,
        live_rows,
        zero_rows,
        zero_rows,
    )
    carried = lax.fori_loop(0, cycle_size - 1, back_turn, back_start)
    query_grad, table_grad, key_grad, value_grad = backward_hop(
        cycle_size - 1,
        carried[0],
        carried[1],
        carried[2],
        carried[3],
        carried[4],
        carried[5],
        carried[6],
    )
    key_grad, value_grad = pass_grads(key_grad, value_grad)
    query_low = query_grad.reshape(shard_len, width).astype(jnp.bfloat16)
    key_low = key_grad.astype(jnp.bfloat16)
    value_low = value_grad.astype(jnp.bfloat16)
    qkv_low = jnp.concatenate([query_low, key_low, value_low], axis=1)
    qkv_grad = jnp.einsum("td,te->de", first_low, qkv_low, preferred_element_type=jnp.float32)
    query_value_grad = jnp.concatenate(
        [
            jnp.sum(query_low.astype(jnp.float32), axis=0),
            jnp.sum(value_low.astype(jnp.float32), axis=0),
        ]
    )
    first_grad = jnp.einsum("te,de->td", qkv_low, qkv_back, preferred_element_type=jnp.float32)
    frames_norm, gain_one_grad, shift_one_grad = norm_back(
        first_grad, first_normed, first_inv, gain_one_back
    )
    frames_grad = middle_grad + frames_norm
    summed = (
        lax.psum_scatter(qkv_grad, ("dp", "blk"), scatter_dimension=1, tiled=True),
        lax.psum_scatter(query_value_grad, ("dp", "blk"), scatter_dimension=0, tiled=True),
        lax.psum_scatter(out_grad, ("dp", "blk"), scatter_dimension=1, tiled=True),
        lax.psum_scatter(out_bias_grad, ("dp", "blk"), scatter_dimension=0, tiled=True),
        lax.psum_scatter(up_grad, ("dp", "blk"), scatter_dimension=1, tiled=True),
        lax.psum_scatter(up_bias_grad, ("dp", "blk"), scatter_dimension=0, tiled=True),
        lax.psum_scatter(down_grad, ("dp", "blk"), scatter_dimension=1, tiled=True),
        lax.psum_scatter(down_bias_grad, ("dp", "blk"), scatter_dimension=0, tiled=True),
        lax.psum_scatter(gain_one_grad, ("dp", "blk"), scatter_dimension=0, tiled=True),
        lax.psum_scatter(shift_one_grad, ("dp", "blk"), scatter_dimension=0, tiled=True),
        lax.psum_scatter(gain_two_grad, ("dp", "blk"), scatter_dimension=0, tiled=True),
        lax.psum_scatter(shift_two_grad, ("dp", "blk"), scatter_dimension=0, tiled=True),
    )
    table_sum = lax.psum(table_grad, ("dp", "blk"))
    return (
        layer_out,
        frames_grad,
        summed[0],
        summed[1],
        summed[2],
        summed[3],
        summed[4],
        summed[5],
        summed[6],
        summed[7],
        summed[8],
        summed[9],
        summed[10],
        summed[11],
        table_sum.T,
    )


AXES = ("dp", "blk")
VMEM_BYTES = 56 * 1024 * 1024
F32 = jnp.float32
LOW = jnp.bfloat16
LANES = 128
NARROW = 6
PAD = 8


def route(move):
    n_dp, n_blk = lax.axis_size("dp"), lax.axis_size("blk")
    pairs = []
    for d in range(n_dp):
        d_bits, b_bits = move[d % 2]
        for b in range(n_blk):
            pairs.append((d * n_blk + b, (d ^ d_bits) * n_blk + (b ^ b_bits)))
    return pairs


def shift(array, move, name="swap"):
    with jax.named_scope(name):
        return lax.ppermute(array, AXES, route(move))


CORE = ((1, 0), (1, 0))
SIDE = ((0, 1), (2, 0))
OTHER_SIDE = ((2, 0), (0, 1))
PACK = ((0, 1), (0, 1))
ALONG_Z = tuple(((4 * turn, 0), (4 * turn, 0)) for turn in (1, 2, 3))


def tied(value, *after):
    return lax.optimization_barrier((value,) + after)[0]


def joined(*groups):
    return lax.optimization_barrier(groups)


def twin(array, name="twin"):
    return shift(array, CORE, name)


def along_z(unit, name):
    return tuple(shift(unit, move, name + "_z") for move in ALONG_Z)


def added(keep, sent):
    return keep.astype(F32) + twin(sent).astype(F32)


def z_sends(plane, name):
    low = plane.astype(LOW)
    return tuple(shift(low[n + 1], move, name + "_z") for n, move in enumerate(ALONG_Z))


def z_sum(plane, arrived):
    return plane[0] + sum(part.astype(F32) for part in arrived)


def unit_of(place, x_turn, y_turn, z_turn, c):
    x, y, z = place[0] ^ x_turn, place[1] ^ y_turn, place[2] ^ z_turn
    return ((z * 2 + y) * 2 + c) * 2 + x


def planes_of(place):
    c0 = place[3]
    found = []
    for plane in range(2):
        c = c0 if plane == 0 else 1 - c0
        for z in range(4):
            for n, (x_turn, y_turn) in enumerate(((0, 0), (1 - c, c), (c, 1 - c), (1, 1))):
                found.append((4 * plane + n, z, unit_of(place, x_turn, y_turn, z, c)))
    return found


def load_units(place, pieces, stage, sems):
    copies = [
        pltpu.make_async_copy(pieces[array].at[z], stage.at[unit], sems.at[n])
        for n, (array, z, unit) in enumerate(planes_of(place))
    ]
    for copy in copies:
        copy.start()
    return copies


def store_units(place, stage, parts, sems):
    copies = [
        pltpu.make_async_copy(stage.at[unit], parts[array].at[z], sems.at[n])
        for n, (array, z, unit) in enumerate(planes_of(place))
    ]
    for copy in copies:
        copy.start()
    for copy in copies:
        copy.wait()


def part_shapes(rows, width):
    return [jax.ShapeDtypeStruct((4, rows, width), LOW)] * 8


def dot_nn(a, b):
    return lax.dot_general(a, b, (((1,), (0,)), ((), ())), preferred_element_type=F32)


def dot_nt(a, b):
    return lax.dot_general(a, b, (((1,), (1,)), ((), ())), preferred_element_type=F32)


def dot_tn(a, b):
    return lax.dot_general(a, b, (((0,), (0,)), ((), ())), preferred_element_type=F32)


ANY = pl.BlockSpec(memory_space=pl.ANY)
SMEM = pl.BlockSpec(memory_space=pltpu.SMEM)
VMEM = pl.BlockSpec(memory_space=pltpu.VMEM)


def call(kernel, in_specs, outs, out_specs, scratch, args, flops, **kwargs):
    moved = sum(math.prod(a.shape) * a.dtype.itemsize for a in list(args) + list(outs))
    return pl.pallas_call(
        kernel,
        out_shape=outs,
        in_specs=in_specs,
        out_specs=out_specs,
        scratch_shapes=scratch,
        compiler_params=pltpu.CompilerParams(vmem_limit_bytes=VMEM_BYTES),
        cost_estimate=pl.CostEstimate(flops=flops, bytes_accessed=moved, transcendentals=0),
        **kwargs,
    )(*args)


def spread_tables(units, width):
    tables = []
    for n in (width // units, 2 * width // units, 4 * width // units):
        lane = np.arange(units * n)
        keep = lane[None, :] // n == np.arange(units)[:, None]
        pick = lane[None, :] % n == np.arange(LANES)[:, None]
        tables.append(jnp.asarray(np.concatenate([keep, pick]), LOW))
    return tables


def project_kernel(
    place, own, other, p0, p1, p2, p3, p4, p5, p6, p7, wide_one, wide_two, wide_four,
    first, queries, keys, values, weight, vectors, up_bias, mate_live, stage, small, sems,
):
    units = stage.shape[0]
    width = own.shape[1]
    rows = stage.shape[1] - PAD
    shard_len = own.shape[0]
    copies = load_units(place, (p0, p1, p2, p3, p4, p5, p6, p7), stage, sems)

    def normed(frames):
        wide = frames.astype(F32)
        center = wide - jnp.mean(wide, axis=1, keepdims=True)
        return center * lax.rsqrt(jnp.mean(center * center, axis=1, keepdims=True) + EPSILON)

    own_normed, mate_normed = normed(own[...]), normed(other[...])
    for copy in copies:
        copy.wait()
    for unit in range(units):
        top = stage[unit, rows : rows + PAD, :].astype(F32)
        small[0, unit : unit + 1, :] = top[0:1]
        small[1, unit : unit + 1, :] = top[1:2]

    mate = unit_of(place, 1, 0, 0, place[3])
    mate_live[...] = stage[mate, rows : rows + PAD, : mate_live.shape[1]].astype(F32)

    def spread(row, slot, table):
        held = small[row, :, slot * LANES : (slot + 1) * LANES].astype(LOW)
        laid = dot_nn(held, table[units:, :]) * table[:units, :].astype(F32)
        return jnp.sum(laid, axis=0, keepdims=True)

    for n in range(NARROW):
        vectors[n : n + 1, :] = spread(0, n, wide_one)
    qv_bias = spread(1, 0, wide_two)
    up_bias[...] = jnp.broadcast_to(spread(1, 1, wide_four), up_bias.shape)
    vectors[NARROW : NARROW + 1, :] = qv_bias[:, :width]
    vectors[NARROW + 1 : NARROW + 2, :] = qv_bias[:, width:]
    for pair in range(units // 2):
        joined = jnp.concatenate(
            [stage[2 * pair, :rows, :].astype(F32), stage[2 * pair + 1, :rows, :].astype(F32)], axis=0
        )
        weight[2 * rows * pair : 2 * rows * (pair + 1), :] = joined.astype(LOW)
    gain, offset = vectors[0:1, :], vectors[1:2, :]
    x = place[0]
    own_at = pl.multiple_of(x * shard_len, shard_len)
    mate_at = pl.multiple_of((1 - x) * shard_len, shard_len)
    first[pl.ds(own_at, shard_len), :] = (own_normed * gain + offset).astype(LOW)
    first[pl.ds(mate_at, shard_len), :] = (mate_normed * gain + offset).astype(LOW)
    mine = first[pl.ds(own_at, shard_len), :]
    queries[...] = (dot_nt(mine, weight[:width, :]) + vectors[NARROW : NARROW + 1, :]).astype(LOW)
    keys[...] = dot_nt(first[...], weight[width : 2 * width, :]).astype(LOW)
    values[...] = (
        dot_nt(first[...], weight[2 * width :, :]) + vectors[NARROW + 1 : NARROW + 2, :]
    ).astype(LOW)


def half_mask(shape, head):
    return (lax.broadcasted_iota(jnp.int32, shape, 1) // HD) == head


def attend_kernel(
    place, lengths, queries, keys, values, curve, own_live, mate_live, probs, mixed, hidden_pairs
):
    q, k, v = queries[...], keys[...], values[...]
    block_len, span = hidden_pairs.shape
    step = pl.program_id(0)

    @pl.when(step == 0)
    def _():
        start = place[0] * block_len
        key_pos = lax.broadcasted_iota(jnp.int32, (1, span), 1)
        query_pos = lax.broadcasted_iota(jnp.int32, (block_len, 1), 0) + start
        key_doc, query_doc = jnp.zeros_like(key_pos), jnp.zeros_like(query_pos)
        end = 0
        for n in range(lengths.shape[1]):
            end = end + lengths[0, n]
            key_doc = key_doc + (key_pos >= end).astype(jnp.int32)
            query_doc = query_doc + (query_pos >= end).astype(jnp.int32)
        one, two = own_live[...].astype(F32), mate_live[2:3, :]
        live = jnp.where(
            place[0] == 0, jnp.concatenate([one, two], axis=1), jnp.concatenate([two, one], axis=1)
        )
        allowed = (query_doc == key_doc) & ((live > 0.5) | (query_pos == key_pos))
        hidden_pairs[...] = jnp.where(allowed, 0.0, MASKED)

    total = jnp.zeros(q.shape, F32)
    for head in range(2):
        q_head = jnp.where(half_mask(q.shape, head), q, 0) * (1.0 / math.sqrt(HD))
        bias = pltpu.roll(
            jnp.broadcast_to(curve[pl.ds(2 * step + head, 1), :], (block_len, block_len + span)),
            span + 1, 1, stride=1, stride_axis=0,
        )[:, :span]
        logits = dot_nt(q_head.astype(LOW), k) + bias + hidden_pairs[...]
        weights = jnp.exp(logits - jnp.max(logits, axis=1, keepdims=True))
        prob = (weights * (1.0 / jnp.sum(weights, axis=1, keepdims=True))).astype(LOW)
        probs[head] = prob
        total = total + dot_nn(prob, jnp.where(half_mask(v.shape, head), v, 0))
    mixed[...] = total


def expand_kernel(
    place, frames, mixed, vectors, up_bias, p0, p1, p2, p3, p4, p5, p6, p7,
    middle, second, active, slope, context, up, out, stage, sems, out_sems,
):
    units, kept, width = stage.shape
    rows = p0.shape[1] - kept
    pieces = (p0, p1, p2, p3, p4, p5, p6, p7)
    copies = []
    for n, (array, z, unit) in enumerate(planes_of(place)):
        ref = pieces[array].at[z]
        at = pl.multiple_of(unit * rows, rows)
        copies.append(pltpu.make_async_copy(ref.at[:rows], up.at[pl.ds(at, rows)], sems.at[n]))
        copies.append(pltpu.make_async_copy(ref.at[rows:], stage.at[unit], out_sems.at[n]))
    for copy in copies:
        copy.start()
    for copy in copies:
        copy.wait()
    each = width // units
    for pair in range(units // 2):
        joined = jnp.concatenate(
            [stage[2 * pair].astype(F32)[:each], stage[2 * pair + 1].astype(F32)[:each]], axis=0
        )
        out[2 * each * pair : 2 * each * (pair + 1), :] = joined.astype(LOW)
    context[...] = mixed[...].astype(LOW)
    mid = frames[...].astype(F32) + (dot_nt(context[...], out[...]) + vectors[4:5, :])
    middle[...] = mid
    center = mid - jnp.mean(mid, axis=1, keepdims=True)
    normed = center * lax.rsqrt(jnp.mean(center * center, axis=1, keepdims=True) + EPSILON)
    second[...] = (normed * vectors[2:3, :] + vectors[3:4, :]).astype(LOW)
    tile = 2 * LANES

    @pl.loop(0, up.shape[0] // tile)
    def _(n):
        at = pl.multiple_of(n * tile, tile)
        hidden = dot_nt(second[...], up[pl.ds(at, tile), :]) + up_bias[0:1, pl.ds(at, tile)]
        cdf = 0.5 * (1.0 + lax.erf(hidden * 0.7071067811865476))
        density = jnp.exp(-0.5 * hidden * hidden) * 0.3989422804014327
        active[:, pl.ds(at, tile)] = (hidden * cdf).astype(LOW)
        slope[:, pl.ds(at, tile)] = cdf + hidden * density


def down_grad_kernel(
    place, active, cotangent, o0, o1, o2, o3, o4, o5, o6, o7, bias_grad, stage, sems
):
    units, rows, width = stage.shape
    each = width // units
    folds = rows // each
    dy = cotangent[...]
    bias_grad[...] = jnp.broadcast_to(
        jnp.sum(dy.astype(F32), axis=0, keepdims=True), bias_grad.shape
    )
    group = 2 * LANES // each if 2 * LANES % each == 0 else 8
    for start in range(0, units, group):
        lane = slice(start * each, (start + group) * each)
        grads = [
            dot_tn(dy[:, lane], active[:, fold * width : (fold + 1) * width]) for fold in range(folds)
        ]
        for n in range(group):
            stage[start + n] = jnp.concatenate(
                [grad[n * each : (n + 1) * each] for grad in grads], axis=0
            ).astype(LOW)
    store_units(place, stage, (o0, o1, o2, o3, o4, o5, o6, o7), sems)


def hidden_grad_kernel(
    place, cotangent, slope, p0, p1, p2, p3, p4, p5, p6, p7,
    down, up_bias_grad, hidden_grad, stage, sems,
):
    units, rows, width = stage.shape
    each = width // units
    folds = rows // each
    copies = load_units(place, (p0, p1, p2, p3, p4, p5, p6, p7), stage, sems)
    for copy in copies:
        copy.wait()
    for pair in range(units // 2):
        one, two = stage[2 * pair].astype(F32), stage[2 * pair + 1].astype(F32)
        for fold in range(folds):
            both = jnp.concatenate(
                [one[fold * each : (fold + 1) * each], two[fold * each : (fold + 1) * each]], axis=0
            )
            down[2 * each * pair : 2 * each * (pair + 1), fold * width : (fold + 1) * width] = (
                both.astype(LOW)
            )
    dy = cotangent[...]
    tile = 2 * LANES
    for n in range(hidden_grad.shape[1] // tile):
        at = slice(n * tile, (n + 1) * tile)
        grad = (dot_nn(dy, down[:, at]) * slope[:, at]).astype(LOW)
        hidden_grad[:, at] = grad
        up_bias_grad[:, at] = jnp.broadcast_to(
            jnp.sum(grad.astype(F32), axis=0, keepdims=True), (up_bias_grad.shape[0], tile)
        )


def middle_grad_kernel(
    cotangent, hidden_grad, middle, vectors, up, out, middle_grad, context_grad, vector_grads, branch_grad
):
    width = cotangent.shape[1]
    second_grad = dot_nn(hidden_grad[...], up[...])
    mid = middle[...]
    center = mid - jnp.mean(mid, axis=1, keepdims=True)
    inv_std = lax.rsqrt(jnp.mean(center * center, axis=1, keepdims=True) + EPSILON)
    normed = center * inv_std
    scaled = second_grad * vectors[2:3, :]
    inner = (
        scaled
        - jnp.mean(scaled, axis=1, keepdims=True)
        - normed * jnp.mean(scaled * normed, axis=1, keepdims=True)
    )
    mid_grad = cotangent[...].astype(F32) + inner * inv_std
    middle_grad[...] = mid_grad
    branch = mid_grad.astype(LOW)
    vector_grads[...] = jnp.concatenate(
        [
            jnp.sum(second_grad * normed, axis=0, keepdims=True),
            jnp.sum(second_grad, axis=0, keepdims=True),
            jnp.sum(branch.astype(F32), axis=0, keepdims=True),
            jnp.zeros((5, width), F32),
        ],
        axis=0,
    )
    branch_grad[...] = branch
    context_grad[...] = dot_nn(branch, out[...]).astype(LOW)


def up_grad_kernel(
    place, hidden_grad, second, branch_grad, context,
    o0, o1, o2, o3, o4, o5, o6, o7, out_stage, up_stage, sems,
):
    units, _, width = up_stage.shape
    each = width // units
    up_rows = hidden_grad.shape[1] // units
    out_grad = dot_tn(branch_grad[...], context[...])
    blank = jnp.zeros((rows_left(each), width), F32)
    for unit in range(units):
        out_stage[unit] = jnp.concatenate(
            [out_grad[unit * each : (unit + 1) * each], blank], axis=0
        ).astype(LOW)
    batch = 8
    for start in range(0, units, batch):
        at = slice(start * up_rows, (start + batch) * up_rows)
        grad = dot_tn(hidden_grad[:, at], second[...]).astype(LOW)
        for n in range(batch):
            up_stage[start + n, :up_rows] = grad[n * up_rows : (n + 1) * up_rows]
            up_stage[start + n, up_rows:] = out_stage[start + n]
    store_units(place, up_stage, (o0, o1, o2, o3, o4, o5, o6, o7), sems)


def rows_left(each):
    return -each % 16


def finish_kernel(active, down, middle, vectors, layer_out):
    layer_out[...] = middle[...] + dot_nt(active[...], down[...]) + vectors[5:6, :]


def attend_back_kernel(
    queries, keys, values, context_grad, mixed, probs, query_grad, key_grad, value_grad, diagonals
):
    q, k, v, dout = queries[...], keys[...], values[...], context_grad[...]
    block_len, span = probs.shape[1:]
    weighted = dout.astype(F32) * mixed[...]
    row = lax.broadcasted_iota(jnp.int32, (block_len, block_len), 0)
    lane = lax.broadcasted_iota(jnp.int32, (block_len, block_len), 1)
    turn = (row + lane == block_len - 1).astype(LOW)
    blank = jnp.zeros((block_len, block_len), F32)
    dq, dk, dv = jnp.zeros(q.shape, F32), jnp.zeros(k.shape, F32), jnp.zeros(v.shape, F32)
    for head in range(2):
        mine = half_mask(q.shape, head)
        dout_head = jnp.where(mine, dout, 0)
        delta = jnp.sum(jnp.where(mine, weighted, 0.0), axis=1, keepdims=True)
        prob = probs[head]
        grad = prob.astype(F32) * (dot_nt(dout_head, v) - delta)
        raw = (grad * (1.0 / math.sqrt(HD))).astype(LOW)
        dq = dq + dot_nn(raw, jnp.where(half_mask(k.shape, head), k, 0))
        dk = dk + dot_tn(raw, jnp.where(mine, q, 0))
        dv = dv + dot_tn(prob, dout_head)
        turned = jnp.concatenate([dot_nn(turn, raw), blank], axis=1)
        sheared = pltpu.roll(turned, 0, 1, stride=1, stride_axis=0)
        diagonals[pl.ds(2 * pl.program_id(0) + head, 1), :] = jnp.sum(sheared, axis=0, keepdims=True) * math.sqrt(HD)
    query_grad[...] = dq.astype(LOW)
    key_grad[...] = dk.astype(LOW)
    value_grad[...] = dv.astype(LOW)


def qkv_grad_kernel(
    place, own_frames, mate_frames, first, query_grad, key_grad, value_grad, weight, vectors,
    diagonals, buckets, vector_grads, down_bias_grad, up_bias_grad, wide_one, wide_two, wide_four,
    o0, o1, o2, o3, o4, o5, o6, o7, own_grad, mate_grad, grads, small, stage, sems,
):
    units, full, width = stage.shape
    rows = full - PAD
    shard_len = own_frames.shape[0]
    x = place[0]
    own_at = pl.multiple_of(x * shard_len, shard_len)
    mate_at = pl.multiple_of((1 - x) * shard_len, shard_len)
    dq, dk, dv = query_grad[...], key_grad[...], value_grad[...]
    grads[:width, :] = dot_tn(dq, first[pl.ds(own_at, shard_len), :])
    grads[width : 2 * width, :] = dot_tn(dk, first[...])
    grads[2 * width :, :] = dot_tn(dv, first[...])

    def first_grad(at):
        return dot_nn(key_grad[pl.ds(at, shard_len), :], weight[width : 2 * width, :]) + dot_nn(
            value_grad[pl.ds(at, shard_len), :], weight[2 * width :, :]
        )

    def normed(frames):
        wide = frames.astype(F32)
        center = wide - jnp.mean(wide, axis=1, keepdims=True)
        return center * lax.rsqrt(jnp.mean(center * center, axis=1, keepdims=True) + EPSILON)

    of_own = first_grad(own_at) + dot_nn(dq, weight[:width, :])
    of_mate = first_grad(mate_at)
    own_grad[...] = of_own
    mate_grad[...] = of_mate.astype(LOW)

    def total(array):
        return jnp.sum(array, axis=0, keepdims=True)

    gain_grad = total(of_own * normed(own_frames[...])) + total(of_mate * normed(mate_frames[...]))
    shift_grad = total(of_own) + total(of_mate)
    narrow = (
        gain_grad, shift_grad, vector_grads[0:1, :], vector_grads[1:2, :], vector_grads[2:3, :],
        down_bias_grad[0:1, :],
    )

    def fold(vector, table):
        kept = (vector * table[:units, :].astype(F32)).astype(LOW)
        return dot_nt(kept, table[units:, :])

    for n, vector in enumerate(narrow):
        small[0, :, n * LANES : (n + 1) * LANES] = fold(vector, wide_one)
    small[1, :, :] = jnp.zeros((units, width), F32)
    both = jnp.concatenate([total(dq.astype(F32)), total(dv.astype(F32))], axis=1)
    small[1, :, :LANES] = fold(both, wide_two)
    small[1, :, LANES : 2 * LANES] = fold(up_bias_grad[0:1, :], wide_four)
    table = lax.dot_general(
        diagonals[...], buckets[...], (((1,), (0,)), ((), ())), precision=HIGHEST, preferred_element_type=F32
    )
    table = jnp.concatenate([table[: H // 2], table[H // 2 :]], axis=1)
    for unit in range(units):
        stage[unit] = jnp.concatenate(
            [
                grads[unit * rows : (unit + 1) * rows, :],
                small[0, unit : unit + 1, :],
                small[1, unit : unit + 1, :],
                table,
            ],
            axis=0,
        ).astype(LOW)
    store_units(place, stage, (o0, o1, o2, o3, o4, o5, o6, o7), sems)


def input_grad_kernel(frames, own_grad, mate_part, middle_grad, vectors, frames_grad):
    wide = frames[...].astype(F32)
    center = wide - jnp.mean(wide, axis=1, keepdims=True)
    inv_std = lax.rsqrt(jnp.mean(center * center, axis=1, keepdims=True) + EPSILON)
    normed = center * inv_std
    scaled = (own_grad[...] + mate_part[...].astype(F32)) * vectors[0:1, :]
    inner = (
        scaled
        - jnp.mean(scaled, axis=1, keepdims=True)
        - normed * jnp.mean(scaled * normed, axis=1, keepdims=True)
    )
    frames_grad[...] = middle_grad[...] + inner * inv_std


def pack_kernel(
    live, qkv, out, up, down, first_gain, first_shift, second_gain, second_shift, out_bias,
    down_bias, qv_bias, up_bias, qkv_unit, up_unit, down_unit,
):
    each, width = out.shape

    def slots(vectors):
        parts = []
        for vector in vectors:
            wide = vector[...].astype(F32)
            parts += [wide, jnp.zeros((1, LANES - wide.shape[1]), F32)]
        left = width - LANES * len(vectors)
        if left:
            parts.append(jnp.zeros((1, left), F32))
        return jnp.concatenate(parts, axis=1)

    narrow = slots((first_gain, first_shift, second_gain, second_shift, out_bias, down_bias))
    wide = slots((qv_bias, up_bias))
    seen = live[...].astype(F32)
    seen = jnp.concatenate([seen, jnp.zeros((1, width - seen.shape[1]), F32)], axis=1)
    blank = jnp.zeros((PAD - 3, width), F32)
    qkv_unit[...] = jnp.concatenate([qkv[...].astype(F32), narrow, wide, seen, blank], axis=0).astype(LOW)
    blank = jnp.zeros((up_unit.shape[0] - up.shape[0] - each, width), F32)
    up_unit[...] = jnp.concatenate(
        [up[...].astype(F32), out[...].astype(F32), blank], axis=0
    ).astype(LOW)
    down_unit[...] = jnp.concatenate(
        [
            down[:, fold * width : (fold + 1) * width].astype(F32)
            for fold in range(down.shape[1] // width)
        ],
        axis=0,
    ).astype(LOW)


def paired_body(
    frames, cotangent, seq_lengths, key_mask, qkv_weight, query_value_bias, out_weight, out_bias,
    up_weight, up_bias, down_weight, down_bias, first_gain, first_shift, second_gain, second_shift,
    rel_bias,
):
    shard_len, width = frames.shape
    x = lax.axis_index("blk")
    d = lax.axis_index("dp")
    core = d % 2
    units = lax.axis_size("dp") * lax.axis_size("blk")
    span = shard_len * lax.axis_size("blk")
    place = jnp.stack([x, (d // 2) % 2, d // 4, core]).astype(jnp.int32)
    each = width // units
    ff = up_weight.shape[1] * units
    qkv_rows, up_rows = qkv_weight.shape[1], up_weight.shape[1]
    folds = ff // width
    down_rows = each * folds
    out_rows = each + rows_left(each)

    def shape(*dims, kind=LOW):
        return jax.ShapeDtypeStruct(dims, kind)

    def row(vector):
        return vector.reshape(1, vector.shape[0])

    packed = (
        row(key_mask), qkv_weight.T, out_weight.T, up_weight.T, down_weight.T, row(first_gain),
        row(first_shift), row(second_gain), row(second_shift), row(out_bias), row(down_bias),
        row(query_value_bias), row(up_bias),
    )
    qkv_unit, up_unit, down_unit = call(
        pack_kernel,
        [VMEM] * len(packed),
        [shape(qkv_rows + PAD, width), shape(up_rows + out_rows, width), shape(down_rows, width)],
        [VMEM] * 3,
        [],
        packed,
        0,
        name="pack",
    )
    def twins(pieces):
        return tuple(pieces) + tuple(twin(piece) for piece in pieces)

    qkv_z = along_z(qkv_unit, "qkv")
    mate_frames = shift(tied(frames, qkv_unit), PACK, "frames_pack")
    qkv_z, mate_frames = joined(qkv_z, mate_frames)
    qkv_own = jnp.stack((qkv_unit,) + qkv_z)
    qkv_side = shift(qkv_own, SIDE, "qkv_1")
    up_first = tied(up_unit, qkv_own)
    up_z = [shift(up_first, move, "up_z") for move in ALONG_Z[:2]]
    qkv_side, up_z = joined(qkv_side, up_z)
    qkv_other = shift(qkv_own, OTHER_SIDE, "qkv_2")
    qkv_across = shift(qkv_side, OTHER_SIDE, "qkv_3")
    up_z.append(shift(tied(up_unit, qkv_side), ALONG_Z[2], "up_z"))
    up_z, qkv_other, qkv_across = joined(up_z, qkv_other, qkv_across)
    qkv_pieces = twins((qkv_own, qkv_side, qkv_other, qkv_across))
    up_own = jnp.stack([up_unit] + up_z)
    up_side = shift(up_own, SIDE, "up_1")
    down_first = tied(down_unit, up_own)
    down_z = [shift(down_first, move, "down_z") for move in ALONG_Z[:2]]

    distance = jnp.arange(span + shard_len, dtype=jnp.int32) - (shard_len - 1) - x * shard_len
    bucket = jnp.clip(distance, -MAXREL, MAXREL) + MAXREL
    bucket_lanes = 3 * LANES
    buckets = (bucket[:, None] == jnp.arange(bucket_lanes, dtype=jnp.int32)[None, :]).astype(LOW)
    curve = lax.dot_general(
        rel_bias, buckets[:, :BUCKETS], (((0,), (1,)), ((), ())), preferred_element_type=F32
    )
    spreads = spread_tables(units, width)
    unit_sems = pltpu.SemaphoreType.DMA((units,))
    first, queries, keys, values, weight, vectors, up_bias_all, mate_live = call(
        project_kernel,
        [SMEM, VMEM, VMEM] + [ANY] * 8 + [VMEM] * 3,
        [
            shape(span, width), shape(shard_len, width), shape(span, width), shape(span, width),
            shape(3 * width, width), shape(8, width, kind=F32), shape(8, ff, kind=F32),
            shape(PAD, shard_len, kind=F32),
        ],
        [VMEM] * 8,
        [
            pltpu.VMEM((units, qkv_rows + PAD, width), LOW), pltpu.VMEM((2, units, width), F32), unit_sems,
        ],
        (tied(place, up_own), frames, mate_frames) + qkv_pieces + tuple(spreads),
        2 * shard_len * width * 5 * width,
        name="project",
    )
    up_side, keys, down_z = joined(up_side, keys, down_z)
    up_other = shift(up_own, OTHER_SIDE, "up_2")
    up_across = shift(up_side, OTHER_SIDE, "up_3")
    down_z.append(shift(tied(down_unit, keys), ALONG_Z[2], "down_z"))
    pairs = H // 2
    pair_lanes = 2 * HD

    def lanes_of(rows):
        return pl.BlockSpec((rows, pair_lanes), lambda n: (0, n))

    def heads_of(*dims):
        return pl.BlockSpec(dims, lambda n: (n,) + (0,) * (len(dims) - 1))

    def whole(*dims):
        return pl.BlockSpec(dims, lambda n: (0,) * len(dims))

    probs, mixed = call(
        attend_kernel,
        [
            SMEM, SMEM, lanes_of(shard_len), lanes_of(span), lanes_of(span), whole(H, span + shard_len),
            whole(1, shard_len), whole(PAD, shard_len),
        ],
        [shape(H, shard_len, span), shape(shard_len, width, kind=F32)],
        [heads_of(2, shard_len, span), lanes_of(shard_len)],
        [pltpu.VMEM((shard_len, span), F32)],
        (
            tied(place, up_side), seq_lengths, queries, keys, values, curve, row(key_mask), mate_live,
        ),
        8 * shard_len * span * width,
        grid=(pairs,),
        name="attend",
    )
    up_other, up_across, mixed, down_z = joined(up_other, up_across, mixed, down_z)
    up_pieces = twins((up_own, up_side, up_other, up_across))
    down_own = jnp.stack([down_unit] + down_z)
    down_side = shift(down_own, SIDE, "down_1")
    down_other = shift(down_own, OTHER_SIDE, "down_2")
    middle, second, active, slope, context, up, out = call(
        expand_kernel,
        [SMEM] + [VMEM] * 4 + [ANY] * 8,
        [
            shape(shard_len, width, kind=F32), shape(shard_len, width), shape(shard_len, ff),
            shape(shard_len, ff, kind=F32), shape(shard_len, width), shape(ff, width), shape(width, width),
        ],
        [VMEM] * 7,
        [pltpu.VMEM((units, out_rows, width), LOW), unit_sems, unit_sems],
        (tied(place, down_own), frames, mixed, vectors, up_bias_all) + up_pieces,
        2 * shard_len * width * (width + ff),
        name="expand",
    )
    down_side, down_other, active = joined(down_side, down_other, active)
    down_across = shift(down_side, OTHER_SIDE, "down_3")
    down_parts = call(
        down_grad_kernel,
        [SMEM, VMEM, VMEM],
        part_shapes(down_rows, width) + [shape(8, width, kind=F32)],
        [ANY] * 8 + [VMEM],
        [pltpu.VMEM((units, down_rows, width), LOW), unit_sems],
        (tied(place, down_side), active, cotangent),
        2 * shard_len * width * ff,
        name="down_grad",
    )
    down_bias_grad = down_parts[8]
    down_pieces = twins((down_own, down_side, down_other, down_across))
    corner = added(down_parts[3], down_parts[7]).astype(LOW)
    turned = shift(corner, OTHER_SIDE, "rs_down_3")
    other = added(down_parts[2], down_parts[6]).astype(LOW)
    side = added(down_parts[1], down_parts[5])
    down, up_bias_grad, hidden_grad = call(
        hidden_grad_kernel,
        [SMEM] + [VMEM] * 2 + [ANY] * 8,
        [shape(width, ff), shape(8, ff, kind=F32), shape(shard_len, ff)],
        [VMEM] * 3,
        [pltpu.VMEM((units, down_rows, width), LOW), unit_sems],
        (tied(place, corner), cotangent, slope) + down_pieces,
        2 * shard_len * width * ff,
        name="hidden_grad",
    )
    turned, other, hidden_grad = joined(turned, other, hidden_grad)
    down_two = shift(other, OTHER_SIDE, "rs_down_2")
    side = (side + turned.astype(F32)).astype(LOW)
    middle_grad, context_grad, vector_grads, branch_grad = call(
        middle_grad_kernel,
        [VMEM] * 6,
        [
            shape(shard_len, width, kind=F32), shape(shard_len, width), shape(8, width, kind=F32),
            shape(shard_len, width),
        ],
        [VMEM] * 4,
        [],
        (tied(cotangent, side), hidden_grad, middle, vectors, up, out),
        2 * shard_len * width * (ff + width),
        name="middle_grad",
    )
    down_two, side, branch_grad = joined(down_two, side, branch_grad)
    down_one = shift(side, SIDE, "rs_down_1")
    up_parts = call(
        up_grad_kernel,
        [SMEM] + [VMEM] * 4,
        part_shapes(up_rows + out_rows, width),
        [ANY] * 8,
        [
            pltpu.VMEM((units, out_rows, width), LOW),
            pltpu.VMEM((units, up_rows + out_rows, width), LOW), unit_sems,
        ],
        (place, hidden_grad, second, branch_grad, context),
        2 * shard_len * width * (ff + width),
        name="up_grad",
    )
    down_one, up_parts = joined(down_one, up_parts)
    corner = added(up_parts[3], up_parts[7]).astype(LOW)
    turned = shift(corner, OTHER_SIDE, "rs_up_3")
    other = added(up_parts[2], up_parts[6]).astype(LOW)
    side = added(up_parts[1], up_parts[5])
    down_sum = added(down_parts[0], down_parts[4]) + down_one.astype(F32) + down_two.astype(F32)
    down_far = shift(down_sum[2:].astype(LOW), ALONG_Z[1], "rs_down_z2")
    query_grad, key_grad, value_grad, diagonals = call(
        attend_back_kernel,
        [
            lanes_of(shard_len), lanes_of(span), lanes_of(span), lanes_of(shard_len), lanes_of(shard_len),
            heads_of(2, shard_len, span),
        ],
        [
            shape(shard_len, width), shape(span, width), shape(span, width),
            shape(H, span + shard_len, kind=F32),
        ],
        [lanes_of(shard_len), lanes_of(span), lanes_of(span), whole(H, span + shard_len)],
        [],
        (queries, keys, values, tied(context_grad, corner, down_sum), mixed, probs),
        16 * shard_len * span * width,
        grid=(pairs,),
        name="attend_back",
    )
    turned, other, query_grad, down_far = joined(turned, other, query_grad, down_far)
    down_two = down_sum[:2] + down_far.astype(F32)
    down_near = shift(down_two[1].astype(LOW), ALONG_Z[0], "rs_down_z1")
    up_two = shift(other, OTHER_SIDE, "rs_up_2")
    side = (side + turned.astype(F32)).astype(LOW)
    up_one = shift(side, SIDE, "rs_up_1")
    qkv_parts = call(
        qkv_grad_kernel,
        [SMEM] + [VMEM] * 16,
        part_shapes(qkv_rows + PAD, width) + [shape(shard_len, width, kind=F32), shape(shard_len, width)],
        [ANY] * 8 + [VMEM] * 2,
        [
            pltpu.VMEM((3 * width, width), F32), pltpu.VMEM((2, units, width), F32),
            pltpu.VMEM((units, qkv_rows + PAD, width), LOW), unit_sems,
        ],
        (
            tied(place, side, down_two), frames, mate_frames, first, query_grad, key_grad, value_grad, weight,
            vectors, diagonals, buckets.astype(F32), vector_grads, down_bias_grad, up_bias_grad,
        ) + tuple(spreads),
        2 * shard_len * width * 10 * width,
        name="qkv_grad",
    )
    down_near, up_one, up_two, qkv_parts = joined(down_near, up_one, up_two, qkv_parts)
    own_grad, mate_grad = qkv_parts[8:]
    corner = added(qkv_parts[3], qkv_parts[7]).astype(LOW)
    turned = shift(corner, OTHER_SIDE, "rs_qkv_3")
    up_sum = added(up_parts[0], up_parts[4]) + up_one.astype(F32) + up_two.astype(F32)
    up_low = up_sum.astype(LOW)
    up_z = [shift(up_low[n + 1], ALONG_Z[n], "rs_up_z") for n in range(2)]
    other = added(qkv_parts[2], qkv_parts[6]).astype(LOW)
    side = added(qkv_parts[1], qkv_parts[5])
    layer_out = call(
        finish_kernel,
        [VMEM] * 4,
        [shape(shard_len, width, kind=F32)],
        [VMEM],
        [],
        (tied(active, corner, up_low), down, middle, vectors),
        2 * shard_len * width * ff,
        name="finish",
    )[0]
    down_sum = down_two[0] + down_near.astype(F32)
    turned, other, up_z, layer_out = joined(turned, other, up_z, layer_out)
    side = (side + turned.astype(F32)).astype(LOW)
    qkv_two = shift(other, OTHER_SIDE, "rs_qkv_2")
    qkv_one = shift(side, SIDE, "rs_qkv_1")
    up_z.append(shift(tied(up_low[3], side), ALONG_Z[2], "rs_up_z"))
    qkv_one, qkv_two, up_z = joined(qkv_one, qkv_two, up_z)
    qkv_sum = added(qkv_parts[0], qkv_parts[4]) + qkv_one.astype(F32) + qkv_two.astype(F32)
    qkv_z = z_sends(qkv_sum, "rs_qkv")
    mate_part = shift(tied(mate_grad, qkv_sum), PACK, "grad_pack")
    up_sum = z_sum(tied(up_sum, qkv_sum), up_z)
    qkv_sum = z_sum(qkv_sum, qkv_z)
    frames_grad = call(
        input_grad_kernel,
        [VMEM] * 5,
        [shape(shard_len, width, kind=F32)],
        [VMEM],
        [],
        (frames, own_grad, mate_part, middle_grad, vectors),
        0,
        name="input_grad",
    )[0]

    down_grad = jnp.concatenate(
        [down_sum[fold * each : (fold + 1) * each] for fold in range(folds)], axis=1
    )
    narrow_sum, wide_sum, table_sum = (
        qkv_sum[qkv_rows], qkv_sum[qkv_rows + 1], qkv_sum[qkv_rows + 2 :],
    )
    table = jnp.concatenate([table_sum[:, :BUCKETS], table_sum[:, bucket_lanes : bucket_lanes + BUCKETS]])
    pieces = [narrow_sum[n * LANES : n * LANES + each] for n in range(NARROW)]
    return (
        layer_out, frames_grad, qkv_sum[:qkv_rows].T, wide_sum[: 2 * each],
        up_sum[up_rows : up_rows + each].T, pieces[4], up_sum[:up_rows].T,
        wide_sum[LANES : LANES + up_rows], down_grad.T, pieces[5], pieces[0], pieces[1], pieces[2],
        pieces[3], table.T,
    )


def paired(mesh):
    return mesh.shape["blk"] == 2 and mesh.shape["dp"] == 16


def solution(mesh):
    placed = (
        P(("dp", "blk"), None),
        P(("dp", "blk"), None),
        P("dp", None),
        P(("dp", "blk")),
        P(None, ("dp", "blk")),
        P(("dp", "blk")),
        P(None, ("dp", "blk")),
        P(("dp", "blk")),
        P(None, ("dp", "blk")),
        P(("dp", "blk")),
        P(None, ("dp", "blk")),
        P(("dp", "blk")),
        P(("dp", "blk")),
        P(("dp", "blk")),
        P(("dp", "blk")),
        P(("dp", "blk")),
        P(),
    )
    return jax.shard_map(
        paired_body if paired(mesh) else body,
        mesh=mesh,
        in_specs=placed,
        out_specs=(
            P(("dp", "blk"), None),
            P(("dp", "blk"), None),
            P(None, ("dp", "blk")),
            P(("dp", "blk")),
            P(None, ("dp", "blk")),
            P(("dp", "blk")),
            P(None, ("dp", "blk")),
            P(("dp", "blk")),
            P(None, ("dp", "blk")),
            P(("dp", "blk")),
            P(("dp", "blk")),
            P(("dp", "blk")),
            P(("dp", "blk")),
            P(("dp", "blk")),
            P(),
        ),
        check_vma=False,
    )
```

```python
import math

import jax
import jax.numpy as jnp
import numpy as np
from jax import lax
from jax.experimental import pallas as pl
from jax.experimental.pallas import tpu as pltpu
from jax.sharding import PartitionSpec as P

H = 12
HD = 64
MAXREL = 160
BLOCK = 256
BUCKETS = 321


EPSILON = 1e-05
MASKED = -2e30
START_PEAK = -1e30
HIGHEST = lax.Precision.HIGHEST


def from_behind(block, axis, distance):
    devices = range(lax.axis_size(axis))
    route = [((i - distance) % len(devices), i) for i in devices]
    return lax.ppermute(block, axis, route)


def layer_norm(values, gain_vec, shift_vec):
    center = values - jnp.mean(values, axis=-1, keepdims=True)
    inv_std = lax.rsqrt(jnp.mean(center * center, axis=-1, keepdims=True) + EPSILON)
    normed = center * inv_std
    return (normed * gain_vec + shift_vec, normed, inv_std)


def norm_back(gradient, normed, inv_std, gain_vec):
    scaled = gradient * gain_vec
    inner = (
        scaled
        - jnp.mean(scaled, axis=-1, keepdims=True)
        - normed * jnp.mean(scaled * normed, axis=-1, keepdims=True)
    )
    return (inner * inv_std, jnp.sum(gradient * normed, axis=0), jnp.sum(gradient, axis=0))


def gelu_parts(values):
    normal_cdf = 0.5 * (1.0 + lax.erf(values * 0.7071067811865476))
    density = jnp.exp(-0.5 * values * values) * 0.3989422804014327
    return (values * normal_cdf, normal_cdf + values * density)


def doc_numbers(seq_ends, positions):
    return jnp.sum((positions[:, None] >= seq_ends[None, :]).astype(jnp.int32), axis=1)


def pair_logits(
    query_block, key_block, query_pos, key_pos, query_doc, key_doc, key_live, table_heads
):
    block_len = query_block.shape[0]
    raw = jnp.einsum(
        "qhd,khd->hqk",
        query_block.reshape(block_len, H, HD),
        key_block.reshape(-1, H, HD),
        preferred_element_type=jnp.float32,
    )
    relative = jnp.clip(key_pos[None, :] - query_pos[:, None], -MAXREL, MAXREL) + MAXREL
    bias = jnp.take(table_heads, relative, axis=1)
    allowed = (query_doc[:, None] == key_doc[None, :]) & (
        (key_live[None, :] > 0.5) | (query_pos[:, None] == key_pos[None, :])
    )
    return jnp.where(allowed[None], raw * (1.0 / math.sqrt(HD)) + bias, MASKED)


def diagonal_sums(gradient, offset):
    heads, block_len, _ = gradient.shape
    flipped = gradient[:, ::-1, :]
    padded = jnp.pad(flipped, ((0, 0), (0, 0), (0, block_len)))
    sheared = padded.reshape(heads, 2 * block_len * block_len)[:, : block_len * (2 * block_len - 1)]
    sheared = sheared.reshape(heads, block_len, 2 * block_len - 1)
    diag_sums = jnp.sum(sheared, axis=1)
    distance = offset + jnp.arange(2 * block_len - 1, dtype=jnp.int32) - (block_len - 1)
    bucket = jnp.clip(distance, -MAXREL, MAXREL) + MAXREL
    onehot = (bucket[:, None] == jnp.arange(BUCKETS, dtype=jnp.int32)[None, :]).astype(jnp.float32)
    return jnp.dot(diag_sums, onehot, precision=HIGHEST)


def body(
    frames,
    cotangent,
    seq_lengths,
    key_mask,
    qkv_weight,
    query_value_bias,
    out_weight,
    out_bias,
    up_weight,
    up_bias,
    down_weight,
    down_bias,
    first_gain,
    first_shift,
    second_gain,
    second_shift,
    rel_bias,
):
    cycle_size = lax.axis_size("blk")
    cycle_place = lax.axis_index("blk")
    shard_len = frames.shape[0]
    width = frames.shape[1]
    block_count = shard_len // BLOCK
    score_scale = 1.0 / math.sqrt(HD)
    seq_ends = jnp.cumsum(seq_lengths[0])
    local_pos = jnp.arange(shard_len, dtype=jnp.int32)
    positions = cycle_place * shard_len + local_pos
    own_docs = doc_numbers(seq_ends, positions)
    table_heads = rel_bias.astype(jnp.float32).T

    def blocked(array):
        return array.reshape((block_count, BLOCK) + array.shape[1:])

    def key_meta(turn):
        source = (cycle_place - turn) % cycle_size
        key_pos = source * shard_len + local_pos
        return (key_pos, doc_numbers(seq_ends, key_pos))

    gathered = (
        lax.all_gather(qkv_weight, ("dp", "blk"), axis=1, tiled=True),
        lax.all_gather(query_value_bias, ("dp", "blk"), axis=0, tiled=True),
        lax.all_gather(out_weight, ("dp", "blk"), axis=1, tiled=True),
        lax.all_gather(out_bias, ("dp", "blk"), axis=0, tiled=True),
        lax.all_gather(up_weight, ("dp", "blk"), axis=1, tiled=True),
        lax.all_gather(up_bias, ("dp", "blk"), axis=0, tiled=True),
        lax.all_gather(down_weight, ("dp", "blk"), axis=1, tiled=True),
        lax.all_gather(down_bias, ("dp", "blk"), axis=0, tiled=True),
        lax.all_gather(first_gain, ("dp", "blk"), axis=0, tiled=True),
        lax.all_gather(first_shift, ("dp", "blk"), axis=0, tiled=True),
        lax.all_gather(second_gain, ("dp", "blk"), axis=0, tiled=True),
        lax.all_gather(second_shift, ("dp", "blk"), axis=0, tiled=True),
    )
    (
        qkv_full,
        qv_bias_full,
        out_full,
        out_bias_full,
        up_full,
        up_bias_full,
        down_full,
        down_bias_full,
        gain_one,
        shift_one,
        gain_two,
        shift_two,
    ) = gathered
    frames_wide = frames.astype(jnp.float32)
    first_out, first_normed, first_inv = layer_norm(
        frames_wide, gain_one.astype(jnp.float32), shift_one.astype(jnp.float32)
    )
    first_low = first_out.astype(jnp.bfloat16)
    projected = jnp.dot(first_low, qkv_full, preferred_element_type=jnp.float32)
    bias_vec = qv_bias_full.astype(jnp.float32)
    queries = (projected[:, :width] + bias_vec[:width]).astype(jnp.bfloat16)
    key_rows = projected[:, width : 2 * width].astype(jnp.bfloat16)
    value_rows = (projected[:, 2 * width :] + bias_vec[width:]).astype(jnp.bfloat16)
    live_rows = key_mask.astype(jnp.bfloat16)
    query_blocks = (blocked(queries), blocked(positions), blocked(own_docs))

    def forward_hop(turn, online_state, key_part, value_part, live_part):
        key_pos, key_doc = key_meta(turn)
        key_items = (
            blocked(key_part),
            blocked(value_part),
            blocked(key_pos),
            blocked(key_doc),
            blocked(live_part),
        )

        def forward_per_query(query_items):
            query_block, query_pos, query_doc, row_peak, row_total, accum = query_items

            def online(carried, key_block_items):
                row_peak, row_total, accum = carried
                key_block, value_block, key_bpos, key_bdoc, key_blive = key_block_items
                logits = pair_logits(
                    query_block,
                    key_block,
                    query_pos,
                    key_bpos,
                    query_doc,
                    key_bdoc,
                    key_blive,
                    table_heads,
                )
                new_peak = jnp.maximum(row_peak, jnp.max(logits, axis=2))
                decay = jnp.exp(row_peak - new_peak)
                weights = jnp.exp(logits - new_peak[:, :, None])
                row_total = row_total * decay + jnp.sum(weights, axis=2)
                accum = accum * decay.T[:, :, None] + jnp.einsum(
                    "hqk,khd->qhd",
                    weights.astype(jnp.bfloat16),
                    value_block.reshape(-1, H, HD),
                    preferred_element_type=jnp.float32,
                )
                return ((new_peak, row_total, accum), None)

            result, unused = lax.scan(online, (row_peak, row_total, accum), key_items)
            return result

        return lax.map(forward_per_query, query_blocks + online_state)

    def cycle_turn(turn, carried):
        online_state, key_part, value_part, live_part = carried
        online_state = forward_hop(turn, online_state, key_part, value_part, live_part)
        key_part, value_part, live_part = from_behind((key_part, value_part, live_part), "blk", 1)
        return (online_state, key_part, value_part, live_part)

    start_state = (
        jnp.full((block_count, H, BLOCK), START_PEAK, jnp.float32),
        jnp.zeros((block_count, H, BLOCK), jnp.float32),
        jnp.zeros((block_count, BLOCK, H, HD), jnp.float32),
    )
    carried = lax.fori_loop(
        0, cycle_size - 1, cycle_turn, (start_state, key_rows, value_rows, live_rows)
    )
    row_peak, row_total, accum = forward_hop(
        cycle_size - 1, carried[0], carried[1], carried[2], carried[3]
    )
    mixed = accum / jnp.transpose(row_total, (0, 2, 1))[:, :, :, None]
    mixed_flat = mixed.reshape(shard_len, width)
    context = mixed_flat.astype(jnp.bfloat16)
    branch = jnp.dot(context, out_full, preferred_element_type=jnp.float32) + out_bias_full.astype(
        jnp.float32
    )
    middle = frames_wide + branch
    second_out, second_normed, second_inv = layer_norm(
        middle, gain_two.astype(jnp.float32), shift_two.astype(jnp.float32)
    )
    second_low = second_out.astype(jnp.bfloat16)
    hidden = jnp.dot(second_low, up_full, preferred_element_type=jnp.float32) + up_bias_full.astype(
        jnp.float32
    )
    active, slope = gelu_parts(hidden)
    active_low = active.astype(jnp.bfloat16)
    layer_out = (
        middle
        + jnp.dot(active_low, down_full, preferred_element_type=jnp.float32)
        + down_bias_full.astype(jnp.float32)
    )
    weights_back = (
        lax.all_gather(qkv_weight, ("dp", "blk"), axis=1, tiled=True),
        lax.all_gather(query_value_bias, ("dp", "blk"), axis=0, tiled=True),
        lax.all_gather(out_weight, ("dp", "blk"), axis=1, tiled=True),
        lax.all_gather(out_bias, ("dp", "blk"), axis=0, tiled=True),
        lax.all_gather(up_weight, ("dp", "blk"), axis=1, tiled=True),
        lax.all_gather(up_bias, ("dp", "blk"), axis=0, tiled=True),
        lax.all_gather(down_weight, ("dp", "blk"), axis=1, tiled=True),
        lax.all_gather(down_bias, ("dp", "blk"), axis=0, tiled=True),
        lax.all_gather(first_gain, ("dp", "blk"), axis=0, tiled=True),
        lax.all_gather(first_shift, ("dp", "blk"), axis=0, tiled=True),
        lax.all_gather(second_gain, ("dp", "blk"), axis=0, tiled=True),
        lax.all_gather(second_shift, ("dp", "blk"), axis=0, tiled=True),
    )
    qkv_back = weights_back[0]
    out_back = weights_back[2]
    up_back = weights_back[4]
    down_back = weights_back[6]
    gain_one_back = weights_back[8].astype(jnp.float32)
    gain_two_back = weights_back[10].astype(jnp.float32)
    grad_wide = cotangent.astype(jnp.float32)
    down_grad = jnp.einsum("tf,td->fd", active_low, cotangent, preferred_element_type=jnp.float32)
    down_bias_grad = jnp.sum(grad_wide, axis=0)
    active_grad = jnp.einsum("td,fd->tf", cotangent, down_back, preferred_element_type=jnp.float32)
    hidden_low = (active_grad * slope).astype(jnp.bfloat16)
    up_grad = jnp.einsum("td,tf->df", second_low, hidden_low, preferred_element_type=jnp.float32)
    up_bias_grad = jnp.sum(hidden_low.astype(jnp.float32), axis=0)
    second_grad = jnp.einsum("tf,df->td", hidden_low, up_back, preferred_element_type=jnp.float32)
    middle_norm, gain_two_grad, shift_two_grad = norm_back(
        second_grad, second_normed, second_inv, gain_two_back
    )
    middle_grad = grad_wide + middle_norm
    branch_low = middle_grad.astype(jnp.bfloat16)
    out_grad = jnp.einsum("td,te->de", context, branch_low, preferred_element_type=jnp.float32)
    out_bias_grad = jnp.sum(branch_low.astype(jnp.float32), axis=0)
    context_low = jnp.einsum(
        "te,de->td", branch_low, out_back, preferred_element_type=jnp.float32
    ).astype(jnp.bfloat16)
    delta = jnp.sum(
        (context_low.astype(jnp.float32) * mixed_flat).reshape(shard_len, H, HD), axis=2
    )
    delta_blocks = jnp.transpose(blocked(delta), (0, 2, 1))
    query_back = (
        blocked(queries),
        blocked(context_low),
        blocked(positions),
        blocked(own_docs),
        row_peak,
        row_total,
        delta_blocks,
    )

    def backward_hop(
        turn, query_grad, table_grad, key_part, value_part, live_part, key_grad, value_grad
    ):
        key_pos, key_doc = key_meta(turn)

        def per_key(carried, key_block_items):
            query_grad, table_grad = carried
            key_block, value_block, key_bpos, key_bdoc, key_blive, key_bgrad, value_bgrad = (
                key_block_items
            )
            key_heads = key_block.reshape(-1, H, HD)
            value_heads = value_block.reshape(-1, H, HD)

            def per_per_query(inner, query_items):
                key_bgrad, value_bgrad, table_grad = inner
                (
                    query_block,
                    dout_block,
                    query_pos,
                    query_doc,
                    peak_block,
                    total_block,
                    delta_block,
                ) = query_items
                logits = pair_logits(
                    query_block,
                    key_block,
                    query_pos,
                    key_bpos,
                    query_doc,
                    key_bdoc,
                    key_blive,
                    table_heads,
                )
                attn_prob = jnp.exp(logits - peak_block[:, :, None]) / total_block[:, :, None]
                dout_heads = dout_block.reshape(-1, H, HD)
                prob_grad = jnp.einsum(
                    "qhd,khd->hqk", dout_heads, value_heads, preferred_element_type=jnp.float32
                )
                logit_grad = attn_prob * (prob_grad - delta_block[:, :, None])
                raw_low = (logit_grad * score_scale).astype(jnp.bfloat16)
                query_part = jnp.einsum(
                    "hqk,khd->qhd", raw_low, key_heads, preferred_element_type=jnp.float32
                ).reshape(-1, width)
                key_bgrad = key_bgrad + jnp.einsum(
                    "hqk,qhd->khd",
                    raw_low,
                    query_block.reshape(-1, H, HD),
                    preferred_element_type=jnp.float32,
                ).reshape(-1, width)
                value_bgrad = value_bgrad + jnp.einsum(
                    "hqk,qhd->khd",
                    attn_prob.astype(jnp.bfloat16),
                    dout_heads,
                    preferred_element_type=jnp.float32,
                ).reshape(-1, width)
                table_grad = table_grad + diagonal_sums(logit_grad, key_bpos[0] - query_pos[0])
                return ((key_bgrad, value_bgrad, table_grad), query_part)

            (key_bgrad, value_bgrad, table_grad), query_parts = lax.scan(
                per_per_query, (key_bgrad, value_bgrad, table_grad), query_back
            )
            return ((query_grad + query_parts, table_grad), (key_bgrad, value_bgrad))

        (query_grad, table_grad), (key_new, value_new) = lax.scan(
            per_key,
            (query_grad, table_grad),
            (
                blocked(key_part),
                blocked(value_part),
                blocked(key_pos),
                blocked(key_doc),
                blocked(live_part),
                blocked(key_grad),
                blocked(value_grad),
            ),
        )
        return (
            query_grad,
            table_grad,
            key_new.reshape(shard_len, width),
            value_new.reshape(shard_len, width),
        )

    def pass_grads(key_grad, value_grad):
        return (
            from_behind(key_grad.astype(jnp.bfloat16), "blk", 1).astype(key_grad.dtype),
            from_behind(value_grad.astype(jnp.bfloat16), "blk", 1).astype(value_grad.dtype),
        )

    def back_turn(turn, carried):
        query_grad, table_grad, key_part, value_part, live_part, key_grad, value_grad = carried
        query_grad, table_grad, key_grad, value_grad = backward_hop(
            turn, query_grad, table_grad, key_part, value_part, live_part, key_grad, value_grad
        )
        key_part, value_part, live_part = from_behind((key_part, value_part, live_part), "blk", 1)
        key_grad, value_grad = pass_grads(key_grad, value_grad)
        return (query_grad, table_grad, key_part, value_part, live_part, key_grad, value_grad)

    zero_rows = jnp.zeros((shard_len, width), jnp.float32)
    back_start = (
        jnp.zeros((block_count, BLOCK, width), jnp.float32),
        jnp.zeros((H, BUCKETS), jnp.float32),
        key_rows,
        value_rows,
        live_rows,
        zero_rows,
        zero_rows,
    )
    carried = lax.fori_loop(0, cycle_size - 1, back_turn, back_start)
    query_grad, table_grad, key_grad, value_grad = backward_hop(
        cycle_size - 1,
        carried[0],
        carried[1],
        carried[2],
        carried[3],
        carried[4],
        carried[5],
        carried[6],
    )
    key_grad, value_grad = pass_grads(key_grad, value_grad)
    query_low = query_grad.reshape(shard_len, width).astype(jnp.bfloat16)
    key_low = key_grad.astype(jnp.bfloat16)
    value_low = value_grad.astype(jnp.bfloat16)
    qkv_low = jnp.concatenate([query_low, key_low, value_low], axis=1)
    qkv_grad = jnp.einsum("td,te->de", first_low, qkv_low, preferred_element_type=jnp.float32)
    query_value_grad = jnp.concatenate(
        [
            jnp.sum(query_low.astype(jnp.float32), axis=0),
            jnp.sum(value_low.astype(jnp.float32), axis=0),
        ]
    )
    first_grad = jnp.einsum("te,de->td", qkv_low, qkv_back, preferred_element_type=jnp.float32)
    frames_norm, gain_one_grad, shift_one_grad = norm_back(
        first_grad, first_normed, first_inv, gain_one_back
    )
    frames_grad = middle_grad + frames_norm
    summed = (
        lax.psum_scatter(qkv_grad, ("dp", "blk"), scatter_dimension=1, tiled=True),
        lax.psum_scatter(query_value_grad, ("dp", "blk"), scatter_dimension=0, tiled=True),
        lax.psum_scatter(out_grad, ("dp", "blk"), scatter_dimension=1, tiled=True),
        lax.psum_scatter(out_bias_grad, ("dp", "blk"), scatter_dimension=0, tiled=True),
        lax.psum_scatter(up_grad, ("dp", "blk"), scatter_dimension=1, tiled=True),
        lax.psum_scatter(up_bias_grad, ("dp", "blk"), scatter_dimension=0, tiled=True),
        lax.psum_scatter(down_grad, ("dp", "blk"), scatter_dimension=1, tiled=True),
        lax.psum_scatter(down_bias_grad, ("dp", "blk"), scatter_dimension=0, tiled=True),
        lax.psum_scatter(gain_one_grad, ("dp", "blk"), scatter_dimension=0, tiled=True),
        lax.psum_scatter(shift_one_grad, ("dp", "blk"), scatter_dimension=0, tiled=True),
        lax.psum_scatter(gain_two_grad, ("dp", "blk"), scatter_dimension=0, tiled=True),
        lax.psum_scatter(shift_two_grad, ("dp", "blk"), scatter_dimension=0, tiled=True),
    )
    table_sum = lax.psum(table_grad, ("dp", "blk"))
    return (
        layer_out,
        frames_grad,
        summed[0],
        summed[1],
        summed[2],
        summed[3],
        summed[4],
        summed[5],
        summed[6],
        summed[7],
        summed[8],
        summed[9],
        summed[10],
        summed[11],
        table_sum.T,
    )


AXES = ("dp", "blk")
F32 = jnp.float32
LOW = jnp.bfloat16
LANES = 128
NARROW = 6
PAD = 8


def route(move):
    n_dp, n_blk = lax.axis_size("dp"), lax.axis_size("blk")
    pairs = []
    for d in range(n_dp):
        d_bits, b_bits = move[d % 2]
        for b in range(n_blk):
            pairs.append((d * n_blk + b, (d ^ d_bits) * n_blk + (b ^ b_bits)))
    return pairs


def shift(array, move, name="swap"):
    with jax.named_scope(name):
        return lax.ppermute(array, AXES, route(move))


CORE = ((1, 0), (1, 0))
SIDE = ((0, 1), (2, 0))
OTHER_SIDE = ((2, 0), (0, 1))
PACK = ((0, 1), (0, 1))
ALONG_Z = tuple(((4 * turn, 0), (4 * turn, 0)) for turn in (1, 2, 3))


def tied(value, *after):
    return lax.optimization_barrier((value,) + after)[0]


def joined(*groups):
    return lax.optimization_barrier(groups)


def twin(array, name="twin"):
    return shift(array, CORE, name)


def along_z(unit, name):
    return tuple(shift(unit, move, name + "_z") for move in ALONG_Z)


def z_sends(plane, name):
    low = plane.astype(LOW)
    return tuple(shift(low[n + 1], move, name + "_z") for n, move in enumerate(ALONG_Z))


def z_sum(plane, arrived):
    return plane[0] + sum(part.astype(F32) for part in arrived)


def unit_of(place, x_turn, y_turn, z_turn, c):
    x, y, z = place[0] ^ x_turn, place[1] ^ y_turn, place[2] ^ z_turn
    return ((z * 2 + y) * 2 + c) * 2 + x


def planes_of(place):
    c0 = place[3]
    found = []
    for plane in range(2):
        c = c0 if plane == 0 else 1 - c0
        for z in range(4):
            for n, (x_turn, y_turn) in enumerate(((0, 0), (1 - c, c), (c, 1 - c), (1, 1))):
                found.append((4 * plane + n, z, unit_of(place, x_turn, y_turn, z, c)))
    return found


def load_units(place, pieces, stage, sems):
    copies = [
        pltpu.make_async_copy(pieces[array].at[z], stage.at[unit], sems.at[n])
        for n, (array, z, unit) in enumerate(planes_of(place))
    ]
    for copy in copies:
        copy.start()
    return copies


def by_plane(place, run):
    for c in range(2):
        pl.when(place[3] == c)(lambda c=c: run(c))


def plane_columns(array, pair, c):
    count = array.shape[1] // (2 * pair)
    return jnp.concatenate(
        [array[:, (2 * n + c) * pair : (2 * n + c + 1) * pair] for n in range(count)], axis=1
    )


def store_wave(place, c, z, stage, parts, sems):
    own, side, other, across = parts
    turn = z ^ place[2]
    targets = (
        (0, 0, own), (1, 0, side if c == 0 else other), (0, 1, other if c == 0 else side), (1, 1, across),
    )
    copies = []
    for n, (x_turn, y_turn, target) in enumerate(targets):
        unit = (z * 2 + (place[1] ^ y_turn)) * 2 + (place[0] ^ x_turn)
        copies.append(pltpu.make_async_copy(stage.at[unit], target.at[turn], sems.at[4 * z + n]))
        copies[-1].start()
    return copies


def part_shapes(rows, width):
    return [jax.ShapeDtypeStruct((4, rows, width), LOW)] * 4


def dot_nn(a, b):
    return lax.dot_general(a, b, (((1,), (0,)), ((), ())), preferred_element_type=F32)


def dot_nt(a, b):
    return lax.dot_general(a, b, (((1,), (1,)), ((), ())), preferred_element_type=F32)


def dot_tn(a, b):
    return lax.dot_general(a, b, (((0,), (0,)), ((), ())), preferred_element_type=F32)


HBM = pl.BlockSpec(memory_space=pltpu.HBM)
SMEM = pl.BlockSpec(memory_space=pltpu.SMEM)
VMEM = pl.BlockSpec(memory_space=pltpu.VMEM)


def call(kernel, in_specs, outs, out_specs, scratch, args, flops, limit=56, **kwargs):
    moved = sum(math.prod(a.shape) * a.dtype.itemsize for a in list(args) + list(outs))
    return pl.pallas_call(
        kernel,
        out_shape=outs,
        in_specs=in_specs,
        out_specs=out_specs,
        scratch_shapes=scratch,
        compiler_params=pltpu.CompilerParams(vmem_limit_bytes=limit * 1024 * 1024),
        cost_estimate=pl.CostEstimate(flops=flops, bytes_accessed=moved, transcendentals=0),
        **kwargs,
    )(*args)


def spread_tables(units, width):
    tables = []
    for n in (width // units, 2 * width // units, 4 * width // units):
        lane = np.arange(units * n)
        keep = lane[None, :] // n == np.arange(units)[:, None]
        pick = lane[None, :] % n == np.arange(LANES)[:, None]
        tables.append(jnp.asarray(np.concatenate([keep, pick]), LOW))
    return tables


def project_kernel(
    place, own, other, p0, p1, p2, p3, p4, p5, p6, p7, wide_one, wide_two, wide_four,
    first, queries, keys, values, weight, vectors, up_bias, mate_live, stage, small, sems,
):
    units = stage.shape[0]
    width = own.shape[1]
    rows = stage.shape[1] - PAD
    shard_len = own.shape[0]
    copies = load_units(place, (p0, p1, p2, p3, p4, p5, p6, p7), stage, sems)

    def normed(frames):
        wide = frames.astype(F32)
        center = wide - jnp.mean(wide, axis=1, keepdims=True)
        return center * lax.rsqrt(jnp.mean(center * center, axis=1, keepdims=True) + EPSILON)

    own_normed, mate_normed = normed(own[...]), normed(other[...])
    for copy in copies:
        copy.wait()
    for unit in range(units):
        top = stage[unit, rows : rows + PAD, :].astype(F32)
        small[0, unit : unit + 1, :] = top[0:1]
        small[1, unit : unit + 1, :] = top[1:2]

    mate = unit_of(place, 1, 0, 0, place[3])
    mate_live[...] = stage[mate, rows : rows + PAD, : mate_live.shape[1]].astype(F32)

    def spread(row, slot, table):
        held = small[row, :, slot * LANES : (slot + 1) * LANES].astype(LOW)
        laid = dot_nn(held, table[units:, :]) * table[:units, :].astype(F32)
        return jnp.sum(laid, axis=0, keepdims=True)

    for n in range(NARROW):
        vectors[n : n + 1, :] = spread(0, n, wide_one)
    qv_bias = spread(1, 0, wide_two)
    up_bias[...] = jnp.broadcast_to(spread(1, 1, wide_four), up_bias.shape)
    vectors[NARROW : NARROW + 1, :] = qv_bias[:, :width]
    vectors[NARROW + 1 : NARROW + 2, :] = qv_bias[:, width:]
    for pair in range(units // 2):
        joined = jnp.concatenate(
            [stage[2 * pair, :rows, :].astype(F32), stage[2 * pair + 1, :rows, :].astype(F32)], axis=0
        )
        weight[2 * rows * pair : 2 * rows * (pair + 1), :] = joined.astype(LOW)
    gain, offset = vectors[0:1, :], vectors[1:2, :]
    x = place[0]
    own_at = pl.multiple_of(x * shard_len, shard_len)
    mate_at = pl.multiple_of((1 - x) * shard_len, shard_len)
    first[pl.ds(own_at, shard_len), :] = (own_normed * gain + offset).astype(LOW)
    first[pl.ds(mate_at, shard_len), :] = (mate_normed * gain + offset).astype(LOW)
    mine = first[pl.ds(own_at, shard_len), :]
    queries[...] = (dot_nt(mine, weight[:width, :]) + vectors[NARROW : NARROW + 1, :]).astype(LOW)
    keys[...] = dot_nt(first[...], weight[width : 2 * width, :]).astype(LOW)
    values[...] = (
        dot_nt(first[...], weight[2 * width :, :]) + vectors[NARROW + 1 : NARROW + 2, :]
    ).astype(LOW)


def half_mask(shape, head):
    return (lax.broadcasted_iota(jnp.int32, shape, 1) // HD) == head


def attend_kernel(
    place, lengths, queries, keys, values, curve, own_live, mate_live, probs, mixed, hidden_pairs
):
    q, k, v = queries[...], keys[...], values[...]
    block_len, span = hidden_pairs.shape
    step = pl.program_id(0)

    @pl.when(step == 0)
    def _():
        start = place[0] * block_len
        key_pos = lax.broadcasted_iota(jnp.int32, (1, span), 1)
        query_pos = lax.broadcasted_iota(jnp.int32, (block_len, 1), 0) + start
        key_doc, query_doc = jnp.zeros_like(key_pos), jnp.zeros_like(query_pos)
        end = 0
        for n in range(lengths.shape[1]):
            end = end + lengths[0, n]
            key_doc = key_doc + (key_pos >= end).astype(jnp.int32)
            query_doc = query_doc + (query_pos >= end).astype(jnp.int32)
        one, two = own_live[...].astype(F32), mate_live[2:3, :]
        live = jnp.where(
            place[0] == 0, jnp.concatenate([one, two], axis=1), jnp.concatenate([two, one], axis=1)
        )
        allowed = (query_doc == key_doc) & ((live > 0.5) | (query_pos == key_pos))
        hidden_pairs[...] = jnp.where(allowed, 0.0, MASKED)

    total = jnp.zeros(q.shape, F32)
    for head in range(2):
        q_head = jnp.where(half_mask(q.shape, head), q, 0) * (1.0 / math.sqrt(HD))
        bias = pltpu.roll(
            jnp.broadcast_to(curve[pl.ds(2 * step + head, 1), :], (block_len, block_len + span)),
            span + 1, 1, stride=1, stride_axis=0,
        )[:, :span]
        logits = dot_nt(q_head.astype(LOW), k) + bias + hidden_pairs[...]
        weights = jnp.exp(logits - jnp.max(logits, axis=1, keepdims=True))
        prob = (weights * (1.0 / jnp.sum(weights, axis=1, keepdims=True))).astype(LOW)
        probs[head] = prob
        total = total + dot_nn(prob, jnp.where(half_mask(v.shape, head), v, 0))
    mixed[...] = total


def load_mixed(place, pieces, up, kept, sems, kept_sems):
    rows = pieces[0].shape[1] - kept.shape[1]
    first, later = [], []
    for n, (array, z, unit) in enumerate(planes_of(place)):
        ref = pieces[array].at[z]
        at = pl.multiple_of(unit * rows, rows)
        first.append(pltpu.make_async_copy(ref.at[rows:], kept.at[unit], kept_sems.at[n]))
        later.append(pltpu.make_async_copy(ref.at[:rows], up.at[pl.ds(at, rows)], sems.at[n]))
    for copy in first + later:
        copy.start()
    return first, later


def join_units(kept, out):
    units = kept.shape[0]
    each = out.shape[0] // units
    for pair in range(units // 2):
        both = jnp.concatenate(
            [kept[2 * pair].astype(F32)[:each], kept[2 * pair + 1].astype(F32)[:each]], axis=0
        )
        out[2 * each * pair : 2 * each * (pair + 1), :] = both.astype(LOW)


def expand_kernel(
    place, frames, mixed, vectors, up_bias, p0, p1, p2, p3, p4, p5, p6, p7,
    middle, second, context, active, slope, up, kept, out, sems, kept_sems,
):
    width = frames.shape[1]
    first, later = load_mixed(place, (p0, p1, p2, p3, p4, p5, p6, p7), up, kept, sems, kept_sems)
    context[...] = mixed[...].astype(LOW)
    for copy in first:
        copy.wait()
    join_units(kept, out)
    mid = frames[...].astype(F32) + (dot_nt(context[...], out[...]) + vectors[4:5, :])
    middle[...] = mid
    center = mid - jnp.mean(mid, axis=1, keepdims=True)
    normed = center * lax.rsqrt(jnp.mean(center * center, axis=1, keepdims=True) + EPSILON)
    second[...] = (normed * vectors[2:3, :] + vectors[3:4, :]).astype(LOW)
    for copy in later:
        copy.wait()
    for n in range(up.shape[0] // width):
        at = slice(n * width, (n + 1) * width)
        hidden = dot_nt(second[...], up[at, :]) + up_bias[0:1, at]
        cdf = 0.5 * (1.0 + lax.erf(hidden * 0.7071067811865476))
        density = jnp.exp(-0.5 * hidden * hidden) * 0.3989422804014327
        active[:, at] = (hidden * cdf).astype(LOW)
        slope[:, at] = cdf + hidden * density


def down_grad_kernel(
    place, active, active_twin, cotangent, cotangent_twin, o0, o1, o2, o3, bias_grad, wide, stage, sems,
):
    units, rows, width = stage.shape
    each = width // (2 * units)
    bias_grad[...] = jnp.broadcast_to(
        jnp.sum(cotangent[...].astype(F32), axis=0, keepdims=True), bias_grad.shape
    )

    def run(c):
        dy, dy_twin = [plane_columns(array[...], 2 * each, c) for array in (cotangent, cotangent_twin)]
        for fold in range(rows // each):
            at = slice(fold * width, (fold + 1) * width)
            grad = dot_tn(dy, active[:, at]) + dot_tn(dy_twin, active_twin[:, at])
            for unit in range(units):
                wide[unit, fold * each : (fold + 1) * each, :] = grad[unit * each : (unit + 1) * each]
        sent = []
        for z in range(4):
            for unit in range(z * units // 4, (z + 1) * units // 4):
                stage[unit] = wide[unit].astype(LOW)
            sent += store_wave(place, c, z, stage, (o0, o1, o2, o3), sems)
        for copy in sent:
            copy.wait()

    by_plane(place, run)


def unfold_units(stage, down):
    units, rows, width = stage.shape
    each = down.shape[0] // units
    for pair in range(units // 2):
        one, two = stage[2 * pair].astype(F32), stage[2 * pair + 1].astype(F32)
        for fold in range(rows // each):
            both = jnp.concatenate(
                [one[fold * each : (fold + 1) * each], two[fold * each : (fold + 1) * each]], axis=0
            )
            down[2 * each * pair : 2 * each * (pair + 1), fold * width : (fold + 1) * width] = (
                both.astype(LOW)
            )


def back_kernel(
    place, cotangent, slope, middle, vectors, p0, p1, p2, p3, p4, p5, p6, p7, u0, u1, u2, u3, u4, u5, u6, u7,
    middle_grad, context_grad, vector_grads, branch_grad, up_bias_grad, hidden_grad,
    stage, down, up, kept, out, stage_sems, sems, kept_sems,
):
    width = cotangent.shape[1]
    down_copies = load_units(place, (p0, p1, p2, p3, p4, p5, p6, p7), stage, stage_sems)
    kept_copies, up_copies = load_mixed(
        place, (u0, u1, u2, u3, u4, u5, u6, u7), up, kept, sems, kept_sems
    )
    for copy in down_copies:
        copy.wait()
    unfold_units(stage, down)
    dy = cotangent[...]
    for n in range(hidden_grad.shape[1] // width):
        at = slice(n * width, (n + 1) * width)
        grad = (dot_nn(dy, down[:, at]) * slope[:, at]).astype(LOW)
        hidden_grad[:, at] = grad
        up_bias_grad[:, at] = jnp.broadcast_to(
            jnp.sum(grad.astype(F32), axis=0, keepdims=True), (up_bias_grad.shape[0], width)
        )
    for copy in kept_copies:
        copy.wait()
    join_units(kept, out)
    for copy in up_copies:
        copy.wait()
    second_grad = dot_nn(hidden_grad[...], up[...])
    mid = middle[...]
    center = mid - jnp.mean(mid, axis=1, keepdims=True)
    inv_std = lax.rsqrt(jnp.mean(center * center, axis=1, keepdims=True) + EPSILON)
    normed = center * inv_std
    scaled = second_grad * vectors[2:3, :]
    inner = (
        scaled
        - jnp.mean(scaled, axis=1, keepdims=True)
        - normed * jnp.mean(scaled * normed, axis=1, keepdims=True)
    )
    mid_grad = cotangent[...].astype(F32) + inner * inv_std
    middle_grad[...] = mid_grad
    branch = mid_grad.astype(LOW)
    vector_grads[...] = jnp.concatenate(
        [
            jnp.sum(second_grad * normed, axis=0, keepdims=True),
            jnp.sum(second_grad, axis=0, keepdims=True),
            jnp.sum(branch.astype(F32), axis=0, keepdims=True),
            jnp.zeros((5, width), F32),
        ],
        axis=0,
    )
    branch_grad[...] = branch
    context_grad[...] = dot_nn(branch, out[...]).astype(LOW)


def up_grad_kernel(
    place, hidden, hidden_twin, second, second_twin, branch, branch_twin, context, context_twin,
    o0, o1, o2, o3, stage, sems,
):
    units, rows, width = stage.shape
    each = width // (2 * units)
    up_rows = hidden.shape[1] // (2 * units)

    def run(c):
        out_grad = dot_tn(plane_columns(branch[...], 2 * each, c), context[...]) + dot_tn(
            plane_columns(branch_twin[...], 2 * each, c), context_twin[...]
        )
        blank = jnp.zeros((rows - up_rows - each, width), F32)
        quarter = units // 4
        sent = []
        for z in range(4):
            at = slice(2 * z * quarter * up_rows, 2 * (z + 1) * quarter * up_rows)
            grad = dot_tn(plane_columns(hidden[:, at], 2 * up_rows, c), second[...]) + dot_tn(
                plane_columns(hidden_twin[:, at], 2 * up_rows, c), second_twin[...]
            )
            for n in range(quarter):
                unit = z * quarter + n
                stage[unit] = jnp.concatenate(
                    [
                        grad[n * up_rows : (n + 1) * up_rows],
                        out_grad[unit * each : (unit + 1) * each],
                        blank,
                    ],
                    axis=0,
                ).astype(LOW)
            sent += store_wave(place, c, z, stage, (o0, o1, o2, o3), sems)
        for copy in sent:
            copy.wait()

    by_plane(place, run)


def rows_left(each):
    return -each % 16


def finish_kernel(
    place, active, middle, vectors, p0, p1, p2, p3, p4, p5, p6, p7, layer_out, stage, down, sems
):
    copies = load_units(place, (p0, p1, p2, p3, p4, p5, p6, p7), stage, sems)
    for copy in copies:
        copy.wait()
    unfold_units(stage, down)
    layer_out[...] = middle[...] + dot_nt(active[...], down[...]) + vectors[5:6, :]


def attend_back_kernel(
    queries, keys, values, context_grad, mixed, probs, grads, diagonals
):
    q, k, v, dout = queries[...], keys[...], values[...], context_grad[...]
    block_len, span = probs.shape[1:]
    weighted = dout.astype(F32) * mixed[...]
    row = lax.broadcasted_iota(jnp.int32, (block_len, block_len), 0)
    lane = lax.broadcasted_iota(jnp.int32, (block_len, block_len), 1)
    turn = (row + lane == block_len - 1).astype(LOW)
    blank = jnp.zeros((block_len, block_len), F32)
    dq, dk, dv = jnp.zeros(q.shape, F32), jnp.zeros(k.shape, F32), jnp.zeros(v.shape, F32)
    for head in range(2):
        mine = half_mask(q.shape, head)
        dout_head = jnp.where(mine, dout, 0)
        delta = jnp.sum(jnp.where(mine, weighted, 0.0), axis=1, keepdims=True)
        prob = probs[head]
        grad = prob.astype(F32) * (dot_nt(dout_head, v) - delta)
        raw = (grad * (1.0 / math.sqrt(HD))).astype(LOW)
        dq = dq + dot_nn(raw, jnp.where(half_mask(k.shape, head), k, 0))
        dk = dk + dot_tn(raw, jnp.where(mine, q, 0))
        dv = dv + dot_tn(prob, dout_head)
        turned = jnp.concatenate([dot_nn(turn, raw), blank], axis=1)
        sheared = pltpu.roll(turned, 0, 1, stride=1, stride_axis=0)
        diagonals[pl.ds(2 * pl.program_id(0) + head, 1), :] = jnp.sum(sheared, axis=0, keepdims=True) * math.sqrt(HD)
    grads[:block_len, :] = dq.astype(LOW)
    grads[block_len : block_len + span, :] = dk.astype(LOW)
    grads[block_len + span :, :] = dv.astype(LOW)


def total(array):
    return jnp.sum(array, axis=0, keepdims=True)


def norm_parts(frames):
    wide = frames.astype(F32)
    center = wide - jnp.mean(wide, axis=1, keepdims=True)
    inv_std = lax.rsqrt(jnp.mean(center * center, axis=1, keepdims=True) + EPSILON)
    return center * inv_std, inv_std


def first_grad_kernel(
    place, own_frames, mate_frames, grads, weight_in, diagonals, vector_grads, down_bias_grad, up_bias_grad,
    own_grad, mate_grad, small, weight, sems,
):
    copy = pltpu.make_async_copy(weight_in, weight, sems.at[0])
    copy.start()
    shard_len, width = own_frames.shape
    span = (grads.shape[0] - shard_len) // 2
    x = place[0]
    own_normed, _ = norm_parts(own_frames[...])
    mate_normed, _ = norm_parts(mate_frames[...])
    dq = grads[:shard_len, :]
    small[4:5, :] = vector_grads[2:3, :]
    small[2:4, :] = vector_grads[0:2, :]
    small[5:6, :] = down_bias_grad[0:1, :]
    small[6:7, :] = total(dq.astype(F32))
    small[7:8, :] = total(grads[shard_len + span :, :].astype(F32))
    for n in range(up_bias_grad.shape[1] // width):
        small[8 + n : 9 + n, :] = up_bias_grad[0:1, n * width : (n + 1) * width]
    small[12:, :] = diagonals[...]
    copy.wait()

    def from_keys(at):
        key_at = pl.multiple_of(shard_len + at, shard_len)
        value_at = pl.multiple_of(shard_len + span + at, shard_len)
        return dot_nn(grads[pl.ds(key_at, shard_len), :], weight[width : 2 * width, :]) + dot_nn(
            grads[pl.ds(value_at, shard_len), :], weight[2 * width :, :]
        )

    of_own = from_keys(x * shard_len) + dot_nn(dq, weight[:width, :])
    of_mate = from_keys((1 - x) * shard_len)
    own_grad[...] = of_own
    mate_grad[...] = of_mate
    small[0:1, :] = total(of_own * own_normed) + total(of_mate * mate_normed)
    small[1:2, :] = total(of_own) + total(of_mate)


def qkv_grad_kernel(
    place, grads, grads_twin, first, first_twin, small_own, small_twin, wide_one, wide_two, wide_four,
    o0, o1, o2, o3, sums, small, stage, sems,
):
    units, full, width = stage.shape
    rows = full - PAD
    span = first.shape[0]
    shard_len = grads.shape[0] - 2 * span
    x = place[0]
    summed = small_own[...] + small_twin[...]

    def fold(vector, table):
        kept = (vector * table[: 2 * units, :].astype(F32)).astype(LOW)
        return dot_nt(kept, table[2 * units :, :])

    for n in range(NARROW):
        small[0, :, n * LANES : (n + 1) * LANES] = fold(summed[n : n + 1, :], wide_one)
    small[1, :, :] = jnp.zeros((2 * units, width), F32)
    both = jnp.concatenate([summed[6:7, :], summed[7:8, :]], axis=1)
    small[1, :, :LANES] = fold(both, wide_two)
    four = jnp.concatenate([summed[8 + n : 9 + n, :] for n in range(4)], axis=1)
    small[1, :, LANES : 2 * LANES] = fold(four, wide_four)
    lanes = 3 * LANES
    distance = (
        lax.broadcasted_iota(jnp.int32, (shard_len + span, lanes), 0) - (shard_len - 1) - x * shard_len
    )
    bucket = jnp.clip(distance, -MAXREL, MAXREL) + MAXREL
    here = (bucket == lax.broadcasted_iota(jnp.int32, (shard_len + span, lanes), 1)).astype(F32).astype(LOW)
    diagonals = summed[12:, :]
    high = diagonals.astype(LOW)
    table = dot_nn(high, here) + dot_nn((diagonals - high.astype(F32)).astype(LOW), here)
    table = jnp.concatenate([table[: H // 2], table[H // 2 :]], axis=1)
    own_at = pl.multiple_of(x * shard_len, shard_len)

    def run(c):
        done = 0
        for part, (at, length) in enumerate(((0, shard_len), (shard_len, span), (shard_len + span, span))):
            spans = []
            for n in range(units // 2):
                low = max((2 * n + c) * 2 * rows - part * width, 0)
                high = min((2 * n + c + 1) * 2 * rows - part * width, width)
                if low < high:
                    spans.append((low, high))
            count = sum(high - low for low, high in spans)
            product = jnp.zeros((count, width), F32)
            for grad, rows_of in ((grads, first), (grads_twin, first_twin)):
                columns = jnp.concatenate([grad[at : at + length, low:high] for low, high in spans], axis=1)
                product = product + dot_tn(
                    columns, rows_of[pl.ds(own_at, shard_len), :] if part == 0 else rows_of[...]
                )
            sums[done : done + count, :] = product
            done += count
        sent = []
        for z in range(4):
            for unit in range(z * units // 4, (z + 1) * units // 4):
                at = 4 * (unit // 2) + 2 * c + unit % 2
                stage[unit] = jnp.concatenate(
                    [
                        sums[unit * rows : (unit + 1) * rows, :],
                        small[0, at : at + 1, :],
                        small[1, at : at + 1, :],
                        table,
                    ],
                    axis=0,
                ).astype(LOW)
            sent += store_wave(place, c, z, stage, (o0, o1, o2, o3), sems)
        for copy in sent:
            copy.wait()

    by_plane(place, run)


def input_grad_kernel(frames, mate_frames, own_grad, mate_grad, middle_grad, vectors, own_part, mate_part):
    def through_norm(of_frames, grad):
        normed, inv_std = norm_parts(of_frames)
        scaled = grad * vectors[0:1, :]
        inner = (
            scaled
            - jnp.mean(scaled, axis=1, keepdims=True)
            - normed * jnp.mean(scaled * normed, axis=1, keepdims=True)
        )
        return inner * inv_std

    own_part[...] = middle_grad[...] + through_norm(frames[...], own_grad[...])
    mate_part[...] = through_norm(mate_frames[...], mate_grad[...]).astype(LOW)


def last_kernel(
    own, z1, z2, z3, own_part, mate_part, qkv, qv_bias, up_bias, table, frames_grad, n0, n1, n2, n3, n4, n5
):
    frames_grad[...] = own_part[...] + mate_part[...].astype(F32)
    rows = qkv.shape[0]
    total = own[...] + z1[...].astype(F32) + z2[...].astype(F32) + z3[...].astype(F32)
    qkv[...] = total[:rows]
    for n, narrow in enumerate((n0, n1, n2, n3, n4, n5)):
        narrow[...] = total[rows : rows + 1, n * LANES : n * LANES + narrow.shape[1]]
    qv_bias[...] = total[rows + 1 : rows + 2, : qv_bias.shape[1]]
    up_bias[...] = total[rows + 1 : rows + 2, LANES : LANES + up_bias.shape[1]]
    for half in range(2):
        at = 3 * LANES * half
        table[half * (H // 2) : (half + 1) * (H // 2), :] = total[rows + 2 : rows + PAD, at : at + BUCKETS]


def pack_kernel(
    live, qkv, out, up, down, first_gain, first_shift, second_gain, second_shift, out_bias,
    down_bias, qv_bias, up_bias, qkv_unit, up_unit, down_unit,
):
    each, width = out.shape

    def slots(vectors):
        parts = []
        for vector in vectors:
            wide = vector[...].astype(F32)
            parts += [wide, jnp.zeros((1, LANES - wide.shape[1]), F32)]
        left = width - LANES * len(vectors)
        if left:
            parts.append(jnp.zeros((1, left), F32))
        return jnp.concatenate(parts, axis=1)

    narrow = slots((first_gain, first_shift, second_gain, second_shift, out_bias, down_bias))
    wide = slots((qv_bias, up_bias))
    seen = live[...].astype(F32)
    seen = jnp.concatenate([seen, jnp.zeros((1, width - seen.shape[1]), F32)], axis=1)
    blank = jnp.zeros((PAD - 3, width), F32)
    qkv_unit[...] = jnp.concatenate([qkv[...].astype(F32), narrow, wide, seen, blank], axis=0).astype(LOW)
    blank = jnp.zeros((up_unit.shape[0] - up.shape[0] - each, width), F32)
    up_unit[...] = jnp.concatenate(
        [up[...].astype(F32), out[...].astype(F32), blank], axis=0
    ).astype(LOW)
    down_unit[...] = jnp.concatenate(
        [
            down[:, fold * width : (fold + 1) * width].astype(F32)
            for fold in range(down.shape[1] // width)
        ],
        axis=0,
    ).astype(LOW)


def paired_body(
    frames, cotangent, seq_lengths, key_mask, qkv_weight, query_value_bias, out_weight, out_bias,
    up_weight, up_bias, down_weight, down_bias, first_gain, first_shift, second_gain, second_shift,
    rel_bias,
):
    shard_len, width = frames.shape
    x = lax.axis_index("blk")
    d = lax.axis_index("dp")
    core = d % 2
    units = lax.axis_size("dp") * lax.axis_size("blk")
    span = shard_len * lax.axis_size("blk")
    place = jnp.stack([x, (d // 2) % 2, d // 4, core]).astype(jnp.int32)
    each = width // units
    ff = up_weight.shape[1] * units
    qkv_rows, up_rows = qkv_weight.shape[1], up_weight.shape[1]
    folds = ff // width
    down_rows = each * folds
    out_rows = each + rows_left(each)

    def shape(*dims, kind=LOW):
        return jax.ShapeDtypeStruct(dims, kind)

    def row(vector):
        return vector.reshape(1, vector.shape[0])

    packed = (
        row(key_mask), qkv_weight.T, out_weight.T, up_weight.T, down_weight.T, row(first_gain),
        row(first_shift), row(second_gain), row(second_shift), row(out_bias), row(down_bias),
        row(query_value_bias), row(up_bias),
    )
    qkv_unit, up_unit, down_unit = call(
        pack_kernel,
        [VMEM] * len(packed),
        [shape(qkv_rows + PAD, width), shape(up_rows + out_rows, width), shape(down_rows, width)],
        [VMEM] * 3,
        [],
        packed,
        0,
        name="pack",
    )
    def twins(pieces):
        return tuple(pieces) + tuple(twin(piece) for piece in pieces)

    cotangent_twin = twin(cotangent)
    qkv_z = along_z(qkv_unit, "qkv")
    mate_frames = shift(tied(frames, qkv_unit), PACK, "frames_pack")
    qkv_z, mate_frames = joined(qkv_z, mate_frames)
    qkv_own = jnp.stack((qkv_unit,) + qkv_z)
    qkv_side = shift(qkv_own, SIDE, "qkv_1")
    up_first = tied(up_unit, *qkv_z)
    up_z = [shift(up_first, move, "up_z") for move in ALONG_Z[:2]]
    qkv_side, up_z = joined(qkv_side, up_z)
    qkv_other = shift(qkv_own, OTHER_SIDE, "qkv_2")
    qkv_across = shift(qkv_side, OTHER_SIDE, "qkv_3")
    up_z.append(shift(tied(up_unit, qkv_side), ALONG_Z[2], "up_z"))
    up_z, qkv_other, qkv_across = joined(up_z, qkv_other, qkv_across)
    qkv_pieces = twins((qkv_own, qkv_side, qkv_other, qkv_across))
    up_own = jnp.stack([up_unit] + up_z)
    up_side = shift(up_own, SIDE, "up_1")
    down_first = tied(down_unit, up_own)
    down_z = [shift(down_first, move, "down_z") for move in ALONG_Z[:2]]

    distance = jnp.arange(span + shard_len, dtype=jnp.int32) - (shard_len - 1) - x * shard_len
    bucket = jnp.clip(distance, -MAXREL, MAXREL) + MAXREL
    bucket_lanes = 3 * LANES
    buckets = (bucket[:, None] == jnp.arange(bucket_lanes, dtype=jnp.int32)[None, :]).astype(LOW)
    curve = lax.dot_general(
        rel_bias, buckets[:, :BUCKETS], (((0,), (1,)), ((), ())), preferred_element_type=F32
    )
    spreads = spread_tables(units, width)
    unit_sems = pltpu.SemaphoreType.DMA((units,))
    first, queries, keys, values, weight, vectors, up_bias_all, mate_live = call(
        project_kernel,
        [SMEM, VMEM, VMEM] + [HBM] * 8 + [VMEM] * 3,
        [
            shape(span, width), shape(shard_len, width), shape(span, width), shape(span, width),
            shape(3 * width, width), shape(8, width, kind=F32), shape(8, ff, kind=F32),
            shape(PAD, shard_len, kind=F32),
        ],
        [VMEM] * 8,
        [
            pltpu.VMEM((units, qkv_rows + PAD, width), LOW), pltpu.VMEM((2, units, width), F32), unit_sems,
        ],
        (tied(place, up_own), frames, mate_frames) + qkv_pieces + tuple(spreads),
        2 * shard_len * width * 5 * width,
        name="project",
    )
    up_side, keys, down_z = joined(up_side, keys, down_z)
    up_other = shift(up_own, OTHER_SIDE, "up_2")
    up_across = shift(up_side, OTHER_SIDE, "up_3")
    down_z.append(shift(tied(down_unit, keys), ALONG_Z[2], "down_z"))
    pairs = H // 2
    pair_lanes = 2 * HD

    def lanes_of(rows):
        return pl.BlockSpec((rows, pair_lanes), lambda n: (0, n))

    def heads_of(*dims):
        return pl.BlockSpec(dims, lambda n: (n,) + (0,) * (len(dims) - 1))

    def whole(*dims):
        return pl.BlockSpec(dims, lambda n: (0,) * len(dims))

    probs, mixed = call(
        attend_kernel,
        [
            SMEM, SMEM, lanes_of(shard_len), lanes_of(span), lanes_of(span), whole(H, span + shard_len),
            whole(1, shard_len), whole(PAD, shard_len),
        ],
        [shape(H, shard_len, span), shape(shard_len, width, kind=F32)],
        [heads_of(2, shard_len, span), lanes_of(shard_len)],
        [pltpu.VMEM((shard_len, span), F32)],
        (
            tied(place, up_side), seq_lengths, queries, keys, values, curve, row(key_mask), mate_live,
        ),
        8 * shard_len * span * width,
        grid=(pairs,),
        name="attend",
    )
    up_other, up_across, mixed, down_z = joined(up_other, up_across, mixed, down_z)
    up_pieces = twins((up_own, up_side, up_other, up_across))
    down_own = jnp.stack([down_unit] + down_z)
    down_side = shift(down_own, SIDE, "down_1")
    down_other = shift(down_own, OTHER_SIDE, "down_2")
    middle, second, context, active, slope = call(
        expand_kernel,
        [SMEM] + [VMEM] * 4 + [HBM] * 8,
        [
            shape(shard_len, width, kind=F32), shape(shard_len, width), shape(shard_len, width),
            shape(shard_len, ff), shape(shard_len, ff, kind=F32),
        ],
        [VMEM] * 5,
        [
            pltpu.VMEM((ff, width), LOW), pltpu.VMEM((units, out_rows, width), LOW),
            pltpu.VMEM((width, width), LOW), unit_sems, unit_sems,
        ],
        (tied(place, down_own), frames, mixed, vectors, up_bias_all) + up_pieces,
        2 * shard_len * width * (width + ff),
        name="expand",
    )
    down_side, down_other, active = joined(down_side, down_other, active)
    down_across = shift(down_side, OTHER_SIDE, "down_3")
    active_twin, context_twin, second_twin = twin(active), twin(context), twin(second)
    first_twin = twin(first)
    half_sems = pltpu.SemaphoreType.DMA((units // 2,))
    down_parts = call(
        down_grad_kernel,
        [SMEM] + [VMEM] * 4,
        part_shapes(down_rows, width) + [shape(8, width, kind=F32)],
        [HBM] * 4 + [VMEM],
        [
            pltpu.VMEM((units // 2, down_rows, width), F32),
            pltpu.VMEM((units // 2, down_rows, width), LOW), half_sems,
        ],
        (tied(place, down_side), active, active_twin, cotangent, cotangent_twin),
        2 * shard_len * width * ff,
        name="down_grad",
    )
    down_across, down_parts = joined(down_across, down_parts)
    down_bias_grad = down_parts[4]
    down_pieces = twins((down_own, down_side, down_other, down_across))
    turned = shift(down_parts[3], OTHER_SIDE, "rs_down_3")
    down_two = shift(down_parts[2], OTHER_SIDE, "rs_down_2")
    middle_grad, context_grad, vector_grads, branch_grad, up_bias_grad, hidden_grad = call(
        back_kernel,
        [SMEM] + [VMEM] * 4 + [HBM] * 16,
        [
            shape(shard_len, width, kind=F32), shape(shard_len, width), shape(8, width, kind=F32),
            shape(shard_len, width), shape(8, ff, kind=F32), shape(shard_len, ff),
        ],
        [VMEM] * 6,
        [
            pltpu.VMEM((units, down_rows, width), LOW), pltpu.VMEM((width, ff), LOW),
            pltpu.VMEM((ff, width), LOW), pltpu.VMEM((units, out_rows, width), LOW),
            pltpu.VMEM((width, width), LOW), unit_sems, unit_sems, unit_sems,
        ],
        (tied(place, down_parts[0]), cotangent, slope, middle, vectors) + down_pieces + up_pieces,
        2 * shard_len * width * (2 * ff + width),
        name="back",
    )
    turned, down_two, hidden_grad = joined(turned, down_two, hidden_grad)
    side = (down_parts[1].astype(F32) + turned.astype(F32)).astype(LOW)
    down_one = shift(side, SIDE, "rs_down_1")
    hidden_twin = twin(hidden_grad)
    branch_twin = twin(branch_grad)
    down_sum = down_parts[0].astype(F32) + down_two.astype(F32)
    up_parts = call(
        up_grad_kernel,
        [SMEM] + [VMEM] * 8,
        part_shapes(up_rows + out_rows, width),
        [HBM] * 4,
        [
            pltpu.VMEM((units // 2, up_rows + out_rows, width), LOW), half_sems,
        ],
        (
            tied(place, down_sum, side), hidden_grad, hidden_twin, second, second_twin, branch_grad, branch_twin,
            context, context_twin,
        ),
        2 * shard_len * width * (ff + width),
        name="up_grad",
    )
    down_one, up_parts = joined(down_one, up_parts)
    turned = shift(up_parts[3], OTHER_SIDE, "rs_up_3")
    up_two = shift(up_parts[2], OTHER_SIDE, "rs_up_2")
    down_sum = down_sum + down_one.astype(F32)
    down_low = down_sum.astype(LOW)
    down_z = [shift(down_low[n + 1], ALONG_Z[n], "rs_down_z") for n in range(2)]
    grads, diagonals = call(
        attend_back_kernel,
        [
            lanes_of(shard_len), lanes_of(span), lanes_of(span), lanes_of(shard_len), lanes_of(shard_len),
            heads_of(2, shard_len, span),
        ],
        [shape(shard_len + 2 * span, width), shape(H, span + shard_len, kind=F32)],
        [lanes_of(shard_len + 2 * span), whole(H, span + shard_len)],
        [],
        (queries, keys, values, tied(context_grad, up_parts[0]), mixed, probs),
        16 * shard_len * span * width,
        grid=(pairs,),
        name="attend_back", limit=24,
    )
    turned, down_z, grads = joined(turned, down_z, grads)
    grads_twin = twin(grads)
    side = (up_parts[1].astype(F32) + turned.astype(F32)).astype(LOW)
    up_one = shift(side, SIDE, "rs_up_1")
    down_z.append(shift(tied(down_low[3], side), ALONG_Z[2], "rs_down_z"))
    own_grad, mate_grad, small = call(
        first_grad_kernel,
        [SMEM] + [VMEM] * 3 + [HBM] + [VMEM] * 4,
        [
            shape(shard_len, width, kind=F32), shape(shard_len, width, kind=F32),
            shape(12 + H, width, kind=F32),
        ],
        [VMEM] * 3,
        [pltpu.VMEM((3 * width, width), LOW), pltpu.SemaphoreType.DMA((1,))],
        (
            tied(place, side), frames, mate_frames, grads, weight, diagonals, vector_grads,
            down_bias_grad, up_bias_grad,
        ),
        2 * shard_len * width * 5 * width,
        name="first_grad", limit=24,
    )
    grads_twin, down_z, small = joined(grads_twin, down_z, small)
    small_twin = twin(small)
    qkv_parts = call(
        qkv_grad_kernel,
        [SMEM] + [VMEM] * 9,
        part_shapes(qkv_rows + PAD, width),
        [HBM] * 4,
        [
            pltpu.VMEM((3 * width // 2, width), F32), pltpu.VMEM((2, units, width), F32),
            pltpu.VMEM((units // 2, qkv_rows + PAD, width), LOW), half_sems,
        ],
        (place, grads, grads_twin, first, first_twin, small, small_twin) + tuple(spreads),
        2 * shard_len * width * 6 * width,
        name="qkv_grad", limit=24,
    )
    up_one, up_two, qkv_parts = joined(up_one, up_two, qkv_parts)
    turned = shift(qkv_parts[3], OTHER_SIDE, "rs_qkv_3")
    qkv_two = shift(qkv_parts[2], OTHER_SIDE, "rs_qkv_2")
    up_sum = up_parts[0].astype(F32) + up_one.astype(F32) + up_two.astype(F32)
    up_low = up_sum.astype(LOW)
    up_z = [shift(up_low[n + 1], ALONG_Z[n], "rs_up_z") for n in range(2)]
    down_sum = z_sum(down_sum, down_z)
    own_part, mate_part = call(
        input_grad_kernel,
        [VMEM] * 6,
        [shape(shard_len, width, kind=F32), shape(shard_len, width)],
        [VMEM] * 2,
        [],
        (frames, mate_frames, own_grad, tied(mate_grad, up_low), middle_grad, vectors),
        0,
        name="input_grad", limit=12,
    )
    layer_out = call(
        finish_kernel,
        [SMEM] + [VMEM] * 3 + [HBM] * 8,
        [shape(shard_len, width, kind=F32)],
        [VMEM],
        [pltpu.VMEM((units, down_rows, width), LOW), pltpu.VMEM((width, ff), LOW), unit_sems],
        (tied(place, up_low), active, middle, vectors) + down_pieces,
        2 * shard_len * width * ff,
        name="finish",
    )[0]
    turned, up_z, mate_part, layer_out = joined(turned, up_z, mate_part, layer_out)
    side = (qkv_parts[1].astype(F32) + turned.astype(F32)).astype(LOW)
    qkv_one = shift(side, SIDE, "rs_qkv_1")
    up_z.append(shift(tied(up_low[3], side), ALONG_Z[2], "rs_up_z"))
    qkv_one, qkv_two, up_z = joined(qkv_one, qkv_two, up_z)
    qkv_sum = qkv_parts[0].astype(F32) + qkv_one.astype(F32) + qkv_two.astype(F32)
    qkv_z = z_sends(qkv_sum, "rs_qkv")
    mate_part = shift(tied(mate_part, qkv_sum), PACK, "grad_pack")
    up_sum = z_sum(tied(up_sum, qkv_sum), up_z)
    up_sum, qkv_z = joined(up_sum, qkv_z)
    last = call(
        last_kernel,
        [VMEM] * 6,
        [
            shape(qkv_rows, width, kind=F32), shape(1, 2 * each, kind=F32), shape(1, up_rows, kind=F32),
            shape(H, BUCKETS, kind=F32), shape(shard_len, width, kind=F32),
        ]
        + [shape(1, each, kind=F32)] * NARROW,
        [VMEM] * (5 + NARROW),
        [],
        (qkv_sum[0],) + tuple(qkv_z) + (own_part, mate_part),
        0,
        name="last", limit=8,
    )
    qkv_grad, qv_bias_grad, up_bias_sum, table, frames_grad = last[:5]
    pieces = [piece.reshape(each) for piece in last[5:]]

    down_grad = jnp.concatenate(
        [down_sum[fold * each : (fold + 1) * each] for fold in range(folds)], axis=1
    )
    return (
        layer_out, frames_grad, qkv_grad.T, qv_bias_grad.reshape(2 * each),
        up_sum[up_rows : up_rows + each].T, pieces[4], up_sum[:up_rows].T, up_bias_sum.reshape(up_rows),
        down_grad.T, pieces[5], pieces[0], pieces[1], pieces[2], pieces[3], table.T,
    )


def paired(mesh):
    return mesh.shape["blk"] == 2 and mesh.shape["dp"] == 16


def solution(mesh):
    placed = (
        P(("dp", "blk"), None),
        P(("dp", "blk"), None),
        P("dp", None),
        P(("dp", "blk")),
        P(None, ("dp", "blk")),
        P(("dp", "blk")),
        P(None, ("dp", "blk")),
        P(("dp", "blk")),
        P(None, ("dp", "blk")),
        P(("dp", "blk")),
        P(None, ("dp", "blk")),
        P(("dp", "blk")),
        P(("dp", "blk")),
        P(("dp", "blk")),
        P(("dp", "blk")),
        P(("dp", "blk")),
        P(),
    )
    return jax.shard_map(
        paired_body if paired(mesh) else body,
        mesh=mesh,
        in_specs=placed,
        out_specs=(
            P(("dp", "blk"), None),
            P(("dp", "blk"), None),
            P(None, ("dp", "blk")),
            P(("dp", "blk")),
            P(None, ("dp", "blk")),
            P(("dp", "blk")),
            P(None, ("dp", "blk")),
            P(("dp", "blk")),
            P(None, ("dp", "blk")),
            P(("dp", "blk")),
            P(("dp", "blk")),
            P(("dp", "blk")),
            P(("dp", "blk")),
            P(("dp", "blk")),
            P(),
        ),
        check_vma=False,
    )
```

```python
import math

import jax
import jax.numpy as jnp
import numpy as np
from jax import lax
from jax.experimental import pallas as pl
from jax.experimental.pallas import tpu as pltpu
from jax.sharding import PartitionSpec as P

H = 12
HD = 64
MAXREL = 160
BLOCK = 256
BUCKETS = 321


EPSILON = 1e-05
MASKED = -2e30
START_PEAK = -1e30
HIGHEST = lax.Precision.HIGHEST


def from_behind(block, axis, distance):
    devices = range(lax.axis_size(axis))
    route = [((i - distance) % len(devices), i) for i in devices]
    return lax.ppermute(block, axis, route)


def layer_norm(values, gain_vec, shift_vec):
    center = values - jnp.mean(values, axis=-1, keepdims=True)
    inv_std = lax.rsqrt(jnp.mean(center * center, axis=-1, keepdims=True) + EPSILON)
    normed = center * inv_std
    return (normed * gain_vec + shift_vec, normed, inv_std)


def norm_back(gradient, normed, inv_std, gain_vec):
    scaled = gradient * gain_vec
    inner = (
        scaled
        - jnp.mean(scaled, axis=-1, keepdims=True)
        - normed * jnp.mean(scaled * normed, axis=-1, keepdims=True)
    )
    return (inner * inv_std, jnp.sum(gradient * normed, axis=0), jnp.sum(gradient, axis=0))


def gelu_parts(values):
    normal_cdf = 0.5 * (1.0 + lax.erf(values * 0.7071067811865476))
    density = jnp.exp(-0.5 * values * values) * 0.3989422804014327
    return (values * normal_cdf, normal_cdf + values * density)


def doc_numbers(seq_ends, positions):
    return jnp.sum((positions[:, None] >= seq_ends[None, :]).astype(jnp.int32), axis=1)


def pair_logits(
    query_block, key_block, query_pos, key_pos, query_doc, key_doc, key_live, table_heads
):
    block_len = query_block.shape[0]
    raw = jnp.einsum(
        "qhd,khd->hqk",
        query_block.reshape(block_len, H, HD),
        key_block.reshape(-1, H, HD),
        preferred_element_type=jnp.float32,
    )
    relative = jnp.clip(key_pos[None, :] - query_pos[:, None], -MAXREL, MAXREL) + MAXREL
    bias = jnp.take(table_heads, relative, axis=1)
    allowed = (query_doc[:, None] == key_doc[None, :]) & (
        (key_live[None, :] > 0.5) | (query_pos[:, None] == key_pos[None, :])
    )
    return jnp.where(allowed[None], raw * (1.0 / math.sqrt(HD)) + bias, MASKED)


def diagonal_sums(gradient, offset):
    heads, block_len, _ = gradient.shape
    flipped = gradient[:, ::-1, :]
    padded = jnp.pad(flipped, ((0, 0), (0, 0), (0, block_len)))
    sheared = padded.reshape(heads, 2 * block_len * block_len)[:, : block_len * (2 * block_len - 1)]
    sheared = sheared.reshape(heads, block_len, 2 * block_len - 1)
    diag_sums = jnp.sum(sheared, axis=1)
    distance = offset + jnp.arange(2 * block_len - 1, dtype=jnp.int32) - (block_len - 1)
    bucket = jnp.clip(distance, -MAXREL, MAXREL) + MAXREL
    onehot = (bucket[:, None] == jnp.arange(BUCKETS, dtype=jnp.int32)[None, :]).astype(jnp.float32)
    return jnp.dot(diag_sums, onehot, precision=HIGHEST)


def body(
    frames,
    cotangent,
    seq_lengths,
    key_mask,
    qkv_weight,
    query_value_bias,
    out_weight,
    out_bias,
    up_weight,
    up_bias,
    down_weight,
    down_bias,
    first_gain,
    first_shift,
    second_gain,
    second_shift,
    rel_bias,
):
    cycle_size = lax.axis_size("blk")
    cycle_place = lax.axis_index("blk")
    shard_len = frames.shape[0]
    width = frames.shape[1]
    block_count = shard_len // BLOCK
    score_scale = 1.0 / math.sqrt(HD)
    seq_ends = jnp.cumsum(seq_lengths[0])
    local_pos = jnp.arange(shard_len, dtype=jnp.int32)
    positions = cycle_place * shard_len + local_pos
    own_docs = doc_numbers(seq_ends, positions)
    table_heads = rel_bias.astype(jnp.float32).T

    def blocked(array):
        return array.reshape((block_count, BLOCK) + array.shape[1:])

    def key_meta(turn):
        source = (cycle_place - turn) % cycle_size
        key_pos = source * shard_len + local_pos
        return (key_pos, doc_numbers(seq_ends, key_pos))

    gathered = (
        lax.all_gather(qkv_weight, ("dp", "blk"), axis=1, tiled=True),
        lax.all_gather(query_value_bias, ("dp", "blk"), axis=0, tiled=True),
        lax.all_gather(out_weight, ("dp", "blk"), axis=1, tiled=True),
        lax.all_gather(out_bias, ("dp", "blk"), axis=0, tiled=True),
        lax.all_gather(up_weight, ("dp", "blk"), axis=1, tiled=True),
        lax.all_gather(up_bias, ("dp", "blk"), axis=0, tiled=True),
        lax.all_gather(down_weight, ("dp", "blk"), axis=1, tiled=True),
        lax.all_gather(down_bias, ("dp", "blk"), axis=0, tiled=True),
        lax.all_gather(first_gain, ("dp", "blk"), axis=0, tiled=True),
        lax.all_gather(first_shift, ("dp", "blk"), axis=0, tiled=True),
        lax.all_gather(second_gain, ("dp", "blk"), axis=0, tiled=True),
        lax.all_gather(second_shift, ("dp", "blk"), axis=0, tiled=True),
    )
    (
        qkv_full,
        qv_bias_full,
        out_full,
        out_bias_full,
        up_full,
        up_bias_full,
        down_full,
        down_bias_full,
        gain_one,
        shift_one,
        gain_two,
        shift_two,
    ) = gathered
    frames_wide = frames.astype(jnp.float32)
    first_out, first_normed, first_inv = layer_norm(
        frames_wide, gain_one.astype(jnp.float32), shift_one.astype(jnp.float32)
    )
    first_low = first_out.astype(jnp.bfloat16)
    projected = jnp.dot(first_low, qkv_full, preferred_element_type=jnp.float32)
    bias_vec = qv_bias_full.astype(jnp.float32)
    queries = (projected[:, :width] + bias_vec[:width]).astype(jnp.bfloat16)
    key_rows = projected[:, width : 2 * width].astype(jnp.bfloat16)
    value_rows = (projected[:, 2 * width :] + bias_vec[width:]).astype(jnp.bfloat16)
    live_rows = key_mask.astype(jnp.bfloat16)
    query_blocks = (blocked(queries), blocked(positions), blocked(own_docs))

    def forward_hop(turn, online_state, key_part, value_part, live_part):
        key_pos, key_doc = key_meta(turn)
        key_items = (
            blocked(key_part),
            blocked(value_part),
            blocked(key_pos),
            blocked(key_doc),
            blocked(live_part),
        )

        def forward_per_query(query_items):
            query_block, query_pos, query_doc, row_peak, row_total, accum = query_items

            def online(carried, key_block_items):
                row_peak, row_total, accum = carried
                key_block, value_block, key_bpos, key_bdoc, key_blive = key_block_items
                logits = pair_logits(
                    query_block,
                    key_block,
                    query_pos,
                    key_bpos,
                    query_doc,
                    key_bdoc,
                    key_blive,
                    table_heads,
                )
                new_peak = jnp.maximum(row_peak, jnp.max(logits, axis=2))
                decay = jnp.exp(row_peak - new_peak)
                weights = jnp.exp(logits - new_peak[:, :, None])
                row_total = row_total * decay + jnp.sum(weights, axis=2)
                accum = accum * decay.T[:, :, None] + jnp.einsum(
                    "hqk,khd->qhd",
                    weights.astype(jnp.bfloat16),
                    value_block.reshape(-1, H, HD),
                    preferred_element_type=jnp.float32,
                )
                return ((new_peak, row_total, accum), None)

            result, unused = lax.scan(online, (row_peak, row_total, accum), key_items)
            return result

        return lax.map(forward_per_query, query_blocks + online_state)

    def cycle_turn(turn, carried):
        online_state, key_part, value_part, live_part = carried
        online_state = forward_hop(turn, online_state, key_part, value_part, live_part)
        key_part, value_part, live_part = from_behind((key_part, value_part, live_part), "blk", 1)
        return (online_state, key_part, value_part, live_part)

    start_state = (
        jnp.full((block_count, H, BLOCK), START_PEAK, jnp.float32),
        jnp.zeros((block_count, H, BLOCK), jnp.float32),
        jnp.zeros((block_count, BLOCK, H, HD), jnp.float32),
    )
    carried = lax.fori_loop(
        0, cycle_size - 1, cycle_turn, (start_state, key_rows, value_rows, live_rows)
    )
    row_peak, row_total, accum = forward_hop(
        cycle_size - 1, carried[0], carried[1], carried[2], carried[3]
    )
    mixed = accum / jnp.transpose(row_total, (0, 2, 1))[:, :, :, None]
    mixed_flat = mixed.reshape(shard_len, width)
    context = mixed_flat.astype(jnp.bfloat16)
    branch = jnp.dot(context, out_full, preferred_element_type=jnp.float32) + out_bias_full.astype(
        jnp.float32
    )
    middle = frames_wide + branch
    second_out, second_normed, second_inv = layer_norm(
        middle, gain_two.astype(jnp.float32), shift_two.astype(jnp.float32)
    )
    second_low = second_out.astype(jnp.bfloat16)
    hidden = jnp.dot(second_low, up_full, preferred_element_type=jnp.float32) + up_bias_full.astype(
        jnp.float32
    )
    active, slope = gelu_parts(hidden)
    active_low = active.astype(jnp.bfloat16)
    layer_out = (
        middle
        + jnp.dot(active_low, down_full, preferred_element_type=jnp.float32)
        + down_bias_full.astype(jnp.float32)
    )
    weights_back = (
        lax.all_gather(qkv_weight, ("dp", "blk"), axis=1, tiled=True),
        lax.all_gather(query_value_bias, ("dp", "blk"), axis=0, tiled=True),
        lax.all_gather(out_weight, ("dp", "blk"), axis=1, tiled=True),
        lax.all_gather(out_bias, ("dp", "blk"), axis=0, tiled=True),
        lax.all_gather(up_weight, ("dp", "blk"), axis=1, tiled=True),
        lax.all_gather(up_bias, ("dp", "blk"), axis=0, tiled=True),
        lax.all_gather(down_weight, ("dp", "blk"), axis=1, tiled=True),
        lax.all_gather(down_bias, ("dp", "blk"), axis=0, tiled=True),
        lax.all_gather(first_gain, ("dp", "blk"), axis=0, tiled=True),
        lax.all_gather(first_shift, ("dp", "blk"), axis=0, tiled=True),
        lax.all_gather(second_gain, ("dp", "blk"), axis=0, tiled=True),
        lax.all_gather(second_shift, ("dp", "blk"), axis=0, tiled=True),
    )
    qkv_back = weights_back[0]
    out_back = weights_back[2]
    up_back = weights_back[4]
    down_back = weights_back[6]
    gain_one_back = weights_back[8].astype(jnp.float32)
    gain_two_back = weights_back[10].astype(jnp.float32)
    grad_wide = cotangent.astype(jnp.float32)
    down_grad = jnp.einsum("tf,td->fd", active_low, cotangent, preferred_element_type=jnp.float32)
    down_bias_grad = jnp.sum(grad_wide, axis=0)
    active_grad = jnp.einsum("td,fd->tf", cotangent, down_back, preferred_element_type=jnp.float32)
    hidden_low = (active_grad * slope).astype(jnp.bfloat16)
    up_grad = jnp.einsum("td,tf->df", second_low, hidden_low, preferred_element_type=jnp.float32)
    up_bias_grad = jnp.sum(hidden_low.astype(jnp.float32), axis=0)
    second_grad = jnp.einsum("tf,df->td", hidden_low, up_back, preferred_element_type=jnp.float32)
    middle_norm, gain_two_grad, shift_two_grad = norm_back(
        second_grad, second_normed, second_inv, gain_two_back
    )
    middle_grad = grad_wide + middle_norm
    branch_low = middle_grad.astype(jnp.bfloat16)
    out_grad = jnp.einsum("td,te->de", context, branch_low, preferred_element_type=jnp.float32)
    out_bias_grad = jnp.sum(branch_low.astype(jnp.float32), axis=0)
    context_low = jnp.einsum(
        "te,de->td", branch_low, out_back, preferred_element_type=jnp.float32
    ).astype(jnp.bfloat16)
    delta = jnp.sum(
        (context_low.astype(jnp.float32) * mixed_flat).reshape(shard_len, H, HD), axis=2
    )
    delta_blocks = jnp.transpose(blocked(delta), (0, 2, 1))
    query_back = (
        blocked(queries),
        blocked(context_low),
        blocked(positions),
        blocked(own_docs),
        row_peak,
        row_total,
        delta_blocks,
    )

    def backward_hop(
        turn, query_grad, table_grad, key_part, value_part, live_part, key_grad, value_grad
    ):
        key_pos, key_doc = key_meta(turn)

        def per_key(carried, key_block_items):
            query_grad, table_grad = carried
            key_block, value_block, key_bpos, key_bdoc, key_blive, key_bgrad, value_bgrad = (
                key_block_items
            )
            key_heads = key_block.reshape(-1, H, HD)
            value_heads = value_block.reshape(-1, H, HD)

            def per_per_query(inner, query_items):
                key_bgrad, value_bgrad, table_grad = inner
                (
                    query_block,
                    dout_block,
                    query_pos,
                    query_doc,
                    peak_block,
                    total_block,
                    delta_block,
                ) = query_items
                logits = pair_logits(
                    query_block,
                    key_block,
                    query_pos,
                    key_bpos,
                    query_doc,
                    key_bdoc,
                    key_blive,
                    table_heads,
                )
                attn_prob = jnp.exp(logits - peak_block[:, :, None]) / total_block[:, :, None]
                dout_heads = dout_block.reshape(-1, H, HD)
                prob_grad = jnp.einsum(
                    "qhd,khd->hqk", dout_heads, value_heads, preferred_element_type=jnp.float32
                )
                logit_grad = attn_prob * (prob_grad - delta_block[:, :, None])
                raw_low = (logit_grad * score_scale).astype(jnp.bfloat16)
                query_part = jnp.einsum(
                    "hqk,khd->qhd", raw_low, key_heads, preferred_element_type=jnp.float32
                ).reshape(-1, width)
                key_bgrad = key_bgrad + jnp.einsum(
                    "hqk,qhd->khd",
                    raw_low,
                    query_block.reshape(-1, H, HD),
                    preferred_element_type=jnp.float32,
                ).reshape(-1, width)
                value_bgrad = value_bgrad + jnp.einsum(
                    "hqk,qhd->khd",
                    attn_prob.astype(jnp.bfloat16),
                    dout_heads,
                    preferred_element_type=jnp.float32,
                ).reshape(-1, width)
                table_grad = table_grad + diagonal_sums(logit_grad, key_bpos[0] - query_pos[0])
                return ((key_bgrad, value_bgrad, table_grad), query_part)

            (key_bgrad, value_bgrad, table_grad), query_parts = lax.scan(
                per_per_query, (key_bgrad, value_bgrad, table_grad), query_back
            )
            return ((query_grad + query_parts, table_grad), (key_bgrad, value_bgrad))

        (query_grad, table_grad), (key_new, value_new) = lax.scan(
            per_key,
            (query_grad, table_grad),
            (
                blocked(key_part),
                blocked(value_part),
                blocked(key_pos),
                blocked(key_doc),
                blocked(live_part),
                blocked(key_grad),
                blocked(value_grad),
            ),
        )
        return (
            query_grad,
            table_grad,
            key_new.reshape(shard_len, width),
            value_new.reshape(shard_len, width),
        )

    def pass_grads(key_grad, value_grad):
        return (
            from_behind(key_grad.astype(jnp.bfloat16), "blk", 1).astype(key_grad.dtype),
            from_behind(value_grad.astype(jnp.bfloat16), "blk", 1).astype(value_grad.dtype),
        )

    def back_turn(turn, carried):
        query_grad, table_grad, key_part, value_part, live_part, key_grad, value_grad = carried
        query_grad, table_grad, key_grad, value_grad = backward_hop(
            turn, query_grad, table_grad, key_part, value_part, live_part, key_grad, value_grad
        )
        key_part, value_part, live_part = from_behind((key_part, value_part, live_part), "blk", 1)
        key_grad, value_grad = pass_grads(key_grad, value_grad)
        return (query_grad, table_grad, key_part, value_part, live_part, key_grad, value_grad)

    zero_rows = jnp.zeros((shard_len, width), jnp.float32)
    back_start = (
        jnp.zeros((block_count, BLOCK, width), jnp.float32),
        jnp.zeros((H, BUCKETS), jnp.float32),
        key_rows,
        value_rows,
        live_rows,
        zero_rows,
        zero_rows,
    )
    carried = lax.fori_loop(0, cycle_size - 1, back_turn, back_start)
    query_grad, table_grad, key_grad, value_grad = backward_hop(
        cycle_size - 1,
        carried[0],
        carried[1],
        carried[2],
        carried[3],
        carried[4],
        carried[5],
        carried[6],
    )
    key_grad, value_grad = pass_grads(key_grad, value_grad)
    query_low = query_grad.reshape(shard_len, width).astype(jnp.bfloat16)
    key_low = key_grad.astype(jnp.bfloat16)
    value_low = value_grad.astype(jnp.bfloat16)
    qkv_low = jnp.concatenate([query_low, key_low, value_low], axis=1)
    qkv_grad = jnp.einsum("td,te->de", first_low, qkv_low, preferred_element_type=jnp.float32)
    query_value_grad = jnp.concatenate(
        [
            jnp.sum(query_low.astype(jnp.float32), axis=0),
            jnp.sum(value_low.astype(jnp.float32), axis=0),
        ]
    )
    first_grad = jnp.einsum("te,de->td", qkv_low, qkv_back, preferred_element_type=jnp.float32)
    frames_norm, gain_one_grad, shift_one_grad = norm_back(
        first_grad, first_normed, first_inv, gain_one_back
    )
    frames_grad = middle_grad + frames_norm
    summed = (
        lax.psum_scatter(qkv_grad, ("dp", "blk"), scatter_dimension=1, tiled=True),
        lax.psum_scatter(query_value_grad, ("dp", "blk"), scatter_dimension=0, tiled=True),
        lax.psum_scatter(out_grad, ("dp", "blk"), scatter_dimension=1, tiled=True),
        lax.psum_scatter(out_bias_grad, ("dp", "blk"), scatter_dimension=0, tiled=True),
        lax.psum_scatter(up_grad, ("dp", "blk"), scatter_dimension=1, tiled=True),
        lax.psum_scatter(up_bias_grad, ("dp", "blk"), scatter_dimension=0, tiled=True),
        lax.psum_scatter(down_grad, ("dp", "blk"), scatter_dimension=1, tiled=True),
        lax.psum_scatter(down_bias_grad, ("dp", "blk"), scatter_dimension=0, tiled=True),
        lax.psum_scatter(gain_one_grad, ("dp", "blk"), scatter_dimension=0, tiled=True),
        lax.psum_scatter(shift_one_grad, ("dp", "blk"), scatter_dimension=0, tiled=True),
        lax.psum_scatter(gain_two_grad, ("dp", "blk"), scatter_dimension=0, tiled=True),
        lax.psum_scatter(shift_two_grad, ("dp", "blk"), scatter_dimension=0, tiled=True),
    )
    table_sum = lax.psum(table_grad, ("dp", "blk"))
    return (
        layer_out,
        frames_grad,
        summed[0],
        summed[1],
        summed[2],
        summed[3],
        summed[4],
        summed[5],
        summed[6],
        summed[7],
        summed[8],
        summed[9],
        summed[10],
        summed[11],
        table_sum.T,
    )


AXES = ("dp", "blk")
F32 = jnp.float32
LOW = jnp.bfloat16
LANES = 128
NARROW = 6
PAD = 8


def route(move):
    n_dp, n_blk = lax.axis_size("dp"), lax.axis_size("blk")
    pairs = []
    for d in range(n_dp):
        d_bits, b_bits = move[d % 2]
        for b in range(n_blk):
            pairs.append((d * n_blk + b, (d ^ d_bits) * n_blk + (b ^ b_bits)))
    return pairs


def shift(array, move, name="swap"):
    with jax.named_scope(name):
        return lax.ppermute(array, AXES, route(move))


CORE = ((1, 0), (1, 0))
SIDE = ((0, 1), (2, 0))
OTHER_SIDE = ((2, 0), (0, 1))
PACK = ((0, 1), (0, 1))
ALONG_Z = tuple(((4 * turn, 0), (4 * turn, 0)) for turn in (1, 2, 3))


def tied(value, *after):
    return lax.optimization_barrier((value,) + after)[0]


def joined(*groups):
    return lax.optimization_barrier(groups)


def twin(array, name="twin"):
    return shift(array, CORE, name)


def along_z(unit, name):
    return tuple(shift(unit, move, name + "_z") for move in ALONG_Z)


def z_sends(plane, name):
    low = plane.astype(LOW)
    return tuple(shift(low[n + 1], move, name + "_z") for n, move in enumerate(ALONG_Z))


def z_sum(plane, arrived):
    return plane[0] + sum(part.astype(F32) for part in arrived)


def unit_of(place, x_turn, y_turn, z_turn, c):
    x, y, z = place[0] ^ x_turn, place[1] ^ y_turn, place[2] ^ z_turn
    return ((z * 2 + y) * 2 + c) * 2 + x


def planes_of(place):
    c0 = place[3]
    found = []
    for plane in range(2):
        c = c0 if plane == 0 else 1 - c0
        for z in range(4):
            for n, (x_turn, y_turn) in enumerate(((0, 0), (1 - c, c), (c, 1 - c), (1, 1))):
                found.append((4 * plane + n, z, unit_of(place, x_turn, y_turn, z, c)))
    return found


def load_units(place, pieces, stage, sems):
    copies = [
        pltpu.make_async_copy(pieces[array].at[z], stage.at[unit], sems.at[n])
        for n, (array, z, unit) in enumerate(planes_of(place))
    ]
    for copy in copies:
        copy.start()
    return copies


def take_columns(place, array, pair, taken, top):
    for c in range(2):

        @pl.when(place[3] == c)
        def _():
            taken[top : top + array.shape[0], :] = jnp.concatenate(
                [
                    array[:, (2 * n + c) * pair : (2 * n + c + 1) * pair]
                    for n in range(array.shape[1] // (2 * pair))
                ],
                axis=1,
            )


def give_units(place, stage, parts):
    c = place[3]
    for part, (x_turn, y_turn) in zip(parts, ((0, 0), (1 - c, c), (c, 1 - c), (1, 1))):
        for turn in range(4):
            unit = ((place[2] ^ turn) * 2 + (place[1] ^ y_turn)) * 2 + (place[0] ^ x_turn)
            if isinstance(part, tuple):
                part[turn // 2][turn % 2] = stage[unit].astype(LOW)
            else:
                part[turn] = stage[unit].astype(LOW)


def part_shapes(rows, width):
    return [jax.ShapeDtypeStruct((4, rows, width), LOW)] * 4


def dot_nn(a, b):
    return lax.dot_general(a, b, (((1,), (0,)), ((), ())), preferred_element_type=F32)


def dot_nt(a, b):
    return lax.dot_general(a, b, (((1,), (1,)), ((), ())), preferred_element_type=F32)


def dot_tn(a, b):
    return lax.dot_general(a, b, (((0,), (0,)), ((), ())), preferred_element_type=F32)


HBM = pl.BlockSpec(memory_space=pltpu.HBM)
SMEM = pl.BlockSpec(memory_space=pltpu.SMEM)
VMEM = pl.BlockSpec(memory_space=pltpu.VMEM)


def call(kernel, in_specs, outs, out_specs, scratch, args, flops, limit=56, **kwargs):
    moved = sum(math.prod(a.shape) * a.dtype.itemsize for a in list(args) + list(outs))
    return pl.pallas_call(
        kernel,
        out_shape=outs,
        in_specs=in_specs,
        out_specs=out_specs,
        scratch_shapes=scratch,
        compiler_params=pltpu.CompilerParams(vmem_limit_bytes=limit * 1024 * 1024),
        cost_estimate=pl.CostEstimate(flops=flops, bytes_accessed=moved, transcendentals=0),
        **kwargs,
    )(*args)


def spread_tables(units, width):
    tables = []
    for n in (width // units, 2 * width // units, 4 * width // units):
        lane = np.arange(units * n)
        keep = lane[None, :] // n == np.arange(units)[:, None]
        pick = lane[None, :] % n == np.arange(LANES)[:, None]
        tables.append(jnp.asarray(np.concatenate([keep, pick]), LOW))
    return tables


def project_kernel(
    place, own, other, p0, p1, p2, p3, p4, p5, p6, p7, wide_one, wide_two, wide_four,
    first, queries, keys, values, weight, vectors, up_bias, mate_live, stage, small, sems,
):
    units = stage.shape[0]
    width = own.shape[1]
    rows = stage.shape[1] - PAD
    shard_len = own.shape[0]
    copies = load_units(place, (p0, p1, p2, p3, p4, p5, p6, p7), stage, sems)

    def normed(frames):
        wide = frames.astype(F32)
        center = wide - jnp.mean(wide, axis=1, keepdims=True)
        return center * lax.rsqrt(jnp.mean(center * center, axis=1, keepdims=True) + EPSILON)

    own_normed, mate_normed = normed(own[...]), normed(other[...])
    for copy in copies:
        copy.wait()
    for unit in range(units):
        top = stage[unit, rows : rows + PAD, :].astype(F32)
        small[0, unit : unit + 1, :] = top[0:1]
        small[1, unit : unit + 1, :] = top[1:2]

    mate = unit_of(place, 1, 0, 0, place[3])
    mate_live[...] = stage[mate, rows : rows + PAD, : mate_live.shape[1]].astype(F32)

    def spread(row, slot, table):
        held = small[row, :, slot * LANES : (slot + 1) * LANES].astype(LOW)
        laid = dot_nn(held, table[units:, :]) * table[:units, :].astype(F32)
        return jnp.sum(laid, axis=0, keepdims=True)

    for n in range(NARROW):
        vectors[n : n + 1, :] = spread(0, n, wide_one)
    qv_bias = spread(1, 0, wide_two)
    up_bias[...] = jnp.broadcast_to(spread(1, 1, wide_four), up_bias.shape)
    vectors[NARROW : NARROW + 1, :] = qv_bias[:, :width]
    vectors[NARROW + 1 : NARROW + 2, :] = qv_bias[:, width:]

    def join(pair, _):
        both = jnp.concatenate(
            [stage[2 * pair, :rows, :].astype(F32), stage[2 * pair + 1, :rows, :].astype(F32)], axis=0
        )
        weight[pl.ds(pl.multiple_of(2 * rows * pair, 2 * rows), 2 * rows), :] = both.astype(LOW)
        return 0

    lax.fori_loop(0, units // 2, join, 0)
    gain, offset = vectors[0:1, :], vectors[1:2, :]
    x = place[0]
    own_at = pl.multiple_of(x * shard_len, shard_len)
    mate_at = pl.multiple_of((1 - x) * shard_len, shard_len)
    first[pl.ds(own_at, shard_len), :] = (own_normed * gain + offset).astype(LOW)
    first[pl.ds(mate_at, shard_len), :] = (mate_normed * gain + offset).astype(LOW)
    mine = first[pl.ds(own_at, shard_len), :]
    queries[...] = (dot_nt(mine, weight[:width, :]) + vectors[NARROW : NARROW + 1, :]).astype(LOW)
    keys[...] = dot_nt(first[...], weight[width : 2 * width, :]).astype(LOW)
    values[...] = (
        dot_nt(first[...], weight[2 * width :, :]) + vectors[NARROW + 1 : NARROW + 2, :]
    ).astype(LOW)


def half_mask(shape, head):
    return (lax.broadcasted_iota(jnp.int32, shape, 1) // HD) == head


def attend_kernel(
    place, lengths, queries, keys, values, curve, own_live, mate_live, probs, mixed, hidden_pairs
):
    q, k, v = queries[...], keys[...], values[...]
    block_len, span = hidden_pairs.shape
    step = pl.program_id(0)

    @pl.when(step == 0)
    def _():
        start = place[0] * block_len
        key_pos = lax.broadcasted_iota(jnp.int32, (1, span), 1)
        query_pos = lax.broadcasted_iota(jnp.int32, (block_len, 1), 0) + start
        key_doc, query_doc = jnp.zeros_like(key_pos), jnp.zeros_like(query_pos)
        end = 0
        for n in range(lengths.shape[1]):
            end = end + lengths[0, n]
            key_doc = key_doc + (key_pos >= end).astype(jnp.int32)
            query_doc = query_doc + (query_pos >= end).astype(jnp.int32)
        one, two = own_live[...].astype(F32), mate_live[2:3, :]
        live = jnp.where(
            place[0] == 0, jnp.concatenate([one, two], axis=1), jnp.concatenate([two, one], axis=1)
        )
        allowed = (query_doc == key_doc) & ((live > 0.5) | (query_pos == key_pos))
        hidden_pairs[...] = jnp.where(allowed, 0.0, MASKED)

    total = jnp.zeros(q.shape, F32)
    for head in range(2):
        q_head = jnp.where(half_mask(q.shape, head), q, 0) * (1.0 / math.sqrt(HD))
        bias = pltpu.roll(
            jnp.broadcast_to(curve[pl.ds(2 * step + head, 1), :], (block_len, block_len + span)),
            span + 1, 1, stride=1, stride_axis=0,
        )[:, :span]
        logits = dot_nt(q_head.astype(LOW), k) + bias + hidden_pairs[...]
        weights = jnp.exp(logits - jnp.max(logits, axis=1, keepdims=True))
        prob = (weights * (1.0 / jnp.sum(weights, axis=1, keepdims=True))).astype(LOW)
        probs[head] = prob
        total = total + dot_nn(prob, jnp.where(half_mask(v.shape, head), v, 0))
    mixed[...] = total


def load_mixed(place, pieces, up, kept, sems, kept_sems):
    rows = pieces[0].shape[1] - kept.shape[1]
    first, later = [], []
    for n, (array, z, unit) in enumerate(planes_of(place)):
        ref = pieces[array].at[z]
        at = pl.multiple_of(unit * rows, rows)
        first.append(pltpu.make_async_copy(ref.at[rows:], kept.at[unit], kept_sems.at[n]))
        later.append(pltpu.make_async_copy(ref.at[:rows], up.at[pl.ds(at, rows)], sems.at[n]))
    for copy in first + later:
        copy.start()
    return first, later


def join_units(kept, out):
    units = kept.shape[0]
    each = out.shape[0] // units

    def join(pair, _):
        both = jnp.concatenate(
            [kept[2 * pair].astype(F32)[:each], kept[2 * pair + 1].astype(F32)[:each]], axis=0
        )
        out[pl.ds(pl.multiple_of(2 * each * pair, 2 * each), 2 * each), :] = both.astype(LOW)
        return 0

    lax.fori_loop(0, units // 2, join, 0)


def expand_kernel(
    place, frames, mixed, vectors, up_bias, p0, p1, p2, p3, p4, p5, p6, p7,
    middle, second, context, active, slope, up, kept, out, sems, kept_sems,
):
    width = frames.shape[1]
    first, later = load_mixed(place, (p0, p1, p2, p3, p4, p5, p6, p7), up, kept, sems, kept_sems)
    context[...] = mixed[...].astype(LOW)
    for copy in first:
        copy.wait()
    join_units(kept, out)
    mid = frames[...].astype(F32) + (dot_nt(context[...], out[...]) + vectors[4:5, :])
    middle[...] = mid
    center = mid - jnp.mean(mid, axis=1, keepdims=True)
    normed = center * lax.rsqrt(jnp.mean(center * center, axis=1, keepdims=True) + EPSILON)
    second[...] = (normed * vectors[2:3, :] + vectors[3:4, :]).astype(LOW)
    for copy in later:
        copy.wait()
    for n in range(up.shape[0] // width):
        at = slice(n * width, (n + 1) * width)
        hidden = dot_nt(second[...], up[at, :]) + up_bias[0:1, at]
        cdf = 0.5 * (1.0 + lax.erf(hidden * 0.7071067811865476))
        density = jnp.exp(-0.5 * hidden * hidden) * 0.3989422804014327
        active[:, at] = (hidden * cdf).astype(LOW)
        slope[:, at] = cdf + hidden * density


def down_grad_kernel(
    place, active, active_twin, cotangent, cotangent_twin, o0, o1, o2, o3, bias_grad, taken, wide,
):
    units, rows, width = wide.shape
    each = width // (2 * units)
    bias_grad[...] = jnp.broadcast_to(
        jnp.sum(cotangent[...].astype(F32), axis=0, keepdims=True), bias_grad.shape
    )

    shard_len = cotangent.shape[0]
    take_columns(place, cotangent, 2 * each, taken, 0)
    take_columns(place, cotangent_twin, 2 * each, taken, shard_len)
    dy, dy_twin = taken[:shard_len, :], taken[shard_len:, :]
    for fold in range(rows // each):
        at = slice(fold * width, (fold + 1) * width)
        grad = dot_tn(dy, active[:, at]) + dot_tn(dy_twin, active_twin[:, at])
        for unit in range(units):
            wide[unit, fold * each : (fold + 1) * each, :] = grad[unit * each : (unit + 1) * each]
    give_units(place, wide, (o0, o1, o2, o3))


def unfold_units(stage, down):
    units, rows, width = stage.shape
    each = down.shape[0] // units

    def unfold(pair, _):
        one, two = stage[2 * pair].astype(F32), stage[2 * pair + 1].astype(F32)
        at = pl.multiple_of(2 * each * pair, 2 * each)
        for fold in range(rows // each):
            both = jnp.concatenate(
                [one[fold * each : (fold + 1) * each], two[fold * each : (fold + 1) * each]], axis=0
            )
            down[pl.ds(at, 2 * each), fold * width : (fold + 1) * width] = both.astype(LOW)
        return 0

    lax.fori_loop(0, units // 2, unfold, 0)


def back_kernel(
    place, cotangent, slope, middle, vectors, p0, p1, p2, p3, p4, p5, p6, p7, u0, u1, u2, u3, u4, u5, u6, u7,
    middle_grad, context_grad, vector_grads, branch_grad, up_bias_grad, hidden_grad,
    stage, down, up, kept, out, stage_sems, sems, kept_sems,
):
    width = cotangent.shape[1]
    down_copies = load_units(place, (p0, p1, p2, p3, p4, p5, p6, p7), stage, stage_sems)
    kept_copies, up_copies = load_mixed(
        place, (u0, u1, u2, u3, u4, u5, u6, u7), up, kept, sems, kept_sems
    )
    for copy in down_copies:
        copy.wait()
    unfold_units(stage, down)
    dy = cotangent[...]
    for n in range(hidden_grad.shape[1] // width):
        at = slice(n * width, (n + 1) * width)
        grad = (dot_nn(dy, down[:, at]) * slope[:, at]).astype(LOW)
        hidden_grad[:, at] = grad
        up_bias_grad[:, at] = jnp.broadcast_to(
            jnp.sum(grad.astype(F32), axis=0, keepdims=True), (up_bias_grad.shape[0], width)
        )
    for copy in kept_copies:
        copy.wait()
    join_units(kept, out)
    for copy in up_copies:
        copy.wait()
    second_grad = dot_nn(hidden_grad[...], up[...])
    mid = middle[...]
    center = mid - jnp.mean(mid, axis=1, keepdims=True)
    inv_std = lax.rsqrt(jnp.mean(center * center, axis=1, keepdims=True) + EPSILON)
    normed = center * inv_std
    scaled = second_grad * vectors[2:3, :]
    inner = (
        scaled
        - jnp.mean(scaled, axis=1, keepdims=True)
        - normed * jnp.mean(scaled * normed, axis=1, keepdims=True)
    )
    mid_grad = cotangent[...].astype(F32) + inner * inv_std
    middle_grad[...] = mid_grad
    branch = mid_grad.astype(LOW)
    vector_grads[...] = jnp.concatenate(
        [
            jnp.sum(second_grad * normed, axis=0, keepdims=True),
            jnp.sum(second_grad, axis=0, keepdims=True),
            jnp.sum(branch.astype(F32), axis=0, keepdims=True),
            jnp.zeros((5, width), F32),
        ],
        axis=0,
    )
    branch_grad[...] = branch
    context_grad[...] = dot_nn(branch, out[...]).astype(LOW)


def up_grad_kernel(
    place, hidden, hidden_twin, second, second_twin, branch, branch_twin, context, context_twin,
    o0, o1, o2, o3, o4, taken, taken_branch, stage,
):
    units, rows, width = stage.shape
    each = width // (2 * units)
    up_rows = hidden.shape[1] // (2 * units)

    shard_len = second.shape[0]
    take_columns(place, branch, 2 * each, taken_branch, 0)
    take_columns(place, branch_twin, 2 * each, taken_branch, shard_len)
    take_columns(place, hidden, 2 * up_rows, taken, 0)
    take_columns(place, hidden_twin, 2 * up_rows, taken, shard_len)
    out_grad = dot_tn(taken_branch[:shard_len, :], context[...]) + dot_tn(
        taken_branch[shard_len:, :], context_twin[...]
    )
    blank = jnp.zeros((rows - up_rows - each, width), F32)
    quarter = units // 4
    for z in range(4):
        at = slice(z * quarter * up_rows, (z + 1) * quarter * up_rows)
        grad = dot_tn(taken[:shard_len, at], second[...]) + dot_tn(taken[shard_len:, at], second_twin[...])
        for n in range(quarter):
            unit = z * quarter + n
            stage[unit] = jnp.concatenate(
                [
                    grad[n * up_rows : (n + 1) * up_rows],
                    out_grad[unit * each : (unit + 1) * each],
                    blank,
                ],
                axis=0,
            ).astype(LOW)
    give_units(place, stage, (o0, o1, (o2, o3), o4))


def rows_left(each):
    return -each % 16


def finish_kernel(
    place, active, middle, vectors, p0, p1, p2, p3, p4, p5, p6, p7, layer_out, stage, down, sems
):
    copies = load_units(place, (p0, p1, p2, p3, p4, p5, p6, p7), stage, sems)
    for copy in copies:
        copy.wait()
    unfold_units(stage, down)
    layer_out[...] = middle[...] + dot_nt(active[...], down[...]) + vectors[5:6, :]


def attend_back_kernel(
    place, queries, keys, values, context_grad, mixed, probs, grads, diagonals
):
    q, k, v, dout = queries[...], keys[...], values[...], context_grad[...]
    block_len, span = probs.shape[1:]
    weighted = dout.astype(F32) * mixed[...]
    row = lax.broadcasted_iota(jnp.int32, (block_len, block_len), 0)
    lane = lax.broadcasted_iota(jnp.int32, (block_len, block_len), 1)
    turn = (row + lane == block_len - 1).astype(LOW)
    blank = jnp.zeros((block_len, block_len), F32)
    dq, dk, dv = jnp.zeros(q.shape, F32), jnp.zeros(k.shape, F32), jnp.zeros(v.shape, F32)
    for head in range(2):
        mine = half_mask(q.shape, head)
        dout_head = jnp.where(mine, dout, 0)
        delta = jnp.sum(jnp.where(mine, weighted, 0.0), axis=1, keepdims=True)
        prob = probs[head]
        grad = prob.astype(F32) * (dot_nt(dout_head, v) - delta)
        raw = (grad * (1.0 / math.sqrt(HD))).astype(LOW)
        dq = dq + dot_nn(raw, jnp.where(half_mask(k.shape, head), k, 0))
        dk = dk + dot_tn(raw, jnp.where(mine, q, 0))
        dv = dv + dot_tn(prob, dout_head)
        turned = jnp.concatenate([dot_nn(turn, raw), blank], axis=1)
        sheared = pltpu.roll(turned, 0, 1, stride=1, stride_axis=0)
        diagonals[pl.ds(2 * pl.program_id(0) + head, 1), :] = jnp.sum(sheared, axis=0, keepdims=True) * math.sqrt(HD)
    own_at = pl.multiple_of(place[0] * block_len, block_len)
    grads[0] = jnp.zeros(k.shape, LOW)
    grads[0, pl.ds(own_at, block_len), :] = dq.astype(LOW)
    grads[1] = dk.astype(LOW)
    grads[2] = dv.astype(LOW)


def total(array):
    return jnp.sum(array, axis=0, keepdims=True)


def norm_parts(frames):
    wide = frames.astype(F32)
    center = wide - jnp.mean(wide, axis=1, keepdims=True)
    inv_std = lax.rsqrt(jnp.mean(center * center, axis=1, keepdims=True) + EPSILON)
    return center * inv_std, inv_std


def first_grad_kernel(
    place, own_frames, mate_frames, grads, weight_in, diagonals, vector_grads, down_bias_grad, up_bias_grad,
    own_grad, mate_grad, small, weight, sems,
):
    copy = pltpu.make_async_copy(weight_in, weight, sems.at[0])
    copy.start()
    shard_len, width = own_frames.shape
    x = place[0]
    own_at = pl.multiple_of(x * shard_len, shard_len)
    mate_at = pl.multiple_of((1 - x) * shard_len, shard_len)
    own_normed, _ = norm_parts(own_frames[...])
    mate_normed, _ = norm_parts(mate_frames[...])
    dq = grads[0, pl.ds(own_at, shard_len), :]
    small[4:5, :] = vector_grads[2:3, :]
    small[2:4, :] = vector_grads[0:2, :]
    small[5:6, :] = down_bias_grad[0:1, :]
    small[6:7, :] = total(dq.astype(F32))
    small[7:8, :] = total(grads[2].astype(F32))
    for n in range(up_bias_grad.shape[1] // width):
        small[8 + n : 9 + n, :] = up_bias_grad[0:1, n * width : (n + 1) * width]
    small[12:, :] = diagonals[...]
    copy.wait()

    def from_keys(at):
        return dot_nn(grads[1, pl.ds(at, shard_len), :], weight[width : 2 * width, :]) + dot_nn(
            grads[2, pl.ds(at, shard_len), :], weight[2 * width :, :]
        )

    of_own = from_keys(own_at) + dot_nn(dq, weight[:width, :])
    of_mate = from_keys(mate_at)
    own_grad[...] = of_own
    mate_grad[...] = of_mate
    small[0:1, :] = total(of_own * own_normed) + total(of_mate * mate_normed)
    small[1:2, :] = total(of_own) + total(of_mate)


def qkv_grad_kernel(
    place, grads, grads_twin, first, first_twin, small_own, small_twin, wide_one, wide_two, wide_four,
    o0, o1, o2, o3, taken, sums, small, stage,
):
    units, full, width = stage.shape
    rows = full - PAD
    span = first.shape[0]
    shard_len = span // 2
    x = place[0]
    summed = small_own[...] + small_twin[...]

    def fold(vector, table):
        kept = (vector * table[: 2 * units, :].astype(F32)).astype(LOW)
        return dot_nt(kept, table[2 * units :, :])

    for n in range(NARROW):
        small[0, :, n * LANES : (n + 1) * LANES] = fold(summed[n : n + 1, :], wide_one)
    small[1, :, :] = jnp.zeros((2 * units, width), F32)
    both = jnp.concatenate([summed[6:7, :], summed[7:8, :]], axis=1)
    small[1, :, :LANES] = fold(both, wide_two)
    four = jnp.concatenate([summed[8 + n : 9 + n, :] for n in range(4)], axis=1)
    small[1, :, LANES : 2 * LANES] = fold(four, wide_four)
    lanes = 3 * LANES
    distance = (
        lax.broadcasted_iota(jnp.int32, (shard_len + span, lanes), 0) - (shard_len - 1) - x * shard_len
    )
    bucket = jnp.clip(distance, -MAXREL, MAXREL) + MAXREL
    here = (bucket == lax.broadcasted_iota(jnp.int32, (shard_len + span, lanes), 1)).astype(F32).astype(LOW)
    diagonals = summed[12:, :]
    high = diagonals.astype(LOW)
    table = dot_nn(high, here) + dot_nn((diagonals - high.astype(F32)).astype(LOW), here)
    table = jnp.concatenate([table[: H // 2], table[H // 2 :]], axis=1)
    for n, array in enumerate((grads, grads_twin)):
        columns = jnp.concatenate([array[part] for part in range(3)], axis=1)
        take_columns(place, columns, 2 * rows, taken, n * span)
    sums[...] = dot_tn(taken[:span, :], first[...]) + dot_tn(taken[span:, :], first_twin[...])
    for unit in range(units):
        at = 4 * (unit // 2) + 2 * place[3] + unit % 2
        stage[unit] = jnp.concatenate(
            [
                sums[unit * rows : (unit + 1) * rows, :],
                small[0, pl.ds(at, 1), :],
                small[1, pl.ds(at, 1), :],
                table,
            ],
            axis=0,
        ).astype(LOW)
    give_units(place, stage, (o0, o1, o2, o3))


def input_grad_kernel(frames, mate_frames, own_grad, mate_grad, middle_grad, vectors, own_part, mate_part):
    def through_norm(of_frames, grad):
        normed, inv_std = norm_parts(of_frames)
        scaled = grad * vectors[0:1, :]
        inner = (
            scaled
            - jnp.mean(scaled, axis=1, keepdims=True)
            - normed * jnp.mean(scaled * normed, axis=1, keepdims=True)
        )
        return inner * inv_std

    own_part[...] = middle_grad[...] + through_norm(frames[...], own_grad[...])
    mate_part[...] = through_norm(mate_frames[...], mate_grad[...]).astype(LOW)


def last_kernel(
    own, z1, z2, z3, own_part, mate_part, qkv, qv_bias, up_bias, table, frames_grad, n0, n1, n2, n3, n4, n5
):
    frames_grad[...] = own_part[...] + mate_part[...].astype(F32)
    rows = qkv.shape[0]
    total = own[...] + z1[...].astype(F32) + z2[...].astype(F32) + z3[...].astype(F32)
    qkv[...] = total[:rows]
    for n, narrow in enumerate((n0, n1, n2, n3, n4, n5)):
        narrow[...] = total[rows : rows + 1, n * LANES : n * LANES + narrow.shape[1]]
    qv_bias[...] = total[rows + 1 : rows + 2, : qv_bias.shape[1]]
    up_bias[...] = total[rows + 1 : rows + 2, LANES : LANES + up_bias.shape[1]]
    for half in range(2):
        at = 3 * LANES * half
        table[half * (H // 2) : (half + 1) * (H // 2), :] = total[rows + 2 : rows + PAD, at : at + BUCKETS]


def pack_kernel(
    live, qkv, out, up, down, first_gain, first_shift, second_gain, second_shift, out_bias,
    down_bias, qv_bias, up_bias, qkv_unit, up_unit, down_unit,
):
    each, width = out.shape

    def slots(vectors):
        parts = []
        for vector in vectors:
            wide = vector[...].astype(F32)
            parts += [wide, jnp.zeros((1, LANES - wide.shape[1]), F32)]
        left = width - LANES * len(vectors)
        if left:
            parts.append(jnp.zeros((1, left), F32))
        return jnp.concatenate(parts, axis=1)

    narrow = slots((first_gain, first_shift, second_gain, second_shift, out_bias, down_bias))
    wide = slots((qv_bias, up_bias))
    seen = live[...].astype(F32)
    seen = jnp.concatenate([seen, jnp.zeros((1, width - seen.shape[1]), F32)], axis=1)
    blank = jnp.zeros((PAD - 3, width), F32)
    qkv_unit[...] = jnp.concatenate([qkv[...].astype(F32), narrow, wide, seen, blank], axis=0).astype(LOW)
    blank = jnp.zeros((up_unit.shape[0] - up.shape[0] - each, width), F32)
    up_unit[...] = jnp.concatenate(
        [up[...].astype(F32), out[...].astype(F32), blank], axis=0
    ).astype(LOW)
    down_unit[...] = jnp.concatenate(
        [
            down[:, fold * width : (fold + 1) * width].astype(F32)
            for fold in range(down.shape[1] // width)
        ],
        axis=0,
    ).astype(LOW)


def paired_body(
    frames, cotangent, seq_lengths, key_mask, qkv_weight, query_value_bias, out_weight, out_bias,
    up_weight, up_bias, down_weight, down_bias, first_gain, first_shift, second_gain, second_shift,
    rel_bias,
):
    shard_len, width = frames.shape
    x = lax.axis_index("blk")
    d = lax.axis_index("dp")
    core = d % 2
    units = lax.axis_size("dp") * lax.axis_size("blk")
    span = shard_len * lax.axis_size("blk")
    place = jnp.stack([x, (d // 2) % 2, d // 4, core]).astype(jnp.int32)
    each = width // units
    ff = up_weight.shape[1] * units
    qkv_rows, up_rows = qkv_weight.shape[1], up_weight.shape[1]
    folds = ff // width
    down_rows = each * folds
    out_rows = each + rows_left(each)

    def shape(*dims, kind=LOW):
        return jax.ShapeDtypeStruct(dims, kind)

    def row(vector):
        return vector.reshape(1, vector.shape[0])

    packed = (
        row(key_mask), qkv_weight.T, out_weight.T, up_weight.T, down_weight.T, row(first_gain),
        row(first_shift), row(second_gain), row(second_shift), row(out_bias), row(down_bias),
        row(query_value_bias), row(up_bias),
    )
    qkv_unit, up_unit, down_unit = call(
        pack_kernel,
        [VMEM] * len(packed),
        [shape(qkv_rows + PAD, width), shape(up_rows + out_rows, width), shape(down_rows, width)],
        [VMEM] * 3,
        [],
        packed,
        0,
        name="pack",
    )
    def twins(pieces):
        return tuple(pieces) + tuple(twin(piece) for piece in pieces)

    cotangent_twin = twin(cotangent)
    qkv_z = along_z(qkv_unit, "qkv")
    mate_frames = shift(tied(frames, qkv_unit), PACK, "frames_pack")
    qkv_z, mate_frames = joined(qkv_z, mate_frames)
    qkv_own = jnp.stack((qkv_unit,) + qkv_z)
    qkv_side = shift(qkv_own, SIDE, "qkv_1")
    up_first = tied(up_unit, *qkv_z)
    up_z = [shift(up_first, move, "up_z") for move in ALONG_Z[:2]]
    qkv_side, up_z, cotangent_twin = joined(qkv_side, up_z, cotangent_twin)
    qkv_other = shift(qkv_own, OTHER_SIDE, "qkv_2")
    qkv_across = shift(qkv_side, OTHER_SIDE, "qkv_3")
    up_z.append(shift(tied(up_unit, qkv_side), ALONG_Z[2], "up_z"))
    up_z, qkv_other, qkv_across = joined(up_z, qkv_other, qkv_across)
    qkv_pieces = twins((qkv_own, qkv_side, qkv_other, qkv_across))
    up_own = jnp.stack([up_unit] + up_z)
    up_side = shift(up_own, SIDE, "up_1")
    down_first = tied(down_unit, up_own)
    down_z = [shift(down_first, move, "down_z") for move in ALONG_Z[:2]]

    distance = jnp.arange(span + shard_len, dtype=jnp.int32) - (shard_len - 1) - x * shard_len
    bucket = jnp.clip(distance, -MAXREL, MAXREL) + MAXREL
    bucket_lanes = 3 * LANES
    buckets = (bucket[:, None] == jnp.arange(bucket_lanes, dtype=jnp.int32)[None, :]).astype(LOW)
    curve = lax.dot_general(
        rel_bias, buckets[:, :BUCKETS], (((0,), (1,)), ((), ())), preferred_element_type=F32
    )
    spreads = spread_tables(units, width)
    unit_sems = pltpu.SemaphoreType.DMA((units,))
    first, queries, keys, values, weight, vectors, up_bias_all, mate_live = call(
        project_kernel,
        [SMEM, VMEM, VMEM] + [HBM] * 8 + [VMEM] * 3,
        [
            shape(span, width), shape(shard_len, width), shape(span, width), shape(span, width),
            shape(3 * width, width), shape(8, width, kind=F32), shape(8, ff, kind=F32),
            shape(PAD, shard_len, kind=F32),
        ],
        [VMEM] * 8,
        [
            pltpu.VMEM((units, qkv_rows + PAD, width), LOW), pltpu.VMEM((2, units, width), F32), unit_sems,
        ],
        (tied(place, up_own), frames, mate_frames) + qkv_pieces + tuple(spreads),
        2 * shard_len * width * 5 * width,
        name="project",
    )
    up_side, keys, down_z = joined(up_side, keys, down_z)
    up_other = shift(up_own, OTHER_SIDE, "up_2")
    up_across = shift(up_side, OTHER_SIDE, "up_3")
    down_z.append(shift(tied(down_unit, keys), ALONG_Z[2], "down_z"))
    pairs = H // 2
    pair_lanes = 2 * HD

    def lanes_of(rows):
        return pl.BlockSpec((rows, pair_lanes), lambda n: (0, n))

    def heads_of(*dims):
        return pl.BlockSpec(dims, lambda n: (n,) + (0,) * (len(dims) - 1))

    def whole(*dims):
        return pl.BlockSpec(dims, lambda n: (0,) * len(dims))

    probs, mixed = call(
        attend_kernel,
        [
            SMEM, SMEM, lanes_of(shard_len), lanes_of(span), lanes_of(span), whole(H, span + shard_len),
            whole(1, shard_len), whole(PAD, shard_len),
        ],
        [shape(H, shard_len, span), shape(shard_len, width, kind=F32)],
        [heads_of(2, shard_len, span), lanes_of(shard_len)],
        [pltpu.VMEM((shard_len, span), F32)],
        (
            tied(place, up_side), seq_lengths, queries, keys, values, curve, row(key_mask), mate_live,
        ),
        8 * shard_len * span * width,
        grid=(pairs,),
        name="attend",
    )
    up_other, up_across, mixed, down_z = joined(up_other, up_across, mixed, down_z)
    up_pieces = twins((up_own, up_side, up_other, up_across))
    down_own = jnp.stack([down_unit] + down_z)
    down_side = shift(down_own, SIDE, "down_1")
    down_other = shift(down_own, OTHER_SIDE, "down_2")
    middle, second, context, active, slope = call(
        expand_kernel,
        [SMEM] + [VMEM] * 4 + [HBM] * 8,
        [
            shape(shard_len, width, kind=F32), shape(shard_len, width), shape(shard_len, width),
            shape(shard_len, ff), shape(shard_len, ff, kind=F32),
        ],
        [VMEM] * 5,
        [
            pltpu.VMEM((ff, width), LOW), pltpu.VMEM((units, out_rows, width), LOW),
            pltpu.VMEM((width, width), LOW), unit_sems, unit_sems,
        ],
        (tied(place, down_own), frames, mixed, vectors, up_bias_all) + up_pieces,
        2 * shard_len * width * (width + ff),
        name="expand",
    )
    down_side, down_other, active = joined(down_side, down_other, active)
    down_across = shift(down_side, OTHER_SIDE, "down_3")
    active_twin, context_twin, second_twin = twin(active), twin(context), twin(second)
    first_twin = twin(first)
    down_parts = call(
        down_grad_kernel,
        [SMEM] + [VMEM] * 4,
        part_shapes(down_rows, width) + [shape(8, width, kind=F32)],
        [VMEM] * 5,
        [
            pltpu.VMEM((span, width // 2), LOW), pltpu.VMEM((units // 2, down_rows, width), F32),
        ],
        (tied(place, down_side), active, active_twin, cotangent, cotangent_twin),
        2 * shard_len * width * ff,
        name="down_grad", limit=24,
    )
    down_across, down_parts = joined(down_across, down_parts)
    down_bias_grad = down_parts[4]
    down_pieces = twins((down_own, down_side, down_other, down_across))
    turned = shift(down_parts[3], OTHER_SIDE, "rs_down_3")
    down_two = shift(down_parts[2], OTHER_SIDE, "rs_down_2")
    middle_grad, context_grad, vector_grads, branch_grad, up_bias_grad, hidden_grad = call(
        back_kernel,
        [SMEM] + [VMEM] * 4 + [HBM] * 16,
        [
            shape(shard_len, width, kind=F32), shape(shard_len, width), shape(8, width, kind=F32),
            shape(shard_len, width), shape(8, ff, kind=F32), shape(shard_len, ff),
        ],
        [VMEM] * 6,
        [
            pltpu.VMEM((units, down_rows, width), LOW), pltpu.VMEM((width, ff), LOW),
            pltpu.VMEM((ff, width), LOW), pltpu.VMEM((units, out_rows, width), LOW),
            pltpu.VMEM((width, width), LOW), unit_sems, unit_sems, unit_sems,
        ],
        (tied(place, down_parts[0]), cotangent, slope, middle, vectors) + down_pieces + up_pieces,
        2 * shard_len * width * (2 * ff + width),
        name="back",
    )
    turned, down_two, hidden_grad, context_twin, second_twin, first_twin = joined(
        turned, down_two, hidden_grad, context_twin, second_twin, first_twin
    )
    side = (down_parts[1].astype(F32) + turned.astype(F32)).astype(LOW)
    down_one = shift(side, SIDE, "rs_down_1")
    hidden_twin = twin(hidden_grad)
    branch_twin = twin(branch_grad)
    down_sum = down_parts[0].astype(F32) + down_two.astype(F32)
    up_parts = call(
        up_grad_kernel,
        [SMEM] + [VMEM] * 8,
        [shape(n, up_rows + out_rows, width) for n in (4, 4, 2, 2, 4)],
        [VMEM] * 5,
        [
            pltpu.VMEM((span, ff // 2), LOW), pltpu.VMEM((span, width // 2), LOW),
            pltpu.VMEM((units // 2, up_rows + out_rows, width), LOW),
        ],
        (
            tied(place, down_sum, side), hidden_grad, hidden_twin, second, second_twin, branch_grad, branch_twin,
            context, context_twin,
        ),
        2 * shard_len * width * (ff + width),
        name="up_grad", limit=28,
    )
    down_one, up_parts = joined(down_one, up_parts)
    turned = shift(up_parts[4], OTHER_SIDE, "rs_up_3")
    up_two = shift(up_parts[2], OTHER_SIDE, "rs_up_2a")
    down_sum = down_sum + down_one.astype(F32)
    down_low = down_sum.astype(LOW)
    down_z = [shift(down_low[n + 1], ALONG_Z[n], "rs_down_z") for n in range(2)]
    grads, diagonals = call(
        attend_back_kernel,
        [
            SMEM, lanes_of(shard_len), lanes_of(span), lanes_of(span), lanes_of(shard_len), lanes_of(shard_len),
            heads_of(2, shard_len, span),
        ],
        [shape(3, span, width), shape(H, span + shard_len, kind=F32)],
        [pl.BlockSpec((3, span, pair_lanes), lambda n: (0, 0, n)), whole(H, span + shard_len)],
        [],
        (place, queries, keys, values, tied(context_grad, up_parts[0]), mixed, probs),
        16 * shard_len * span * width,
        grid=(pairs,),
        name="attend_back", limit=24,
    )
    turned, up_two, down_z, grads = joined(turned, up_two, down_z, grads)
    up_rest = shift(up_parts[3], OTHER_SIDE, "rs_up_2b")
    grads_twin = twin(grads)
    side = (up_parts[1].astype(F32) + turned.astype(F32)).astype(LOW)
    up_one = shift(side, SIDE, "rs_up_1")
    own_grad, mate_grad, small = call(
        first_grad_kernel,
        [SMEM] + [VMEM] * 3 + [HBM] + [VMEM] * 4,
        [
            shape(shard_len, width, kind=F32), shape(shard_len, width, kind=F32),
            shape(12 + H, width, kind=F32),
        ],
        [VMEM] * 3,
        [pltpu.VMEM((3 * width, width), LOW), pltpu.SemaphoreType.DMA((1,))],
        (
            tied(place, side), frames, mate_frames, grads, weight, diagonals, vector_grads,
            down_bias_grad, up_bias_grad,
        ),
        2 * shard_len * width * 5 * width,
        name="first_grad", limit=24,
    )
    grads_twin, small = joined(grads_twin, small)
    down_z.append(shift(tied(down_low[3], small), ALONG_Z[2], "rs_down_z"))
    small_twin = twin(small)
    qkv_parts = call(
        qkv_grad_kernel,
        [SMEM] + [VMEM] * 9,
        part_shapes(qkv_rows + PAD, width),
        [VMEM] * 4,
        [
            pltpu.VMEM((2 * span, 3 * width // 2), LOW), pltpu.VMEM((3 * width // 2, width), F32),
            pltpu.VMEM((2, units, width), F32), pltpu.VMEM((units // 2, qkv_rows + PAD, width), LOW),
        ],
        (place, grads, grads_twin, first, first_twin, small, small_twin) + tuple(spreads),
        2 * shard_len * width * 6 * width,
        name="qkv_grad", limit=28,
    )
    up_one, up_rest, down_z, qkv_parts = joined(up_one, up_rest, down_z, qkv_parts)
    turned = shift(qkv_parts[3], OTHER_SIDE, "rs_qkv_3")
    qkv_two = shift(qkv_parts[2], OTHER_SIDE, "rs_qkv_2")
    up_sum = [
        up_parts[0][n].astype(F32) + up_one[n].astype(F32) + (up_two, up_rest)[n // 2][n % 2].astype(F32)
        for n in range(4)
    ]
    up_low = [part.astype(LOW) for part in up_sum]
    up_z = [shift(up_low[n + 1], ALONG_Z[n], "rs_up_z") for n in range(2)]
    down_sum = z_sum(down_sum, down_z)
    own_part, mate_part = call(
        input_grad_kernel,
        [VMEM] * 6,
        [shape(shard_len, width, kind=F32), shape(shard_len, width)],
        [VMEM] * 2,
        [],
        (frames, mate_frames, own_grad, tied(mate_grad, *up_low), middle_grad, vectors),
        0,
        name="input_grad", limit=12,
    )
    turned, mate_part = joined(turned, mate_part)
    side = (qkv_parts[1].astype(F32) + turned.astype(F32)).astype(LOW)
    qkv_one = shift(side, SIDE, "rs_qkv_1")
    up_z, side_after = joined(up_z, side)
    up_z.append(shift(tied(up_low[3], side_after), ALONG_Z[2], "rs_up_z"))
    layer_out = call(
        finish_kernel,
        [SMEM] + [VMEM] * 3 + [HBM] * 8,
        [shape(shard_len, width, kind=F32)],
        [VMEM],
        [pltpu.VMEM((units, down_rows, width), LOW), pltpu.VMEM((width, ff), LOW), unit_sems],
        (tied(place, side_after), active, middle, vectors) + down_pieces,
        2 * shard_len * width * ff,
        name="finish",
    )[0]
    qkv_one, qkv_two, up_z, layer_out = joined(qkv_one, qkv_two, up_z, layer_out)
    qkv_sum = qkv_parts[0].astype(F32) + qkv_one.astype(F32) + qkv_two.astype(F32)
    qkv_z = z_sends(qkv_sum, "rs_qkv")
    mate_part = shift(tied(mate_part, qkv_sum), PACK, "grad_pack")
    up_sum = z_sum(tied(up_sum[:1], qkv_sum), up_z)
    up_sum, qkv_z = joined(up_sum, qkv_z)
    last = call(
        last_kernel,
        [VMEM] * 6,
        [
            shape(qkv_rows, width, kind=F32), shape(1, 2 * each, kind=F32), shape(1, up_rows, kind=F32),
            shape(H, BUCKETS, kind=F32), shape(shard_len, width, kind=F32),
        ]
        + [shape(1, each, kind=F32)] * NARROW,
        [VMEM] * (5 + NARROW),
        [],
        (qkv_sum[0],) + tuple(qkv_z) + (own_part, mate_part),
        0,
        name="last", limit=8,
    )
    qkv_grad, qv_bias_grad, up_bias_sum, table, frames_grad = last[:5]
    pieces = [piece.reshape(each) for piece in last[5:]]

    down_grad = jnp.concatenate(
        [down_sum[fold * each : (fold + 1) * each] for fold in range(folds)], axis=1
    )
    return (
        layer_out, frames_grad, qkv_grad.T, qv_bias_grad.reshape(2 * each),
        up_sum[up_rows : up_rows + each].T, pieces[4], up_sum[:up_rows].T, up_bias_sum.reshape(up_rows),
        down_grad.T, pieces[5], pieces[0], pieces[1], pieces[2], pieces[3], table.T,
    )


def paired(mesh):
    return mesh.shape["blk"] == 2 and mesh.shape["dp"] == 16


def solution(mesh):
    placed = (
        P(("dp", "blk"), None),
        P(("dp", "blk"), None),
        P("dp", None),
        P(("dp", "blk")),
        P(None, ("dp", "blk")),
        P(("dp", "blk")),
        P(None, ("dp", "blk")),
        P(("dp", "blk")),
        P(None, ("dp", "blk")),
        P(("dp", "blk")),
        P(None, ("dp", "blk")),
        P(("dp", "blk")),
        P(("dp", "blk")),
        P(("dp", "blk")),
        P(("dp", "blk")),
        P(("dp", "blk")),
        P(),
    )
    return jax.shard_map(
        paired_body if paired(mesh) else body,
        mesh=mesh,
        in_specs=placed,
        out_specs=(
            P(("dp", "blk"), None),
            P(("dp", "blk"), None),
            P(None, ("dp", "blk")),
            P(("dp", "blk")),
            P(None, ("dp", "blk")),
            P(("dp", "blk")),
            P(None, ("dp", "blk")),
            P(("dp", "blk")),
            P(None, ("dp", "blk")),
            P(("dp", "blk")),
            P(("dp", "blk")),
            P(("dp", "blk")),
            P(("dp", "blk")),
            P(("dp", "blk")),
            P(),
        ),
        check_vma=False,
    )
```

```python
import math

import jax
import jax.numpy as jnp
import numpy as np
from jax import lax
from jax.experimental import pallas as pl
from jax.experimental.pallas import tpu as pltpu
from jax.sharding import PartitionSpec as P

H = 12
HD = 64
MAXREL = 160
BLOCK = 256
BUCKETS = 321


EPSILON = 1e-05
MASKED = -2e30
START_PEAK = -1e30
HIGHEST = lax.Precision.HIGHEST


def from_behind(block, axis, distance):
    devices = range(lax.axis_size(axis))
    route = [((i - distance) % len(devices), i) for i in devices]
    return lax.ppermute(block, axis, route)


def layer_norm(values, gain_vec, shift_vec):
    center = values - jnp.mean(values, axis=-1, keepdims=True)
    inv_std = lax.rsqrt(jnp.mean(center * center, axis=-1, keepdims=True) + EPSILON)
    normed = center * inv_std
    return (normed * gain_vec + shift_vec, normed, inv_std)


def norm_back(gradient, normed, inv_std, gain_vec):
    scaled = gradient * gain_vec
    inner = (
        scaled
        - jnp.mean(scaled, axis=-1, keepdims=True)
        - normed * jnp.mean(scaled * normed, axis=-1, keepdims=True)
    )
    return (inner * inv_std, jnp.sum(gradient * normed, axis=0), jnp.sum(gradient, axis=0))


def gelu_parts(values):
    normal_cdf = 0.5 * (1.0 + lax.erf(values * 0.7071067811865476))
    density = jnp.exp(-0.5 * values * values) * 0.3989422804014327
    return (values * normal_cdf, normal_cdf + values * density)


def doc_numbers(seq_ends, positions):
    return jnp.sum((positions[:, None] >= seq_ends[None, :]).astype(jnp.int32), axis=1)


def pair_logits(
    query_block, key_block, query_pos, key_pos, query_doc, key_doc, key_live, table_heads
):
    block_len = query_block.shape[0]
    raw = jnp.einsum(
        "qhd,khd->hqk",
        query_block.reshape(block_len, H, HD),
        key_block.reshape(-1, H, HD),
        preferred_element_type=jnp.float32,
    )
    relative = jnp.clip(key_pos[None, :] - query_pos[:, None], -MAXREL, MAXREL) + MAXREL
    bias = jnp.take(table_heads, relative, axis=1)
    allowed = (query_doc[:, None] == key_doc[None, :]) & (
        (key_live[None, :] > 0.5) | (query_pos[:, None] == key_pos[None, :])
    )
    return jnp.where(allowed[None], raw * (1.0 / math.sqrt(HD)) + bias, MASKED)


def diagonal_sums(gradient, offset):
    heads, block_len, _ = gradient.shape
    flipped = gradient[:, ::-1, :]
    padded = jnp.pad(flipped, ((0, 0), (0, 0), (0, block_len)))
    sheared = padded.reshape(heads, 2 * block_len * block_len)[:, : block_len * (2 * block_len - 1)]
    sheared = sheared.reshape(heads, block_len, 2 * block_len - 1)
    diag_sums = jnp.sum(sheared, axis=1)
    distance = offset + jnp.arange(2 * block_len - 1, dtype=jnp.int32) - (block_len - 1)
    bucket = jnp.clip(distance, -MAXREL, MAXREL) + MAXREL
    onehot = (bucket[:, None] == jnp.arange(BUCKETS, dtype=jnp.int32)[None, :]).astype(jnp.float32)
    return jnp.dot(diag_sums, onehot, precision=HIGHEST)


def body(
    frames,
    cotangent,
    seq_lengths,
    key_mask,
    qkv_weight,
    query_value_bias,
    out_weight,
    out_bias,
    up_weight,
    up_bias,
    down_weight,
    down_bias,
    first_gain,
    first_shift,
    second_gain,
    second_shift,
    rel_bias,
):
    cycle_size = lax.axis_size("blk")
    cycle_place = lax.axis_index("blk")
    shard_len = frames.shape[0]
    width = frames.shape[1]
    block_count = shard_len // BLOCK
    score_scale = 1.0 / math.sqrt(HD)
    seq_ends = jnp.cumsum(seq_lengths[0])
    local_pos = jnp.arange(shard_len, dtype=jnp.int32)
    positions = cycle_place * shard_len + local_pos
    own_docs = doc_numbers(seq_ends, positions)
    table_heads = rel_bias.astype(jnp.float32).T

    def blocked(array):
        return array.reshape((block_count, BLOCK) + array.shape[1:])

    def key_meta(turn):
        source = (cycle_place - turn) % cycle_size
        key_pos = source * shard_len + local_pos
        return (key_pos, doc_numbers(seq_ends, key_pos))

    gathered = (
        lax.all_gather(qkv_weight, ("dp", "blk"), axis=1, tiled=True),
        lax.all_gather(query_value_bias, ("dp", "blk"), axis=0, tiled=True),
        lax.all_gather(out_weight, ("dp", "blk"), axis=1, tiled=True),
        lax.all_gather(out_bias, ("dp", "blk"), axis=0, tiled=True),
        lax.all_gather(up_weight, ("dp", "blk"), axis=1, tiled=True),
        lax.all_gather(up_bias, ("dp", "blk"), axis=0, tiled=True),
        lax.all_gather(down_weight, ("dp", "blk"), axis=1, tiled=True),
        lax.all_gather(down_bias, ("dp", "blk"), axis=0, tiled=True),
        lax.all_gather(first_gain, ("dp", "blk"), axis=0, tiled=True),
        lax.all_gather(first_shift, ("dp", "blk"), axis=0, tiled=True),
        lax.all_gather(second_gain, ("dp", "blk"), axis=0, tiled=True),
        lax.all_gather(second_shift, ("dp", "blk"), axis=0, tiled=True),
    )
    (
        qkv_full,
        qv_bias_full,
        out_full,
        out_bias_full,
        up_full,
        up_bias_full,
        down_full,
        down_bias_full,
        gain_one,
        shift_one,
        gain_two,
        shift_two,
    ) = gathered
    frames_wide = frames.astype(jnp.float32)
    first_out, first_normed, first_inv = layer_norm(
        frames_wide, gain_one.astype(jnp.float32), shift_one.astype(jnp.float32)
    )
    first_low = first_out.astype(jnp.bfloat16)
    projected = jnp.dot(first_low, qkv_full, preferred_element_type=jnp.float32)
    bias_vec = qv_bias_full.astype(jnp.float32)
    queries = (projected[:, :width] + bias_vec[:width]).astype(jnp.bfloat16)
    key_rows = projected[:, width : 2 * width].astype(jnp.bfloat16)
    value_rows = (projected[:, 2 * width :] + bias_vec[width:]).astype(jnp.bfloat16)
    live_rows = key_mask.astype(jnp.bfloat16)
    query_blocks = (blocked(queries), blocked(positions), blocked(own_docs))

    def forward_hop(turn, online_state, key_part, value_part, live_part):
        key_pos, key_doc = key_meta(turn)
        key_items = (
            blocked(key_part),
            blocked(value_part),
            blocked(key_pos),
            blocked(key_doc),
            blocked(live_part),
        )

        def forward_per_query(query_items):
            query_block, query_pos, query_doc, row_peak, row_total, accum = query_items

            def online(carried, key_block_items):
                row_peak, row_total, accum = carried
                key_block, value_block, key_bpos, key_bdoc, key_blive = key_block_items
                logits = pair_logits(
                    query_block,
                    key_block,
                    query_pos,
                    key_bpos,
                    query_doc,
                    key_bdoc,
                    key_blive,
                    table_heads,
                )
                new_peak = jnp.maximum(row_peak, jnp.max(logits, axis=2))
                decay = jnp.exp(row_peak - new_peak)
                weights = jnp.exp(logits - new_peak[:, :, None])
                row_total = row_total * decay + jnp.sum(weights, axis=2)
                accum = accum * decay.T[:, :, None] + jnp.einsum(
                    "hqk,khd->qhd",
                    weights.astype(jnp.bfloat16),
                    value_block.reshape(-1, H, HD),
                    preferred_element_type=jnp.float32,
                )
                return ((new_peak, row_total, accum), None)

            result, unused = lax.scan(online, (row_peak, row_total, accum), key_items)
            return result

        return lax.map(forward_per_query, query_blocks + online_state)

    def cycle_turn(turn, carried):
        online_state, key_part, value_part, live_part = carried
        online_state = forward_hop(turn, online_state, key_part, value_part, live_part)
        key_part, value_part, live_part = from_behind((key_part, value_part, live_part), "blk", 1)
        return (online_state, key_part, value_part, live_part)

    start_state = (
        jnp.full((block_count, H, BLOCK), START_PEAK, jnp.float32),
        jnp.zeros((block_count, H, BLOCK), jnp.float32),
        jnp.zeros((block_count, BLOCK, H, HD), jnp.float32),
    )
    carried = lax.fori_loop(
        0, cycle_size - 1, cycle_turn, (start_state, key_rows, value_rows, live_rows)
    )
    row_peak, row_total, accum = forward_hop(
        cycle_size - 1, carried[0], carried[1], carried[2], carried[3]
    )
    mixed = accum / jnp.transpose(row_total, (0, 2, 1))[:, :, :, None]
    mixed_flat = mixed.reshape(shard_len, width)
    context = mixed_flat.astype(jnp.bfloat16)
    branch = jnp.dot(context, out_full, preferred_element_type=jnp.float32) + out_bias_full.astype(
        jnp.float32
    )
    middle = frames_wide + branch
    second_out, second_normed, second_inv = layer_norm(
        middle, gain_two.astype(jnp.float32), shift_two.astype(jnp.float32)
    )
    second_low = second_out.astype(jnp.bfloat16)
    hidden = jnp.dot(second_low, up_full, preferred_element_type=jnp.float32) + up_bias_full.astype(
        jnp.float32
    )
    active, slope = gelu_parts(hidden)
    active_low = active.astype(jnp.bfloat16)
    layer_out = (
        middle
        + jnp.dot(active_low, down_full, preferred_element_type=jnp.float32)
        + down_bias_full.astype(jnp.float32)
    )
    weights_back = (
        lax.all_gather(qkv_weight, ("dp", "blk"), axis=1, tiled=True),
        lax.all_gather(query_value_bias, ("dp", "blk"), axis=0, tiled=True),
        lax.all_gather(out_weight, ("dp", "blk"), axis=1, tiled=True),
        lax.all_gather(out_bias, ("dp", "blk"), axis=0, tiled=True),
        lax.all_gather(up_weight, ("dp", "blk"), axis=1, tiled=True),
        lax.all_gather(up_bias, ("dp", "blk"), axis=0, tiled=True),
        lax.all_gather(down_weight, ("dp", "blk"), axis=1, tiled=True),
        lax.all_gather(down_bias, ("dp", "blk"), axis=0, tiled=True),
        lax.all_gather(first_gain, ("dp", "blk"), axis=0, tiled=True),
        lax.all_gather(first_shift, ("dp", "blk"), axis=0, tiled=True),
        lax.all_gather(second_gain, ("dp", "blk"), axis=0, tiled=True),
        lax.all_gather(second_shift, ("dp", "blk"), axis=0, tiled=True),
    )
    qkv_back = weights_back[0]
    out_back = weights_back[2]
    up_back = weights_back[4]
    down_back = weights_back[6]
    gain_one_back = weights_back[8].astype(jnp.float32)
    gain_two_back = weights_back[10].astype(jnp.float32)
    grad_wide = cotangent.astype(jnp.float32)
    down_grad = jnp.einsum("tf,td->fd", active_low, cotangent, preferred_element_type=jnp.float32)
    down_bias_grad = jnp.sum(grad_wide, axis=0)
    active_grad = jnp.einsum("td,fd->tf", cotangent, down_back, preferred_element_type=jnp.float32)
    hidden_low = (active_grad * slope).astype(jnp.bfloat16)
    up_grad = jnp.einsum("td,tf->df", second_low, hidden_low, preferred_element_type=jnp.float32)
    up_bias_grad = jnp.sum(hidden_low.astype(jnp.float32), axis=0)
    second_grad = jnp.einsum("tf,df->td", hidden_low, up_back, preferred_element_type=jnp.float32)
    middle_norm, gain_two_grad, shift_two_grad = norm_back(
        second_grad, second_normed, second_inv, gain_two_back
    )
    middle_grad = grad_wide + middle_norm
    branch_low = middle_grad.astype(jnp.bfloat16)
    out_grad = jnp.einsum("td,te->de", context, branch_low, preferred_element_type=jnp.float32)
    out_bias_grad = jnp.sum(branch_low.astype(jnp.float32), axis=0)
    context_low = jnp.einsum(
        "te,de->td", branch_low, out_back, preferred_element_type=jnp.float32
    ).astype(jnp.bfloat16)
    delta = jnp.sum(
        (context_low.astype(jnp.float32) * mixed_flat).reshape(shard_len, H, HD), axis=2
    )
    delta_blocks = jnp.transpose(blocked(delta), (0, 2, 1))
    query_back = (
        blocked(queries),
        blocked(context_low),
        blocked(positions),
        blocked(own_docs),
        row_peak,
        row_total,
        delta_blocks,
    )

    def backward_hop(
        turn, query_grad, table_grad, key_part, value_part, live_part, key_grad, value_grad
    ):
        key_pos, key_doc = key_meta(turn)

        def per_key(carried, key_block_items):
            query_grad, table_grad = carried
            key_block, value_block, key_bpos, key_bdoc, key_blive, key_bgrad, value_bgrad = (
                key_block_items
            )
            key_heads = key_block.reshape(-1, H, HD)
            value_heads = value_block.reshape(-1, H, HD)

            def per_per_query(inner, query_items):
                key_bgrad, value_bgrad, table_grad = inner
                (
                    query_block,
                    dout_block,
                    query_pos,
                    query_doc,
                    peak_block,
                    total_block,
                    delta_block,
                ) = query_items
                logits = pair_logits(
                    query_block,
                    key_block,
                    query_pos,
                    key_bpos,
                    query_doc,
                    key_bdoc,
                    key_blive,
                    table_heads,
                )
                attn_prob = jnp.exp(logits - peak_block[:, :, None]) / total_block[:, :, None]
                dout_heads = dout_block.reshape(-1, H, HD)
                prob_grad = jnp.einsum(
                    "qhd,khd->hqk", dout_heads, value_heads, preferred_element_type=jnp.float32
                )
                logit_grad = attn_prob * (prob_grad - delta_block[:, :, None])
                raw_low = (logit_grad * score_scale).astype(jnp.bfloat16)
                query_part = jnp.einsum(
                    "hqk,khd->qhd", raw_low, key_heads, preferred_element_type=jnp.float32
                ).reshape(-1, width)
                key_bgrad = key_bgrad + jnp.einsum(
                    "hqk,qhd->khd",
                    raw_low,
                    query_block.reshape(-1, H, HD),
                    preferred_element_type=jnp.float32,
                ).reshape(-1, width)
                value_bgrad = value_bgrad + jnp.einsum(
                    "hqk,qhd->khd",
                    attn_prob.astype(jnp.bfloat16),
                    dout_heads,
                    preferred_element_type=jnp.float32,
                ).reshape(-1, width)
                table_grad = table_grad + diagonal_sums(logit_grad, key_bpos[0] - query_pos[0])
                return ((key_bgrad, value_bgrad, table_grad), query_part)

            (key_bgrad, value_bgrad, table_grad), query_parts = lax.scan(
                per_per_query, (key_bgrad, value_bgrad, table_grad), query_back
            )
            return ((query_grad + query_parts, table_grad), (key_bgrad, value_bgrad))

        (query_grad, table_grad), (key_new, value_new) = lax.scan(
            per_key,
            (query_grad, table_grad),
            (
                blocked(key_part),
                blocked(value_part),
                blocked(key_pos),
                blocked(key_doc),
                blocked(live_part),
                blocked(key_grad),
                blocked(value_grad),
            ),
        )
        return (
            query_grad,
            table_grad,
            key_new.reshape(shard_len, width),
            value_new.reshape(shard_len, width),
        )

    def pass_grads(key_grad, value_grad):
        return (
            from_behind(key_grad.astype(jnp.bfloat16), "blk", 1).astype(key_grad.dtype),
            from_behind(value_grad.astype(jnp.bfloat16), "blk", 1).astype(value_grad.dtype),
        )

    def back_turn(turn, carried):
        query_grad, table_grad, key_part, value_part, live_part, key_grad, value_grad = carried
        query_grad, table_grad, key_grad, value_grad = backward_hop(
            turn, query_grad, table_grad, key_part, value_part, live_part, key_grad, value_grad
        )
        key_part, value_part, live_part = from_behind((key_part, value_part, live_part), "blk", 1)
        key_grad, value_grad = pass_grads(key_grad, value_grad)
        return (query_grad, table_grad, key_part, value_part, live_part, key_grad, value_grad)

    zero_rows = jnp.zeros((shard_len, width), jnp.float32)
    back_start = (
        jnp.zeros((block_count, BLOCK, width), jnp.float32),
        jnp.zeros((H, BUCKETS), jnp.float32),
        key_rows,
        value_rows,
        live_rows,
        zero_rows,
        zero_rows,
    )
    carried = lax.fori_loop(0, cycle_size - 1, back_turn, back_start)
    query_grad, table_grad, key_grad, value_grad = backward_hop(
        cycle_size - 1,
        carried[0],
        carried[1],
        carried[2],
        carried[3],
        carried[4],
        carried[5],
        carried[6],
    )
    key_grad, value_grad = pass_grads(key_grad, value_grad)
    query_low = query_grad.reshape(shard_len, width).astype(jnp.bfloat16)
    key_low = key_grad.astype(jnp.bfloat16)
    value_low = value_grad.astype(jnp.bfloat16)
    qkv_low = jnp.concatenate([query_low, key_low, value_low], axis=1)
    qkv_grad = jnp.einsum("td,te->de", first_low, qkv_low, preferred_element_type=jnp.float32)
    query_value_grad = jnp.concatenate(
        [
            jnp.sum(query_low.astype(jnp.float32), axis=0),
            jnp.sum(value_low.astype(jnp.float32), axis=0),
        ]
    )
    first_grad = jnp.einsum("te,de->td", qkv_low, qkv_back, preferred_element_type=jnp.float32)
    frames_norm, gain_one_grad, shift_one_grad = norm_back(
        first_grad, first_normed, first_inv, gain_one_back
    )
    frames_grad = middle_grad + frames_norm
    summed = (
        lax.psum_scatter(qkv_grad, ("dp", "blk"), scatter_dimension=1, tiled=True),
        lax.psum_scatter(query_value_grad, ("dp", "blk"), scatter_dimension=0, tiled=True),
        lax.psum_scatter(out_grad, ("dp", "blk"), scatter_dimension=1, tiled=True),
        lax.psum_scatter(out_bias_grad, ("dp", "blk"), scatter_dimension=0, tiled=True),
        lax.psum_scatter(up_grad, ("dp", "blk"), scatter_dimension=1, tiled=True),
        lax.psum_scatter(up_bias_grad, ("dp", "blk"), scatter_dimension=0, tiled=True),
        lax.psum_scatter(down_grad, ("dp", "blk"), scatter_dimension=1, tiled=True),
        lax.psum_scatter(down_bias_grad, ("dp", "blk"), scatter_dimension=0, tiled=True),
        lax.psum_scatter(gain_one_grad, ("dp", "blk"), scatter_dimension=0, tiled=True),
        lax.psum_scatter(shift_one_grad, ("dp", "blk"), scatter_dimension=0, tiled=True),
        lax.psum_scatter(gain_two_grad, ("dp", "blk"), scatter_dimension=0, tiled=True),
        lax.psum_scatter(shift_two_grad, ("dp", "blk"), scatter_dimension=0, tiled=True),
    )
    table_sum = lax.psum(table_grad, ("dp", "blk"))
    return (
        layer_out,
        frames_grad,
        summed[0],
        summed[1],
        summed[2],
        summed[3],
        summed[4],
        summed[5],
        summed[6],
        summed[7],
        summed[8],
        summed[9],
        summed[10],
        summed[11],
        table_sum.T,
    )


AXES = ("dp", "blk")
F32 = jnp.float32
LOW = jnp.bfloat16
LANES = 128
NARROW = 6
PAD = 8


def route(move):
    n_dp, n_blk = lax.axis_size("dp"), lax.axis_size("blk")
    pairs = []
    for d in range(n_dp):
        d_bits, b_bits = move[d % 2]
        for b in range(n_blk):
            pairs.append((d * n_blk + b, (d ^ d_bits) * n_blk + (b ^ b_bits)))
    return pairs


def shift(array, move, name="swap"):
    with jax.named_scope(name):
        return lax.ppermute(array, AXES, route(move))


CORE = ((1, 0), (1, 0))
SIDE = ((0, 1), (2, 0))
OTHER_SIDE = ((2, 0), (0, 1))
PACK = ((0, 1), (0, 1))
ALONG_Z = tuple(((4 * turn, 0), (4 * turn, 0)) for turn in (1, 2, 3))


def tied(value, *after):
    return lax.optimization_barrier((value,) + after)[0]


def joined(*groups):
    return lax.optimization_barrier(groups)


def twin(array, name="twin"):
    return shift(array, CORE, name)


def along_z(unit, name):
    return tuple(shift(unit, move, name + "_z") for move in ALONG_Z)


def z_sends(plane, name):
    low = plane.astype(LOW)
    return tuple(shift(low[n + 1], move, name + "_z") for n, move in enumerate(ALONG_Z))


def z_sum(plane, arrived):
    return plane[0] + sum(part.astype(F32) for part in arrived)


def unit_of(place, x_turn, y_turn, z_turn, c):
    x, y, z = place[0] ^ x_turn, place[1] ^ y_turn, place[2] ^ z_turn
    return ((z * 2 + y) * 2 + c) * 2 + x


def each_unit(place, visit):
    def step(z, _):
        for plane in range(2):
            c = place[3] if plane == 0 else 1 - place[3]
            for n, (x_turn, y_turn) in enumerate(((0, 0), (1 - c, c), (c, 1 - c), (1, 1))):
                visit(4 * plane + n, z, unit_of(place, x_turn, y_turn, z, c))
        return 0

    lax.fori_loop(0, 4, step, 0)


def take_columns(place, array, pair, taken, top):
    for c in range(2):

        @pl.when(place[3] == c)
        def _():
            taken[top : top + array.shape[0], :] = jnp.concatenate(
                [
                    array[:, (2 * n + c) * pair : (2 * n + c + 1) * pair]
                    for n in range(array.shape[1] // (2 * pair))
                ],
                axis=1,
            )


def give_units(place, stage, parts):
    c = place[3]
    for part, (x_turn, y_turn) in zip(parts, ((0, 0), (1 - c, c), (c, 1 - c), (1, 1))):
        halves = part if isinstance(part, tuple) else (part,)
        for half, ref in enumerate(halves):
            start = half * ref.shape[0]

            def give(turn, _, ref=ref, start=start, x_turn=x_turn, y_turn=y_turn):
                unit = ((place[2] ^ (start + turn)) * 2 + (place[1] ^ y_turn)) * 2 + (place[0] ^ x_turn)
                ref[turn] = stage[unit].astype(LOW)
                return 0

            lax.fori_loop(0, ref.shape[0], give, 0)


def part_shapes(rows, width):
    return [jax.ShapeDtypeStruct((4, rows, width), LOW)] * 4


def dot_nn(a, b):
    return lax.dot_general(a, b, (((1,), (0,)), ((), ())), preferred_element_type=F32)


def dot_nt(a, b):
    return lax.dot_general(a, b, (((1,), (1,)), ((), ())), preferred_element_type=F32)


def dot_tn(a, b):
    return lax.dot_general(a, b, (((0,), (0,)), ((), ())), preferred_element_type=F32)


HBM = pl.BlockSpec(memory_space=pltpu.HBM)
SMEM = pl.BlockSpec(memory_space=pltpu.SMEM)
VMEM = pl.BlockSpec(memory_space=pltpu.VMEM)


def call(kernel, in_specs, outs, out_specs, scratch, args, flops, limit=56, **kwargs):
    moved = sum(math.prod(a.shape) * a.dtype.itemsize for a in list(args) + list(outs))
    return pl.pallas_call(
        kernel,
        out_shape=outs,
        in_specs=in_specs,
        out_specs=out_specs,
        scratch_shapes=scratch,
        compiler_params=pltpu.CompilerParams(vmem_limit_bytes=limit * 1024 * 1024),
        cost_estimate=pl.CostEstimate(flops=flops, bytes_accessed=moved, transcendentals=0),
        **kwargs,
    )(*args)


def spread_tables(units, width, lanes):
    tables = []
    for n in (width // units, 2 * width // units, 4 * width // units):
        lane = lanes[None, : units * n]
        row = jnp.arange(units + LANES, dtype=jnp.int32)[:, None]
        tables.append(
            jnp.where(row < units, lane // n == row, lane % n == row - units).astype(F32).astype(LOW)
        )
    return tables


def project_kernel(
    place, own, other, p0, p1, p2, p3, p4, p5, p6, p7, wide_one, wide_two, wide_four,
    first, queries, keys, values, vectors, up_bias, mate_live, weight_out, stage, small, weight, sems,
):
    units = stage.shape[0]
    width = own.shape[1]
    rows = stage.shape[1] - PAD
    shard_len = own.shape[0]
    pieces = (p0, p1, p2, p3, p4, p5, p6, p7)

    def fill(array, z, unit):
        stage[unit] = pieces[array][z]

    each_unit(place, fill)

    def normed(frames):
        wide = frames.astype(F32)
        center = wide - jnp.mean(wide, axis=1, keepdims=True)
        return center * lax.rsqrt(jnp.mean(center * center, axis=1, keepdims=True) + EPSILON)

    own_normed, mate_normed = normed(own[...]), normed(other[...])
    for unit in range(units):
        top = stage[unit, rows : rows + PAD, :].astype(F32)
        small[0, unit : unit + 1, :] = top[0:1]
        small[1, unit : unit + 1, :] = top[1:2]

    mate = unit_of(place, 1, 0, 0, place[3])
    mate_live[...] = stage[mate, rows : rows + PAD, : mate_live.shape[1]].astype(F32)

    def spread(row, slot, table):
        held = small[row, :, slot * LANES : (slot + 1) * LANES].astype(LOW)
        laid = dot_nn(held, table[units:, :]) * table[:units, :].astype(F32)
        return jnp.sum(laid, axis=0, keepdims=True)

    for n in range(NARROW):
        vectors[n : n + 1, :] = spread(0, n, wide_one)
    qv_bias = spread(1, 0, wide_two)
    up_bias[...] = jnp.broadcast_to(spread(1, 1, wide_four), up_bias.shape)
    vectors[NARROW : NARROW + 1, :] = qv_bias[:, :width]
    vectors[NARROW + 1 : NARROW + 2, :] = qv_bias[:, width:]

    def join(pair, _):
        both = jnp.concatenate(
            [stage[2 * pair, :rows, :].astype(F32), stage[2 * pair + 1, :rows, :].astype(F32)], axis=0
        )
        weight[pl.ds(pl.multiple_of(2 * rows * pair, 2 * rows), 2 * rows), :] = both.astype(LOW)
        return 0

    lax.fori_loop(0, units // 2, join, 0)
    copy = pltpu.make_async_copy(weight, weight_out, sems.at[0])
    copy.start()
    gain, offset = vectors[0:1, :], vectors[1:2, :]
    x = place[0]
    own_at = pl.multiple_of(x * shard_len, shard_len)
    mate_at = pl.multiple_of((1 - x) * shard_len, shard_len)
    first[pl.ds(own_at, shard_len), :] = (own_normed * gain + offset).astype(LOW)
    first[pl.ds(mate_at, shard_len), :] = (mate_normed * gain + offset).astype(LOW)
    mine = first[pl.ds(own_at, shard_len), :]
    queries[...] = (dot_nt(mine, weight[:width, :]) + vectors[NARROW : NARROW + 1, :]).astype(LOW)
    keys[...] = dot_nt(first[...], weight[width : 2 * width, :]).astype(LOW)
    values[...] = (
        dot_nt(first[...], weight[2 * width :, :]) + vectors[NARROW + 1 : NARROW + 2, :]
    ).astype(LOW)
    copy.wait()


def half_mask(shape, head):
    return (lax.broadcasted_iota(jnp.int32, shape, 1) // HD) == head


def bias_kernel(curve, bias):
    heads, block_len, span = bias.shape

    def shear(head, _):
        bias[head] = pltpu.roll(
            jnp.broadcast_to(curve[pl.ds(head, 1), :], (block_len, block_len + span)),
            span + 1, 1, stride=1, stride_axis=0,
        )[:, :span].astype(LOW)
        return 0

    lax.fori_loop(0, heads, shear, 0)


def attend_kernel(
    place, lengths, queries, keys, values, bias, own_live, mate_live, probs, mixed, hidden_pairs
):
    block_len, span = hidden_pairs.shape

    @pl.when(pl.program_id(0) == 0)
    def _():
        start = place[0] * block_len
        key_pos = lax.broadcasted_iota(jnp.int32, (1, span), 1)
        query_pos = lax.broadcasted_iota(jnp.int32, (block_len, 1), 0) + start
        key_doc, query_doc = jnp.zeros_like(key_pos), jnp.zeros_like(query_pos)
        end = 0
        for n in range(lengths.shape[1]):
            end = end + lengths[0, n]
            key_doc = key_doc + (key_pos >= end).astype(jnp.int32)
            query_doc = query_doc + (query_pos >= end).astype(jnp.int32)
        one, two = own_live[...].astype(F32), mate_live[2:3, :]
        live = jnp.where(
            place[0] == 0, jnp.concatenate([one, two], axis=1), jnp.concatenate([two, one], axis=1)
        )
        allowed = (query_doc == key_doc) & ((live > 0.5) | (query_pos == key_pos))
        hidden_pairs[...] = jnp.where(allowed, 0.0, MASKED)

    for pair in range(queries.shape[1] // (2 * HD)):
        lane = slice(2 * HD * pair, 2 * HD * (pair + 1))
        q, k, v = queries[:, lane], keys[:, lane], values[:, lane]
        total = jnp.zeros(q.shape, F32)
        for head in range(2):
            n = 2 * pair + head
            q_head = jnp.where(half_mask(q.shape, head), q, 0) * (1.0 / math.sqrt(HD))
            logits = dot_nt(q_head.astype(LOW), k) + bias[n].astype(F32) + hidden_pairs[...]
            weights = jnp.exp(logits - jnp.max(logits, axis=1, keepdims=True))
            prob = (weights * (1.0 / jnp.sum(weights, axis=1, keepdims=True))).astype(LOW)
            probs[n] = prob
            total = total + dot_nn(prob, jnp.where(half_mask(v.shape, head), v, 0))
        mixed[:, lane] = total


def join_units(kept, out):
    units = kept.shape[0]
    each = out.shape[0] // units

    def join(pair, _):
        both = jnp.concatenate(
            [kept[2 * pair].astype(F32)[:each], kept[2 * pair + 1].astype(F32)[:each]], axis=0
        )
        out[pl.ds(pl.multiple_of(2 * each * pair, 2 * each), 2 * each), :] = both.astype(LOW)
        return 0

    lax.fori_loop(0, units // 2, join, 0)


def expand_kernel(
    place, frames, mixed, vectors, up_bias, p0, p1, p2, p3, p4, p5, p6, p7,
    middle, second, context, active, slope, up, kept, out,
):
    width = frames.shape[1]
    pieces = (p0, p1, p2, p3, p4, p5, p6, p7)
    rows = p0.shape[1] - kept.shape[1]

    def fill(array, z, unit):
        kept[unit] = pieces[array][z, rows:]
        up[pl.ds(pl.multiple_of(unit * rows, rows), rows), :] = pieces[array][z, :rows]

    each_unit(place, fill)
    context[...] = mixed[...].astype(LOW)
    join_units(kept, out)
    mid = frames[...].astype(F32) + (dot_nt(context[...], out[...]) + vectors[4:5, :])
    middle[...] = mid
    center = mid - jnp.mean(mid, axis=1, keepdims=True)
    normed = center * lax.rsqrt(jnp.mean(center * center, axis=1, keepdims=True) + EPSILON)
    second[...] = (normed * vectors[2:3, :] + vectors[3:4, :]).astype(LOW)
    for n in range(up.shape[0] // width):
        at = slice(n * width, (n + 1) * width)
        hidden = dot_nt(second[...], up[at, :]) + up_bias[0:1, at]
        cdf = 0.5 * (1.0 + lax.erf(hidden * 0.7071067811865476))
        density = jnp.exp(-0.5 * hidden * hidden) * 0.3989422804014327
        active[:, at] = (hidden * cdf).astype(LOW)
        slope[:, at] = cdf + hidden * density


def down_grad_kernel(
    place, active, active_twin, cotangent, cotangent_twin, o0, o1, o2, o3, bias_grad, taken, wide,
):
    units, rows, width = wide.shape
    each = width // (2 * units)
    bias_grad[...] = jnp.broadcast_to(
        jnp.sum(cotangent[...].astype(F32), axis=0, keepdims=True), bias_grad.shape
    )

    shard_len = cotangent.shape[0]
    take_columns(place, cotangent, 2 * each, taken, 0)
    take_columns(place, cotangent_twin, 2 * each, taken, shard_len)
    dy, dy_twin = taken[:shard_len, :], taken[shard_len:, :]
    for fold in range(rows // each):
        at = slice(fold * width, (fold + 1) * width)
        grad = dot_tn(dy, active[:, at]) + dot_tn(dy_twin, active_twin[:, at])
        for unit in range(units):
            wide[unit, fold * each : (fold + 1) * each, :] = grad[unit * each : (unit + 1) * each]
    give_units(place, wide, (o0, o1, o2, o3))


def unfold_units(stage, down):
    units, rows, width = stage.shape
    each = down.shape[0] // units

    def unfold(pair, _):
        one, two = stage[2 * pair].astype(F32), stage[2 * pair + 1].astype(F32)
        at = pl.multiple_of(2 * each * pair, 2 * each)
        for fold in range(rows // each):
            both = jnp.concatenate(
                [one[fold * each : (fold + 1) * each], two[fold * each : (fold + 1) * each]], axis=0
            )
            down[pl.ds(at, 2 * each), fold * width : (fold + 1) * width] = both.astype(LOW)
        return 0

    lax.fori_loop(0, units // 2, unfold, 0)


def back_kernel(
    place, cotangent, slope, middle, vectors, p0, p1, p2, p3, p4, p5, p6, p7, u0, u1, u2, u3, u4, u5, u6, u7,
    middle_grad, context_grad, vector_grads, branch_grad, up_bias_grad, hidden_grad,
    stage, down, up, kept, out,
):
    width = cotangent.shape[1]
    down_pieces, up_pieces = (p0, p1, p2, p3, p4, p5, p6, p7), (u0, u1, u2, u3, u4, u5, u6, u7)
    rows = u0.shape[1] - kept.shape[1]

    def fill(array, z, unit):
        stage[unit] = down_pieces[array][z]
        kept[unit] = up_pieces[array][z, rows:]
        up[pl.ds(pl.multiple_of(unit * rows, rows), rows), :] = up_pieces[array][z, :rows]

    each_unit(place, fill)
    unfold_units(stage, down)
    dy = cotangent[...]
    for n in range(hidden_grad.shape[1] // width):
        at = slice(n * width, (n + 1) * width)
        grad = (dot_nn(dy, down[:, at]) * slope[:, at]).astype(LOW)
        hidden_grad[:, at] = grad
        up_bias_grad[:, at] = jnp.broadcast_to(
            jnp.sum(grad.astype(F32), axis=0, keepdims=True), (up_bias_grad.shape[0], width)
        )
    join_units(kept, out)
    second_grad = dot_nn(hidden_grad[...], up[...])
    mid = middle[...]
    center = mid - jnp.mean(mid, axis=1, keepdims=True)
    inv_std = lax.rsqrt(jnp.mean(center * center, axis=1, keepdims=True) + EPSILON)
    normed = center * inv_std
    scaled = second_grad * vectors[2:3, :]
    inner = (
        scaled
        - jnp.mean(scaled, axis=1, keepdims=True)
        - normed * jnp.mean(scaled * normed, axis=1, keepdims=True)
    )
    mid_grad = cotangent[...].astype(F32) + inner * inv_std
    middle_grad[...] = mid_grad
    branch = mid_grad.astype(LOW)
    vector_grads[...] = jnp.concatenate(
        [
            jnp.sum(second_grad * normed, axis=0, keepdims=True),
            jnp.sum(second_grad, axis=0, keepdims=True),
            jnp.sum(branch.astype(F32), axis=0, keepdims=True),
            jnp.zeros((5, width), F32),
        ],
        axis=0,
    )
    branch_grad[...] = branch
    context_grad[...] = dot_nn(branch, out[...]).astype(LOW)


def up_grad_kernel(
    place, hidden, hidden_twin, second, second_twin, branch, branch_twin, context, context_twin,
    o0, o1, o2, o3, o4, taken, taken_branch, stage,
):
    units, rows, width = stage.shape
    each = width // (2 * units)
    up_rows = hidden.shape[1] // (2 * units)

    shard_len = second.shape[0]
    take_columns(place, branch, 2 * each, taken_branch, 0)
    take_columns(place, branch_twin, 2 * each, taken_branch, shard_len)
    take_columns(place, hidden, 2 * up_rows, taken, 0)
    take_columns(place, hidden_twin, 2 * up_rows, taken, shard_len)
    out_grad = dot_tn(taken_branch[:shard_len, :], context[...]) + dot_tn(
        taken_branch[shard_len:, :], context_twin[...]
    )
    blank = jnp.zeros((rows - up_rows - each, width), F32)
    quarter = units // 4
    for z in range(4):
        at = slice(z * quarter * up_rows, (z + 1) * quarter * up_rows)
        grad = dot_tn(taken[:shard_len, at], second[...]) + dot_tn(taken[shard_len:, at], second_twin[...])
        for n in range(quarter):
            unit = z * quarter + n
            stage[unit] = jnp.concatenate(
                [
                    grad[n * up_rows : (n + 1) * up_rows],
                    out_grad[unit * each : (unit + 1) * each],
                    blank,
                ],
                axis=0,
            ).astype(LOW)
    give_units(place, stage, (o0, o1, (o2, o3), o4))


def rows_left(each):
    return -each % 16


def finish_kernel(
    place, active, middle, vectors, p0, p1, p2, p3, p4, p5, p6, p7, layer_out, stage, down
):
    pieces = (p0, p1, p2, p3, p4, p5, p6, p7)

    def fill(array, z, unit):
        stage[unit] = pieces[array][z]

    each_unit(place, fill)
    unfold_units(stage, down)
    layer_out[...] = middle[...] + dot_nt(active[...], down[...]) + vectors[5:6, :]


def attend_back_kernel(
    place, queries, keys, values, context_grad, mixed, probs, grads, diagonals
):
    q, k, v, dout = queries[...], keys[...], values[...], context_grad[...]
    block_len, span = probs.shape[1:]
    weighted = dout.astype(F32) * mixed[...]
    row = lax.broadcasted_iota(jnp.int32, (block_len, block_len), 0)
    lane = lax.broadcasted_iota(jnp.int32, (block_len, block_len), 1)
    turn = (row + lane == block_len - 1).astype(LOW)
    blank = jnp.zeros((block_len, block_len), F32)
    dq, dk, dv = jnp.zeros(q.shape, F32), jnp.zeros(k.shape, F32), jnp.zeros(v.shape, F32)
    for head in range(2):
        mine = half_mask(q.shape, head)
        dout_head = jnp.where(mine, dout, 0)
        delta = jnp.sum(jnp.where(mine, weighted, 0.0), axis=1, keepdims=True)
        prob = probs[head]
        grad = prob.astype(F32) * (dot_nt(dout_head, v) - delta)
        raw = (grad * (1.0 / math.sqrt(HD))).astype(LOW)
        dq = dq + dot_nn(raw, jnp.where(half_mask(k.shape, head), k, 0))
        dk = dk + dot_tn(raw, jnp.where(mine, q, 0))
        dv = dv + dot_tn(prob, dout_head)
        turned = jnp.concatenate([dot_nn(turn, raw), blank], axis=1)
        sheared = pltpu.roll(turned, 0, 1, stride=1, stride_axis=0)
        diagonals[pl.ds(2 * pl.program_id(0) + head, 1), :] = jnp.sum(sheared, axis=0, keepdims=True) * math.sqrt(HD)
    own_at = pl.multiple_of(place[0] * block_len, block_len)
    grads[0] = jnp.zeros(k.shape, LOW)
    grads[0, pl.ds(own_at, block_len), :] = dq.astype(LOW)
    grads[1] = dk.astype(LOW)
    grads[2] = dv.astype(LOW)


def total(array):
    return jnp.sum(array, axis=0, keepdims=True)


def norm_parts(frames):
    wide = frames.astype(F32)
    center = wide - jnp.mean(wide, axis=1, keepdims=True)
    inv_std = lax.rsqrt(jnp.mean(center * center, axis=1, keepdims=True) + EPSILON)
    return center * inv_std, inv_std


def first_grad_kernel(
    place, own_frames, mate_frames, grads, weight_in, diagonals, vector_grads, down_bias_grad, up_bias_grad,
    own_grad, mate_grad, small, weight, sems,
):
    copy = pltpu.make_async_copy(weight_in, weight, sems.at[0])
    copy.start()
    shard_len, width = own_frames.shape
    x = place[0]
    own_at = pl.multiple_of(x * shard_len, shard_len)
    mate_at = pl.multiple_of((1 - x) * shard_len, shard_len)
    own_normed, _ = norm_parts(own_frames[...])
    mate_normed, _ = norm_parts(mate_frames[...])
    dq = grads[0, pl.ds(own_at, shard_len), :]
    small[4:5, :] = vector_grads[2:3, :]
    small[2:4, :] = vector_grads[0:2, :]
    small[5:6, :] = down_bias_grad[0:1, :]
    small[6:7, :] = total(dq.astype(F32))
    small[7:8, :] = total(grads[2].astype(F32))
    for n in range(up_bias_grad.shape[1] // width):
        small[8 + n : 9 + n, :] = up_bias_grad[0:1, n * width : (n + 1) * width]
    small[12:, :] = diagonals[...]
    copy.wait()

    def from_keys(at):
        return dot_nn(grads[1, pl.ds(at, shard_len), :], weight[width : 2 * width, :]) + dot_nn(
            grads[2, pl.ds(at, shard_len), :], weight[2 * width :, :]
        )

    of_own = from_keys(own_at) + dot_nn(dq, weight[:width, :])
    of_mate = from_keys(mate_at)
    own_grad[...] = of_own
    mate_grad[...] = of_mate
    small[0:1, :] = total(of_own * own_normed) + total(of_mate * mate_normed)
    small[1:2, :] = total(of_own) + total(of_mate)


def qkv_grad_kernel(
    place, grads, grads_twin, first, first_twin, small_own, small_twin, wide_one, wide_two, wide_four,
    o0, o1, o2, o3, taken, sums, small, tables, stage,
):
    units, full, width = stage.shape
    rows = full - PAD
    span = first.shape[0]
    shard_len = span // 2
    x = place[0]
    summed = small_own[...] + small_twin[...]

    def fold(vector, table):
        kept = (vector * table[: 2 * units, :].astype(F32)).astype(LOW)
        return dot_nt(kept, table[2 * units :, :])

    for n in range(NARROW):
        small[0, :, n * LANES : (n + 1) * LANES] = fold(summed[n : n + 1, :], wide_one)
    small[1, :, :] = jnp.zeros((2 * units, width), F32)
    both = jnp.concatenate([summed[6:7, :], summed[7:8, :]], axis=1)
    small[1, :, :LANES] = fold(both, wide_two)
    four = jnp.concatenate([summed[8 + n : 9 + n, :] for n in range(4)], axis=1)
    small[1, :, LANES : 2 * LANES] = fold(four, wide_four)
    lanes = 3 * LANES
    distance = (
        lax.broadcasted_iota(jnp.int32, (shard_len + span, lanes), 0) - (shard_len - 1) - x * shard_len
    )
    bucket = jnp.clip(distance, -MAXREL, MAXREL) + MAXREL
    here = (bucket == lax.broadcasted_iota(jnp.int32, (shard_len + span, lanes), 1)).astype(F32).astype(LOW)
    diagonals = summed[12:, :]
    high = diagonals.astype(LOW)
    table = dot_nn(high, here) + dot_nn((diagonals - high.astype(F32)).astype(LOW), here)
    table = jnp.concatenate([table[: H // 2], table[H // 2 :]], axis=1)
    for n, array in enumerate((grads, grads_twin)):
        columns = jnp.concatenate([array[part] for part in range(3)], axis=1)
        take_columns(place, columns, 2 * rows, taken, n * span)
    sums[...] = dot_tn(taken[:span, :], first[...]) + dot_tn(taken[span:, :], first_twin[...])

    def pack(unit, _):
        at = 4 * (unit // 2) + 2 * place[3] + unit % 2
        stage[unit] = jnp.concatenate(
            [
                sums[pl.ds(pl.multiple_of(unit * rows, rows), rows), :],
                small[0, pl.ds(at, 1), :],
                small[1, pl.ds(at, 1), :],
                tables[...],
            ],
            axis=0,
        ).astype(LOW)
        return 0

    tables[...] = table
    lax.fori_loop(0, units, pack, 0)
    give_units(place, stage, (o0, o1, o2, o3))


def input_grad_kernel(frames, mate_frames, own_grad, mate_grad, middle_grad, vectors, own_part, mate_part):
    def through_norm(of_frames, grad):
        normed, inv_std = norm_parts(of_frames)
        scaled = grad * vectors[0:1, :]
        inner = (
            scaled
            - jnp.mean(scaled, axis=1, keepdims=True)
            - normed * jnp.mean(scaled * normed, axis=1, keepdims=True)
        )
        return inner * inv_std

    own_part[...] = middle_grad[...] + through_norm(frames[...], own_grad[...])
    mate_part[...] = through_norm(mate_frames[...], mate_grad[...]).astype(LOW)


def last_kernel(
    own, z1, z2, z3, own_part, mate_part, qkv, qv_bias, up_bias, table, frames_grad, n0, n1, n2, n3, n4, n5
):
    frames_grad[...] = own_part[...] + mate_part[...].astype(F32)
    rows = qkv.shape[0]
    total = own[...] + z1[...].astype(F32) + z2[...].astype(F32) + z3[...].astype(F32)
    qkv[...] = total[:rows]
    for n, narrow in enumerate((n0, n1, n2, n3, n4, n5)):
        narrow[...] = total[rows : rows + 1, n * LANES : n * LANES + narrow.shape[1]]
    qv_bias[...] = total[rows + 1 : rows + 2, : qv_bias.shape[1]]
    up_bias[...] = total[rows + 1 : rows + 2, LANES : LANES + up_bias.shape[1]]
    for half in range(2):
        at = 3 * LANES * half
        table[half * (H // 2) : (half + 1) * (H // 2), :] = total[rows + 2 : rows + PAD, at : at + BUCKETS]


def pack_kernel(
    live, qkv, out, up, down, first_gain, first_shift, second_gain, second_shift, out_bias,
    down_bias, qv_bias, up_bias, qkv_unit, up_unit, down_unit,
):
    each, width = out.shape

    def slots(vectors):
        parts = []
        for vector in vectors:
            wide = vector[...].astype(F32)
            parts += [wide, jnp.zeros((1, LANES - wide.shape[1]), F32)]
        left = width - LANES * len(vectors)
        if left:
            parts.append(jnp.zeros((1, left), F32))
        return jnp.concatenate(parts, axis=1)

    narrow = slots((first_gain, first_shift, second_gain, second_shift, out_bias, down_bias))
    wide = slots((qv_bias, up_bias))
    seen = live[...].astype(F32)
    seen = jnp.concatenate([seen, jnp.zeros((1, width - seen.shape[1]), F32)], axis=1)
    blank = jnp.zeros((PAD - 3, width), F32)
    qkv_unit[...] = jnp.concatenate([qkv[...].astype(F32), narrow, wide, seen, blank], axis=0).astype(LOW)
    blank = jnp.zeros((up_unit.shape[0] - up.shape[0] - each, width), F32)
    up_unit[...] = jnp.concatenate(
        [up[...].astype(F32), out[...].astype(F32), blank], axis=0
    ).astype(LOW)
    down_unit[...] = jnp.concatenate(
        [
            down[:, fold * width : (fold + 1) * width].astype(F32)
            for fold in range(down.shape[1] // width)
        ],
        axis=0,
    ).astype(LOW)


def paired_body(
    frames, cotangent, seq_lengths, key_mask, qkv_weight, query_value_bias, out_weight, out_bias,
    up_weight, up_bias, down_weight, down_bias, first_gain, first_shift, second_gain, second_shift,
    rel_bias,
):
    shard_len, width = frames.shape
    x = lax.axis_index("blk")
    d = lax.axis_index("dp")
    core = d % 2
    units = lax.axis_size("dp") * lax.axis_size("blk")
    span = shard_len * lax.axis_size("blk")
    place = jnp.stack([x, (d // 2) % 2, d // 4, core]).astype(jnp.int32)
    each = width // units
    ff = up_weight.shape[1] * units
    qkv_rows, up_rows = qkv_weight.shape[1], up_weight.shape[1]
    folds = ff // width
    down_rows = each * folds
    out_rows = each + rows_left(each)

    def shape(*dims, kind=LOW):
        return jax.ShapeDtypeStruct(dims, kind)

    def row(vector):
        return vector.reshape(1, vector.shape[0])

    packed = (
        row(key_mask), qkv_weight.T, out_weight.T, up_weight.T, down_weight.T, row(first_gain),
        row(first_shift), row(second_gain), row(second_shift), row(out_bias), row(down_bias),
        row(query_value_bias), row(up_bias),
    )
    qkv_unit, up_unit, down_unit = call(
        pack_kernel,
        [VMEM] * len(packed),
        [shape(qkv_rows + PAD, width), shape(up_rows + out_rows, width), shape(down_rows, width)],
        [VMEM] * 3,
        [],
        packed,
        0,
        name="pack",
    )
    def twins(pieces):
        return tuple(pieces) + tuple(twin(piece) for piece in pieces)

    distance = jnp.arange(span + shard_len, dtype=jnp.int32) - (shard_len - 1) - x * shard_len
    bucket = jnp.clip(distance, -MAXREL, MAXREL) + MAXREL
    bucket_lanes = 3 * LANES
    buckets = (bucket[:, None] == jnp.arange(bucket_lanes, dtype=jnp.int32)[None, :]).astype(LOW)
    curve = lax.dot_general(
        rel_bias, buckets[:, :BUCKETS], (((0,), (1,)), ((), ())), preferred_element_type=F32
    )
    bias = call(
        bias_kernel, [VMEM], [shape(H, shard_len, span)], [VMEM], [], (tied(curve, qkv_unit),), 0, name="bias"
    )[0]
    spreads = spread_tables(units, width, tied(jnp.arange(ff, dtype=jnp.int32), qkv_unit))
    cotangent_twin = twin(cotangent)
    qkv_z = along_z(qkv_unit, "qkv")
    mate_frames = shift(tied(frames, qkv_unit), PACK, "frames_pack")
    qkv_z, mate_frames, bias, place, spreads = joined(qkv_z, mate_frames, bias, place, spreads)
    qkv_own = jnp.stack((qkv_unit,) + qkv_z)
    qkv_side = shift(qkv_own, SIDE, "qkv_1")
    up_first = tied(up_unit, *qkv_z)
    up_z = [shift(up_first, move, "up_z") for move in ALONG_Z[:2]]
    qkv_side, up_z, cotangent_twin = joined(qkv_side, up_z, cotangent_twin)
    qkv_other = shift(qkv_own, OTHER_SIDE, "qkv_2")
    qkv_across = shift(qkv_side, OTHER_SIDE, "qkv_3")
    up_z.append(shift(tied(up_unit, qkv_side), ALONG_Z[2], "up_z"))
    up_z, qkv_other, qkv_across = joined(up_z, qkv_other, qkv_across)
    qkv_pieces = twins((qkv_own, qkv_side, qkv_other, qkv_across))
    up_own = jnp.stack([up_unit] + up_z)
    up_side = shift(up_own, SIDE, "up_1")
    down_first = tied(down_unit, up_own)
    down_z = [shift(down_first, move, "down_z") for move in ALONG_Z[:2]]

    unit_sems = pltpu.SemaphoreType.DMA((units,))
    first, queries, keys, values, vectors, up_bias_all, mate_live, weight = call(
        project_kernel,
        [SMEM] + [VMEM] * 13,
        [
            shape(span, width), shape(shard_len, width), shape(span, width), shape(span, width),
            shape(8, width, kind=F32), shape(8, ff, kind=F32), shape(PAD, shard_len, kind=F32),
            shape(3 * width, width),
        ],
        [VMEM] * 7 + [HBM],
        [
            pltpu.VMEM((units, qkv_rows + PAD, width), LOW), pltpu.VMEM((2, units, width), F32),
            pltpu.VMEM((3 * width, width), LOW), pltpu.SemaphoreType.DMA((1,)),
        ],
        (tied(place, up_own), frames, mate_frames) + qkv_pieces + tuple(spreads),
        2 * shard_len * width * 5 * width,
        name="project",
    )
    up_side, keys, down_z = joined(up_side, keys, down_z)
    up_other = shift(up_own, OTHER_SIDE, "up_2")
    up_across = shift(up_side, OTHER_SIDE, "up_3")
    down_z.append(shift(tied(down_unit, keys), ALONG_Z[2], "down_z"))
    pairs = H // 2
    pair_lanes = 2 * HD

    def lanes_of(rows, count=1):
        return pl.BlockSpec((rows, count * pair_lanes), lambda n: (0, n))

    def heads_of(*dims):
        return pl.BlockSpec(dims, lambda n: (n,) + (0,) * (len(dims) - 1))

    def whole(*dims):
        return pl.BlockSpec(dims, lambda n: (0,) * len(dims))

    probs, mixed = call(
        attend_kernel,
        [
            SMEM, SMEM, lanes_of(shard_len, 2), lanes_of(span, 2), lanes_of(span, 2),
            heads_of(4, shard_len, span), whole(1, shard_len), whole(PAD, shard_len),
        ],
        [shape(H, shard_len, span), shape(shard_len, width, kind=F32)],
        [heads_of(4, shard_len, span), lanes_of(shard_len, 2)],
        [pltpu.VMEM((shard_len, span), F32)],
        (
            tied(place, up_side), seq_lengths, queries, keys, values, bias, row(key_mask), mate_live,
        ),
        8 * shard_len * span * width,
        grid=(pairs // 2,),
        name="attend",
    )
    up_other, up_across, mixed, down_z = joined(up_other, up_across, mixed, down_z)
    up_pieces = twins((up_own, up_side, up_other, up_across))
    down_own = jnp.stack([down_unit] + down_z)
    down_side = shift(down_own, SIDE, "down_1")
    down_other = shift(down_own, OTHER_SIDE, "down_2")
    middle, second, context, active, slope = call(
        expand_kernel,
        [SMEM] + [VMEM] * 12,
        [
            shape(shard_len, width, kind=F32), shape(shard_len, width), shape(shard_len, width),
            shape(shard_len, ff), shape(shard_len, ff, kind=F32),
        ],
        [VMEM] * 5,
        [
            pltpu.VMEM((ff, width), LOW), pltpu.VMEM((units, out_rows, width), LOW),
            pltpu.VMEM((width, width), LOW),
        ],
        (tied(place, down_own), frames, mixed, vectors, up_bias_all) + up_pieces,
        2 * shard_len * width * (width + ff),
        name="expand", limit=36,
    )
    down_side, down_other, active = joined(down_side, down_other, active)
    down_across = shift(down_side, OTHER_SIDE, "down_3")
    active_twin, context_twin, second_twin = twin(active), twin(context), twin(second)
    first_twin = twin(first)
    down_parts = call(
        down_grad_kernel,
        [SMEM] + [VMEM] * 4,
        part_shapes(down_rows, width) + [shape(8, width, kind=F32)],
        [VMEM] * 5,
        [
            pltpu.VMEM((span, width // 2), LOW), pltpu.VMEM((units // 2, down_rows, width), F32),
        ],
        (tied(place, down_side), active, active_twin, cotangent, cotangent_twin),
        2 * shard_len * width * ff,
        name="down_grad", limit=24,
    )
    down_across, down_parts = joined(down_across, down_parts)
    down_bias_grad = down_parts[4]
    down_pieces = twins((down_own, down_side, down_other, down_across))
    turned = shift(down_parts[3], OTHER_SIDE, "rs_down_3")
    down_two = shift(down_parts[2], OTHER_SIDE, "rs_down_2")
    middle_grad, context_grad, vector_grads, branch_grad, up_bias_grad, hidden_grad = call(
        back_kernel,
        [SMEM] + [VMEM] * 20,
        [
            shape(shard_len, width, kind=F32), shape(shard_len, width), shape(8, width, kind=F32),
            shape(shard_len, width), shape(8, ff, kind=F32), shape(shard_len, ff),
        ],
        [VMEM] * 6,
        [
            pltpu.VMEM((units, down_rows, width), LOW), pltpu.VMEM((width, ff), LOW),
            pltpu.VMEM((ff, width), LOW), pltpu.VMEM((units, out_rows, width), LOW),
            pltpu.VMEM((width, width), LOW),
        ],
        (tied(place, down_parts[0]), cotangent, slope, middle, vectors) + down_pieces + up_pieces,
        2 * shard_len * width * (2 * ff + width),
        name="back", limit=48,
    )
    turned, down_two, hidden_grad, context_twin, second_twin, first_twin = joined(
        turned, down_two, hidden_grad, context_twin, second_twin, first_twin
    )
    side = (down_parts[1].astype(F32) + turned.astype(F32)).astype(LOW)
    down_one = shift(side, SIDE, "rs_down_1")
    hidden_twin = twin(hidden_grad)
    branch_twin = twin(branch_grad)
    down_sum = down_parts[0].astype(F32) + down_two.astype(F32)
    up_parts = call(
        up_grad_kernel,
        [SMEM] + [VMEM] * 8,
        [shape(n, up_rows + out_rows, width) for n in (4, 4, 2, 2, 4)],
        [VMEM] * 5,
        [
            pltpu.VMEM((span, ff // 2), LOW), pltpu.VMEM((span, width // 2), LOW),
            pltpu.VMEM((units // 2, up_rows + out_rows, width), LOW),
        ],
        (
            tied(place, down_sum, side), hidden_grad, hidden_twin, second, second_twin, branch_grad, branch_twin,
            context, context_twin,
        ),
        2 * shard_len * width * (ff + width),
        name="up_grad", limit=28,
    )
    down_one, up_parts = joined(down_one, up_parts)
    turned = shift(up_parts[4], OTHER_SIDE, "rs_up_3")
    up_two = shift(up_parts[2], OTHER_SIDE, "rs_up_2a")
    down_sum = down_sum + down_one.astype(F32)
    down_low = down_sum.astype(LOW)
    down_z = [shift(down_low[n + 1], ALONG_Z[n], "rs_down_z") for n in range(2)]
    grads, diagonals = call(
        attend_back_kernel,
        [
            SMEM, lanes_of(shard_len), lanes_of(span), lanes_of(span), lanes_of(shard_len), lanes_of(shard_len),
            heads_of(2, shard_len, span),
        ],
        [shape(3, span, width), shape(H, span + shard_len, kind=F32)],
        [pl.BlockSpec((3, span, pair_lanes), lambda n: (0, 0, n)), whole(H, span + shard_len)],
        [],
        (place, queries, keys, values, tied(context_grad, up_parts[0]), mixed, probs),
        16 * shard_len * span * width,
        grid=(pairs,),
        name="attend_back", limit=24,
    )
    turned, up_two, down_z, grads = joined(turned, up_two, down_z, grads)
    up_rest = shift(up_parts[3], OTHER_SIDE, "rs_up_2b")
    grads_twin = twin(grads)
    side = (up_parts[1].astype(F32) + turned.astype(F32)).astype(LOW)
    up_one = shift(side, SIDE, "rs_up_1")
    own_grad, mate_grad, small = call(
        first_grad_kernel,
        [SMEM] + [VMEM] * 3 + [HBM] + [VMEM] * 4,
        [
            shape(shard_len, width, kind=F32), shape(shard_len, width, kind=F32),
            shape(12 + H, width, kind=F32),
        ],
        [VMEM] * 3,
        [pltpu.VMEM((3 * width, width), LOW), pltpu.SemaphoreType.DMA((1,))],
        (
            tied(place, side), frames, mate_frames, grads, weight, diagonals, vector_grads,
            down_bias_grad, up_bias_grad,
        ),
        2 * shard_len * width * 5 * width,
        name="first_grad", limit=24,
    )
    grads_twin, small = joined(grads_twin, small)
    down_z.append(shift(tied(down_low[3], small), ALONG_Z[2], "rs_down_z"))
    small_twin = twin(small)
    qkv_parts = call(
        qkv_grad_kernel,
        [SMEM] + [VMEM] * 9,
        part_shapes(qkv_rows + PAD, width),
        [VMEM] * 4,
        [
            pltpu.VMEM((2 * span, 3 * width // 2), LOW), pltpu.VMEM((3 * width // 2, width), F32),
            pltpu.VMEM((2, units, width), F32), pltpu.VMEM((H // 2, width), F32),
            pltpu.VMEM((units // 2, qkv_rows + PAD, width), LOW),
        ],
        (place, grads, grads_twin, first, first_twin, small, small_twin) + tuple(spreads),
        2 * shard_len * width * 6 * width,
        name="qkv_grad", limit=28,
    )
    up_one, up_rest, down_z, qkv_parts = joined(up_one, up_rest, down_z, qkv_parts)
    turned = shift(qkv_parts[3], OTHER_SIDE, "rs_qkv_3")
    qkv_two = shift(qkv_parts[2], OTHER_SIDE, "rs_qkv_2")
    up_sum = [
        up_parts[0][n].astype(F32) + up_one[n].astype(F32) + (up_two, up_rest)[n // 2][n % 2].astype(F32)
        for n in range(4)
    ]
    up_low = [part.astype(LOW) for part in up_sum]
    up_z = [shift(up_low[n + 1], ALONG_Z[n], "rs_up_z") for n in range(2)]
    down_sum = z_sum(down_sum, down_z)
    own_part, mate_part = call(
        input_grad_kernel,
        [VMEM] * 6,
        [shape(shard_len, width, kind=F32), shape(shard_len, width)],
        [VMEM] * 2,
        [],
        (frames, mate_frames, own_grad, tied(mate_grad, *up_low), middle_grad, vectors),
        0,
        name="input_grad", limit=12,
    )
    turned, mate_part = joined(turned, mate_part)
    side = (qkv_parts[1].astype(F32) + turned.astype(F32)).astype(LOW)
    qkv_one = shift(side, SIDE, "rs_qkv_1")
    up_z, side_after = joined(up_z, side)
    up_z.append(shift(tied(up_low[3], side_after), ALONG_Z[2], "rs_up_z"))
    layer_out = call(
        finish_kernel,
        [SMEM] + [VMEM] * 11,
        [shape(shard_len, width, kind=F32)],
        [VMEM],
        [pltpu.VMEM((units, down_rows, width), LOW), pltpu.VMEM((width, ff), LOW)],
        (tied(place, side_after), active, middle, vectors) + down_pieces,
        2 * shard_len * width * ff,
        name="finish",
    )[0]
    qkv_one, qkv_two, up_z, layer_out = joined(qkv_one, qkv_two, up_z, layer_out)
    qkv_sum = qkv_parts[0].astype(F32) + qkv_one.astype(F32) + qkv_two.astype(F32)
    qkv_z = z_sends(qkv_sum, "rs_qkv")
    up_sum = z_sum(tied(up_sum[:1], qkv_sum), up_z)
    mate_part = shift(tied(mate_part, up_sum), PACK, "grad_pack")
    up_sum, qkv_z = joined(up_sum, qkv_z)
    last = call(
        last_kernel,
        [VMEM] * 6,
        [
            shape(qkv_rows, width, kind=F32), shape(1, 2 * each, kind=F32), shape(1, up_rows, kind=F32),
            shape(H, BUCKETS, kind=F32), shape(shard_len, width, kind=F32),
        ]
        + [shape(1, each, kind=F32)] * NARROW,
        [VMEM] * (5 + NARROW),
        [],
        (qkv_sum[0],) + tuple(qkv_z) + (own_part, mate_part),
        0,
        name="last", limit=8,
    )
    qkv_grad, qv_bias_grad, up_bias_sum, table, frames_grad = last[:5]
    pieces = [piece.reshape(each) for piece in last[5:]]

    down_grad = jnp.concatenate(
        [down_sum[fold * each : (fold + 1) * each] for fold in range(folds)], axis=1
    )
    return (
        layer_out, frames_grad, qkv_grad.T, qv_bias_grad.reshape(2 * each),
        up_sum[up_rows : up_rows + each].T, pieces[4], up_sum[:up_rows].T, up_bias_sum.reshape(up_rows),
        down_grad.T, pieces[5], pieces[0], pieces[1], pieces[2], pieces[3], table.T,
    )


def paired(mesh):
    return mesh.shape["blk"] == 2 and mesh.shape["dp"] == 16


def solution(mesh):
    placed = (
        P(("dp", "blk"), None),
        P(("dp", "blk"), None),
        P("dp", None),
        P(("dp", "blk")),
        P(None, ("dp", "blk")),
        P(("dp", "blk")),
        P(None, ("dp", "blk")),
        P(("dp", "blk")),
        P(None, ("dp", "blk")),
        P(("dp", "blk")),
        P(None, ("dp", "blk")),
        P(("dp", "blk")),
        P(("dp", "blk")),
        P(("dp", "blk")),
        P(("dp", "blk")),
        P(("dp", "blk")),
        P(),
    )
    return jax.shard_map(
        paired_body if paired(mesh) else body,
        mesh=mesh,
        in_specs=placed,
        out_specs=(
            P(("dp", "blk"), None),
            P(("dp", "blk"), None),
            P(None, ("dp", "blk")),
            P(("dp", "blk")),
            P(None, ("dp", "blk")),
            P(("dp", "blk")),
            P(None, ("dp", "blk")),
            P(("dp", "blk")),
            P(None, ("dp", "blk")),
            P(("dp", "blk")),
            P(("dp", "blk")),
            P(("dp", "blk")),
            P(("dp", "blk")),
            P(("dp", "blk")),
            P(),
        ),
        check_vma=False,
    )
```

```python
import math

import jax
import jax.numpy as jnp
import numpy as np
from jax import lax
from jax.experimental import pallas as pl
from jax.experimental.pallas import tpu as pltpu
from jax.sharding import PartitionSpec as P

H = 12
HD = 64
MAXREL = 160
BLOCK = 256
BUCKETS = 321


EPSILON = 1e-05
MASKED = -2e30
START_PEAK = -1e30
HIGHEST = lax.Precision.HIGHEST


def from_behind(block, axis, distance):
    devices = range(lax.axis_size(axis))
    route = [((i - distance) % len(devices), i) for i in devices]
    return lax.ppermute(block, axis, route)


def layer_norm(values, gain_vec, shift_vec):
    center = values - jnp.mean(values, axis=-1, keepdims=True)
    inv_std = lax.rsqrt(jnp.mean(center * center, axis=-1, keepdims=True) + EPSILON)
    normed = center * inv_std
    return (normed * gain_vec + shift_vec, normed, inv_std)


def norm_back(gradient, normed, inv_std, gain_vec):
    scaled = gradient * gain_vec
    inner = (
        scaled
        - jnp.mean(scaled, axis=-1, keepdims=True)
        - normed * jnp.mean(scaled * normed, axis=-1, keepdims=True)
    )
    return (inner * inv_std, jnp.sum(gradient * normed, axis=0), jnp.sum(gradient, axis=0))


def gelu_parts(values):
    normal_cdf = 0.5 * (1.0 + lax.erf(values * 0.7071067811865476))
    density = jnp.exp(-0.5 * values * values) * 0.3989422804014327
    return (values * normal_cdf, normal_cdf + values * density)


def doc_numbers(seq_ends, positions):
    return jnp.sum((positions[:, None] >= seq_ends[None, :]).astype(jnp.int32), axis=1)


def pair_logits(
    query_block, key_block, query_pos, key_pos, query_doc, key_doc, key_live, table_heads
):
    block_len = query_block.shape[0]
    raw = jnp.einsum(
        "qhd,khd->hqk",
        query_block.reshape(block_len, H, HD),
        key_block.reshape(-1, H, HD),
        preferred_element_type=jnp.float32,
    )
    relative = jnp.clip(key_pos[None, :] - query_pos[:, None], -MAXREL, MAXREL) + MAXREL
    bias = jnp.take(table_heads, relative, axis=1)
    allowed = (query_doc[:, None] == key_doc[None, :]) & (
        (key_live[None, :] > 0.5) | (query_pos[:, None] == key_pos[None, :])
    )
    return jnp.where(allowed[None], raw * (1.0 / math.sqrt(HD)) + bias, MASKED)


def diagonal_sums(gradient, offset):
    heads, block_len, _ = gradient.shape
    flipped = gradient[:, ::-1, :]
    padded = jnp.pad(flipped, ((0, 0), (0, 0), (0, block_len)))
    sheared = padded.reshape(heads, 2 * block_len * block_len)[:, : block_len * (2 * block_len - 1)]
    sheared = sheared.reshape(heads, block_len, 2 * block_len - 1)
    diag_sums = jnp.sum(sheared, axis=1)
    distance = offset + jnp.arange(2 * block_len - 1, dtype=jnp.int32) - (block_len - 1)
    bucket = jnp.clip(distance, -MAXREL, MAXREL) + MAXREL
    onehot = (bucket[:, None] == jnp.arange(BUCKETS, dtype=jnp.int32)[None, :]).astype(jnp.float32)
    return jnp.dot(diag_sums, onehot, precision=HIGHEST)


def body(
    frames,
    cotangent,
    seq_lengths,
    key_mask,
    qkv_weight,
    query_value_bias,
    out_weight,
    out_bias,
    up_weight,
    up_bias,
    down_weight,
    down_bias,
    first_gain,
    first_shift,
    second_gain,
    second_shift,
    rel_bias,
):
    cycle_size = lax.axis_size("blk")
    cycle_place = lax.axis_index("blk")
    shard_len = frames.shape[0]
    width = frames.shape[1]
    block_count = shard_len // BLOCK
    score_scale = 1.0 / math.sqrt(HD)
    seq_ends = jnp.cumsum(seq_lengths[0])
    local_pos = jnp.arange(shard_len, dtype=jnp.int32)
    positions = cycle_place * shard_len + local_pos
    own_docs = doc_numbers(seq_ends, positions)
    table_heads = rel_bias.astype(jnp.float32).T

    def blocked(array):
        return array.reshape((block_count, BLOCK) + array.shape[1:])

    def key_meta(turn):
        source = (cycle_place - turn) % cycle_size
        key_pos = source * shard_len + local_pos
        return (key_pos, doc_numbers(seq_ends, key_pos))

    gathered = (
        lax.all_gather(qkv_weight, ("dp", "blk"), axis=1, tiled=True),
        lax.all_gather(query_value_bias, ("dp", "blk"), axis=0, tiled=True),
        lax.all_gather(out_weight, ("dp", "blk"), axis=1, tiled=True),
        lax.all_gather(out_bias, ("dp", "blk"), axis=0, tiled=True),
        lax.all_gather(up_weight, ("dp", "blk"), axis=1, tiled=True),
        lax.all_gather(up_bias, ("dp", "blk"), axis=0, tiled=True),
        lax.all_gather(down_weight, ("dp", "blk"), axis=1, tiled=True),
        lax.all_gather(down_bias, ("dp", "blk"), axis=0, tiled=True),
        lax.all_gather(first_gain, ("dp", "blk"), axis=0, tiled=True),
        lax.all_gather(first_shift, ("dp", "blk"), axis=0, tiled=True),
        lax.all_gather(second_gain, ("dp", "blk"), axis=0, tiled=True),
        lax.all_gather(second_shift, ("dp", "blk"), axis=0, tiled=True),
    )
    (
        qkv_full,
        qv_bias_full,
        out_full,
        out_bias_full,
        up_full,
        up_bias_full,
        down_full,
        down_bias_full,
        gain_one,
        shift_one,
        gain_two,
        shift_two,
    ) = gathered
    frames_wide = frames.astype(jnp.float32)
    first_out, first_normed, first_inv = layer_norm(
        frames_wide, gain_one.astype(jnp.float32), shift_one.astype(jnp.float32)
    )
    first_low = first_out.astype(jnp.bfloat16)
    projected = jnp.dot(first_low, qkv_full, preferred_element_type=jnp.float32)
    bias_vec = qv_bias_full.astype(jnp.float32)
    queries = (projected[:, :width] + bias_vec[:width]).astype(jnp.bfloat16)
    key_rows = projected[:, width : 2 * width].astype(jnp.bfloat16)
    value_rows = (projected[:, 2 * width :] + bias_vec[width:]).astype(jnp.bfloat16)
    live_rows = key_mask.astype(jnp.bfloat16)
    query_blocks = (blocked(queries), blocked(positions), blocked(own_docs))

    def forward_hop(turn, online_state, key_part, value_part, live_part):
        key_pos, key_doc = key_meta(turn)
        key_items = (
            blocked(key_part),
            blocked(value_part),
            blocked(key_pos),
            blocked(key_doc),
            blocked(live_part),
        )

        def forward_per_query(query_items):
            query_block, query_pos, query_doc, row_peak, row_total, accum = query_items

            def online(carried, key_block_items):
                row_peak, row_total, accum = carried
                key_block, value_block, key_bpos, key_bdoc, key_blive = key_block_items
                logits = pair_logits(
                    query_block,
                    key_block,
                    query_pos,
                    key_bpos,
                    query_doc,
                    key_bdoc,
                    key_blive,
                    table_heads,
                )
                new_peak = jnp.maximum(row_peak, jnp.max(logits, axis=2))
                decay = jnp.exp(row_peak - new_peak)
                weights = jnp.exp(logits - new_peak[:, :, None])
                row_total = row_total * decay + jnp.sum(weights, axis=2)
                accum = accum * decay.T[:, :, None] + jnp.einsum(
                    "hqk,khd->qhd",
                    weights.astype(jnp.bfloat16),
                    value_block.reshape(-1, H, HD),
                    preferred_element_type=jnp.float32,
                )
                return ((new_peak, row_total, accum), None)

            result, unused = lax.scan(online, (row_peak, row_total, accum), key_items)
            return result

        return lax.map(forward_per_query, query_blocks + online_state)

    def cycle_turn(turn, carried):
        online_state, key_part, value_part, live_part = carried
        online_state = forward_hop(turn, online_state, key_part, value_part, live_part)
        key_part, value_part, live_part = from_behind((key_part, value_part, live_part), "blk", 1)
        return (online_state, key_part, value_part, live_part)

    start_state = (
        jnp.full((block_count, H, BLOCK), START_PEAK, jnp.float32),
        jnp.zeros((block_count, H, BLOCK), jnp.float32),
        jnp.zeros((block_count, BLOCK, H, HD), jnp.float32),
    )
    carried = lax.fori_loop(
        0, cycle_size - 1, cycle_turn, (start_state, key_rows, value_rows, live_rows)
    )
    row_peak, row_total, accum = forward_hop(
        cycle_size - 1, carried[0], carried[1], carried[2], carried[3]
    )
    mixed = accum / jnp.transpose(row_total, (0, 2, 1))[:, :, :, None]
    mixed_flat = mixed.reshape(shard_len, width)
    context = mixed_flat.astype(jnp.bfloat16)
    branch = jnp.dot(context, out_full, preferred_element_type=jnp.float32) + out_bias_full.astype(
        jnp.float32
    )
    middle = frames_wide + branch
    second_out, second_normed, second_inv = layer_norm(
        middle, gain_two.astype(jnp.float32), shift_two.astype(jnp.float32)
    )
    second_low = second_out.astype(jnp.bfloat16)
    hidden = jnp.dot(second_low, up_full, preferred_element_type=jnp.float32) + up_bias_full.astype(
        jnp.float32
    )
    active, slope = gelu_parts(hidden)
    active_low = active.astype(jnp.bfloat16)
    layer_out = (
        middle
        + jnp.dot(active_low, down_full, preferred_element_type=jnp.float32)
        + down_bias_full.astype(jnp.float32)
    )
    weights_back = (
        lax.all_gather(qkv_weight, ("dp", "blk"), axis=1, tiled=True),
        lax.all_gather(query_value_bias, ("dp", "blk"), axis=0, tiled=True),
        lax.all_gather(out_weight, ("dp", "blk"), axis=1, tiled=True),
        lax.all_gather(out_bias, ("dp", "blk"), axis=0, tiled=True),
        lax.all_gather(up_weight, ("dp", "blk"), axis=1, tiled=True),
        lax.all_gather(up_bias, ("dp", "blk"), axis=0, tiled=True),
        lax.all_gather(down_weight, ("dp", "blk"), axis=1, tiled=True),
        lax.all_gather(down_bias, ("dp", "blk"), axis=0, tiled=True),
        lax.all_gather(first_gain, ("dp", "blk"), axis=0, tiled=True),
        lax.all_gather(first_shift, ("dp", "blk"), axis=0, tiled=True),
        lax.all_gather(second_gain, ("dp", "blk"), axis=0, tiled=True),
        lax.all_gather(second_shift, ("dp", "blk"), axis=0, tiled=True),
    )
    qkv_back = weights_back[0]
    out_back = weights_back[2]
    up_back = weights_back[4]
    down_back = weights_back[6]
    gain_one_back = weights_back[8].astype(jnp.float32)
    gain_two_back = weights_back[10].astype(jnp.float32)
    grad_wide = cotangent.astype(jnp.float32)
    down_grad = jnp.einsum("tf,td->fd", active_low, cotangent, preferred_element_type=jnp.float32)
    down_bias_grad = jnp.sum(grad_wide, axis=0)
    active_grad = jnp.einsum("td,fd->tf", cotangent, down_back, preferred_element_type=jnp.float32)
    hidden_low = (active_grad * slope).astype(jnp.bfloat16)
    up_grad = jnp.einsum("td,tf->df", second_low, hidden_low, preferred_element_type=jnp.float32)
    up_bias_grad = jnp.sum(hidden_low.astype(jnp.float32), axis=0)
    second_grad = jnp.einsum("tf,df->td", hidden_low, up_back, preferred_element_type=jnp.float32)
    middle_norm, gain_two_grad, shift_two_grad = norm_back(
        second_grad, second_normed, second_inv, gain_two_back
    )
    middle_grad = grad_wide + middle_norm
    branch_low = middle_grad.astype(jnp.bfloat16)
    out_grad = jnp.einsum("td,te->de", context, branch_low, preferred_element_type=jnp.float32)
    out_bias_grad = jnp.sum(branch_low.astype(jnp.float32), axis=0)
    context_low = jnp.einsum(
        "te,de->td", branch_low, out_back, preferred_element_type=jnp.float32
    ).astype(jnp.bfloat16)
    delta = jnp.sum(
        (context_low.astype(jnp.float32) * mixed_flat).reshape(shard_len, H, HD), axis=2
    )
    delta_blocks = jnp.transpose(blocked(delta), (0, 2, 1))
    query_back = (
        blocked(queries),
        blocked(context_low),
        blocked(positions),
        blocked(own_docs),
        row_peak,
        row_total,
        delta_blocks,
    )

    def backward_hop(
        turn, query_grad, table_grad, key_part, value_part, live_part, key_grad, value_grad
    ):
        key_pos, key_doc = key_meta(turn)

        def per_key(carried, key_block_items):
            query_grad, table_grad = carried
            key_block, value_block, key_bpos, key_bdoc, key_blive, key_bgrad, value_bgrad = (
                key_block_items
            )
            key_heads = key_block.reshape(-1, H, HD)
            value_heads = value_block.reshape(-1, H, HD)

            def per_per_query(inner, query_items):
                key_bgrad, value_bgrad, table_grad = inner
                (
                    query_block,
                    dout_block,
                    query_pos,
                    query_doc,
                    peak_block,
                    total_block,
                    delta_block,
                ) = query_items
                logits = pair_logits(
                    query_block,
                    key_block,
                    query_pos,
                    key_bpos,
                    query_doc,
                    key_bdoc,
                    key_blive,
                    table_heads,
                )
                attn_prob = jnp.exp(logits - peak_block[:, :, None]) / total_block[:, :, None]
                dout_heads = dout_block.reshape(-1, H, HD)
                prob_grad = jnp.einsum(
                    "qhd,khd->hqk", dout_heads, value_heads, preferred_element_type=jnp.float32
                )
                logit_grad = attn_prob * (prob_grad - delta_block[:, :, None])
                raw_low = (logit_grad * score_scale).astype(jnp.bfloat16)
                query_part = jnp.einsum(
                    "hqk,khd->qhd", raw_low, key_heads, preferred_element_type=jnp.float32
                ).reshape(-1, width)
                key_bgrad = key_bgrad + jnp.einsum(
                    "hqk,qhd->khd",
                    raw_low,
                    query_block.reshape(-1, H, HD),
                    preferred_element_type=jnp.float32,
                ).reshape(-1, width)
                value_bgrad = value_bgrad + jnp.einsum(
                    "hqk,qhd->khd",
                    attn_prob.astype(jnp.bfloat16),
                    dout_heads,
                    preferred_element_type=jnp.float32,
                ).reshape(-1, width)
                table_grad = table_grad + diagonal_sums(logit_grad, key_bpos[0] - query_pos[0])
                return ((key_bgrad, value_bgrad, table_grad), query_part)

            (key_bgrad, value_bgrad, table_grad), query_parts = lax.scan(
                per_per_query, (key_bgrad, value_bgrad, table_grad), query_back
            )
            return ((query_grad + query_parts, table_grad), (key_bgrad, value_bgrad))

        (query_grad, table_grad), (key_new, value_new) = lax.scan(
            per_key,
            (query_grad, table_grad),
            (
                blocked(key_part),
                blocked(value_part),
                blocked(key_pos),
                blocked(key_doc),
                blocked(live_part),
                blocked(key_grad),
                blocked(value_grad),
            ),
        )
        return (
            query_grad,
            table_grad,
            key_new.reshape(shard_len, width),
            value_new.reshape(shard_len, width),
        )

    def pass_grads(key_grad, value_grad):
        return (
            from_behind(key_grad.astype(jnp.bfloat16), "blk", 1).astype(key_grad.dtype),
            from_behind(value_grad.astype(jnp.bfloat16), "blk", 1).astype(value_grad.dtype),
        )

    def back_turn(turn, carried):
        query_grad, table_grad, key_part, value_part, live_part, key_grad, value_grad = carried
        query_grad, table_grad, key_grad, value_grad = backward_hop(
            turn, query_grad, table_grad, key_part, value_part, live_part, key_grad, value_grad
        )
        key_part, value_part, live_part = from_behind((key_part, value_part, live_part), "blk", 1)
        key_grad, value_grad = pass_grads(key_grad, value_grad)
        return (query_grad, table_grad, key_part, value_part, live_part, key_grad, value_grad)

    zero_rows = jnp.zeros((shard_len, width), jnp.float32)
    back_start = (
        jnp.zeros((block_count, BLOCK, width), jnp.float32),
        jnp.zeros((H, BUCKETS), jnp.float32),
        key_rows,
        value_rows,
        live_rows,
        zero_rows,
        zero_rows,
    )
    carried = lax.fori_loop(0, cycle_size - 1, back_turn, back_start)
    query_grad, table_grad, key_grad, value_grad = backward_hop(
        cycle_size - 1,
        carried[0],
        carried[1],
        carried[2],
        carried[3],
        carried[4],
        carried[5],
        carried[6],
    )
    key_grad, value_grad = pass_grads(key_grad, value_grad)
    query_low = query_grad.reshape(shard_len, width).astype(jnp.bfloat16)
    key_low = key_grad.astype(jnp.bfloat16)
    value_low = value_grad.astype(jnp.bfloat16)
    qkv_low = jnp.concatenate([query_low, key_low, value_low], axis=1)
    qkv_grad = jnp.einsum("td,te->de", first_low, qkv_low, preferred_element_type=jnp.float32)
    query_value_grad = jnp.concatenate(
        [
            jnp.sum(query_low.astype(jnp.float32), axis=0),
            jnp.sum(value_low.astype(jnp.float32), axis=0),
        ]
    )
    first_grad = jnp.einsum("te,de->td", qkv_low, qkv_back, preferred_element_type=jnp.float32)
    frames_norm, gain_one_grad, shift_one_grad = norm_back(
        first_grad, first_normed, first_inv, gain_one_back
    )
    frames_grad = middle_grad + frames_norm
    summed = (
        lax.psum_scatter(qkv_grad, ("dp", "blk"), scatter_dimension=1, tiled=True),
        lax.psum_scatter(query_value_grad, ("dp", "blk"), scatter_dimension=0, tiled=True),
        lax.psum_scatter(out_grad, ("dp", "blk"), scatter_dimension=1, tiled=True),
        lax.psum_scatter(out_bias_grad, ("dp", "blk"), scatter_dimension=0, tiled=True),
        lax.psum_scatter(up_grad, ("dp", "blk"), scatter_dimension=1, tiled=True),
        lax.psum_scatter(up_bias_grad, ("dp", "blk"), scatter_dimension=0, tiled=True),
        lax.psum_scatter(down_grad, ("dp", "blk"), scatter_dimension=1, tiled=True),
        lax.psum_scatter(down_bias_grad, ("dp", "blk"), scatter_dimension=0, tiled=True),
        lax.psum_scatter(gain_one_grad, ("dp", "blk"), scatter_dimension=0, tiled=True),
        lax.psum_scatter(shift_one_grad, ("dp", "blk"), scatter_dimension=0, tiled=True),
        lax.psum_scatter(gain_two_grad, ("dp", "blk"), scatter_dimension=0, tiled=True),
        lax.psum_scatter(shift_two_grad, ("dp", "blk"), scatter_dimension=0, tiled=True),
    )
    table_sum = lax.psum(table_grad, ("dp", "blk"))
    return (
        layer_out,
        frames_grad,
        summed[0],
        summed[1],
        summed[2],
        summed[3],
        summed[4],
        summed[5],
        summed[6],
        summed[7],
        summed[8],
        summed[9],
        summed[10],
        summed[11],
        table_sum.T,
    )


AXES = ("dp", "blk")
F32 = jnp.float32
LOW = jnp.bfloat16
LANES = 128
NARROW = 6
PAD = 8


def route(move):
    n_dp, n_blk = lax.axis_size("dp"), lax.axis_size("blk")
    pairs = []
    for d in range(n_dp):
        d_bits, b_bits = move[d % 2]
        for b in range(n_blk):
            pairs.append((d * n_blk + b, (d ^ d_bits) * n_blk + (b ^ b_bits)))
    return pairs


def shift(array, move, name="swap"):
    with jax.named_scope(name):
        return lax.ppermute(array, AXES, route(move))


CORE = ((1, 0), (1, 0))
SIDE = ((0, 1), (2, 0))
OTHER_SIDE = ((2, 0), (0, 1))
PACK = ((0, 1), (0, 1))
ALONG_Z = tuple(((4 * turn, 0), (4 * turn, 0)) for turn in (1, 2, 3))


def tied(value, *after):
    return lax.optimization_barrier((value,) + after)[0]


def joined(*groups):
    return lax.optimization_barrier(groups)


def twin(array, name="twin"):
    return shift(array, CORE, name)


def along_z(unit, name):
    return tuple(shift(unit, move, name + "_z") for move in ALONG_Z)


def z_sends(plane, name):
    low = plane.astype(LOW)
    return tuple(shift(low[n + 1], move, name + "_z") for n, move in enumerate(ALONG_Z))


def z_sum(plane, arrived):
    return plane[0] + sum(part.astype(F32) for part in arrived)


def unit_of(place, x_turn, y_turn, z_turn, c):
    x, y, z = place[0] ^ x_turn, place[1] ^ y_turn, place[2] ^ z_turn
    return ((z * 2 + y) * 2 + c) * 2 + x


def each_unit(place, visit):
    def step(z, _):
        for plane in range(2):
            c = place[3] if plane == 0 else 1 - place[3]
            for n, (x_turn, y_turn) in enumerate(((0, 0), (1 - c, c), (c, 1 - c), (1, 1))):
                visit(4 * plane + n, z, unit_of(place, x_turn, y_turn, z, c))
        return 0

    lax.fori_loop(0, 4, step, 0)


def take_columns(place, array, pair, taken, top):
    for c in range(2):

        @pl.when(place[3] == c)
        def _():
            taken[top : top + array.shape[0], :] = jnp.concatenate(
                [
                    array[:, (2 * n + c) * pair : (2 * n + c + 1) * pair]
                    for n in range(array.shape[1] // (2 * pair))
                ],
                axis=1,
            )


def give_units(place, stage, parts):
    c = place[3]
    for part, (x_turn, y_turn) in zip(parts, ((0, 0), (1 - c, c), (c, 1 - c), (1, 1))):
        halves = part if isinstance(part, tuple) else (part,)
        for half, ref in enumerate(halves):
            start = half * ref.shape[0]

            def give(turn, _, ref=ref, start=start, x_turn=x_turn, y_turn=y_turn):
                unit = ((place[2] ^ (start + turn)) * 2 + (place[1] ^ y_turn)) * 2 + (place[0] ^ x_turn)
                ref[turn] = stage[unit].astype(LOW)
                return 0

            lax.fori_loop(0, ref.shape[0], give, 0)


def part_shapes(rows, width):
    return [jax.ShapeDtypeStruct((4, rows, width), LOW)] * 4


def dot_nn(a, b):
    return lax.dot_general(a, b, (((1,), (0,)), ((), ())), preferred_element_type=F32)


def dot_nt(a, b):
    return lax.dot_general(a, b, (((1,), (1,)), ((), ())), preferred_element_type=F32)


def dot_tn(a, b):
    return lax.dot_general(a, b, (((0,), (0,)), ((), ())), preferred_element_type=F32)


HBM = pl.BlockSpec(memory_space=pltpu.HBM)
SMEM = pl.BlockSpec(memory_space=pltpu.SMEM)
VMEM = pl.BlockSpec(memory_space=pltpu.VMEM)


def call(kernel, in_specs, outs, out_specs, scratch, args, flops, limit=56, **kwargs):
    moved = sum(math.prod(a.shape) * a.dtype.itemsize for a in list(args) + list(outs))
    return pl.pallas_call(
        kernel,
        out_shape=outs,
        in_specs=in_specs,
        out_specs=out_specs,
        scratch_shapes=scratch,
        compiler_params=pltpu.CompilerParams(vmem_limit_bytes=limit * 1024 * 1024),
        cost_estimate=pl.CostEstimate(flops=flops, bytes_accessed=moved, transcendentals=0),
        **kwargs,
    )(*args)


def spread_tables(units, width, lanes):
    tables = []
    for n in (width // units, 2 * width // units, 4 * width // units):
        lane = lanes[None, : units * n]
        row = jnp.arange(units + LANES, dtype=jnp.int32)[:, None]
        tables.append(
            jnp.where(row < units, lane // n == row, lane % n == row - units).astype(F32).astype(LOW)
        )
    return tables


def project_kernel(
    place, own, other, p0, p1, p2, p3, p4, p5, p6, p7, wide_one, wide_two, wide_four,
    first, queries, keys, values, vectors, up_bias, mate_live, weight_out, stage, small, weight, sems,
):
    units = stage.shape[0]
    width = own.shape[1]
    rows = stage.shape[1] - PAD
    shard_len = own.shape[0]
    pieces = (p0, p1, p2, p3, p4, p5, p6, p7)

    def fill(array, z, unit):
        stage[unit] = pieces[array][z]

    each_unit(place, fill)

    def normed(frames):
        wide = frames.astype(F32)
        center = wide - jnp.mean(wide, axis=1, keepdims=True)
        return center * lax.rsqrt(jnp.mean(center * center, axis=1, keepdims=True) + EPSILON)

    own_normed, mate_normed = normed(own[...]), normed(other[...])
    for unit in range(units):
        top = stage[unit, rows : rows + PAD, :].astype(F32)
        small[0, unit : unit + 1, :] = top[0:1]
        small[1, unit : unit + 1, :] = top[1:2]

    mate = unit_of(place, 1, 0, 0, place[3])
    mate_live[...] = stage[mate, rows : rows + PAD, : mate_live.shape[1]].astype(F32)

    def spread(row, slot, table):
        held = small[row, :, slot * LANES : (slot + 1) * LANES].astype(LOW)
        laid = dot_nn(held, table[units:, :]) * table[:units, :].astype(F32)
        return jnp.sum(laid, axis=0, keepdims=True)

    for n in range(NARROW):
        vectors[n : n + 1, :] = spread(0, n, wide_one)
    qv_bias = spread(1, 0, wide_two)
    up_bias[...] = jnp.broadcast_to(spread(1, 1, wide_four), up_bias.shape)
    vectors[NARROW : NARROW + 1, :] = qv_bias[:, :width]
    vectors[NARROW + 1 : NARROW + 2, :] = qv_bias[:, width:]

    def join(pair, _):
        both = jnp.concatenate(
            [stage[2 * pair, :rows, :].astype(F32), stage[2 * pair + 1, :rows, :].astype(F32)], axis=0
        )
        weight[pl.ds(pl.multiple_of(2 * rows * pair, 2 * rows), 2 * rows), :] = both.astype(LOW)
        return 0

    lax.fori_loop(0, units // 2, join, 0)
    copy = pltpu.make_async_copy(weight, weight_out, sems.at[0])
    copy.start()
    gain, offset = vectors[0:1, :], vectors[1:2, :]
    x = place[0]
    own_at = pl.multiple_of(x * shard_len, shard_len)
    mate_at = pl.multiple_of((1 - x) * shard_len, shard_len)
    first[pl.ds(own_at, shard_len), :] = (own_normed * gain + offset).astype(LOW)
    first[pl.ds(mate_at, shard_len), :] = (mate_normed * gain + offset).astype(LOW)
    mine = first[pl.ds(own_at, shard_len), :]
    queries[...] = (dot_nt(mine, weight[:width, :]) + vectors[NARROW : NARROW + 1, :]).astype(LOW)
    keys[...] = dot_nt(first[...], weight[width : 2 * width, :]).astype(LOW)
    values[...] = (
        dot_nt(first[...], weight[2 * width :, :]) + vectors[NARROW + 1 : NARROW + 2, :]
    ).astype(LOW)
    copy.wait()


def half_mask(shape, head):
    return (lax.broadcasted_iota(jnp.int32, shape, 1) // HD) == head


def bias_kernel(curve, bias):
    heads, block_len, span = bias.shape

    def shear(head, _):
        bias[head] = pltpu.roll(
            jnp.broadcast_to(curve[pl.ds(head, 1), :], (block_len, block_len + span)),
            span + 1, 1, stride=1, stride_axis=0,
        )[:, :span].astype(LOW)
        return 0

    lax.fori_loop(0, heads, shear, 0)


def attend_kernel(
    place, lengths, queries, keys, values, bias, own_live, mate_live, probs, mixed, hidden_pairs
):
    block_len, span = hidden_pairs.shape

    @pl.when(pl.program_id(0) == 0)
    def _():
        start = place[0] * block_len
        key_pos = lax.broadcasted_iota(jnp.int32, (1, span), 1)
        query_pos = lax.broadcasted_iota(jnp.int32, (block_len, 1), 0) + start
        key_doc, query_doc = jnp.zeros_like(key_pos), jnp.zeros_like(query_pos)
        end = 0
        for n in range(lengths.shape[1]):
            end = end + lengths[0, n]
            key_doc = key_doc + (key_pos >= end).astype(jnp.int32)
            query_doc = query_doc + (query_pos >= end).astype(jnp.int32)
        one, two = own_live[...].astype(F32), mate_live[2:3, :]
        live = jnp.where(
            place[0] == 0, jnp.concatenate([one, two], axis=1), jnp.concatenate([two, one], axis=1)
        )
        allowed = (query_doc == key_doc) & ((live > 0.5) | (query_pos == key_pos))
        hidden_pairs[...] = jnp.where(allowed, 0.0, MASKED)

    for pair in range(queries.shape[1] // (2 * HD)):
        lane = slice(2 * HD * pair, 2 * HD * (pair + 1))
        q, k, v = queries[:, lane], keys[:, lane], values[:, lane]
        total = jnp.zeros(q.shape, F32)
        for head in range(2):
            n = 2 * pair + head
            q_head = jnp.where(half_mask(q.shape, head), q, 0) * (1.0 / math.sqrt(HD))
            logits = dot_nt(q_head.astype(LOW), k) + bias[n].astype(F32) + hidden_pairs[...]
            weights = jnp.exp(logits - jnp.max(logits, axis=1, keepdims=True))
            prob = (weights * (1.0 / jnp.sum(weights, axis=1, keepdims=True))).astype(LOW)
            probs[n] = prob
            total = total + dot_nn(prob, jnp.where(half_mask(v.shape, head), v, 0))
        mixed[:, lane] = total


def join_units(kept, out):
    units = kept.shape[0]
    each = out.shape[0] // units

    def join(pair, _):
        both = jnp.concatenate(
            [kept[2 * pair].astype(F32)[:each], kept[2 * pair + 1].astype(F32)[:each]], axis=0
        )
        out[pl.ds(pl.multiple_of(2 * each * pair, 2 * each), 2 * each), :] = both.astype(LOW)
        return 0

    lax.fori_loop(0, units // 2, join, 0)


def expand_kernel(
    place, frames, mixed, vectors, up_bias, p0, p1, p2, p3, p4, p5, p6, p7,
    middle, second, context, active, slope, up, kept, out,
):
    width = frames.shape[1]
    pieces = (p0, p1, p2, p3, p4, p5, p6, p7)
    rows = p0.shape[1] - kept.shape[1]

    def fill(array, z, unit):
        kept[unit] = pieces[array][z, rows:]
        up[pl.ds(pl.multiple_of(unit * rows, rows), rows), :] = pieces[array][z, :rows]

    each_unit(place, fill)
    context[...] = mixed[...].astype(LOW)
    join_units(kept, out)
    mid = frames[...].astype(F32) + (dot_nt(context[...], out[...]) + vectors[4:5, :])
    middle[...] = mid
    center = mid - jnp.mean(mid, axis=1, keepdims=True)
    normed = center * lax.rsqrt(jnp.mean(center * center, axis=1, keepdims=True) + EPSILON)
    second[...] = (normed * vectors[2:3, :] + vectors[3:4, :]).astype(LOW)
    for n in range(up.shape[0] // width):
        at = slice(n * width, (n + 1) * width)
        hidden = dot_nt(second[...], up[at, :]) + up_bias[0:1, at]
        cdf = 0.5 * (1.0 + lax.erf(hidden * 0.7071067811865476))
        density = jnp.exp(-0.5 * hidden * hidden) * 0.3989422804014327
        active[:, at] = (hidden * cdf).astype(LOW)
        slope[:, at] = cdf + hidden * density


def down_grad_kernel(
    place, active, active_twin, cotangent, cotangent_twin, o0, o1, o2, o3, bias_grad, taken, wide,
):
    units, rows, width = wide.shape
    each = width // (2 * units)
    bias_grad[...] = jnp.broadcast_to(
        jnp.sum(cotangent[...].astype(F32), axis=0, keepdims=True), bias_grad.shape
    )

    shard_len = cotangent.shape[0]
    take_columns(place, cotangent, 2 * each, taken, 0)
    take_columns(place, cotangent_twin, 2 * each, taken, shard_len)
    dy, dy_twin = taken[:shard_len, :], taken[shard_len:, :]
    for fold in range(rows // each):
        at = slice(fold * width, (fold + 1) * width)
        grad = dot_tn(dy, active[:, at]) + dot_tn(dy_twin, active_twin[:, at])
        for unit in range(units):
            wide[unit, fold * each : (fold + 1) * each, :] = grad[unit * each : (unit + 1) * each]
    give_units(place, wide, (o0, o1, o2, o3))


def unfold_units(stage, down):
    units, rows, width = stage.shape
    each = down.shape[0] // units

    def unfold(pair, _):
        one, two = stage[2 * pair].astype(F32), stage[2 * pair + 1].astype(F32)
        at = pl.multiple_of(2 * each * pair, 2 * each)
        for fold in range(rows // each):
            both = jnp.concatenate(
                [one[fold * each : (fold + 1) * each], two[fold * each : (fold + 1) * each]], axis=0
            )
            down[pl.ds(at, 2 * each), fold * width : (fold + 1) * width] = both.astype(LOW)
        return 0

    lax.fori_loop(0, units // 2, unfold, 0)


def back_kernel(
    place, cotangent, slope, middle, vectors, p0, p1, p2, p3, p4, p5, p6, p7, u0, u1, u2, u3, u4, u5, u6, u7,
    middle_grad, context_grad, vector_grads, branch_grad, up_bias_grad, hidden_grad,
    stage, down, up, kept, out,
):
    width = cotangent.shape[1]
    down_pieces, up_pieces = (p0, p1, p2, p3, p4, p5, p6, p7), (u0, u1, u2, u3, u4, u5, u6, u7)
    rows = u0.shape[1] - kept.shape[1]

    def fill(array, z, unit):
        stage[unit] = down_pieces[array][z]
        kept[unit] = up_pieces[array][z, rows:]
        up[pl.ds(pl.multiple_of(unit * rows, rows), rows), :] = up_pieces[array][z, :rows]

    each_unit(place, fill)
    unfold_units(stage, down)
    dy = cotangent[...]
    for n in range(hidden_grad.shape[1] // width):
        at = slice(n * width, (n + 1) * width)
        grad = (dot_nn(dy, down[:, at]) * slope[:, at]).astype(LOW)
        hidden_grad[:, at] = grad
        up_bias_grad[:, at] = jnp.broadcast_to(
            jnp.sum(grad.astype(F32), axis=0, keepdims=True), (up_bias_grad.shape[0], width)
        )
    join_units(kept, out)
    second_grad = dot_nn(hidden_grad[...], up[...])
    mid = middle[...]
    center = mid - jnp.mean(mid, axis=1, keepdims=True)
    inv_std = lax.rsqrt(jnp.mean(center * center, axis=1, keepdims=True) + EPSILON)
    normed = center * inv_std
    scaled = second_grad * vectors[2:3, :]
    inner = (
        scaled
        - jnp.mean(scaled, axis=1, keepdims=True)
        - normed * jnp.mean(scaled * normed, axis=1, keepdims=True)
    )
    mid_grad = cotangent[...].astype(F32) + inner * inv_std
    middle_grad[...] = mid_grad
    branch = mid_grad.astype(LOW)
    vector_grads[...] = jnp.concatenate(
        [
            jnp.sum(second_grad * normed, axis=0, keepdims=True),
            jnp.sum(second_grad, axis=0, keepdims=True),
            jnp.sum(branch.astype(F32), axis=0, keepdims=True),
            jnp.zeros((5, width), F32),
        ],
        axis=0,
    )
    branch_grad[...] = branch
    context_grad[...] = dot_nn(branch, out[...]).astype(LOW)


def up_grad_kernel(
    place, hidden, hidden_twin, second, second_twin, branch, branch_twin, context, context_twin,
    o0, o1, o2, o3, o4, taken, taken_branch, stage,
):
    units, rows, width = stage.shape
    each = width // (2 * units)
    up_rows = hidden.shape[1] // (2 * units)

    shard_len = second.shape[0]
    take_columns(place, branch, 2 * each, taken_branch, 0)
    take_columns(place, branch_twin, 2 * each, taken_branch, shard_len)
    take_columns(place, hidden, 2 * up_rows, taken, 0)
    take_columns(place, hidden_twin, 2 * up_rows, taken, shard_len)
    out_grad = dot_tn(taken_branch[:shard_len, :], context[...]) + dot_tn(
        taken_branch[shard_len:, :], context_twin[...]
    )
    blank = jnp.zeros((rows - up_rows - each, width), F32)
    quarter = units // 4
    for z in range(4):
        at = slice(z * quarter * up_rows, (z + 1) * quarter * up_rows)
        grad = dot_tn(taken[:shard_len, at], second[...]) + dot_tn(taken[shard_len:, at], second_twin[...])
        for n in range(quarter):
            unit = z * quarter + n
            stage[unit] = jnp.concatenate(
                [
                    grad[n * up_rows : (n + 1) * up_rows],
                    out_grad[unit * each : (unit + 1) * each],
                    blank,
                ],
                axis=0,
            ).astype(LOW)
    give_units(place, stage, (o0, o1, (o2, o3), o4))


def rows_left(each):
    return -each % 16


def finish_kernel(
    place, active, middle, vectors, p0, p1, p2, p3, p4, p5, p6, p7, layer_out, stage, down
):
    pieces = (p0, p1, p2, p3, p4, p5, p6, p7)

    def fill(array, z, unit):
        stage[unit] = pieces[array][z]

    each_unit(place, fill)
    unfold_units(stage, down)
    layer_out[...] = middle[...] + dot_nt(active[...], down[...]) + vectors[5:6, :]


def attend_back_kernel(
    place, queries, keys, values, context_grad, mixed, probs, grads, diagonals
):
    q, k, v, dout = queries[...], keys[...], values[...], context_grad[...]
    block_len, span = probs.shape[1:]
    weighted = dout.astype(F32) * mixed[...]
    row = lax.broadcasted_iota(jnp.int32, (block_len, block_len), 0)
    lane = lax.broadcasted_iota(jnp.int32, (block_len, block_len), 1)
    turn = (row + lane == block_len - 1).astype(LOW)
    blank = jnp.zeros((block_len, block_len), F32)
    dq, dk, dv = jnp.zeros(q.shape, F32), jnp.zeros(k.shape, F32), jnp.zeros(v.shape, F32)
    for head in range(2):
        mine = half_mask(q.shape, head)
        dout_head = jnp.where(mine, dout, 0)
        delta = jnp.sum(jnp.where(mine, weighted, 0.0), axis=1, keepdims=True)
        prob = probs[head]
        grad = prob.astype(F32) * (dot_nt(dout_head, v) - delta)
        raw = (grad * (1.0 / math.sqrt(HD))).astype(LOW)
        dq = dq + dot_nn(raw, jnp.where(half_mask(k.shape, head), k, 0))
        dk = dk + dot_tn(raw, jnp.where(mine, q, 0))
        dv = dv + dot_tn(prob, dout_head)
        turned = jnp.concatenate([dot_nn(turn, raw), blank], axis=1)
        sheared = pltpu.roll(turned, 0, 1, stride=1, stride_axis=0)
        diagonals[pl.ds(2 * pl.program_id(0) + head, 1), :] = jnp.sum(sheared, axis=0, keepdims=True) * math.sqrt(HD)
    own_at = pl.multiple_of(place[0] * block_len, block_len)
    grads[0] = jnp.zeros(k.shape, LOW)
    grads[0, pl.ds(own_at, block_len), :] = dq.astype(LOW)
    grads[1] = dk.astype(LOW)
    grads[2] = dv.astype(LOW)


def total(array):
    return jnp.sum(array, axis=0, keepdims=True)


def norm_parts(frames):
    wide = frames.astype(F32)
    center = wide - jnp.mean(wide, axis=1, keepdims=True)
    inv_std = lax.rsqrt(jnp.mean(center * center, axis=1, keepdims=True) + EPSILON)
    return center * inv_std, inv_std


def first_grad_kernel(
    place, own_frames, mate_frames, grads, weight_in, diagonals, vector_grads, down_bias_grad, up_bias_grad,
    own_grad, mate_grad, small, weight, sems,
):
    copy = pltpu.make_async_copy(weight_in, weight, sems.at[0])
    copy.start()
    shard_len, width = own_frames.shape
    x = place[0]
    own_at = pl.multiple_of(x * shard_len, shard_len)
    mate_at = pl.multiple_of((1 - x) * shard_len, shard_len)
    own_normed, _ = norm_parts(own_frames[...])
    mate_normed, _ = norm_parts(mate_frames[...])
    dq = grads[0, pl.ds(own_at, shard_len), :]
    small[4:5, :] = vector_grads[2:3, :]
    small[2:4, :] = vector_grads[0:2, :]
    small[5:6, :] = down_bias_grad[0:1, :]
    small[6:7, :] = total(dq.astype(F32))
    small[7:8, :] = total(grads[2].astype(F32))
    for n in range(up_bias_grad.shape[1] // width):
        small[8 + n : 9 + n, :] = up_bias_grad[0:1, n * width : (n + 1) * width]
    small[12:, :] = diagonals[...]
    copy.wait()

    def from_keys(at):
        return dot_nn(grads[1, pl.ds(at, shard_len), :], weight[width : 2 * width, :]) + dot_nn(
            grads[2, pl.ds(at, shard_len), :], weight[2 * width :, :]
        )

    of_own = from_keys(own_at) + dot_nn(dq, weight[:width, :])
    of_mate = from_keys(mate_at)
    own_grad[...] = of_own
    mate_grad[...] = of_mate
    small[0:1, :] = total(of_own * own_normed) + total(of_mate * mate_normed)
    small[1:2, :] = total(of_own) + total(of_mate)


def qkv_grad_kernel(
    place, grads, grads_twin, first, first_twin, small_own, small_twin, wide_one, wide_two, wide_four,
    o0, o1, o2, o3, taken, sums, small, tables, stage,
):
    units, full, width = stage.shape
    rows = full - PAD
    span = first.shape[0]
    shard_len = span // 2
    x = place[0]
    summed = small_own[...] + small_twin[...]

    def fold(vector, table):
        kept = (vector * table[: 2 * units, :].astype(F32)).astype(LOW)
        return dot_nt(kept, table[2 * units :, :])

    for n in range(NARROW):
        small[0, :, n * LANES : (n + 1) * LANES] = fold(summed[n : n + 1, :], wide_one)
    small[1, :, :] = jnp.zeros((2 * units, width), F32)
    both = jnp.concatenate([summed[6:7, :], summed[7:8, :]], axis=1)
    small[1, :, :LANES] = fold(both, wide_two)
    four = jnp.concatenate([summed[8 + n : 9 + n, :] for n in range(4)], axis=1)
    small[1, :, LANES : 2 * LANES] = fold(four, wide_four)
    lanes = 3 * LANES
    distance = (
        lax.broadcasted_iota(jnp.int32, (shard_len + span, lanes), 0) - (shard_len - 1) - x * shard_len
    )
    bucket = jnp.clip(distance, -MAXREL, MAXREL) + MAXREL
    here = (bucket == lax.broadcasted_iota(jnp.int32, (shard_len + span, lanes), 1)).astype(F32).astype(LOW)
    diagonals = summed[12:, :]
    high = diagonals.astype(LOW)
    table = dot_nn(high, here) + dot_nn((diagonals - high.astype(F32)).astype(LOW), here)
    table = jnp.concatenate([table[: H // 2], table[H // 2 :]], axis=1)
    for n, array in enumerate((grads, grads_twin)):
        columns = jnp.concatenate([array[part] for part in range(3)], axis=1)
        take_columns(place, columns, 2 * rows, taken, n * span)
    sums[...] = dot_tn(taken[:span, :], first[...]) + dot_tn(taken[span:, :], first_twin[...])

    def pack(unit, _):
        at = 4 * (unit // 2) + 2 * place[3] + unit % 2
        stage[unit] = jnp.concatenate(
            [
                sums[pl.ds(pl.multiple_of(unit * rows, rows), rows), :],
                small[0, pl.ds(at, 1), :],
                small[1, pl.ds(at, 1), :],
                tables[...],
            ],
            axis=0,
        ).astype(LOW)
        return 0

    tables[...] = table
    lax.fori_loop(0, units, pack, 0)
    give_units(place, stage, (o0, o1, o2, o3))


def input_grad_kernel(frames, mate_frames, own_grad, mate_grad, middle_grad, vectors, own_part, mate_part):
    def through_norm(of_frames, grad):
        normed, inv_std = norm_parts(of_frames)
        scaled = grad * vectors[0:1, :]
        inner = (
            scaled
            - jnp.mean(scaled, axis=1, keepdims=True)
            - normed * jnp.mean(scaled * normed, axis=1, keepdims=True)
        )
        return inner * inv_std

    own_part[...] = middle_grad[...] + through_norm(frames[...], own_grad[...])
    mate_part[...] = through_norm(mate_frames[...], mate_grad[...]).astype(LOW)


def last_kernel(
    own, z1, z2, z3, own_part, mate_part, qkv, qv_bias, up_bias, table, frames_grad, n0, n1, n2, n3, n4, n5
):
    frames_grad[...] = own_part[...] + mate_part[...].astype(F32)
    rows = qkv.shape[0]
    total = own[...] + z1[...].astype(F32) + z2[...].astype(F32) + z3[...].astype(F32)
    qkv[...] = total[:rows]
    for n, narrow in enumerate((n0, n1, n2, n3, n4, n5)):
        narrow[...] = total[rows : rows + 1, n * LANES : n * LANES + narrow.shape[1]]
    qv_bias[...] = total[rows + 1 : rows + 2, : qv_bias.shape[1]]
    up_bias[...] = total[rows + 1 : rows + 2, LANES : LANES + up_bias.shape[1]]
    for half in range(2):
        at = 3 * LANES * half
        table[half * (H // 2) : (half + 1) * (H // 2), :] = total[rows + 2 : rows + PAD, at : at + BUCKETS]


def pack_kernel(
    live, qkv, out, up, down, first_gain, first_shift, second_gain, second_shift, out_bias,
    down_bias, qv_bias, up_bias, qkv_unit, up_unit, down_unit,
):
    each, width = out.shape

    def slots(vectors):
        parts = []
        for vector in vectors:
            wide = vector[...].astype(F32)
            parts += [wide, jnp.zeros((1, LANES - wide.shape[1]), F32)]
        left = width - LANES * len(vectors)
        if left:
            parts.append(jnp.zeros((1, left), F32))
        return jnp.concatenate(parts, axis=1)

    narrow = slots((first_gain, first_shift, second_gain, second_shift, out_bias, down_bias))
    wide = slots((qv_bias, up_bias))
    seen = live[...].astype(F32)
    seen = jnp.concatenate([seen, jnp.zeros((1, width - seen.shape[1]), F32)], axis=1)
    blank = jnp.zeros((PAD - 3, width), F32)
    qkv_unit[...] = jnp.concatenate([qkv[...].astype(F32), narrow, wide, seen, blank], axis=0).astype(LOW)
    blank = jnp.zeros((up_unit.shape[0] - up.shape[0] - each, width), F32)
    up_unit[...] = jnp.concatenate(
        [up[...].astype(F32), out[...].astype(F32), blank], axis=0
    ).astype(LOW)
    down_unit[...] = jnp.concatenate(
        [
            down[:, fold * width : (fold + 1) * width].astype(F32)
            for fold in range(down.shape[1] // width)
        ],
        axis=0,
    ).astype(LOW)


def paired_body(
    frames, cotangent, seq_lengths, key_mask, qkv_weight, query_value_bias, out_weight, out_bias,
    up_weight, up_bias, down_weight, down_bias, first_gain, first_shift, second_gain, second_shift,
    rel_bias,
):
    shard_len, width = frames.shape
    x = lax.axis_index("blk")
    d = lax.axis_index("dp")
    core = d % 2
    units = lax.axis_size("dp") * lax.axis_size("blk")
    span = shard_len * lax.axis_size("blk")
    place = jnp.stack([x, (d // 2) % 2, d // 4, core]).astype(jnp.int32)
    each = width // units
    ff = up_weight.shape[1] * units
    qkv_rows, up_rows = qkv_weight.shape[1], up_weight.shape[1]
    folds = ff // width
    down_rows = each * folds
    out_rows = each + rows_left(each)

    def shape(*dims, kind=LOW):
        return jax.ShapeDtypeStruct(dims, kind)

    def row(vector):
        return vector.reshape(1, vector.shape[0])

    packed = (
        row(key_mask), qkv_weight.T, out_weight.T, up_weight.T, down_weight.T, row(first_gain),
        row(first_shift), row(second_gain), row(second_shift), row(out_bias), row(down_bias),
        row(query_value_bias), row(up_bias),
    )
    qkv_unit, up_unit, down_unit = call(
        pack_kernel,
        [VMEM] * len(packed),
        [shape(qkv_rows + PAD, width), shape(up_rows + out_rows, width), shape(down_rows, width)],
        [VMEM] * 3,
        [],
        packed,
        0,
        name="pack",
    )
    def twins(pieces):
        return tuple(pieces) + tuple(twin(piece) for piece in pieces)

    distance = jnp.arange(span + shard_len, dtype=jnp.int32) - (shard_len - 1) - x * shard_len
    bucket = jnp.clip(distance, -MAXREL, MAXREL) + MAXREL
    bucket_lanes = 3 * LANES
    buckets = (bucket[:, None] == jnp.arange(bucket_lanes, dtype=jnp.int32)[None, :]).astype(LOW)
    curve = lax.dot_general(
        rel_bias, buckets[:, :BUCKETS], (((0,), (1,)), ((), ())), preferred_element_type=F32
    )
    bias = call(
        bias_kernel, [VMEM], [shape(H, shard_len, span)], [VMEM], [], (tied(curve, qkv_unit),), 0, name="bias"
    )[0]
    spreads = spread_tables(units, width, tied(jnp.arange(ff, dtype=jnp.int32), qkv_unit))
    cotangent_twin = twin(cotangent)
    qkv_z = along_z(qkv_unit, "qkv")
    mate_frames = shift(tied(frames, qkv_unit), PACK, "frames_pack")
    qkv_z, mate_frames, bias, place, spreads = joined(qkv_z, mate_frames, bias, place, spreads)
    qkv_own = jnp.stack((qkv_unit,) + qkv_z)
    qkv_side = shift(qkv_own, SIDE, "qkv_1")
    up_first = tied(up_unit, *qkv_z)
    up_z = [shift(up_first, move, "up_z") for move in ALONG_Z[:2]]
    qkv_side, up_z, cotangent_twin = joined(qkv_side, up_z, cotangent_twin)
    qkv_other = shift(qkv_own, OTHER_SIDE, "qkv_2")
    qkv_across = shift(qkv_side, OTHER_SIDE, "qkv_3")
    up_z.append(shift(tied(up_unit, qkv_side), ALONG_Z[2], "up_z"))
    up_z, qkv_other, qkv_across = joined(up_z, qkv_other, qkv_across)
    qkv_pieces = twins((qkv_own, qkv_side, qkv_other, qkv_across))
    up_own = jnp.stack([up_unit] + up_z)
    up_side = shift(up_own, SIDE, "up_1")
    down_first = tied(down_unit, up_own)
    down_z = [shift(down_first, move, "down_z") for move in ALONG_Z[:2]]

    unit_sems = pltpu.SemaphoreType.DMA((units,))
    first, queries, keys, values, vectors, up_bias_all, mate_live, weight = call(
        project_kernel,
        [SMEM] + [VMEM] * 13,
        [
            shape(span, width), shape(shard_len, width), shape(span, width), shape(span, width),
            shape(8, width, kind=F32), shape(8, ff, kind=F32), shape(PAD, shard_len, kind=F32),
            shape(3 * width, width),
        ],
        [VMEM] * 7 + [HBM],
        [
            pltpu.VMEM((units, qkv_rows + PAD, width), LOW), pltpu.VMEM((2, units, width), F32),
            pltpu.VMEM((3 * width, width), LOW), pltpu.SemaphoreType.DMA((1,)),
        ],
        (tied(place, up_own), frames, mate_frames) + qkv_pieces + tuple(spreads),
        2 * shard_len * width * 5 * width,
        name="project",
    )
    up_side, keys, down_z = joined(up_side, keys, down_z)
    up_other = shift(up_own, OTHER_SIDE, "up_2")
    up_across = shift(up_side, OTHER_SIDE, "up_3")
    down_z.append(shift(tied(down_unit, keys), ALONG_Z[2], "down_z"))
    pairs = H // 2
    pair_lanes = 2 * HD

    def lanes_of(rows, count=1):
        return pl.BlockSpec((rows, count * pair_lanes), lambda n: (0, n))

    def heads_of(*dims):
        return pl.BlockSpec(dims, lambda n: (n,) + (0,) * (len(dims) - 1))

    def whole(*dims):
        return pl.BlockSpec(dims, lambda n: (0,) * len(dims))

    probs, mixed = call(
        attend_kernel,
        [
            SMEM, SMEM, lanes_of(shard_len, 2), lanes_of(span, 2), lanes_of(span, 2),
            heads_of(4, shard_len, span), whole(1, shard_len), whole(PAD, shard_len),
        ],
        [shape(H, shard_len, span), shape(shard_len, width, kind=F32)],
        [heads_of(4, shard_len, span), lanes_of(shard_len, 2)],
        [pltpu.VMEM((shard_len, span), F32)],
        (
            tied(place, up_side), seq_lengths, queries, keys, values, bias, row(key_mask), mate_live,
        ),
        8 * shard_len * span * width,
        grid=(pairs // 2,),
        name="attend",
    )
    up_other, up_across, mixed, down_z = joined(up_other, up_across, mixed, down_z)
    up_pieces = twins((up_own, up_side, up_other, up_across))
    down_own = jnp.stack([down_unit] + down_z)
    down_side = shift(down_own, SIDE, "down_1")
    down_other = shift(down_own, OTHER_SIDE, "down_2")
    middle, second, context, active, slope = call(
        expand_kernel,
        [SMEM] + [VMEM] * 12,
        [
            shape(shard_len, width, kind=F32), shape(shard_len, width), shape(shard_len, width),
            shape(shard_len, ff), shape(shard_len, ff, kind=F32),
        ],
        [VMEM] * 5,
        [
            pltpu.VMEM((ff, width), LOW), pltpu.VMEM((units, out_rows, width), LOW),
            pltpu.VMEM((width, width), LOW),
        ],
        (tied(place, down_own), frames, mixed, vectors, up_bias_all) + up_pieces,
        2 * shard_len * width * (width + ff),
        name="expand", limit=36,
    )
    down_side, down_other, active = joined(down_side, down_other, active)
    down_across = shift(down_side, OTHER_SIDE, "down_3")
    active_twin, context_twin, second_twin = twin(active), twin(context), twin(second)
    first_twin = twin(first)
    down_parts = call(
        down_grad_kernel,
        [SMEM] + [VMEM] * 4,
        part_shapes(down_rows, width) + [shape(8, width, kind=F32)],
        [VMEM] * 5,
        [
            pltpu.VMEM((span, width // 2), LOW), pltpu.VMEM((units // 2, down_rows, width), F32),
        ],
        (tied(place, down_side), active, active_twin, cotangent, cotangent_twin),
        2 * shard_len * width * ff,
        name="down_grad", limit=24,
    )
    down_across, down_parts = joined(down_across, down_parts)
    down_bias_grad = down_parts[4]
    down_pieces = twins((down_own, down_side, down_other, down_across))
    turned = shift(down_parts[3], OTHER_SIDE, "rs_down_3")
    down_two = shift(down_parts[2], OTHER_SIDE, "rs_down_2")
    middle_grad, context_grad, vector_grads, branch_grad, up_bias_grad, hidden_grad = call(
        back_kernel,
        [SMEM] + [VMEM] * 20,
        [
            shape(shard_len, width, kind=F32), shape(shard_len, width), shape(8, width, kind=F32),
            shape(shard_len, width), shape(8, ff, kind=F32), shape(shard_len, ff),
        ],
        [VMEM] * 6,
        [
            pltpu.VMEM((units, down_rows, width), LOW), pltpu.VMEM((width, ff), LOW),
            pltpu.VMEM((ff, width), LOW), pltpu.VMEM((units, out_rows, width), LOW),
            pltpu.VMEM((width, width), LOW),
        ],
        (tied(place, down_parts[0]), cotangent, slope, middle, vectors) + down_pieces + up_pieces,
        2 * shard_len * width * (2 * ff + width),
        name="back", limit=48,
    )
    turned, down_two, hidden_grad, context_twin, second_twin, first_twin = joined(
        turned, down_two, hidden_grad, context_twin, second_twin, first_twin
    )
    side = (down_parts[1].astype(F32) + turned.astype(F32)).astype(LOW)
    down_one = shift(side, SIDE, "rs_down_1")
    hidden_twin = twin(hidden_grad)
    branch_twin = twin(branch_grad)
    down_sum = down_parts[0].astype(F32) + down_two.astype(F32)
    up_parts = call(
        up_grad_kernel,
        [SMEM] + [VMEM] * 8,
        [shape(n, up_rows + out_rows, width) for n in (4, 4, 2, 2, 4)],
        [VMEM] * 5,
        [
            pltpu.VMEM((span, ff // 2), LOW), pltpu.VMEM((span, width // 2), LOW),
            pltpu.VMEM((units // 2, up_rows + out_rows, width), LOW),
        ],
        (
            tied(place, down_sum, side), hidden_grad, hidden_twin, second, second_twin, branch_grad, branch_twin,
            context, context_twin,
        ),
        2 * shard_len * width * (ff + width),
        name="up_grad", limit=28,
    )
    down_one = tied(down_one, up_parts[0])
    turned = shift(up_parts[4], OTHER_SIDE, "rs_up_3")
    up_two = shift(up_parts[2], OTHER_SIDE, "rs_up_2a")
    down_sum = down_sum + down_one.astype(F32)
    down_low = down_sum.astype(LOW)
    down_z = [shift(down_low[n + 1], ALONG_Z[n], "rs_down_z") for n in range(2)]
    grads, diagonals = call(
        attend_back_kernel,
        [
            SMEM, lanes_of(shard_len), lanes_of(span), lanes_of(span), lanes_of(shard_len), lanes_of(shard_len),
            heads_of(2, shard_len, span),
        ],
        [shape(3, span, width), shape(H, span + shard_len, kind=F32)],
        [pl.BlockSpec((3, span, pair_lanes), lambda n: (0, 0, n)), whole(H, span + shard_len)],
        [],
        (place, queries, keys, values, tied(context_grad, up_parts[0], down_sum), mixed, probs),
        16 * shard_len * span * width,
        grid=(pairs,),
        name="attend_back", limit=24,
    )
    turned, up_two, down_z, grads = joined(turned, up_two, down_z, grads)
    up_rest = shift(up_parts[3], OTHER_SIDE, "rs_up_2b")
    grads_twin = twin(grads)
    side = (up_parts[1].astype(F32) + turned.astype(F32)).astype(LOW)
    up_one = shift(side, SIDE, "rs_up_1")
    own_grad, mate_grad, small = call(
        first_grad_kernel,
        [SMEM] + [VMEM] * 3 + [HBM] + [VMEM] * 4,
        [
            shape(shard_len, width, kind=F32), shape(shard_len, width, kind=F32),
            shape(12 + H, width, kind=F32),
        ],
        [VMEM] * 3,
        [pltpu.VMEM((3 * width, width), LOW), pltpu.SemaphoreType.DMA((1,))],
        (
            tied(place, side), frames, mate_frames, grads, weight, diagonals, vector_grads,
            down_bias_grad, up_bias_grad,
        ),
        2 * shard_len * width * 5 * width,
        name="first_grad", limit=24,
    )
    grads_twin, small = joined(grads_twin, small)
    down_z.append(shift(tied(down_low[3], small), ALONG_Z[2], "rs_down_z"))
    small_twin = twin(small)
    qkv_parts = call(
        qkv_grad_kernel,
        [SMEM] + [VMEM] * 9,
        part_shapes(qkv_rows + PAD, width),
        [VMEM] * 4,
        [
            pltpu.VMEM((2 * span, 3 * width // 2), LOW), pltpu.VMEM((3 * width // 2, width), F32),
            pltpu.VMEM((2, units, width), F32), pltpu.VMEM((H // 2, width), F32),
            pltpu.VMEM((units // 2, qkv_rows + PAD, width), LOW),
        ],
        (place, grads, grads_twin, first, first_twin, small, small_twin) + tuple(spreads),
        2 * shard_len * width * 6 * width,
        name="qkv_grad", limit=28,
    )
    up_one, up_rest, down_z = tied((up_one, up_rest, down_z), qkv_parts[0])
    turned = shift(qkv_parts[3], OTHER_SIDE, "rs_qkv_3")
    qkv_two = shift(qkv_parts[2], OTHER_SIDE, "rs_qkv_2")
    up_sum = [
        up_parts[0][n].astype(F32) + up_one[n].astype(F32) + (up_two, up_rest)[n // 2][n % 2].astype(F32)
        for n in range(4)
    ]
    up_low = [part.astype(LOW) for part in up_sum]
    up_z = [shift(up_low[n + 1], ALONG_Z[n], "rs_up_z") for n in range(2)]
    down_sum = z_sum(down_sum, down_z)
    own_part, mate_part = call(
        input_grad_kernel,
        [VMEM] * 6,
        [shape(shard_len, width, kind=F32), shape(shard_len, width)],
        [VMEM] * 2,
        [],
        (frames, mate_frames, own_grad, tied(mate_grad, *up_low), middle_grad, vectors),
        0,
        name="input_grad", limit=12,
    )
    turned, mate_part = joined(turned, mate_part)
    side = (qkv_parts[1].astype(F32) + turned.astype(F32)).astype(LOW)
    qkv_one = shift(side, SIDE, "rs_qkv_1")
    up_z, side_after = joined(up_z, side)
    up_z.append(shift(tied(up_low[3], side_after), ALONG_Z[2], "rs_up_z"))
    layer_out = call(
        finish_kernel,
        [SMEM] + [VMEM] * 11,
        [shape(shard_len, width, kind=F32)],
        [VMEM],
        [pltpu.VMEM((units, down_rows, width), LOW), pltpu.VMEM((width, ff), LOW)],
        (tied(place, side_after), active, middle, vectors) + down_pieces,
        2 * shard_len * width * ff,
        name="finish",
    )[0]
    qkv_one, qkv_two, up_z, layer_out = joined(qkv_one, qkv_two, up_z, layer_out)
    qkv_sum = qkv_parts[0].astype(F32) + qkv_one.astype(F32) + qkv_two.astype(F32)
    qkv_z = z_sends(qkv_sum, "rs_qkv")
    up_sum = z_sum(tied(up_sum[:1], qkv_sum), up_z)
    mate_part = shift(tied(mate_part, up_sum), PACK, "grad_pack")
    up_sum, qkv_z = joined(up_sum, qkv_z)
    last = call(
        last_kernel,
        [VMEM] * 6,
        [
            shape(qkv_rows, width, kind=F32), shape(1, 2 * each, kind=F32), shape(1, up_rows, kind=F32),
            shape(H, BUCKETS, kind=F32), shape(shard_len, width, kind=F32),
        ]
        + [shape(1, each, kind=F32)] * NARROW,
        [VMEM] * (5 + NARROW),
        [],
        (qkv_sum[0],) + tuple(qkv_z) + (own_part, mate_part),
        0,
        name="last", limit=8,
    )
    qkv_grad, qv_bias_grad, up_bias_sum, table, frames_grad = last[:5]
    pieces = [piece.reshape(each) for piece in last[5:]]

    down_grad = jnp.concatenate(
        [down_sum[fold * each : (fold + 1) * each] for fold in range(folds)], axis=1
    )
    return (
        layer_out, frames_grad, qkv_grad.T, qv_bias_grad.reshape(2 * each),
        up_sum[up_rows : up_rows + each].T, pieces[4], up_sum[:up_rows].T, up_bias_sum.reshape(up_rows),
        down_grad.T, pieces[5], pieces[0], pieces[1], pieces[2], pieces[3], table.T,
    )


def paired(mesh):
    return mesh.shape["blk"] == 2 and mesh.shape["dp"] == 16


def solution(mesh):
    placed = (
        P(("dp", "blk"), None),
        P(("dp", "blk"), None),
        P("dp", None),
        P(("dp", "blk")),
        P(None, ("dp", "blk")),
        P(("dp", "blk")),
        P(None, ("dp", "blk")),
        P(("dp", "blk")),
        P(None, ("dp", "blk")),
        P(("dp", "blk")),
        P(None, ("dp", "blk")),
        P(("dp", "blk")),
        P(("dp", "blk")),
        P(("dp", "blk")),
        P(("dp", "blk")),
        P(("dp", "blk")),
        P(),
    )
    return jax.shard_map(
        paired_body if paired(mesh) else body,
        mesh=mesh,
        in_specs=placed,
        out_specs=(
            P(("dp", "blk"), None),
            P(("dp", "blk"), None),
            P(None, ("dp", "blk")),
            P(("dp", "blk")),
            P(None, ("dp", "blk")),
            P(("dp", "blk")),
            P(None, ("dp", "blk")),
            P(("dp", "blk")),
            P(None, ("dp", "blk")),
            P(("dp", "blk")),
            P(("dp", "blk")),
            P(("dp", "blk")),
            P(("dp", "blk")),
            P(("dp", "blk")),
            P(),
        ),
        check_vma=False,
    )
```

```python
import math

import jax
import jax.numpy as jnp
import numpy as np
from jax import lax
from jax.experimental import pallas as pl
from jax.experimental.pallas import tpu as pltpu
from jax.sharding import PartitionSpec as P

H = 12
HD = 64
MAXREL = 160
BLOCK = 256
BUCKETS = 321


EPSILON = 1e-05
MASKED = -2e30
START_PEAK = -1e30
HIGHEST = lax.Precision.HIGHEST


def from_behind(block, axis, distance):
    devices = range(lax.axis_size(axis))
    route = [((i - distance) % len(devices), i) for i in devices]
    return lax.ppermute(block, axis, route)


def layer_norm(values, gain_vec, shift_vec):
    center = values - jnp.mean(values, axis=-1, keepdims=True)
    inv_std = lax.rsqrt(jnp.mean(center * center, axis=-1, keepdims=True) + EPSILON)
    normed = center * inv_std
    return (normed * gain_vec + shift_vec, normed, inv_std)


def norm_back(gradient, normed, inv_std, gain_vec):
    scaled = gradient * gain_vec
    inner = (
        scaled
        - jnp.mean(scaled, axis=-1, keepdims=True)
        - normed * jnp.mean(scaled * normed, axis=-1, keepdims=True)
    )
    return (inner * inv_std, jnp.sum(gradient * normed, axis=0), jnp.sum(gradient, axis=0))


def gelu_parts(values):
    normal_cdf = 0.5 * (1.0 + lax.erf(values * 0.7071067811865476))
    density = jnp.exp(-0.5 * values * values) * 0.3989422804014327
    return (values * normal_cdf, normal_cdf + values * density)


def doc_numbers(seq_ends, positions):
    return jnp.sum((positions[:, None] >= seq_ends[None, :]).astype(jnp.int32), axis=1)


def pair_logits(
    query_block, key_block, query_pos, key_pos, query_doc, key_doc, key_live, table_heads
):
    block_len = query_block.shape[0]
    raw = jnp.einsum(
        "qhd,khd->hqk",
        query_block.reshape(block_len, H, HD),
        key_block.reshape(-1, H, HD),
        preferred_element_type=jnp.float32,
    )
    relative = jnp.clip(key_pos[None, :] - query_pos[:, None], -MAXREL, MAXREL) + MAXREL
    bias = jnp.take(table_heads, relative, axis=1)
    allowed = (query_doc[:, None] == key_doc[None, :]) & (
        (key_live[None, :] > 0.5) | (query_pos[:, None] == key_pos[None, :])
    )
    return jnp.where(allowed[None], raw * (1.0 / math.sqrt(HD)) + bias, MASKED)


def diagonal_sums(gradient, offset):
    heads, block_len, _ = gradient.shape
    flipped = gradient[:, ::-1, :]
    padded = jnp.pad(flipped, ((0, 0), (0, 0), (0, block_len)))
    sheared = padded.reshape(heads, 2 * block_len * block_len)[:, : block_len * (2 * block_len - 1)]
    sheared = sheared.reshape(heads, block_len, 2 * block_len - 1)
    diag_sums = jnp.sum(sheared, axis=1)
    distance = offset + jnp.arange(2 * block_len - 1, dtype=jnp.int32) - (block_len - 1)
    bucket = jnp.clip(distance, -MAXREL, MAXREL) + MAXREL
    onehot = (bucket[:, None] == jnp.arange(BUCKETS, dtype=jnp.int32)[None, :]).astype(jnp.float32)
    return jnp.dot(diag_sums, onehot, precision=HIGHEST)


def body(
    frames,
    cotangent,
    seq_lengths,
    key_mask,
    qkv_weight,
    query_value_bias,
    out_weight,
    out_bias,
    up_weight,
    up_bias,
    down_weight,
    down_bias,
    first_gain,
    first_shift,
    second_gain,
    second_shift,
    rel_bias,
):
    cycle_size = lax.axis_size("blk")
    cycle_place = lax.axis_index("blk")
    shard_len = frames.shape[0]
    width = frames.shape[1]
    block_count = shard_len // BLOCK
    score_scale = 1.0 / math.sqrt(HD)
    seq_ends = jnp.cumsum(seq_lengths[0])
    local_pos = jnp.arange(shard_len, dtype=jnp.int32)
    positions = cycle_place * shard_len + local_pos
    own_docs = doc_numbers(seq_ends, positions)
    table_heads = rel_bias.astype(jnp.float32).T

    def blocked(array):
        return array.reshape((block_count, BLOCK) + array.shape[1:])

    def key_meta(turn):
        source = (cycle_place - turn) % cycle_size
        key_pos = source * shard_len + local_pos
        return (key_pos, doc_numbers(seq_ends, key_pos))

    gathered = (
        lax.all_gather(qkv_weight, ("dp", "blk"), axis=1, tiled=True),
        lax.all_gather(query_value_bias, ("dp", "blk"), axis=0, tiled=True),
        lax.all_gather(out_weight, ("dp", "blk"), axis=1, tiled=True),
        lax.all_gather(out_bias, ("dp", "blk"), axis=0, tiled=True),
        lax.all_gather(up_weight, ("dp", "blk"), axis=1, tiled=True),
        lax.all_gather(up_bias, ("dp", "blk"), axis=0, tiled=True),
        lax.all_gather(down_weight, ("dp", "blk"), axis=1, tiled=True),
        lax.all_gather(down_bias, ("dp", "blk"), axis=0, tiled=True),
        lax.all_gather(first_gain, ("dp", "blk"), axis=0, tiled=True),
        lax.all_gather(first_shift, ("dp", "blk"), axis=0, tiled=True),
        lax.all_gather(second_gain, ("dp", "blk"), axis=0, tiled=True),
        lax.all_gather(second_shift, ("dp", "blk"), axis=0, tiled=True),
    )
    (
        qkv_full,
        qv_bias_full,
        out_full,
        out_bias_full,
        up_full,
        up_bias_full,
        down_full,
        down_bias_full,
        gain_one,
        shift_one,
        gain_two,
        shift_two,
    ) = gathered
    frames_wide = frames.astype(jnp.float32)
    first_out, first_normed, first_inv = layer_norm(
        frames_wide, gain_one.astype(jnp.float32), shift_one.astype(jnp.float32)
    )
    first_low = first_out.astype(jnp.bfloat16)
    projected = jnp.dot(first_low, qkv_full, preferred_element_type=jnp.float32)
    bias_vec = qv_bias_full.astype(jnp.float32)
    queries = (projected[:, :width] + bias_vec[:width]).astype(jnp.bfloat16)
    key_rows = projected[:, width : 2 * width].astype(jnp.bfloat16)
    value_rows = (projected[:, 2 * width :] + bias_vec[width:]).astype(jnp.bfloat16)
    live_rows = key_mask.astype(jnp.bfloat16)
    query_blocks = (blocked(queries), blocked(positions), blocked(own_docs))

    def forward_hop(turn, online_state, key_part, value_part, live_part):
        key_pos, key_doc = key_meta(turn)
        key_items = (
            blocked(key_part),
            blocked(value_part),
            blocked(key_pos),
            blocked(key_doc),
            blocked(live_part),
        )

        def forward_per_query(query_items):
            query_block, query_pos, query_doc, row_peak, row_total, accum = query_items

            def online(carried, key_block_items):
                row_peak, row_total, accum = carried
                key_block, value_block, key_bpos, key_bdoc, key_blive = key_block_items
                logits = pair_logits(
                    query_block,
                    key_block,
                    query_pos,
                    key_bpos,
                    query_doc,
                    key_bdoc,
                    key_blive,
                    table_heads,
                )
                new_peak = jnp.maximum(row_peak, jnp.max(logits, axis=2))
                decay = jnp.exp(row_peak - new_peak)
                weights = jnp.exp(logits - new_peak[:, :, None])
                row_total = row_total * decay + jnp.sum(weights, axis=2)
                accum = accum * decay.T[:, :, None] + jnp.einsum(
                    "hqk,khd->qhd",
                    weights.astype(jnp.bfloat16),
                    value_block.reshape(-1, H, HD),
                    preferred_element_type=jnp.float32,
                )
                return ((new_peak, row_total, accum), None)

            result, unused = lax.scan(online, (row_peak, row_total, accum), key_items)
            return result

        return lax.map(forward_per_query, query_blocks + online_state)

    def cycle_turn(turn, carried):
        online_state, key_part, value_part, live_part = carried
        online_state = forward_hop(turn, online_state, key_part, value_part, live_part)
        key_part, value_part, live_part = from_behind((key_part, value_part, live_part), "blk", 1)
        return (online_state, key_part, value_part, live_part)

    start_state = (
        jnp.full((block_count, H, BLOCK), START_PEAK, jnp.float32),
        jnp.zeros((block_count, H, BLOCK), jnp.float32),
        jnp.zeros((block_count, BLOCK, H, HD), jnp.float32),
    )
    carried = lax.fori_loop(
        0, cycle_size - 1, cycle_turn, (start_state, key_rows, value_rows, live_rows)
    )
    row_peak, row_total, accum = forward_hop(
        cycle_size - 1, carried[0], carried[1], carried[2], carried[3]
    )
    mixed = accum / jnp.transpose(row_total, (0, 2, 1))[:, :, :, None]
    mixed_flat = mixed.reshape(shard_len, width)
    context = mixed_flat.astype(jnp.bfloat16)
    branch = jnp.dot(context, out_full, preferred_element_type=jnp.float32) + out_bias_full.astype(
        jnp.float32
    )
    middle = frames_wide + branch
    second_out, second_normed, second_inv = layer_norm(
        middle, gain_two.astype(jnp.float32), shift_two.astype(jnp.float32)
    )
    second_low = second_out.astype(jnp.bfloat16)
    hidden = jnp.dot(second_low, up_full, preferred_element_type=jnp.float32) + up_bias_full.astype(
        jnp.float32
    )
    active, slope = gelu_parts(hidden)
    active_low = active.astype(jnp.bfloat16)
    layer_out = (
        middle
        + jnp.dot(active_low, down_full, preferred_element_type=jnp.float32)
        + down_bias_full.astype(jnp.float32)
    )
    weights_back = (
        lax.all_gather(qkv_weight, ("dp", "blk"), axis=1, tiled=True),
        lax.all_gather(query_value_bias, ("dp", "blk"), axis=0, tiled=True),
        lax.all_gather(out_weight, ("dp", "blk"), axis=1, tiled=True),
        lax.all_gather(out_bias, ("dp", "blk"), axis=0, tiled=True),
        lax.all_gather(up_weight, ("dp", "blk"), axis=1, tiled=True),
        lax.all_gather(up_bias, ("dp", "blk"), axis=0, tiled=True),
        lax.all_gather(down_weight, ("dp", "blk"), axis=1, tiled=True),
        lax.all_gather(down_bias, ("dp", "blk"), axis=0, tiled=True),
        lax.all_gather(first_gain, ("dp", "blk"), axis=0, tiled=True),
        lax.all_gather(first_shift, ("dp", "blk"), axis=0, tiled=True),
        lax.all_gather(second_gain, ("dp", "blk"), axis=0, tiled=True),
        lax.all_gather(second_shift, ("dp", "blk"), axis=0, tiled=True),
    )
    qkv_back = weights_back[0]
    out_back = weights_back[2]
    up_back = weights_back[4]
    down_back = weights_back[6]
    gain_one_back = weights_back[8].astype(jnp.float32)
    gain_two_back = weights_back[10].astype(jnp.float32)
    grad_wide = cotangent.astype(jnp.float32)
    down_grad = jnp.einsum("tf,td->fd", active_low, cotangent, preferred_element_type=jnp.float32)
    down_bias_grad = jnp.sum(grad_wide, axis=0)
    active_grad = jnp.einsum("td,fd->tf", cotangent, down_back, preferred_element_type=jnp.float32)
    hidden_low = (active_grad * slope).astype(jnp.bfloat16)
    up_grad = jnp.einsum("td,tf->df", second_low, hidden_low, preferred_element_type=jnp.float32)
    up_bias_grad = jnp.sum(hidden_low.astype(jnp.float32), axis=0)
    second_grad = jnp.einsum("tf,df->td", hidden_low, up_back, preferred_element_type=jnp.float32)
    middle_norm, gain_two_grad, shift_two_grad = norm_back(
        second_grad, second_normed, second_inv, gain_two_back
    )
    middle_grad = grad_wide + middle_norm
    branch_low = middle_grad.astype(jnp.bfloat16)
    out_grad = jnp.einsum("td,te->de", context, branch_low, preferred_element_type=jnp.float32)
    out_bias_grad = jnp.sum(branch_low.astype(jnp.float32), axis=0)
    context_low = jnp.einsum(
        "te,de->td", branch_low, out_back, preferred_element_type=jnp.float32
    ).astype(jnp.bfloat16)
    delta = jnp.sum(
        (context_low.astype(jnp.float32) * mixed_flat).reshape(shard_len, H, HD), axis=2
    )
    delta_blocks = jnp.transpose(blocked(delta), (0, 2, 1))
    query_back = (
        blocked(queries),
        blocked(context_low),
        blocked(positions),
        blocked(own_docs),
        row_peak,
        row_total,
        delta_blocks,
    )

    def backward_hop(
        turn, query_grad, table_grad, key_part, value_part, live_part, key_grad, value_grad
    ):
        key_pos, key_doc = key_meta(turn)

        def per_key(carried, key_block_items):
            query_grad, table_grad = carried
            key_block, value_block, key_bpos, key_bdoc, key_blive, key_bgrad, value_bgrad = (
                key_block_items
            )
            key_heads = key_block.reshape(-1, H, HD)
            value_heads = value_block.reshape(-1, H, HD)

            def per_per_query(inner, query_items):
                key_bgrad, value_bgrad, table_grad = inner
                (
                    query_block,
                    dout_block,
                    query_pos,
                    query_doc,
                    peak_block,
                    total_block,
                    delta_block,
                ) = query_items
                logits = pair_logits(
                    query_block,
                    key_block,
                    query_pos,
                    key_bpos,
                    query_doc,
                    key_bdoc,
                    key_blive,
                    table_heads,
                )
                attn_prob = jnp.exp(logits - peak_block[:, :, None]) / total_block[:, :, None]
                dout_heads = dout_block.reshape(-1, H, HD)
                prob_grad = jnp.einsum(
                    "qhd,khd->hqk", dout_heads, value_heads, preferred_element_type=jnp.float32
                )
                logit_grad = attn_prob * (prob_grad - delta_block[:, :, None])
                raw_low = (logit_grad * score_scale).astype(jnp.bfloat16)
                query_part = jnp.einsum(
                    "hqk,khd->qhd", raw_low, key_heads, preferred_element_type=jnp.float32
                ).reshape(-1, width)
                key_bgrad = key_bgrad + jnp.einsum(
                    "hqk,qhd->khd",
                    raw_low,
                    query_block.reshape(-1, H, HD),
                    preferred_element_type=jnp.float32,
                ).reshape(-1, width)
                value_bgrad = value_bgrad + jnp.einsum(
                    "hqk,qhd->khd",
                    attn_prob.astype(jnp.bfloat16),
                    dout_heads,
                    preferred_element_type=jnp.float32,
                ).reshape(-1, width)
                table_grad = table_grad + diagonal_sums(logit_grad, key_bpos[0] - query_pos[0])
                return ((key_bgrad, value_bgrad, table_grad), query_part)

            (key_bgrad, value_bgrad, table_grad), query_parts = lax.scan(
                per_per_query, (key_bgrad, value_bgrad, table_grad), query_back
            )
            return ((query_grad + query_parts, table_grad), (key_bgrad, value_bgrad))

        (query_grad, table_grad), (key_new, value_new) = lax.scan(
            per_key,
            (query_grad, table_grad),
            (
                blocked(key_part),
                blocked(value_part),
                blocked(key_pos),
                blocked(key_doc),
                blocked(live_part),
                blocked(key_grad),
                blocked(value_grad),
            ),
        )
        return (
            query_grad,
            table_grad,
            key_new.reshape(shard_len, width),
            value_new.reshape(shard_len, width),
        )

    def pass_grads(key_grad, value_grad):
        return (
            from_behind(key_grad.astype(jnp.bfloat16), "blk", 1).astype(key_grad.dtype),
            from_behind(value_grad.astype(jnp.bfloat16), "blk", 1).astype(value_grad.dtype),
        )

    def back_turn(turn, carried):
        query_grad, table_grad, key_part, value_part, live_part, key_grad, value_grad = carried
        query_grad, table_grad, key_grad, value_grad = backward_hop(
            turn, query_grad, table_grad, key_part, value_part, live_part, key_grad, value_grad
        )
        key_part, value_part, live_part = from_behind((key_part, value_part, live_part), "blk", 1)
        key_grad, value_grad = pass_grads(key_grad, value_grad)
        return (query_grad, table_grad, key_part, value_part, live_part, key_grad, value_grad)

    zero_rows = jnp.zeros((shard_len, width), jnp.float32)
    back_start = (
        jnp.zeros((block_count, BLOCK, width), jnp.float32),
        jnp.zeros((H, BUCKETS), jnp.float32),
        key_rows,
        value_rows,
        live_rows,
        zero_rows,
        zero_rows,
    )
    carried = lax.fori_loop(0, cycle_size - 1, back_turn, back_start)
    query_grad, table_grad, key_grad, value_grad = backward_hop(
        cycle_size - 1,
        carried[0],
        carried[1],
        carried[2],
        carried[3],
        carried[4],
        carried[5],
        carried[6],
    )
    key_grad, value_grad = pass_grads(key_grad, value_grad)
    query_low = query_grad.reshape(shard_len, width).astype(jnp.bfloat16)
    key_low = key_grad.astype(jnp.bfloat16)
    value_low = value_grad.astype(jnp.bfloat16)
    qkv_low = jnp.concatenate([query_low, key_low, value_low], axis=1)
    qkv_grad = jnp.einsum("td,te->de", first_low, qkv_low, preferred_element_type=jnp.float32)
    query_value_grad = jnp.concatenate(
        [
            jnp.sum(query_low.astype(jnp.float32), axis=0),
            jnp.sum(value_low.astype(jnp.float32), axis=0),
        ]
    )
    first_grad = jnp.einsum("te,de->td", qkv_low, qkv_back, preferred_element_type=jnp.float32)
    frames_norm, gain_one_grad, shift_one_grad = norm_back(
        first_grad, first_normed, first_inv, gain_one_back
    )
    frames_grad = middle_grad + frames_norm
    summed = (
        lax.psum_scatter(qkv_grad, ("dp", "blk"), scatter_dimension=1, tiled=True),
        lax.psum_scatter(query_value_grad, ("dp", "blk"), scatter_dimension=0, tiled=True),
        lax.psum_scatter(out_grad, ("dp", "blk"), scatter_dimension=1, tiled=True),
        lax.psum_scatter(out_bias_grad, ("dp", "blk"), scatter_dimension=0, tiled=True),
        lax.psum_scatter(up_grad, ("dp", "blk"), scatter_dimension=1, tiled=True),
        lax.psum_scatter(up_bias_grad, ("dp", "blk"), scatter_dimension=0, tiled=True),
        lax.psum_scatter(down_grad, ("dp", "blk"), scatter_dimension=1, tiled=True),
        lax.psum_scatter(down_bias_grad, ("dp", "blk"), scatter_dimension=0, tiled=True),
        lax.psum_scatter(gain_one_grad, ("dp", "blk"), scatter_dimension=0, tiled=True),
        lax.psum_scatter(shift_one_grad, ("dp", "blk"), scatter_dimension=0, tiled=True),
        lax.psum_scatter(gain_two_grad, ("dp", "blk"), scatter_dimension=0, tiled=True),
        lax.psum_scatter(shift_two_grad, ("dp", "blk"), scatter_dimension=0, tiled=True),
    )
    table_sum = lax.psum(table_grad, ("dp", "blk"))
    return (
        layer_out,
        frames_grad,
        summed[0],
        summed[1],
        summed[2],
        summed[3],
        summed[4],
        summed[5],
        summed[6],
        summed[7],
        summed[8],
        summed[9],
        summed[10],
        summed[11],
        table_sum.T,
    )


AXES = ("dp", "blk")
F32 = jnp.float32
LOW = jnp.bfloat16
LANES = 128
NARROW = 6
PAD = 8


def route(move):
    n_dp, n_blk = lax.axis_size("dp"), lax.axis_size("blk")
    pairs = []
    for d in range(n_dp):
        d_bits, b_bits = move[d % 2]
        for b in range(n_blk):
            pairs.append((d * n_blk + b, (d ^ d_bits) * n_blk + (b ^ b_bits)))
    return pairs


def shift(array, move, name="swap"):
    with jax.named_scope(name):
        return lax.ppermute(array, AXES, route(move))


CORE = ((1, 0), (1, 0))
SIDE = ((0, 1), (2, 0))
OTHER_SIDE = ((2, 0), (0, 1))
PACK = ((0, 1), (0, 1))
ALONG_Z = tuple(((4 * turn, 0), (4 * turn, 0)) for turn in (1, 2, 3))


def tied(value, *after):
    return lax.optimization_barrier((value,) + after)[0]


def joined(*groups):
    return lax.optimization_barrier(groups)


def twin(array, name="twin"):
    return shift(array, CORE, name)


def along_z(unit, name):
    return tuple(shift(unit, move, name + "_z") for move in ALONG_Z)


def z_sends(plane, name):
    low = plane.astype(LOW)
    return tuple(shift(low[n + 1], move, name + "_z") for n, move in enumerate(ALONG_Z))


def z_sum(plane, arrived):
    return plane[0] + sum(part.astype(F32) for part in arrived)


def unit_of(place, x_turn, y_turn, z_turn, c):
    x, y, z = place[0] ^ x_turn, place[1] ^ y_turn, place[2] ^ z_turn
    return ((z * 2 + y) * 2 + c) * 2 + x


def each_unit(place, visit):
    def step(z, _):
        for plane in range(2):
            c = place[3] if plane == 0 else 1 - place[3]
            for n, (x_turn, y_turn) in enumerate(((0, 0), (1 - c, c), (c, 1 - c), (1, 1))):
                visit(4 * plane + n, z, unit_of(place, x_turn, y_turn, z, c))
        return 0

    lax.fori_loop(0, 4, step, 0)


def take_columns(place, array, pair, taken, top):
    for c in range(2):

        @pl.when(place[3] == c)
        def _():
            taken[top : top + array.shape[0], :] = jnp.concatenate(
                [
                    array[:, (2 * n + c) * pair : (2 * n + c + 1) * pair]
                    for n in range(array.shape[1] // (2 * pair))
                ],
                axis=1,
            )


def give_units(place, stage, parts):
    c = place[3]
    for part, (x_turn, y_turn) in zip(parts, ((0, 0), (1 - c, c), (c, 1 - c), (1, 1))):
        halves = part if isinstance(part, tuple) else (part,)
        for half, ref in enumerate(halves):
            start = half * ref.shape[0]

            def give(turn, _, ref=ref, start=start, x_turn=x_turn, y_turn=y_turn):
                unit = ((place[2] ^ (start + turn)) * 2 + (place[1] ^ y_turn)) * 2 + (place[0] ^ x_turn)
                ref[turn] = stage[unit].astype(LOW)
                return 0

            lax.fori_loop(0, ref.shape[0], give, 0)


def part_shapes(rows, width):
    return [jax.ShapeDtypeStruct((4, rows, width), LOW)] * 4


def dot_nn(a, b):
    return lax.dot_general(a, b, (((1,), (0,)), ((), ())), preferred_element_type=F32)


def dot_nt(a, b):
    return lax.dot_general(a, b, (((1,), (1,)), ((), ())), preferred_element_type=F32)


def dot_tn(a, b):
    return lax.dot_general(a, b, (((0,), (0,)), ((), ())), preferred_element_type=F32)


HBM = pl.BlockSpec(memory_space=pltpu.HBM)
SMEM = pl.BlockSpec(memory_space=pltpu.SMEM)
VMEM = pl.BlockSpec(memory_space=pltpu.VMEM)


def call(kernel, in_specs, outs, out_specs, scratch, args, flops, limit=56, **kwargs):
    moved = sum(math.prod(a.shape) * a.dtype.itemsize for a in list(args) + list(outs))
    return pl.pallas_call(
        kernel,
        out_shape=outs,
        in_specs=in_specs,
        out_specs=out_specs,
        scratch_shapes=scratch,
        compiler_params=pltpu.CompilerParams(vmem_limit_bytes=limit * 1024 * 1024),
        cost_estimate=pl.CostEstimate(flops=flops, bytes_accessed=moved, transcendentals=0),
        **kwargs,
    )(*args)


def spread_tables(units, width, lanes):
    tables = []
    for n in (width // units, 2 * width // units, 4 * width // units):
        lane = lanes[None, : units * n]
        row = jnp.arange(units + LANES, dtype=jnp.int32)[:, None]
        tables.append(
            jnp.where(row < units, lane // n == row, lane % n == row - units).astype(F32).astype(LOW)
        )
    return tables


def project_kernel(
    place, own, other, p0, p1, p2, p3, p4, p5, p6, p7, wide_one, wide_two, wide_four,
    first, queries, keys, values, vectors, up_bias, mate_live, weight_out, stage, small, weight, sems,
):
    units = stage.shape[0]
    width = own.shape[1]
    rows = stage.shape[1] - PAD
    shard_len = own.shape[0]
    pieces = (p0, p1, p2, p3, p4, p5, p6, p7)

    def fill(array, z, unit):
        stage[unit] = pieces[array][z]

    each_unit(place, fill)

    def normed(frames):
        wide = frames.astype(F32)
        center = wide - jnp.mean(wide, axis=1, keepdims=True)
        return center * lax.rsqrt(jnp.mean(center * center, axis=1, keepdims=True) + EPSILON)

    own_normed, mate_normed = normed(own[...]), normed(other[...])
    for unit in range(units):
        top = stage[unit, rows : rows + PAD, :].astype(F32)
        small[0, unit : unit + 1, :] = top[0:1]
        small[1, unit : unit + 1, :] = top[1:2]

    mate = unit_of(place, 1, 0, 0, place[3])
    mate_live[...] = stage[mate, rows : rows + PAD, : mate_live.shape[1]].astype(F32)

    def spread(row, slot, table):
        held = small[row, :, slot * LANES : (slot + 1) * LANES].astype(LOW)
        laid = dot_nn(held, table[units:, :]) * table[:units, :].astype(F32)
        return jnp.sum(laid, axis=0, keepdims=True)

    for n in range(NARROW):
        vectors[n : n + 1, :] = spread(0, n, wide_one)
    qv_bias = spread(1, 0, wide_two)
    up_bias[...] = jnp.broadcast_to(spread(1, 1, wide_four), up_bias.shape)
    vectors[NARROW : NARROW + 1, :] = qv_bias[:, :width]
    vectors[NARROW + 1 : NARROW + 2, :] = qv_bias[:, width:]

    def join(pair, _):
        both = jnp.concatenate(
            [stage[2 * pair, :rows, :].astype(F32), stage[2 * pair + 1, :rows, :].astype(F32)], axis=0
        )
        weight[pl.ds(pl.multiple_of(2 * rows * pair, 2 * rows), 2 * rows), :] = both.astype(LOW)
        return 0

    lax.fori_loop(0, units // 2, join, 0)
    copy = pltpu.make_async_copy(weight, weight_out, sems.at[0])
    copy.start()
    gain, offset = vectors[0:1, :], vectors[1:2, :]
    x = place[0]
    own_at = pl.multiple_of(x * shard_len, shard_len)
    mate_at = pl.multiple_of((1 - x) * shard_len, shard_len)
    first[pl.ds(own_at, shard_len), :] = (own_normed * gain + offset).astype(LOW)
    first[pl.ds(mate_at, shard_len), :] = (mate_normed * gain + offset).astype(LOW)
    mine = first[pl.ds(own_at, shard_len), :]
    queries[...] = (dot_nt(mine, weight[:width, :]) + vectors[NARROW : NARROW + 1, :]).astype(LOW)
    keys[...] = dot_nt(first[...], weight[width : 2 * width, :]).astype(LOW)
    values[...] = (
        dot_nt(first[...], weight[2 * width :, :]) + vectors[NARROW + 1 : NARROW + 2, :]
    ).astype(LOW)
    copy.wait()


def half_mask(shape, head):
    return (lax.broadcasted_iota(jnp.int32, shape, 1) // HD) == head


def bias_kernel(curve, bias):
    heads, block_len, span = bias.shape

    def shear(head, _):
        bias[head] = pltpu.roll(
            jnp.broadcast_to(curve[pl.ds(head, 1), :], (block_len, block_len + span)),
            span + 1, 1, stride=1, stride_axis=0,
        )[:, :span].astype(LOW)
        return 0

    lax.fori_loop(0, heads, shear, 0)


def attend_kernel(
    place, lengths, queries, keys, values, bias, own_live, mate_live, probs, mixed, hidden_pairs
):
    block_len, span = hidden_pairs.shape

    @pl.when(pl.program_id(0) == 0)
    def _():
        start = place[0] * block_len
        key_pos = lax.broadcasted_iota(jnp.int32, (1, span), 1)
        query_pos = lax.broadcasted_iota(jnp.int32, (block_len, 1), 0) + start
        key_doc, query_doc = jnp.zeros_like(key_pos), jnp.zeros_like(query_pos)
        end = 0
        for n in range(lengths.shape[1]):
            end = end + lengths[0, n]
            key_doc = key_doc + (key_pos >= end).astype(jnp.int32)
            query_doc = query_doc + (query_pos >= end).astype(jnp.int32)
        one, two = own_live[...].astype(F32), mate_live[2:3, :]
        live = jnp.where(
            place[0] == 0, jnp.concatenate([one, two], axis=1), jnp.concatenate([two, one], axis=1)
        )
        allowed = (query_doc == key_doc) & ((live > 0.5) | (query_pos == key_pos))
        hidden_pairs[...] = jnp.where(allowed, 0.0, MASKED)

    for pair in range(queries.shape[1] // (2 * HD)):
        lane = slice(2 * HD * pair, 2 * HD * (pair + 1))
        q, k, v = queries[:, lane], keys[:, lane], values[:, lane]
        total = jnp.zeros(q.shape, F32)
        for head in range(2):
            n = 2 * pair + head
            q_head = jnp.where(half_mask(q.shape, head), q, 0) * (1.0 / math.sqrt(HD))
            logits = dot_nt(q_head.astype(LOW), k) + bias[n].astype(F32) + hidden_pairs[...]
            weights = jnp.exp(logits - jnp.max(logits, axis=1, keepdims=True))
            prob = (weights * (1.0 / jnp.sum(weights, axis=1, keepdims=True))).astype(LOW)
            probs[n] = prob
            total = total + dot_nn(prob, jnp.where(half_mask(v.shape, head), v, 0))
        mixed[:, lane] = total


def join_units(kept, out):
    units = kept.shape[0]
    each = out.shape[0] // units

    def join(pair, _):
        both = jnp.concatenate(
            [kept[2 * pair].astype(F32)[:each], kept[2 * pair + 1].astype(F32)[:each]], axis=0
        )
        out[pl.ds(pl.multiple_of(2 * each * pair, 2 * each), 2 * each), :] = both.astype(LOW)
        return 0

    lax.fori_loop(0, units // 2, join, 0)


def expand_kernel(
    place, frames, mixed, vectors, up_bias, p0, p1, p2, p3, p4, p5, p6, p7,
    middle, second, context, active, slope, up, kept, out,
):
    width = frames.shape[1]
    pieces = (p0, p1, p2, p3, p4, p5, p6, p7)
    rows = p0.shape[1] - kept.shape[1]

    def fill(array, z, unit):
        kept[unit] = pieces[array][z, rows:]
        up[pl.ds(pl.multiple_of(unit * rows, rows), rows), :] = pieces[array][z, :rows]

    each_unit(place, fill)
    context[...] = mixed[...].astype(LOW)
    join_units(kept, out)
    mid = frames[...].astype(F32) + (dot_nt(context[...], out[...]) + vectors[4:5, :])
    middle[...] = mid
    center = mid - jnp.mean(mid, axis=1, keepdims=True)
    normed = center * lax.rsqrt(jnp.mean(center * center, axis=1, keepdims=True) + EPSILON)
    second[...] = (normed * vectors[2:3, :] + vectors[3:4, :]).astype(LOW)
    for n in range(up.shape[0] // width):
        at = slice(n * width, (n + 1) * width)
        hidden = dot_nt(second[...], up[at, :]) + up_bias[0:1, at]
        cdf = 0.5 * (1.0 + lax.erf(hidden * 0.7071067811865476))
        density = jnp.exp(-0.5 * hidden * hidden) * 0.3989422804014327
        active[:, at] = (hidden * cdf).astype(LOW)
        slope[:, at] = cdf + hidden * density


def down_grad_kernel(
    place, active, active_twin, cotangent, cotangent_twin, o0, o1, o2, o3, bias_grad, taken, wide,
):
    units, rows, width = wide.shape
    each = width // (2 * units)
    bias_grad[...] = jnp.broadcast_to(
        jnp.sum(cotangent[...].astype(F32), axis=0, keepdims=True), bias_grad.shape
    )

    shard_len = cotangent.shape[0]
    take_columns(place, cotangent, 2 * each, taken, 0)
    take_columns(place, cotangent_twin, 2 * each, taken, shard_len)
    dy, dy_twin = taken[:shard_len, :], taken[shard_len:, :]
    for fold in range(rows // each):
        at = slice(fold * width, (fold + 1) * width)
        grad = dot_tn(dy, active[:, at]) + dot_tn(dy_twin, active_twin[:, at])
        for unit in range(units):
            wide[unit, fold * each : (fold + 1) * each, :] = grad[unit * each : (unit + 1) * each]
    give_units(place, wide, (o0, o1, o2, o3))


def unfold_units(stage, down):
    units, rows, width = stage.shape
    each = down.shape[0] // units

    def unfold(pair, _):
        one, two = stage[2 * pair].astype(F32), stage[2 * pair + 1].astype(F32)
        at = pl.multiple_of(2 * each * pair, 2 * each)
        for fold in range(rows // each):
            both = jnp.concatenate(
                [one[fold * each : (fold + 1) * each], two[fold * each : (fold + 1) * each]], axis=0
            )
            down[pl.ds(at, 2 * each), fold * width : (fold + 1) * width] = both.astype(LOW)
        return 0

    lax.fori_loop(0, units // 2, unfold, 0)


def back_kernel(
    place, cotangent, slope, middle, vectors, p0, p1, p2, p3, p4, p5, p6, p7, u0, u1, u2, u3, u4, u5, u6, u7,
    middle_grad, context_grad, vector_grads, branch_grad, up_bias_grad, hidden_grad,
    stage, down, up, kept, out,
):
    width = cotangent.shape[1]
    down_pieces, up_pieces = (p0, p1, p2, p3, p4, p5, p6, p7), (u0, u1, u2, u3, u4, u5, u6, u7)
    rows = u0.shape[1] - kept.shape[1]

    def fill(array, z, unit):
        stage[unit] = down_pieces[array][z]
        kept[unit] = up_pieces[array][z, rows:]
        up[pl.ds(pl.multiple_of(unit * rows, rows), rows), :] = up_pieces[array][z, :rows]

    each_unit(place, fill)
    unfold_units(stage, down)
    dy = cotangent[...]
    for n in range(hidden_grad.shape[1] // width):
        at = slice(n * width, (n + 1) * width)
        grad = (dot_nn(dy, down[:, at]) * slope[:, at]).astype(LOW)
        hidden_grad[:, at] = grad
        up_bias_grad[:, at] = jnp.broadcast_to(
            jnp.sum(grad.astype(F32), axis=0, keepdims=True), (up_bias_grad.shape[0], width)
        )
    join_units(kept, out)
    second_grad = dot_nn(hidden_grad[...], up[...])
    mid = middle[...]
    center = mid - jnp.mean(mid, axis=1, keepdims=True)
    inv_std = lax.rsqrt(jnp.mean(center * center, axis=1, keepdims=True) + EPSILON)
    normed = center * inv_std
    scaled = second_grad * vectors[2:3, :]
    inner = (
        scaled
        - jnp.mean(scaled, axis=1, keepdims=True)
        - normed * jnp.mean(scaled * normed, axis=1, keepdims=True)
    )
    mid_grad = cotangent[...].astype(F32) + inner * inv_std
    middle_grad[...] = mid_grad
    branch = mid_grad.astype(LOW)
    vector_grads[...] = jnp.concatenate(
        [
            jnp.sum(second_grad * normed, axis=0, keepdims=True),
            jnp.sum(second_grad, axis=0, keepdims=True),
            jnp.sum(branch.astype(F32), axis=0, keepdims=True),
            jnp.zeros((5, width), F32),
        ],
        axis=0,
    )
    branch_grad[...] = branch
    context_grad[...] = dot_nn(branch, out[...]).astype(LOW)


def up_grad_kernel(
    place, hidden, hidden_twin, second, second_twin, branch, branch_twin, context, context_twin,
    o0, o1, o2, o3, o4, taken, taken_branch, stage,
):
    units, rows, width = stage.shape
    each = width // (2 * units)
    up_rows = hidden.shape[1] // (2 * units)

    shard_len = second.shape[0]
    take_columns(place, branch, 2 * each, taken_branch, 0)
    take_columns(place, branch_twin, 2 * each, taken_branch, shard_len)
    take_columns(place, hidden, 2 * up_rows, taken, 0)
    take_columns(place, hidden_twin, 2 * up_rows, taken, shard_len)
    out_grad = dot_tn(taken_branch[:shard_len, :], context[...]) + dot_tn(
        taken_branch[shard_len:, :], context_twin[...]
    )
    blank = jnp.zeros((rows - up_rows - each, width), F32)
    quarter = units // 4
    for z in range(4):
        at = slice(z * quarter * up_rows, (z + 1) * quarter * up_rows)
        grad = dot_tn(taken[:shard_len, at], second[...]) + dot_tn(taken[shard_len:, at], second_twin[...])
        for n in range(quarter):
            unit = z * quarter + n
            stage[unit] = jnp.concatenate(
                [
                    grad[n * up_rows : (n + 1) * up_rows],
                    out_grad[unit * each : (unit + 1) * each],
                    blank,
                ],
                axis=0,
            ).astype(LOW)
    give_units(place, stage, (o0, o1, (o2, o3), o4))


def rows_left(each):
    return -each % 16


def finish_kernel(
    place, active, middle, vectors, p0, p1, p2, p3, p4, p5, p6, p7, layer_out, stage, down
):
    pieces = (p0, p1, p2, p3, p4, p5, p6, p7)

    def fill(array, z, unit):
        stage[unit] = pieces[array][z]

    each_unit(place, fill)
    unfold_units(stage, down)
    layer_out[...] = middle[...] + dot_nt(active[...], down[...]) + vectors[5:6, :]


def attend_back_kernel(
    place, queries, keys, values, context_grad, mixed, probs, grads, diagonals
):
    q, k, v, dout = queries[...], keys[...], values[...], context_grad[...]
    block_len, span = probs.shape[1:]
    weighted = dout.astype(F32) * mixed[...]
    row = lax.broadcasted_iota(jnp.int32, (block_len, block_len), 0)
    lane = lax.broadcasted_iota(jnp.int32, (block_len, block_len), 1)
    turn = (row + lane == block_len - 1).astype(LOW)
    blank = jnp.zeros((block_len, block_len), F32)
    dq, dk, dv = jnp.zeros(q.shape, F32), jnp.zeros(k.shape, F32), jnp.zeros(v.shape, F32)
    for head in range(2):
        mine = half_mask(q.shape, head)
        dout_head = jnp.where(mine, dout, 0)
        delta = jnp.sum(jnp.where(mine, weighted, 0.0), axis=1, keepdims=True)
        prob = probs[head]
        grad = prob.astype(F32) * (dot_nt(dout_head, v) - delta)
        raw = (grad * (1.0 / math.sqrt(HD))).astype(LOW)
        dq = dq + dot_nn(raw, jnp.where(half_mask(k.shape, head), k, 0))
        dk = dk + dot_tn(raw, jnp.where(mine, q, 0))
        dv = dv + dot_tn(prob, dout_head)
        turned = jnp.concatenate([dot_nn(turn, raw), blank], axis=1)
        sheared = pltpu.roll(turned, 0, 1, stride=1, stride_axis=0)
        diagonals[pl.ds(2 * pl.program_id(0) + head, 1), :] = jnp.sum(sheared, axis=0, keepdims=True) * math.sqrt(HD)
    own_at = pl.multiple_of(place[0] * block_len, block_len)
    grads[0] = jnp.zeros(k.shape, LOW)
    grads[0, pl.ds(own_at, block_len), :] = dq.astype(LOW)
    grads[1] = dk.astype(LOW)
    grads[2] = dv.astype(LOW)


def total(array):
    return jnp.sum(array, axis=0, keepdims=True)


def norm_parts(frames):
    wide = frames.astype(F32)
    center = wide - jnp.mean(wide, axis=1, keepdims=True)
    inv_std = lax.rsqrt(jnp.mean(center * center, axis=1, keepdims=True) + EPSILON)
    return center * inv_std, inv_std


def first_grad_kernel(
    place, own_frames, mate_frames, grads, weight_in, diagonals, vector_grads, down_bias_grad, up_bias_grad,
    own_grad, mate_grad, small, weight, sems,
):
    copy = pltpu.make_async_copy(weight_in, weight, sems.at[0])
    copy.start()
    shard_len, width = own_frames.shape
    x = place[0]
    own_at = pl.multiple_of(x * shard_len, shard_len)
    mate_at = pl.multiple_of((1 - x) * shard_len, shard_len)
    own_normed, _ = norm_parts(own_frames[...])
    mate_normed, _ = norm_parts(mate_frames[...])
    dq = grads[0, pl.ds(own_at, shard_len), :]
    small[4:5, :] = vector_grads[2:3, :]
    small[2:4, :] = vector_grads[0:2, :]
    small[5:6, :] = down_bias_grad[0:1, :]
    small[6:7, :] = total(dq.astype(F32))
    small[7:8, :] = total(grads[2].astype(F32))
    for n in range(up_bias_grad.shape[1] // width):
        small[8 + n : 9 + n, :] = up_bias_grad[0:1, n * width : (n + 1) * width]
    small[12:, :] = diagonals[...]
    copy.wait()

    def from_keys(at):
        return dot_nn(grads[1, pl.ds(at, shard_len), :], weight[width : 2 * width, :]) + dot_nn(
            grads[2, pl.ds(at, shard_len), :], weight[2 * width :, :]
        )

    of_own = from_keys(own_at) + dot_nn(dq, weight[:width, :])
    of_mate = from_keys(mate_at)
    own_grad[...] = of_own
    mate_grad[...] = of_mate
    small[0:1, :] = total(of_own * own_normed) + total(of_mate * mate_normed)
    small[1:2, :] = total(of_own) + total(of_mate)


def qkv_grad_kernel(
    place, grads, grads_twin, first, first_twin, small_own, small_twin, wide_one, wide_two, wide_four,
    o0, o1, o2, o3, taken, sums, small, tables, stage,
):
    units, full, width = stage.shape
    rows = full - PAD
    span = first.shape[0]
    shard_len = span // 2
    x = place[0]
    summed = small_own[...] + small_twin[...]

    def fold(vector, table):
        kept = (vector * table[: 2 * units, :].astype(F32)).astype(LOW)
        return dot_nt(kept, table[2 * units :, :])

    for n in range(NARROW):
        small[0, :, n * LANES : (n + 1) * LANES] = fold(summed[n : n + 1, :], wide_one)
    small[1, :, :] = jnp.zeros((2 * units, width), F32)
    both = jnp.concatenate([summed[6:7, :], summed[7:8, :]], axis=1)
    small[1, :, :LANES] = fold(both, wide_two)
    four = jnp.concatenate([summed[8 + n : 9 + n, :] for n in range(4)], axis=1)
    small[1, :, LANES : 2 * LANES] = fold(four, wide_four)
    lanes = 3 * LANES
    distance = (
        lax.broadcasted_iota(jnp.int32, (shard_len + span, lanes), 0) - (shard_len - 1) - x * shard_len
    )
    bucket = jnp.clip(distance, -MAXREL, MAXREL) + MAXREL
    here = (bucket == lax.broadcasted_iota(jnp.int32, (shard_len + span, lanes), 1)).astype(F32).astype(LOW)
    diagonals = summed[12:, :]
    high = diagonals.astype(LOW)
    table = dot_nn(high, here) + dot_nn((diagonals - high.astype(F32)).astype(LOW), here)
    table = jnp.concatenate([table[: H // 2], table[H // 2 :]], axis=1)
    for n, array in enumerate((grads, grads_twin)):
        columns = jnp.concatenate([array[part] for part in range(3)], axis=1)
        take_columns(place, columns, 2 * rows, taken, n * span)
    sums[...] = dot_tn(taken[:span, :], first[...]) + dot_tn(taken[span:, :], first_twin[...])

    def pack(unit, _):
        at = 4 * (unit // 2) + 2 * place[3] + unit % 2
        stage[unit] = jnp.concatenate(
            [
                sums[pl.ds(pl.multiple_of(unit * rows, rows), rows), :],
                small[0, pl.ds(at, 1), :],
                small[1, pl.ds(at, 1), :],
                tables[...],
            ],
            axis=0,
        ).astype(LOW)
        return 0

    tables[...] = table
    lax.fori_loop(0, units, pack, 0)
    give_units(place, stage, (o0, o1, o2, o3))


def input_grad_kernel(frames, mate_frames, own_grad, mate_grad, middle_grad, vectors, own_part, mate_part):
    def through_norm(of_frames, grad):
        normed, inv_std = norm_parts(of_frames)
        scaled = grad * vectors[0:1, :]
        inner = (
            scaled
            - jnp.mean(scaled, axis=1, keepdims=True)
            - normed * jnp.mean(scaled * normed, axis=1, keepdims=True)
        )
        return inner * inv_std

    own_part[...] = middle_grad[...] + through_norm(frames[...], own_grad[...])
    mate_part[...] = through_norm(mate_frames[...], mate_grad[...]).astype(LOW)


def last_kernel(
    own, z1, z2, z3, own_part, mate_part, qkv, qv_bias, up_bias, table, frames_grad, n0, n1, n2, n3, n4, n5
):
    frames_grad[...] = own_part[...] + mate_part[...].astype(F32)
    rows = qkv.shape[0]
    total = own[...] + z1[...].astype(F32) + z2[...].astype(F32) + z3[...].astype(F32)
    qkv[...] = total[:rows]
    for n, narrow in enumerate((n0, n1, n2, n3, n4, n5)):
        narrow[...] = total[rows : rows + 1, n * LANES : n * LANES + narrow.shape[1]]
    qv_bias[...] = total[rows + 1 : rows + 2, : qv_bias.shape[1]]
    up_bias[...] = total[rows + 1 : rows + 2, LANES : LANES + up_bias.shape[1]]
    for half in range(2):
        at = 3 * LANES * half
        table[half * (H // 2) : (half + 1) * (H // 2), :] = total[rows + 2 : rows + PAD, at : at + BUCKETS]


def pack_kernel(
    live, qkv, out, up, down, first_gain, first_shift, second_gain, second_shift, out_bias,
    down_bias, qv_bias, up_bias, qkv_unit, up_unit, down_unit,
):
    each, width = out.shape

    def slots(vectors):
        parts = []
        for vector in vectors:
            wide = vector[...].astype(F32)
            parts += [wide, jnp.zeros((1, LANES - wide.shape[1]), F32)]
        left = width - LANES * len(vectors)
        if left:
            parts.append(jnp.zeros((1, left), F32))
        return jnp.concatenate(parts, axis=1)

    narrow = slots((first_gain, first_shift, second_gain, second_shift, out_bias, down_bias))
    wide = slots((qv_bias, up_bias))
    seen = live[...].astype(F32)
    seen = jnp.concatenate([seen, jnp.zeros((1, width - seen.shape[1]), F32)], axis=1)
    blank = jnp.zeros((PAD - 3, width), F32)
    qkv_unit[...] = jnp.concatenate([qkv[...].astype(F32), narrow, wide, seen, blank], axis=0).astype(LOW)
    blank = jnp.zeros((up_unit.shape[0] - up.shape[0] - each, width), F32)
    up_unit[...] = jnp.concatenate(
        [up[...].astype(F32), out[...].astype(F32), blank], axis=0
    ).astype(LOW)
    down_unit[...] = jnp.concatenate(
        [
            down[:, fold * width : (fold + 1) * width].astype(F32)
            for fold in range(down.shape[1] // width)
        ],
        axis=0,
    ).astype(LOW)


def paired_body(
    frames, cotangent, seq_lengths, key_mask, qkv_weight, query_value_bias, out_weight, out_bias,
    up_weight, up_bias, down_weight, down_bias, first_gain, first_shift, second_gain, second_shift,
    rel_bias,
):
    shard_len, width = frames.shape
    x = lax.axis_index("blk")
    d = lax.axis_index("dp")
    core = d % 2
    units = lax.axis_size("dp") * lax.axis_size("blk")
    span = shard_len * lax.axis_size("blk")
    place = jnp.stack([x, (d // 2) % 2, d // 4, core]).astype(jnp.int32)
    each = width // units
    ff = up_weight.shape[1] * units
    qkv_rows, up_rows = qkv_weight.shape[1], up_weight.shape[1]
    folds = ff // width
    down_rows = each * folds
    out_rows = each + rows_left(each)

    def shape(*dims, kind=LOW):
        return jax.ShapeDtypeStruct(dims, kind)

    def row(vector):
        return vector.reshape(1, vector.shape[0])

    packed = (
        row(key_mask), qkv_weight.T, out_weight.T, up_weight.T, down_weight.T, row(first_gain),
        row(first_shift), row(second_gain), row(second_shift), row(out_bias), row(down_bias),
        row(query_value_bias), row(up_bias),
    )
    qkv_unit, up_unit, down_unit = call(
        pack_kernel,
        [VMEM] * len(packed),
        [shape(qkv_rows + PAD, width), shape(up_rows + out_rows, width), shape(down_rows, width)],
        [VMEM] * 3,
        [],
        packed,
        0,
        name="pack",
    )
    def twins(pieces):
        return tuple(pieces) + tuple(twin(piece) for piece in pieces)

    distance = jnp.arange(span + shard_len, dtype=jnp.int32) - (shard_len - 1) - x * shard_len
    bucket = jnp.clip(distance, -MAXREL, MAXREL) + MAXREL
    bucket_lanes = 3 * LANES
    buckets = (bucket[:, None] == jnp.arange(bucket_lanes, dtype=jnp.int32)[None, :]).astype(LOW)
    curve = lax.dot_general(
        rel_bias, buckets[:, :BUCKETS], (((0,), (1,)), ((), ())), preferred_element_type=F32
    )
    bias = call(
        bias_kernel, [VMEM], [shape(H, shard_len, span)], [VMEM], [], (tied(curve, qkv_unit),), 0, name="bias"
    )[0]
    spreads = spread_tables(units, width, tied(jnp.arange(ff, dtype=jnp.int32), qkv_unit))
    cotangent_twin = twin(cotangent)
    qkv_z = along_z(qkv_unit, "qkv")
    mate_frames = shift(tied(frames, qkv_unit), PACK, "frames_pack")
    qkv_z, mate_frames, bias, place, spreads = joined(qkv_z, mate_frames, bias, place, spreads)
    qkv_own = jnp.stack((qkv_unit,) + qkv_z)
    qkv_side = shift(qkv_own, SIDE, "qkv_1")
    up_first = tied(up_unit, *qkv_z)
    up_z = [shift(up_first, move, "up_z") for move in ALONG_Z[:2]]
    qkv_side, up_z, cotangent_twin = joined(qkv_side, up_z, cotangent_twin)
    qkv_other = shift(qkv_own, OTHER_SIDE, "qkv_2")
    qkv_across = shift(qkv_side, OTHER_SIDE, "qkv_3")
    up_z.append(shift(tied(up_unit, qkv_side), ALONG_Z[2], "up_z"))
    up_z, qkv_other, qkv_across = joined(up_z, qkv_other, qkv_across)
    qkv_pieces = twins((qkv_own, qkv_side, qkv_other, qkv_across))
    up_own = jnp.stack([up_unit] + up_z)
    up_side = shift(up_own, SIDE, "up_1")
    down_first = tied(down_unit, up_own)
    down_z = [shift(down_first, move, "down_z") for move in ALONG_Z[:2]]

    unit_sems = pltpu.SemaphoreType.DMA((units,))
    first, queries, keys, values, vectors, up_bias_all, mate_live, weight = call(
        project_kernel,
        [SMEM] + [VMEM] * 13,
        [
            shape(span, width), shape(shard_len, width), shape(span, width), shape(span, width),
            shape(8, width, kind=F32), shape(8, ff, kind=F32), shape(PAD, shard_len, kind=F32),
            shape(3 * width, width),
        ],
        [VMEM] * 7 + [HBM],
        [
            pltpu.VMEM((units, qkv_rows + PAD, width), LOW), pltpu.VMEM((2, units, width), F32),
            pltpu.VMEM((3 * width, width), LOW), pltpu.SemaphoreType.DMA((1,)),
        ],
        (tied(place, up_own), frames, mate_frames) + qkv_pieces + tuple(spreads),
        2 * shard_len * width * 5 * width,
        name="project",
    )
    up_side, keys, down_z = joined(up_side, keys, down_z)
    up_other = shift(up_own, OTHER_SIDE, "up_2")
    up_across = shift(up_side, OTHER_SIDE, "up_3")
    down_z.append(shift(tied(down_unit, keys), ALONG_Z[2], "down_z"))
    pairs = H // 2
    pair_lanes = 2 * HD

    def lanes_of(rows, count=1):
        return pl.BlockSpec((rows, count * pair_lanes), lambda n: (0, n))

    def heads_of(*dims):
        return pl.BlockSpec(dims, lambda n: (n,) + (0,) * (len(dims) - 1))

    def whole(*dims):
        return pl.BlockSpec(dims, lambda n: (0,) * len(dims))

    probs, mixed = call(
        attend_kernel,
        [
            SMEM, SMEM, lanes_of(shard_len, 2), lanes_of(span, 2), lanes_of(span, 2),
            heads_of(4, shard_len, span), whole(1, shard_len), whole(PAD, shard_len),
        ],
        [shape(H, shard_len, span), shape(shard_len, width, kind=F32)],
        [heads_of(4, shard_len, span), lanes_of(shard_len, 2)],
        [pltpu.VMEM((shard_len, span), F32)],
        (
            tied(place, up_side), seq_lengths, queries, keys, values, bias, row(key_mask), mate_live,
        ),
        8 * shard_len * span * width,
        grid=(pairs // 2,),
        name="attend",
    )
    up_other, up_across, mixed, down_z = joined(up_other, up_across, mixed, down_z)
    up_pieces = twins((up_own, up_side, up_other, up_across))
    down_own = jnp.stack([down_unit] + down_z)
    down_side = shift(down_own, SIDE, "down_1")
    down_other = shift(down_own, OTHER_SIDE, "down_2")
    middle, second, context, active, slope = call(
        expand_kernel,
        [SMEM] + [VMEM] * 12,
        [
            shape(shard_len, width, kind=F32), shape(shard_len, width), shape(shard_len, width),
            shape(shard_len, ff), shape(shard_len, ff, kind=F32),
        ],
        [VMEM] * 5,
        [
            pltpu.VMEM((ff, width), LOW), pltpu.VMEM((units, out_rows, width), LOW),
            pltpu.VMEM((width, width), LOW),
        ],
        (tied(place, down_own), frames, mixed, vectors, up_bias_all) + up_pieces,
        2 * shard_len * width * (width + ff),
        name="expand", limit=36,
    )
    down_side, down_other, active = joined(down_side, down_other, active)
    down_across = shift(down_side, OTHER_SIDE, "down_3")
    active_twin, context_twin, second_twin = twin(active), twin(context), twin(second)
    first_twin = twin(first)
    down_parts = call(
        down_grad_kernel,
        [SMEM] + [VMEM] * 4,
        part_shapes(down_rows, width) + [shape(8, width, kind=F32)],
        [VMEM] * 5,
        [
            pltpu.VMEM((span, width // 2), LOW), pltpu.VMEM((units // 2, down_rows, width), F32),
        ],
        (tied(place, down_side), active, active_twin, cotangent, cotangent_twin),
        2 * shard_len * width * ff,
        name="down_grad", limit=24,
    )
    down_across, down_parts = joined(down_across, down_parts)
    down_bias_grad = down_parts[4]
    down_pieces = twins((down_own, down_side, down_other, down_across))
    turned = shift(down_parts[3], OTHER_SIDE, "rs_down_3")
    down_two = shift(down_parts[2], OTHER_SIDE, "rs_down_2")
    middle_grad, context_grad, vector_grads, branch_grad, up_bias_grad, hidden_grad = call(
        back_kernel,
        [SMEM] + [VMEM] * 20,
        [
            shape(shard_len, width, kind=F32), shape(shard_len, width), shape(8, width, kind=F32),
            shape(shard_len, width), shape(8, ff, kind=F32), shape(shard_len, ff),
        ],
        [VMEM] * 6,
        [
            pltpu.VMEM((units, down_rows, width), LOW), pltpu.VMEM((width, ff), LOW),
            pltpu.VMEM((ff, width), LOW), pltpu.VMEM((units, out_rows, width), LOW),
            pltpu.VMEM((width, width), LOW),
        ],
        (tied(place, down_parts[0]), cotangent, slope, middle, vectors) + down_pieces + up_pieces,
        2 * shard_len * width * (2 * ff + width),
        name="back", limit=48,
    )
    turned, down_two, hidden_grad, context_twin, second_twin, first_twin = joined(
        turned, down_two, hidden_grad, context_twin, second_twin, first_twin
    )
    side = (down_parts[1].astype(F32) + turned.astype(F32)).astype(LOW)
    down_one = shift(side, SIDE, "rs_down_1")
    hidden_twin = twin(hidden_grad)
    branch_twin = twin(branch_grad)
    down_sum = down_parts[0].astype(F32) + down_two.astype(F32)
    up_parts = call(
        up_grad_kernel,
        [SMEM] + [VMEM] * 8,
        [shape(n, up_rows + out_rows, width) for n in (4, 4, 2, 2, 4)],
        [VMEM] * 5,
        [
            pltpu.VMEM((span, ff // 2), LOW), pltpu.VMEM((span, width // 2), LOW),
            pltpu.VMEM((units // 2, up_rows + out_rows, width), LOW),
        ],
        (
            tied(place, down_sum, side), hidden_grad, hidden_twin, second, second_twin, branch_grad, branch_twin,
            context, context_twin,
        ),
        2 * shard_len * width * (ff + width),
        name="up_grad", limit=28,
    )
    down_one = tied(down_one, up_parts[0])
    turned = shift(up_parts[4], OTHER_SIDE, "rs_up_3")
    up_two = shift(up_parts[2], OTHER_SIDE, "rs_up_2a")
    down_sum = down_sum + down_one.astype(F32)
    down_low = down_sum.astype(LOW)
    down_z = [shift(down_low[n + 1], ALONG_Z[n], "rs_down_z") for n in range(2)]
    grads, diagonals = call(
        attend_back_kernel,
        [
            SMEM, lanes_of(shard_len), lanes_of(span), lanes_of(span), lanes_of(shard_len), lanes_of(shard_len),
            heads_of(2, shard_len, span),
        ],
        [shape(3, span, width), shape(H, span + shard_len, kind=F32)],
        [pl.BlockSpec((3, span, pair_lanes), lambda n: (0, 0, n)), whole(H, span + shard_len)],
        [],
        (place, queries, keys, values, tied(context_grad, up_parts[0], down_sum), mixed, probs),
        16 * shard_len * span * width,
        grid=(pairs,),
        name="attend_back", limit=24,
    )
    turned, up_two, down_z, grads = joined(turned, up_two, down_z, grads)
    up_rest = shift(up_parts[3], OTHER_SIDE, "rs_up_2b")
    grads_twin = twin(grads)
    side = (up_parts[1].astype(F32) + turned.astype(F32)).astype(LOW)
    up_one = shift(side, SIDE, "rs_up_1")
    own_grad, mate_grad, small = call(
        first_grad_kernel,
        [SMEM] + [VMEM] * 3 + [HBM] + [VMEM] * 4,
        [
            shape(shard_len, width, kind=F32), shape(shard_len, width, kind=F32),
            shape(12 + H, width, kind=F32),
        ],
        [VMEM] * 3,
        [pltpu.VMEM((3 * width, width), LOW), pltpu.SemaphoreType.DMA((1,))],
        (
            tied(place, side), frames, mate_frames, grads, weight, diagonals, vector_grads,
            down_bias_grad, up_bias_grad,
        ),
        2 * shard_len * width * 5 * width,
        name="first_grad", limit=24,
    )
    grads_twin, small = joined(grads_twin, small)
    down_z.append(shift(tied(down_low[3], small), ALONG_Z[2], "rs_down_z"))
    small_twin = twin(small)
    qkv_parts = call(
        qkv_grad_kernel,
        [SMEM] + [VMEM] * 9,
        part_shapes(qkv_rows + PAD, width),
        [VMEM] * 4,
        [
            pltpu.VMEM((2 * span, 3 * width // 2), LOW), pltpu.VMEM((3 * width // 2, width), F32),
            pltpu.VMEM((2, units, width), F32), pltpu.VMEM((H // 2, width), F32),
            pltpu.VMEM((units // 2, qkv_rows + PAD, width), LOW),
        ],
        (place, grads, grads_twin, first, first_twin, small, small_twin) + tuple(spreads),
        2 * shard_len * width * 6 * width,
        name="qkv_grad", limit=28,
    )
    up_one, up_rest, down_z = tied((up_one, up_rest, down_z), qkv_parts[0])
    turned = shift(qkv_parts[3], OTHER_SIDE, "rs_qkv_3")
    qkv_two = shift(qkv_parts[2], OTHER_SIDE, "rs_qkv_2")
    up_sum = [
        up_parts[0][n].astype(F32) + up_one[n].astype(F32) + (up_two, up_rest)[n // 2][n % 2].astype(F32)
        for n in range(4)
    ]
    up_low = [part.astype(LOW) for part in up_sum]
    up_z = [shift(up_low[n + 1], ALONG_Z[n], "rs_up_z") for n in range(2)]
    down_sum = z_sum(down_sum, down_z)
    own_part, mate_part = call(
        input_grad_kernel,
        [VMEM] * 6,
        [shape(shard_len, width, kind=F32), shape(shard_len, width)],
        [VMEM] * 2,
        [],
        (frames, mate_frames, own_grad, tied(mate_grad, *up_low), middle_grad, vectors),
        0,
        name="input_grad", limit=12,
    )
    turned, mate_part = joined(turned, mate_part)
    side = (qkv_parts[1].astype(F32) + turned.astype(F32)).astype(LOW)
    qkv_one = shift(side, SIDE, "rs_qkv_1")
    up_z, side_after = joined(up_z, side)
    up_z.append(shift(tied(up_low[3], side_after), ALONG_Z[2], "rs_up_z"))
    layer_out = call(
        finish_kernel,
        [SMEM] + [VMEM] * 11,
        [shape(shard_len, width, kind=F32)],
        [VMEM],
        [pltpu.VMEM((units, down_rows, width), LOW), pltpu.VMEM((width, ff), LOW)],
        (tied(place, side_after), active, middle, vectors) + down_pieces,
        2 * shard_len * width * ff,
        name="finish",
    )[0]
    qkv_one, qkv_two, up_z, layer_out = joined(qkv_one, qkv_two, up_z, layer_out)
    qkv_sum = qkv_parts[0].astype(F32) + qkv_one.astype(F32) + qkv_two.astype(F32)
    qkv_z = z_sends(qkv_sum, "rs_qkv")
    up_sum = z_sum(tied(up_sum[:1], qkv_sum), up_z)
    mate_part = shift(tied(mate_part, up_sum), PACK, "grad_pack")
    last = call(
        last_kernel,
        [VMEM] * 6,
        [
            shape(qkv_rows, width, kind=F32), shape(1, 2 * each, kind=F32), shape(1, up_rows, kind=F32),
            shape(H, BUCKETS, kind=F32), shape(shard_len, width, kind=F32),
        ]
        + [shape(1, each, kind=F32)] * NARROW,
        [VMEM] * (5 + NARROW),
        [],
        (qkv_sum[0],) + tuple(qkv_z) + (own_part, mate_part),
        0,
        name="last", limit=8,
    )
    qkv_grad, qv_bias_grad, up_bias_sum, table, frames_grad = last[:5]
    pieces = [piece.reshape(each) for piece in last[5:]]

    down_grad = jnp.concatenate(
        [down_sum[fold * each : (fold + 1) * each] for fold in range(folds)], axis=1
    )
    return (
        layer_out, frames_grad, qkv_grad.T, qv_bias_grad.reshape(2 * each),
        up_sum[up_rows : up_rows + each].T, pieces[4], up_sum[:up_rows].T, up_bias_sum.reshape(up_rows),
        down_grad.T, pieces[5], pieces[0], pieces[1], pieces[2], pieces[3], table.T,
    )


def paired(mesh):
    return mesh.shape["blk"] == 2 and mesh.shape["dp"] == 16


def solution(mesh):
    placed = (
        P(("dp", "blk"), None),
        P(("dp", "blk"), None),
        P("dp", None),
        P(("dp", "blk")),
        P(None, ("dp", "blk")),
        P(("dp", "blk")),
        P(None, ("dp", "blk")),
        P(("dp", "blk")),
        P(None, ("dp", "blk")),
        P(("dp", "blk")),
        P(None, ("dp", "blk")),
        P(("dp", "blk")),
        P(("dp", "blk")),
        P(("dp", "blk")),
        P(("dp", "blk")),
        P(("dp", "blk")),
        P(),
    )
    return jax.shard_map(
        paired_body if paired(mesh) else body,
        mesh=mesh,
        in_specs=placed,
        out_specs=(
            P(("dp", "blk"), None),
            P(("dp", "blk"), None),
            P(None, ("dp", "blk")),
            P(("dp", "blk")),
            P(None, ("dp", "blk")),
            P(("dp", "blk")),
            P(None, ("dp", "blk")),
            P(("dp", "blk")),
            P(None, ("dp", "blk")),
            P(("dp", "blk")),
            P(("dp", "blk")),
            P(("dp", "blk")),
            P(("dp", "blk")),
            P(("dp", "blk")),
            P(),
        ),
        check_vma=False,
    )
```

```python
import math

import jax
import jax.numpy as jnp
import numpy as np
from jax import lax
from jax.experimental import pallas as pl
from jax.experimental.pallas import tpu as pltpu
from jax.sharding import PartitionSpec as P

H = 12
HD = 64
MAXREL = 160
BLOCK = 256
BUCKETS = 321


EPSILON = 1e-05
MASKED = -2e30
START_PEAK = -1e30
HIGHEST = lax.Precision.HIGHEST


def from_behind(block, axis, distance):
    devices = range(lax.axis_size(axis))
    route = [((i - distance) % len(devices), i) for i in devices]
    return lax.ppermute(block, axis, route)


def layer_norm(values, gain_vec, shift_vec):
    center = values - jnp.mean(values, axis=-1, keepdims=True)
    inv_std = lax.rsqrt(jnp.mean(center * center, axis=-1, keepdims=True) + EPSILON)
    normed = center * inv_std
    return (normed * gain_vec + shift_vec, normed, inv_std)


def norm_back(gradient, normed, inv_std, gain_vec):
    scaled = gradient * gain_vec
    inner = (
        scaled
        - jnp.mean(scaled, axis=-1, keepdims=True)
        - normed * jnp.mean(scaled * normed, axis=-1, keepdims=True)
    )
    return (inner * inv_std, jnp.sum(gradient * normed, axis=0), jnp.sum(gradient, axis=0))


def gelu_parts(values):
    normal_cdf = 0.5 * (1.0 + lax.erf(values * 0.7071067811865476))
    density = jnp.exp(-0.5 * values * values) * 0.3989422804014327
    return (values * normal_cdf, normal_cdf + values * density)


def doc_numbers(seq_ends, positions):
    return jnp.sum((positions[:, None] >= seq_ends[None, :]).astype(jnp.int32), axis=1)


def pair_logits(
    query_block, key_block, query_pos, key_pos, query_doc, key_doc, key_live, table_heads
):
    block_len = query_block.shape[0]
    raw = jnp.einsum(
        "qhd,khd->hqk",
        query_block.reshape(block_len, H, HD),
        key_block.reshape(-1, H, HD),
        preferred_element_type=jnp.float32,
    )
    relative = jnp.clip(key_pos[None, :] - query_pos[:, None], -MAXREL, MAXREL) + MAXREL
    bias = jnp.take(table_heads, relative, axis=1)
    allowed = (query_doc[:, None] == key_doc[None, :]) & (
        (key_live[None, :] > 0.5) | (query_pos[:, None] == key_pos[None, :])
    )
    return jnp.where(allowed[None], raw * (1.0 / math.sqrt(HD)) + bias, MASKED)


def diagonal_sums(gradient, offset):
    heads, block_len, _ = gradient.shape
    flipped = gradient[:, ::-1, :]
    padded = jnp.pad(flipped, ((0, 0), (0, 0), (0, block_len)))
    sheared = padded.reshape(heads, 2 * block_len * block_len)[:, : block_len * (2 * block_len - 1)]
    sheared = sheared.reshape(heads, block_len, 2 * block_len - 1)
    diag_sums = jnp.sum(sheared, axis=1)
    distance = offset + jnp.arange(2 * block_len - 1, dtype=jnp.int32) - (block_len - 1)
    bucket = jnp.clip(distance, -MAXREL, MAXREL) + MAXREL
    onehot = (bucket[:, None] == jnp.arange(BUCKETS, dtype=jnp.int32)[None, :]).astype(jnp.float32)
    return jnp.dot(diag_sums, onehot, precision=HIGHEST)


def body(
    frames,
    cotangent,
    seq_lengths,
    key_mask,
    qkv_weight,
    query_value_bias,
    out_weight,
    out_bias,
    up_weight,
    up_bias,
    down_weight,
    down_bias,
    first_gain,
    first_shift,
    second_gain,
    second_shift,
    rel_bias,
):
    cycle_size = lax.axis_size("blk")
    cycle_place = lax.axis_index("blk")
    shard_len = frames.shape[0]
    width = frames.shape[1]
    block_count = shard_len // BLOCK
    score_scale = 1.0 / math.sqrt(HD)
    seq_ends = jnp.cumsum(seq_lengths[0])
    local_pos = jnp.arange(shard_len, dtype=jnp.int32)
    positions = cycle_place * shard_len + local_pos
    own_docs = doc_numbers(seq_ends, positions)
    table_heads = rel_bias.astype(jnp.float32).T

    def blocked(array):
        return array.reshape((block_count, BLOCK) + array.shape[1:])

    def key_meta(turn):
        source = (cycle_place - turn) % cycle_size
        key_pos = source * shard_len + local_pos
        return (key_pos, doc_numbers(seq_ends, key_pos))

    gathered = (
        lax.all_gather(qkv_weight, ("dp", "blk"), axis=1, tiled=True),
        lax.all_gather(query_value_bias, ("dp", "blk"), axis=0, tiled=True),
        lax.all_gather(out_weight, ("dp", "blk"), axis=1, tiled=True),
        lax.all_gather(out_bias, ("dp", "blk"), axis=0, tiled=True),
        lax.all_gather(up_weight, ("dp", "blk"), axis=1, tiled=True),
        lax.all_gather(up_bias, ("dp", "blk"), axis=0, tiled=True),
        lax.all_gather(down_weight, ("dp", "blk"), axis=1, tiled=True),
        lax.all_gather(down_bias, ("dp", "blk"), axis=0, tiled=True),
        lax.all_gather(first_gain, ("dp", "blk"), axis=0, tiled=True),
        lax.all_gather(first_shift, ("dp", "blk"), axis=0, tiled=True),
        lax.all_gather(second_gain, ("dp", "blk"), axis=0, tiled=True),
        lax.all_gather(second_shift, ("dp", "blk"), axis=0, tiled=True),
    )
    (
        qkv_full,
        qv_bias_full,
        out_full,
        out_bias_full,
        up_full,
        up_bias_full,
        down_full,
        down_bias_full,
        gain_one,
        shift_one,
        gain_two,
        shift_two,
    ) = gathered
    frames_wide = frames.astype(jnp.float32)
    first_out, first_normed, first_inv = layer_norm(
        frames_wide, gain_one.astype(jnp.float32), shift_one.astype(jnp.float32)
    )
    first_low = first_out.astype(jnp.bfloat16)
    projected = jnp.dot(first_low, qkv_full, preferred_element_type=jnp.float32)
    bias_vec = qv_bias_full.astype(jnp.float32)
    queries = (projected[:, :width] + bias_vec[:width]).astype(jnp.bfloat16)
    key_rows = projected[:, width : 2 * width].astype(jnp.bfloat16)
    value_rows = (projected[:, 2 * width :] + bias_vec[width:]).astype(jnp.bfloat16)
    live_rows = key_mask.astype(jnp.bfloat16)
    query_blocks = (blocked(queries), blocked(positions), blocked(own_docs))

    def forward_hop(turn, online_state, key_part, value_part, live_part):
        key_pos, key_doc = key_meta(turn)
        key_items = (
            blocked(key_part),
            blocked(value_part),
            blocked(key_pos),
            blocked(key_doc),
            blocked(live_part),
        )

        def forward_per_query(query_items):
            query_block, query_pos, query_doc, row_peak, row_total, accum = query_items

            def online(carried, key_block_items):
                row_peak, row_total, accum = carried
                key_block, value_block, key_bpos, key_bdoc, key_blive = key_block_items
                logits = pair_logits(
                    query_block,
                    key_block,
                    query_pos,
                    key_bpos,
                    query_doc,
                    key_bdoc,
                    key_blive,
                    table_heads,
                )
                new_peak = jnp.maximum(row_peak, jnp.max(logits, axis=2))
                decay = jnp.exp(row_peak - new_peak)
                weights = jnp.exp(logits - new_peak[:, :, None])
                row_total = row_total * decay + jnp.sum(weights, axis=2)
                accum = accum * decay.T[:, :, None] + jnp.einsum(
                    "hqk,khd->qhd",
                    weights.astype(jnp.bfloat16),
                    value_block.reshape(-1, H, HD),
                    preferred_element_type=jnp.float32,
                )
                return ((new_peak, row_total, accum), None)

            result, unused = lax.scan(online, (row_peak, row_total, accum), key_items)
            return result

        return lax.map(forward_per_query, query_blocks + online_state)

    def cycle_turn(turn, carried):
        online_state, key_part, value_part, live_part = carried
        online_state = forward_hop(turn, online_state, key_part, value_part, live_part)
        key_part, value_part, live_part = from_behind((key_part, value_part, live_part), "blk", 1)
        return (online_state, key_part, value_part, live_part)

    start_state = (
        jnp.full((block_count, H, BLOCK), START_PEAK, jnp.float32),
        jnp.zeros((block_count, H, BLOCK), jnp.float32),
        jnp.zeros((block_count, BLOCK, H, HD), jnp.float32),
    )
    carried = lax.fori_loop(
        0, cycle_size - 1, cycle_turn, (start_state, key_rows, value_rows, live_rows)
    )
    row_peak, row_total, accum = forward_hop(
        cycle_size - 1, carried[0], carried[1], carried[2], carried[3]
    )
    mixed = accum / jnp.transpose(row_total, (0, 2, 1))[:, :, :, None]
    mixed_flat = mixed.reshape(shard_len, width)
    context = mixed_flat.astype(jnp.bfloat16)
    branch = jnp.dot(context, out_full, preferred_element_type=jnp.float32) + out_bias_full.astype(
        jnp.float32
    )
    middle = frames_wide + branch
    second_out, second_normed, second_inv = layer_norm(
        middle, gain_two.astype(jnp.float32), shift_two.astype(jnp.float32)
    )
    second_low = second_out.astype(jnp.bfloat16)
    hidden = jnp.dot(second_low, up_full, preferred_element_type=jnp.float32) + up_bias_full.astype(
        jnp.float32
    )
    active, slope = gelu_parts(hidden)
    active_low = active.astype(jnp.bfloat16)
    layer_out = (
        middle
        + jnp.dot(active_low, down_full, preferred_element_type=jnp.float32)
        + down_bias_full.astype(jnp.float32)
    )
    weights_back = (
        lax.all_gather(qkv_weight, ("dp", "blk"), axis=1, tiled=True),
        lax.all_gather(query_value_bias, ("dp", "blk"), axis=0, tiled=True),
        lax.all_gather(out_weight, ("dp", "blk"), axis=1, tiled=True),
        lax.all_gather(out_bias, ("dp", "blk"), axis=0, tiled=True),
        lax.all_gather(up_weight, ("dp", "blk"), axis=1, tiled=True),
        lax.all_gather(up_bias, ("dp", "blk"), axis=0, tiled=True),
        lax.all_gather(down_weight, ("dp", "blk"), axis=1, tiled=True),
        lax.all_gather(down_bias, ("dp", "blk"), axis=0, tiled=True),
        lax.all_gather(first_gain, ("dp", "blk"), axis=0, tiled=True),
        lax.all_gather(first_shift, ("dp", "blk"), axis=0, tiled=True),
        lax.all_gather(second_gain, ("dp", "blk"), axis=0, tiled=True),
        lax.all_gather(second_shift, ("dp", "blk"), axis=0, tiled=True),
    )
    qkv_back = weights_back[0]
    out_back = weights_back[2]
    up_back = weights_back[4]
    down_back = weights_back[6]
    gain_one_back = weights_back[8].astype(jnp.float32)
    gain_two_back = weights_back[10].astype(jnp.float32)
    grad_wide = cotangent.astype(jnp.float32)
    down_grad = jnp.einsum("tf,td->fd", active_low, cotangent, preferred_element_type=jnp.float32)
    down_bias_grad = jnp.sum(grad_wide, axis=0)
    active_grad = jnp.einsum("td,fd->tf", cotangent, down_back, preferred_element_type=jnp.float32)
    hidden_low = (active_grad * slope).astype(jnp.bfloat16)
    up_grad = jnp.einsum("td,tf->df", second_low, hidden_low, preferred_element_type=jnp.float32)
    up_bias_grad = jnp.sum(hidden_low.astype(jnp.float32), axis=0)
    second_grad = jnp.einsum("tf,df->td", hidden_low, up_back, preferred_element_type=jnp.float32)
    middle_norm, gain_two_grad, shift_two_grad = norm_back(
        second_grad, second_normed, second_inv, gain_two_back
    )
    middle_grad = grad_wide + middle_norm
    branch_low = middle_grad.astype(jnp.bfloat16)
    out_grad = jnp.einsum("td,te->de", context, branch_low, preferred_element_type=jnp.float32)
    out_bias_grad = jnp.sum(branch_low.astype(jnp.float32), axis=0)
    context_low = jnp.einsum(
        "te,de->td", branch_low, out_back, preferred_element_type=jnp.float32
    ).astype(jnp.bfloat16)
    delta = jnp.sum(
        (context_low.astype(jnp.float32) * mixed_flat).reshape(shard_len, H, HD), axis=2
    )
    delta_blocks = jnp.transpose(blocked(delta), (0, 2, 1))
    query_back = (
        blocked(queries),
        blocked(context_low),
        blocked(positions),
        blocked(own_docs),
        row_peak,
        row_total,
        delta_blocks,
    )

    def backward_hop(
        turn, query_grad, table_grad, key_part, value_part, live_part, key_grad, value_grad
    ):
        key_pos, key_doc = key_meta(turn)

        def per_key(carried, key_block_items):
            query_grad, table_grad = carried
            key_block, value_block, key_bpos, key_bdoc, key_blive, key_bgrad, value_bgrad = (
                key_block_items
            )
            key_heads = key_block.reshape(-1, H, HD)
            value_heads = value_block.reshape(-1, H, HD)

            def per_per_query(inner, query_items):
                key_bgrad, value_bgrad, table_grad = inner
                (
                    query_block,
                    dout_block,
                    query_pos,
                    query_doc,
                    peak_block,
                    total_block,
                    delta_block,
                ) = query_items
                logits = pair_logits(
                    query_block,
                    key_block,
                    query_pos,
                    key_bpos,
                    query_doc,
                    key_bdoc,
                    key_blive,
                    table_heads,
                )
                attn_prob = jnp.exp(logits - peak_block[:, :, None]) / total_block[:, :, None]
                dout_heads = dout_block.reshape(-1, H, HD)
                prob_grad = jnp.einsum(
                    "qhd,khd->hqk", dout_heads, value_heads, preferred_element_type=jnp.float32
                )
                logit_grad = attn_prob * (prob_grad - delta_block[:, :, None])
                raw_low = (logit_grad * score_scale).astype(jnp.bfloat16)
                query_part = jnp.einsum(
                    "hqk,khd->qhd", raw_low, key_heads, preferred_element_type=jnp.float32
                ).reshape(-1, width)
                key_bgrad = key_bgrad + jnp.einsum(
                    "hqk,qhd->khd",
                    raw_low,
                    query_block.reshape(-1, H, HD),
                    preferred_element_type=jnp.float32,
                ).reshape(-1, width)
                value_bgrad = value_bgrad + jnp.einsum(
                    "hqk,qhd->khd",
                    attn_prob.astype(jnp.bfloat16),
                    dout_heads,
                    preferred_element_type=jnp.float32,
                ).reshape(-1, width)
                table_grad = table_grad + diagonal_sums(logit_grad, key_bpos[0] - query_pos[0])
                return ((key_bgrad, value_bgrad, table_grad), query_part)

            (key_bgrad, value_bgrad, table_grad), query_parts = lax.scan(
                per_per_query, (key_bgrad, value_bgrad, table_grad), query_back
            )
            return ((query_grad + query_parts, table_grad), (key_bgrad, value_bgrad))

        (query_grad, table_grad), (key_new, value_new) = lax.scan(
            per_key,
            (query_grad, table_grad),
            (
                blocked(key_part),
                blocked(value_part),
                blocked(key_pos),
                blocked(key_doc),
                blocked(live_part),
                blocked(key_grad),
                blocked(value_grad),
            ),
        )
        return (
            query_grad,
            table_grad,
            key_new.reshape(shard_len, width),
            value_new.reshape(shard_len, width),
        )

    def pass_grads(key_grad, value_grad):
        return (
            from_behind(key_grad.astype(jnp.bfloat16), "blk", 1).astype(key_grad.dtype),
            from_behind(value_grad.astype(jnp.bfloat16), "blk", 1).astype(value_grad.dtype),
        )

    def back_turn(turn, carried):
        query_grad, table_grad, key_part, value_part, live_part, key_grad, value_grad = carried
        query_grad, table_grad, key_grad, value_grad = backward_hop(
            turn, query_grad, table_grad, key_part, value_part, live_part, key_grad, value_grad
        )
        key_part, value_part, live_part = from_behind((key_part, value_part, live_part), "blk", 1)
        key_grad, value_grad = pass_grads(key_grad, value_grad)
        return (query_grad, table_grad, key_part, value_part, live_part, key_grad, value_grad)

    zero_rows = jnp.zeros((shard_len, width), jnp.float32)
    back_start = (
        jnp.zeros((block_count, BLOCK, width), jnp.float32),
        jnp.zeros((H, BUCKETS), jnp.float32),
        key_rows,
        value_rows,
        live_rows,
        zero_rows,
        zero_rows,
    )
    carried = lax.fori_loop(0, cycle_size - 1, back_turn, back_start)
    query_grad, table_grad, key_grad, value_grad = backward_hop(
        cycle_size - 1,
        carried[0],
        carried[1],
        carried[2],
        carried[3],
        carried[4],
        carried[5],
        carried[6],
    )
    key_grad, value_grad = pass_grads(key_grad, value_grad)
    query_low = query_grad.reshape(shard_len, width).astype(jnp.bfloat16)
    key_low = key_grad.astype(jnp.bfloat16)
    value_low = value_grad.astype(jnp.bfloat16)
    qkv_low = jnp.concatenate([query_low, key_low, value_low], axis=1)
    qkv_grad = jnp.einsum("td,te->de", first_low, qkv_low, preferred_element_type=jnp.float32)
    query_value_grad = jnp.concatenate(
        [
            jnp.sum(query_low.astype(jnp.float32), axis=0),
            jnp.sum(value_low.astype(jnp.float32), axis=0),
        ]
    )
    first_grad = jnp.einsum("te,de->td", qkv_low, qkv_back, preferred_element_type=jnp.float32)
    frames_norm, gain_one_grad, shift_one_grad = norm_back(
        first_grad, first_normed, first_inv, gain_one_back
    )
    frames_grad = middle_grad + frames_norm
    summed = (
        lax.psum_scatter(qkv_grad, ("dp", "blk"), scatter_dimension=1, tiled=True),
        lax.psum_scatter(query_value_grad, ("dp", "blk"), scatter_dimension=0, tiled=True),
        lax.psum_scatter(out_grad, ("dp", "blk"), scatter_dimension=1, tiled=True),
        lax.psum_scatter(out_bias_grad, ("dp", "blk"), scatter_dimension=0, tiled=True),
        lax.psum_scatter(up_grad, ("dp", "blk"), scatter_dimension=1, tiled=True),
        lax.psum_scatter(up_bias_grad, ("dp", "blk"), scatter_dimension=0, tiled=True),
        lax.psum_scatter(down_grad, ("dp", "blk"), scatter_dimension=1, tiled=True),
        lax.psum_scatter(down_bias_grad, ("dp", "blk"), scatter_dimension=0, tiled=True),
        lax.psum_scatter(gain_one_grad, ("dp", "blk"), scatter_dimension=0, tiled=True),
        lax.psum_scatter(shift_one_grad, ("dp", "blk"), scatter_dimension=0, tiled=True),
        lax.psum_scatter(gain_two_grad, ("dp", "blk"), scatter_dimension=0, tiled=True),
        lax.psum_scatter(shift_two_grad, ("dp", "blk"), scatter_dimension=0, tiled=True),
    )
    table_sum = lax.psum(table_grad, ("dp", "blk"))
    return (
        layer_out,
        frames_grad,
        summed[0],
        summed[1],
        summed[2],
        summed[3],
        summed[4],
        summed[5],
        summed[6],
        summed[7],
        summed[8],
        summed[9],
        summed[10],
        summed[11],
        table_sum.T,
    )


AXES = ("dp", "blk")
F32 = jnp.float32
LOW = jnp.bfloat16
LANES = 128
NARROW = 6
PAD = 8


def route(move):
    n_dp, n_blk = lax.axis_size("dp"), lax.axis_size("blk")
    pairs = []
    for d in range(n_dp):
        d_bits, b_bits = move[d % 2]
        for b in range(n_blk):
            pairs.append((d * n_blk + b, (d ^ d_bits) * n_blk + (b ^ b_bits)))
    return pairs


def shift(array, move, name="swap"):
    with jax.named_scope(name):
        return lax.ppermute(array, AXES, route(move))


CORE = ((1, 0), (1, 0))
SIDE = ((0, 1), (2, 0))
OTHER_SIDE = ((2, 0), (0, 1))
PACK = ((0, 1), (0, 1))
ALONG_Z = tuple(((4 * turn, 0), (4 * turn, 0)) for turn in (1, 2, 3))


def tied(value, *after):
    return lax.optimization_barrier((value,) + after)[0]


def joined(*groups):
    return lax.optimization_barrier(groups)


def twin(array, name="twin"):
    return shift(array, CORE, name)


def along_z(unit, name):
    return tuple(shift(unit, move, name + "_z") for move in ALONG_Z)


def z_sends(plane, name):
    low = plane.astype(LOW)
    return tuple(shift(low[n + 1], move, name + "_z") for n, move in enumerate(ALONG_Z))


def z_sum(plane, arrived):
    return plane[0] + sum(part.astype(F32) for part in arrived)


def unit_of(place, x_turn, y_turn, z_turn, c):
    x, y, z = place[0] ^ x_turn, place[1] ^ y_turn, place[2] ^ z_turn
    return ((z * 2 + y) * 2 + c) * 2 + x


def each_unit(place, visit):
    def step(z, _):
        for plane in range(2):
            c = place[3] if plane == 0 else 1 - place[3]
            for n, (x_turn, y_turn) in enumerate(((0, 0), (1 - c, c), (c, 1 - c), (1, 1))):
                visit(4 * plane + n, z, unit_of(place, x_turn, y_turn, z, c))
        return 0

    lax.fori_loop(0, 4, step, 0)


def take_columns(place, array, pair, taken, top):
    for c in range(2):

        @pl.when(place[3] == c)
        def _():
            taken[top : top + array.shape[0], :] = jnp.concatenate(
                [
                    array[:, (2 * n + c) * pair : (2 * n + c + 1) * pair]
                    for n in range(array.shape[1] // (2 * pair))
                ],
                axis=1,
            )


def give_units(place, stage, parts):
    c = place[3]
    for part, (x_turn, y_turn) in zip(parts, ((0, 0), (1 - c, c), (c, 1 - c), (1, 1))):
        halves = part if isinstance(part, tuple) else (part,)
        for half, ref in enumerate(halves):
            start = half * ref.shape[0]

            def give(turn, _, ref=ref, start=start, x_turn=x_turn, y_turn=y_turn):
                unit = ((place[2] ^ (start + turn)) * 2 + (place[1] ^ y_turn)) * 2 + (place[0] ^ x_turn)
                ref[turn] = stage[unit].astype(LOW)
                return 0

            lax.fori_loop(0, ref.shape[0], give, 0)


def part_shapes(rows, width):
    return [jax.ShapeDtypeStruct((4, rows, width), LOW)] * 4


def dot_nn(a, b):
    return lax.dot_general(a, b, (((1,), (0,)), ((), ())), preferred_element_type=F32)


def dot_nt(a, b):
    return lax.dot_general(a, b, (((1,), (1,)), ((), ())), preferred_element_type=F32)


def dot_tn(a, b):
    return lax.dot_general(a, b, (((0,), (0,)), ((), ())), preferred_element_type=F32)


HBM = pl.BlockSpec(memory_space=pltpu.HBM)
SMEM = pl.BlockSpec(memory_space=pltpu.SMEM)
VMEM = pl.BlockSpec(memory_space=pltpu.VMEM)


def call(kernel, in_specs, outs, out_specs, scratch, args, flops, limit=56, **kwargs):
    moved = sum(math.prod(a.shape) * a.dtype.itemsize for a in list(args) + list(outs))
    return pl.pallas_call(
        kernel,
        out_shape=outs,
        in_specs=in_specs,
        out_specs=out_specs,
        scratch_shapes=scratch,
        compiler_params=pltpu.CompilerParams(vmem_limit_bytes=limit * 1024 * 1024),
        cost_estimate=pl.CostEstimate(flops=flops, bytes_accessed=moved, transcendentals=0),
        **kwargs,
    )(*args)


def spread_tables(units, width, lanes):
    tables = []
    for n in (width // units, 2 * width // units, 4 * width // units):
        lane = lanes[None, : units * n]
        row = jnp.arange(units + LANES, dtype=jnp.int32)[:, None]
        tables.append(
            jnp.where(row < units, lane // n == row, lane % n == row - units).astype(F32).astype(LOW)
        )
    return tables


def project_kernel(
    place, own, other, p0, p1, p2, p3, p4, p5, p6, p7, wide_one, wide_two, wide_four,
    first, queries, keys, values, vectors, up_bias, mate_live, weight_out, stage, small, weight, sems,
):
    units = stage.shape[0]
    width = own.shape[1]
    rows = stage.shape[1] - PAD
    shard_len = own.shape[0]
    pieces = (p0, p1, p2, p3, p4, p5, p6, p7)

    def fill(array, z, unit):
        stage[unit] = pieces[array][z]

    each_unit(place, fill)

    def normed(frames):
        wide = frames.astype(F32)
        center = wide - jnp.mean(wide, axis=1, keepdims=True)
        return center * lax.rsqrt(jnp.mean(center * center, axis=1, keepdims=True) + EPSILON)

    own_normed, mate_normed = normed(own[...]), normed(other[...])
    for unit in range(units):
        top = stage[unit, rows : rows + PAD, :].astype(F32)
        small[0, unit : unit + 1, :] = top[0:1]
        small[1, unit : unit + 1, :] = top[1:2]

    mate = unit_of(place, 1, 0, 0, place[3])
    mate_live[...] = stage[mate, rows : rows + PAD, : mate_live.shape[1]].astype(F32)

    def spread(row, slot, table):
        held = small[row, :, slot * LANES : (slot + 1) * LANES].astype(LOW)
        laid = dot_nn(held, table[units:, :]) * table[:units, :].astype(F32)
        return jnp.sum(laid, axis=0, keepdims=True)

    for n in range(NARROW):
        vectors[n : n + 1, :] = spread(0, n, wide_one)
    qv_bias = spread(1, 0, wide_two)
    up_bias[...] = jnp.broadcast_to(spread(1, 1, wide_four), up_bias.shape)
    vectors[NARROW : NARROW + 1, :] = qv_bias[:, :width]
    vectors[NARROW + 1 : NARROW + 2, :] = qv_bias[:, width:]

    def join(pair, _):
        both = jnp.concatenate(
            [stage[2 * pair, :rows, :].astype(F32), stage[2 * pair + 1, :rows, :].astype(F32)], axis=0
        )
        weight[pl.ds(pl.multiple_of(2 * rows * pair, 2 * rows), 2 * rows), :] = both.astype(LOW)
        return 0

    lax.fori_loop(0, units // 2, join, 0)
    copy = pltpu.make_async_copy(weight, weight_out, sems.at[0])
    copy.start()
    gain, offset = vectors[0:1, :], vectors[1:2, :]
    x = place[0]
    own_at = pl.multiple_of(x * shard_len, shard_len)
    mate_at = pl.multiple_of((1 - x) * shard_len, shard_len)
    first[pl.ds(own_at, shard_len), :] = (own_normed * gain + offset).astype(LOW)
    first[pl.ds(mate_at, shard_len), :] = (mate_normed * gain + offset).astype(LOW)
    mine = first[pl.ds(own_at, shard_len), :]
    queries[...] = (dot_nt(mine, weight[:width, :]) + vectors[NARROW : NARROW + 1, :]).astype(LOW)
    keys[...] = dot_nt(first[...], weight[width : 2 * width, :]).astype(LOW)
    values[...] = (
        dot_nt(first[...], weight[2 * width :, :]) + vectors[NARROW + 1 : NARROW + 2, :]
    ).astype(LOW)
    copy.wait()


def half_mask(shape, head):
    return (lax.broadcasted_iota(jnp.int32, shape, 1) // HD) == head


def bias_kernel(curve, bias):
    heads, block_len, span = bias.shape

    def shear(head, _):
        bias[head] = pltpu.roll(
            jnp.broadcast_to(curve[pl.ds(head, 1), :], (block_len, block_len + span)),
            span + 1, 1, stride=1, stride_axis=0,
        )[:, :span].astype(LOW)
        return 0

    lax.fori_loop(0, heads, shear, 0)


def attend_kernel(
    place, lengths, queries, keys, values, bias, own_live, mate_live, probs, mixed, hidden_pairs
):
    block_len, span = hidden_pairs.shape

    @pl.when(pl.program_id(0) == 0)
    def _():
        start = place[0] * block_len
        key_pos = lax.broadcasted_iota(jnp.int32, (1, span), 1)
        query_pos = lax.broadcasted_iota(jnp.int32, (block_len, 1), 0) + start
        key_doc, query_doc = jnp.zeros_like(key_pos), jnp.zeros_like(query_pos)
        end = 0
        for n in range(lengths.shape[1]):
            end = end + lengths[0, n]
            key_doc = key_doc + (key_pos >= end).astype(jnp.int32)
            query_doc = query_doc + (query_pos >= end).astype(jnp.int32)
        one, two = own_live[...].astype(F32), mate_live[2:3, :]
        live = jnp.where(
            place[0] == 0, jnp.concatenate([one, two], axis=1), jnp.concatenate([two, one], axis=1)
        )
        allowed = (query_doc == key_doc) & ((live > 0.5) | (query_pos == key_pos))
        hidden_pairs[...] = jnp.where(allowed, 0.0, MASKED)

    for pair in range(queries.shape[1] // (2 * HD)):
        lane = slice(2 * HD * pair, 2 * HD * (pair + 1))
        q, k, v = queries[:, lane], keys[:, lane], values[:, lane]
        total = jnp.zeros(q.shape, F32)
        for head in range(2):
            n = 2 * pair + head
            q_head = jnp.where(half_mask(q.shape, head), q, 0) * (1.0 / math.sqrt(HD))
            logits = dot_nt(q_head.astype(LOW), k) + bias[n].astype(F32) + hidden_pairs[...]
            weights = jnp.exp(logits - jnp.max(logits, axis=1, keepdims=True))
            prob = (weights * (1.0 / jnp.sum(weights, axis=1, keepdims=True))).astype(LOW)
            probs[n] = prob
            total = total + dot_nn(prob, jnp.where(half_mask(v.shape, head), v, 0))
        mixed[:, lane] = total


def join_units(kept, out):
    units = kept.shape[0]
    each = out.shape[0] // units

    def join(pair, _):
        both = jnp.concatenate(
            [kept[2 * pair].astype(F32)[:each], kept[2 * pair + 1].astype(F32)[:each]], axis=0
        )
        out[pl.ds(pl.multiple_of(2 * each * pair, 2 * each), 2 * each), :] = both.astype(LOW)
        return 0

    lax.fori_loop(0, units // 2, join, 0)


def expand_kernel(
    place, frames, mixed, vectors, up_bias, p0, p1, p2, p3, p4, p5, p6, p7,
    middle, second, context, active, slope, up, kept, out,
):
    width = frames.shape[1]
    pieces = (p0, p1, p2, p3, p4, p5, p6, p7)
    rows = p0.shape[1] - kept.shape[1]

    def fill(array, z, unit):
        kept[unit] = pieces[array][z, rows:]
        up[pl.ds(pl.multiple_of(unit * rows, rows), rows), :] = pieces[array][z, :rows]

    each_unit(place, fill)
    context[...] = mixed[...].astype(LOW)
    join_units(kept, out)
    mid = frames[...].astype(F32) + (dot_nt(context[...], out[...]) + vectors[4:5, :])
    middle[...] = mid
    center = mid - jnp.mean(mid, axis=1, keepdims=True)
    normed = center * lax.rsqrt(jnp.mean(center * center, axis=1, keepdims=True) + EPSILON)
    second[...] = (normed * vectors[2:3, :] + vectors[3:4, :]).astype(LOW)
    for n in range(up.shape[0] // width):
        at = slice(n * width, (n + 1) * width)
        hidden = dot_nt(second[...], up[at, :]) + up_bias[0:1, at]
        cdf = 0.5 * (1.0 + lax.erf(hidden * 0.7071067811865476))
        density = jnp.exp(-0.5 * hidden * hidden) * 0.3989422804014327
        active[:, at] = (hidden * cdf).astype(LOW)
        slope[:, at] = cdf + hidden * density


def down_grad_kernel(
    place, active, active_twin, cotangent, cotangent_twin, o0, o1, o2, o3, bias_grad, taken, wide,
):
    units, rows, width = wide.shape
    each = width // (2 * units)
    bias_grad[...] = jnp.broadcast_to(
        jnp.sum(cotangent[...].astype(F32), axis=0, keepdims=True), bias_grad.shape
    )

    shard_len = cotangent.shape[0]
    take_columns(place, cotangent, 2 * each, taken, 0)
    take_columns(place, cotangent_twin, 2 * each, taken, shard_len)
    dy, dy_twin = taken[:shard_len, :], taken[shard_len:, :]
    for fold in range(rows // each):
        at = slice(fold * width, (fold + 1) * width)
        grad = dot_tn(dy, active[:, at]) + dot_tn(dy_twin, active_twin[:, at])
        for unit in range(units):
            wide[unit, fold * each : (fold + 1) * each, :] = grad[unit * each : (unit + 1) * each]
    give_units(place, wide, (o0, o1, o2, o3))


def unfold_units(stage, down):
    units, rows, width = stage.shape
    each = down.shape[0] // units

    def unfold(pair, _):
        one, two = stage[2 * pair].astype(F32), stage[2 * pair + 1].astype(F32)
        at = pl.multiple_of(2 * each * pair, 2 * each)
        for fold in range(rows // each):
            both = jnp.concatenate(
                [one[fold * each : (fold + 1) * each], two[fold * each : (fold + 1) * each]], axis=0
            )
            down[pl.ds(at, 2 * each), fold * width : (fold + 1) * width] = both.astype(LOW)
        return 0

    lax.fori_loop(0, units // 2, unfold, 0)


def back_kernel(
    place, cotangent, slope, middle, vectors, p0, p1, p2, p3, p4, p5, p6, p7, u0, u1, u2, u3, u4, u5, u6, u7,
    middle_grad, context_grad, vector_grads, branch_grad, up_bias_grad, hidden_grad,
    stage, down, up, kept, out,
):
    width = cotangent.shape[1]
    down_pieces, up_pieces = (p0, p1, p2, p3, p4, p5, p6, p7), (u0, u1, u2, u3, u4, u5, u6, u7)
    rows = u0.shape[1] - kept.shape[1]

    def fill(array, z, unit):
        stage[unit] = down_pieces[array][z]
        kept[unit] = up_pieces[array][z, rows:]
        up[pl.ds(pl.multiple_of(unit * rows, rows), rows), :] = up_pieces[array][z, :rows]

    each_unit(place, fill)
    unfold_units(stage, down)
    dy = cotangent[...]
    for n in range(hidden_grad.shape[1] // width):
        at = slice(n * width, (n + 1) * width)
        grad = (dot_nn(dy, down[:, at]) * slope[:, at]).astype(LOW)
        hidden_grad[:, at] = grad
        up_bias_grad[:, at] = jnp.broadcast_to(
            jnp.sum(grad.astype(F32), axis=0, keepdims=True), (up_bias_grad.shape[0], width)
        )
    join_units(kept, out)
    second_grad = dot_nn(hidden_grad[...], up[...])
    mid = middle[...]
    center = mid - jnp.mean(mid, axis=1, keepdims=True)
    inv_std = lax.rsqrt(jnp.mean(center * center, axis=1, keepdims=True) + EPSILON)
    normed = center * inv_std
    scaled = second_grad * vectors[2:3, :]
    inner = (
        scaled
        - jnp.mean(scaled, axis=1, keepdims=True)
        - normed * jnp.mean(scaled * normed, axis=1, keepdims=True)
    )
    mid_grad = cotangent[...].astype(F32) + inner * inv_std
    middle_grad[...] = mid_grad
    branch = mid_grad.astype(LOW)
    vector_grads[...] = jnp.concatenate(
        [
            jnp.sum(second_grad * normed, axis=0, keepdims=True),
            jnp.sum(second_grad, axis=0, keepdims=True),
            jnp.sum(branch.astype(F32), axis=0, keepdims=True),
            jnp.zeros((5, width), F32),
        ],
        axis=0,
    )
    branch_grad[...] = branch
    context_grad[...] = dot_nn(branch, out[...]).astype(LOW)


def up_grad_kernel(
    place, hidden, hidden_twin, second, second_twin, branch, branch_twin, context, context_twin,
    o0, o1, o2, o3, o4, taken, taken_branch, stage,
):
    units, rows, width = stage.shape
    each = width // (2 * units)
    up_rows = hidden.shape[1] // (2 * units)

    shard_len = second.shape[0]
    take_columns(place, branch, 2 * each, taken_branch, 0)
    take_columns(place, branch_twin, 2 * each, taken_branch, shard_len)
    take_columns(place, hidden, 2 * up_rows, taken, 0)
    take_columns(place, hidden_twin, 2 * up_rows, taken, shard_len)
    out_grad = dot_tn(taken_branch[:shard_len, :], context[...]) + dot_tn(
        taken_branch[shard_len:, :], context_twin[...]
    )
    blank = jnp.zeros((rows - up_rows - each, width), F32)
    quarter = units // 4
    for z in range(4):
        at = slice(z * quarter * up_rows, (z + 1) * quarter * up_rows)
        grad = dot_tn(taken[:shard_len, at], second[...]) + dot_tn(taken[shard_len:, at], second_twin[...])
        for n in range(quarter):
            unit = z * quarter + n
            stage[unit] = jnp.concatenate(
                [
                    grad[n * up_rows : (n + 1) * up_rows],
                    out_grad[unit * each : (unit + 1) * each],
                    blank,
                ],
                axis=0,
            ).astype(LOW)
    give_units(place, stage, (o0, o1, (o2, o3), o4))


def rows_left(each):
    return -each % 16


def finish_kernel(
    place, active, middle, vectors, p0, p1, p2, p3, p4, p5, p6, p7, layer_out, stage, down
):
    pieces = (p0, p1, p2, p3, p4, p5, p6, p7)

    def fill(array, z, unit):
        stage[unit] = pieces[array][z]

    each_unit(place, fill)
    unfold_units(stage, down)
    layer_out[...] = middle[...] + dot_nt(active[...], down[...]) + vectors[5:6, :]


def attend_back_kernel(
    place, queries, keys, values, context_grad, mixed, probs, grads, diagonals
):
    def of_pair(pair, _):
        lanes = pl.ds(pl.multiple_of(2 * HD * pair, 2 * HD), 2 * HD)
        q, k, v, dout = queries[:, lanes], keys[:, lanes], values[:, lanes], context_grad[:, lanes]
        block_len, span = probs.shape[1:]
        weighted = dout.astype(F32) * mixed[:, lanes]
        row = lax.broadcasted_iota(jnp.int32, (block_len, block_len), 0)
        lane = lax.broadcasted_iota(jnp.int32, (block_len, block_len), 1)
        turn = (row + lane == block_len - 1).astype(LOW)
        blank = jnp.zeros((block_len, block_len), F32)
        dq, dk, dv = jnp.zeros(q.shape, F32), jnp.zeros(k.shape, F32), jnp.zeros(v.shape, F32)
        for head in range(2):
            mine = half_mask(q.shape, head)
            dout_head = jnp.where(mine, dout, 0)
            delta = jnp.sum(jnp.where(mine, weighted, 0.0), axis=1, keepdims=True)
            prob = probs[2 * pair + head]
            grad = prob.astype(F32) * (dot_nt(dout_head, v) - delta)
            raw = (grad * (1.0 / math.sqrt(HD))).astype(LOW)
            dq = dq + dot_nn(raw, jnp.where(half_mask(k.shape, head), k, 0))
            dk = dk + dot_tn(raw, jnp.where(mine, q, 0))
            dv = dv + dot_tn(prob, dout_head)
            turned = jnp.concatenate([dot_nn(turn, raw), blank], axis=1)
            sheared = pltpu.roll(turned, 0, 1, stride=1, stride_axis=0)
            diagonals[pl.ds(4 * pl.program_id(0) + 2 * pair + head, 1), :] = jnp.sum(sheared, axis=0, keepdims=True) * math.sqrt(HD)
        own_at = pl.multiple_of(place[0] * block_len, block_len)
        grads[0, :, lanes] = jnp.zeros(k.shape, LOW)
        grads[0, pl.ds(own_at, block_len), lanes] = dq.astype(LOW)
        grads[1, :, lanes] = dk.astype(LOW)
        grads[2, :, lanes] = dv.astype(LOW)
        return 0

    lax.fori_loop(0, queries.shape[1] // (2 * HD), of_pair, 0)


def total(array):
    return jnp.sum(array, axis=0, keepdims=True)


def norm_parts(frames):
    wide = frames.astype(F32)
    center = wide - jnp.mean(wide, axis=1, keepdims=True)
    inv_std = lax.rsqrt(jnp.mean(center * center, axis=1, keepdims=True) + EPSILON)
    return center * inv_std, inv_std


def first_grad_kernel(
    place, own_frames, mate_frames, grads, weight_in, diagonals, vector_grads, down_bias_grad, up_bias_grad,
    own_grad, mate_grad, small, weight, sems,
):
    copy = pltpu.make_async_copy(weight_in, weight, sems.at[0])
    copy.start()
    shard_len, width = own_frames.shape
    x = place[0]
    own_at = pl.multiple_of(x * shard_len, shard_len)
    mate_at = pl.multiple_of((1 - x) * shard_len, shard_len)
    own_normed, _ = norm_parts(own_frames[...])
    mate_normed, _ = norm_parts(mate_frames[...])
    dq = grads[0, pl.ds(own_at, shard_len), :]
    small[4:5, :] = vector_grads[2:3, :]
    small[2:4, :] = vector_grads[0:2, :]
    small[5:6, :] = down_bias_grad[0:1, :]
    small[6:7, :] = total(dq.astype(F32))
    small[7:8, :] = total(grads[2].astype(F32))
    for n in range(up_bias_grad.shape[1] // width):
        small[8 + n : 9 + n, :] = up_bias_grad[0:1, n * width : (n + 1) * width]
    small[12:, :] = diagonals[...]
    copy.wait()

    def from_keys(at):
        return dot_nn(grads[1, pl.ds(at, shard_len), :], weight[width : 2 * width, :]) + dot_nn(
            grads[2, pl.ds(at, shard_len), :], weight[2 * width :, :]
        )

    of_own = from_keys(own_at) + dot_nn(dq, weight[:width, :])
    of_mate = from_keys(mate_at)
    own_grad[...] = of_own
    mate_grad[...] = of_mate
    small[0:1, :] = total(of_own * own_normed) + total(of_mate * mate_normed)
    small[1:2, :] = total(of_own) + total(of_mate)


def qkv_grad_kernel(
    place, grads, grads_twin, first, first_twin, small_own, small_twin, wide_one, wide_two, wide_four,
    o0, o1, o2, o3, taken, sums, small, tables, stage,
):
    units, full, width = stage.shape
    rows = full - PAD
    span = first.shape[0]
    shard_len = span // 2
    x = place[0]
    summed = small_own[...] + small_twin[...]

    def fold(vector, table):
        kept = (vector * table[: 2 * units, :].astype(F32)).astype(LOW)
        return dot_nt(kept, table[2 * units :, :])

    for n in range(NARROW):
        small[0, :, n * LANES : (n + 1) * LANES] = fold(summed[n : n + 1, :], wide_one)
    small[1, :, :] = jnp.zeros((2 * units, width), F32)
    both = jnp.concatenate([summed[6:7, :], summed[7:8, :]], axis=1)
    small[1, :, :LANES] = fold(both, wide_two)
    four = jnp.concatenate([summed[8 + n : 9 + n, :] for n in range(4)], axis=1)
    small[1, :, LANES : 2 * LANES] = fold(four, wide_four)
    lanes = 3 * LANES
    distance = (
        lax.broadcasted_iota(jnp.int32, (shard_len + span, lanes), 0) - (shard_len - 1) - x * shard_len
    )
    bucket = jnp.clip(distance, -MAXREL, MAXREL) + MAXREL
    here = (bucket == lax.broadcasted_iota(jnp.int32, (shard_len + span, lanes), 1)).astype(F32).astype(LOW)
    diagonals = summed[12:, :]
    high = diagonals.astype(LOW)
    table = dot_nn(high, here) + dot_nn((diagonals - high.astype(F32)).astype(LOW), here)
    table = jnp.concatenate([table[: H // 2], table[H // 2 :]], axis=1)
    for n, array in enumerate((grads, grads_twin)):
        columns = jnp.concatenate([array[part] for part in range(3)], axis=1)
        take_columns(place, columns, 2 * rows, taken, n * span)
    sums[...] = dot_tn(taken[:span, :], first[...]) + dot_tn(taken[span:, :], first_twin[...])

    def pack(unit, _):
        at = 4 * (unit // 2) + 2 * place[3] + unit % 2
        stage[unit] = jnp.concatenate(
            [
                sums[pl.ds(pl.multiple_of(unit * rows, rows), rows), :],
                small[0, pl.ds(at, 1), :],
                small[1, pl.ds(at, 1), :],
                tables[...],
            ],
            axis=0,
        ).astype(LOW)
        return 0

    tables[...] = table
    lax.fori_loop(0, units, pack, 0)
    give_units(place, stage, (o0, o1, o2, o3))


def input_grad_kernel(frames, mate_frames, own_grad, mate_grad, middle_grad, vectors, own_part, mate_part):
    def through_norm(of_frames, grad):
        normed, inv_std = norm_parts(of_frames)
        scaled = grad * vectors[0:1, :]
        inner = (
            scaled
            - jnp.mean(scaled, axis=1, keepdims=True)
            - normed * jnp.mean(scaled * normed, axis=1, keepdims=True)
        )
        return inner * inv_std

    own_part[...] = middle_grad[...] + through_norm(frames[...], own_grad[...])
    mate_part[...] = through_norm(mate_frames[...], mate_grad[...]).astype(LOW)


def last_kernel(
    own, z1, z2, z3, own_part, mate_part, qkv, qv_bias, up_bias, table, frames_grad, n0, n1, n2, n3, n4, n5
):
    frames_grad[...] = own_part[...] + mate_part[...].astype(F32)
    rows = qkv.shape[0]
    total = own[...] + z1[...].astype(F32) + z2[...].astype(F32) + z3[...].astype(F32)
    qkv[...] = total[:rows]
    for n, narrow in enumerate((n0, n1, n2, n3, n4, n5)):
        narrow[...] = total[rows : rows + 1, n * LANES : n * LANES + narrow.shape[1]]
    qv_bias[...] = total[rows + 1 : rows + 2, : qv_bias.shape[1]]
    up_bias[...] = total[rows + 1 : rows + 2, LANES : LANES + up_bias.shape[1]]
    for half in range(2):
        at = 3 * LANES * half
        table[half * (H // 2) : (half + 1) * (H // 2), :] = total[rows + 2 : rows + PAD, at : at + BUCKETS]


def pack_kernel(
    live, qkv, out, up, down, first_gain, first_shift, second_gain, second_shift, out_bias,
    down_bias, qv_bias, up_bias, qkv_unit, up_unit, down_unit,
):
    each, width = out.shape

    def slots(vectors):
        parts = []
        for vector in vectors:
            wide = vector[...].astype(F32)
            parts += [wide, jnp.zeros((1, LANES - wide.shape[1]), F32)]
        left = width - LANES * len(vectors)
        if left:
            parts.append(jnp.zeros((1, left), F32))
        return jnp.concatenate(parts, axis=1)

    narrow = slots((first_gain, first_shift, second_gain, second_shift, out_bias, down_bias))
    wide = slots((qv_bias, up_bias))
    seen = live[...].astype(F32)
    seen = jnp.concatenate([seen, jnp.zeros((1, width - seen.shape[1]), F32)], axis=1)
    blank = jnp.zeros((PAD - 3, width), F32)
    qkv_unit[...] = jnp.concatenate([qkv[...].astype(F32), narrow, wide, seen, blank], axis=0).astype(LOW)
    blank = jnp.zeros((up_unit.shape[0] - up.shape[0] - each, width), F32)
    up_unit[...] = jnp.concatenate(
        [up[...].astype(F32), out[...].astype(F32), blank], axis=0
    ).astype(LOW)
    down_unit[...] = jnp.concatenate(
        [
            down[:, fold * width : (fold + 1) * width].astype(F32)
            for fold in range(down.shape[1] // width)
        ],
        axis=0,
    ).astype(LOW)


def paired_body(
    frames, cotangent, seq_lengths, key_mask, qkv_weight, query_value_bias, out_weight, out_bias,
    up_weight, up_bias, down_weight, down_bias, first_gain, first_shift, second_gain, second_shift,
    rel_bias,
):
    shard_len, width = frames.shape
    x = lax.axis_index("blk")
    d = lax.axis_index("dp")
    core = d % 2
    units = lax.axis_size("dp") * lax.axis_size("blk")
    span = shard_len * lax.axis_size("blk")
    place = jnp.stack([x, (d // 2) % 2, d // 4, core]).astype(jnp.int32)
    each = width // units
    ff = up_weight.shape[1] * units
    qkv_rows, up_rows = qkv_weight.shape[1], up_weight.shape[1]
    folds = ff // width
    down_rows = each * folds
    out_rows = each + rows_left(each)

    def shape(*dims, kind=LOW):
        return jax.ShapeDtypeStruct(dims, kind)

    def row(vector):
        return vector.reshape(1, vector.shape[0])

    packed = (
        row(key_mask), qkv_weight.T, out_weight.T, up_weight.T, down_weight.T, row(first_gain),
        row(first_shift), row(second_gain), row(second_shift), row(out_bias), row(down_bias),
        row(query_value_bias), row(up_bias),
    )
    qkv_unit, up_unit, down_unit = call(
        pack_kernel,
        [VMEM] * len(packed),
        [shape(qkv_rows + PAD, width), shape(up_rows + out_rows, width), shape(down_rows, width)],
        [VMEM] * 3,
        [],
        packed,
        0,
        name="pack",
    )
    def twins(pieces):
        return tuple(pieces) + tuple(twin(piece) for piece in pieces)

    distance = jnp.arange(span + shard_len, dtype=jnp.int32) - (shard_len - 1) - x * shard_len
    bucket = jnp.clip(distance, -MAXREL, MAXREL) + MAXREL
    bucket_lanes = 3 * LANES
    buckets = (bucket[:, None] == jnp.arange(bucket_lanes, dtype=jnp.int32)[None, :]).astype(LOW)
    curve = lax.dot_general(
        rel_bias, buckets[:, :BUCKETS], (((0,), (1,)), ((), ())), preferred_element_type=F32
    )
    bias = call(
        bias_kernel, [VMEM], [shape(H, shard_len, span)], [VMEM], [], (tied(curve, qkv_unit),), 0, name="bias"
    )[0]
    spreads = spread_tables(units, width, tied(jnp.arange(ff, dtype=jnp.int32), qkv_unit))
    cotangent_twin = twin(cotangent)
    qkv_z = along_z(qkv_unit, "qkv")
    mate_frames = shift(tied(frames, qkv_unit), PACK, "frames_pack")
    qkv_z, mate_frames, bias, place, spreads = joined(qkv_z, mate_frames, bias, place, spreads)
    qkv_own = jnp.stack((qkv_unit,) + qkv_z)
    qkv_side = shift(qkv_own, SIDE, "qkv_1")
    up_first = tied(up_unit, *qkv_z)
    up_z = [shift(up_first, move, "up_z") for move in ALONG_Z[:2]]
    qkv_side, up_z, cotangent_twin = joined(qkv_side, up_z, cotangent_twin)
    qkv_other = shift(qkv_own, OTHER_SIDE, "qkv_2")
    qkv_across = shift(qkv_side, OTHER_SIDE, "qkv_3")
    up_z.append(shift(tied(up_unit, qkv_side), ALONG_Z[2], "up_z"))
    up_z, qkv_other, qkv_across = joined(up_z, qkv_other, qkv_across)
    qkv_pieces = twins((qkv_own, qkv_side, qkv_other, qkv_across))
    up_own = jnp.stack([up_unit] + up_z)
    up_side = shift(up_own, SIDE, "up_1")
    down_first = tied(down_unit, up_own)
    down_z = [shift(down_first, move, "down_z") for move in ALONG_Z[:2]]

    unit_sems = pltpu.SemaphoreType.DMA((units,))
    first, queries, keys, values, vectors, up_bias_all, mate_live, weight = call(
        project_kernel,
        [SMEM] + [VMEM] * 13,
        [
            shape(span, width), shape(shard_len, width), shape(span, width), shape(span, width),
            shape(8, width, kind=F32), shape(8, ff, kind=F32), shape(PAD, shard_len, kind=F32),
            shape(3 * width, width),
        ],
        [VMEM] * 7 + [HBM],
        [
            pltpu.VMEM((units, qkv_rows + PAD, width), LOW), pltpu.VMEM((2, units, width), F32),
            pltpu.VMEM((3 * width, width), LOW), pltpu.SemaphoreType.DMA((1,)),
        ],
        (tied(place, up_own), frames, mate_frames) + qkv_pieces + tuple(spreads),
        2 * shard_len * width * 5 * width,
        name="project",
    )
    up_side, keys, down_z = joined(up_side, keys, down_z)
    up_other = shift(up_own, OTHER_SIDE, "up_2")
    up_across = shift(up_side, OTHER_SIDE, "up_3")
    down_z.append(shift(tied(down_unit, keys), ALONG_Z[2], "down_z"))
    pairs = H // 2
    pair_lanes = 2 * HD

    def lanes_of(rows, count=1):
        return pl.BlockSpec((rows, count * pair_lanes), lambda n: (0, n))

    def heads_of(*dims):
        return pl.BlockSpec(dims, lambda n: (n,) + (0,) * (len(dims) - 1))

    def whole(*dims):
        return pl.BlockSpec(dims, lambda n: (0,) * len(dims))

    probs, mixed = call(
        attend_kernel,
        [
            SMEM, SMEM, lanes_of(shard_len, 2), lanes_of(span, 2), lanes_of(span, 2),
            heads_of(4, shard_len, span), whole(1, shard_len), whole(PAD, shard_len),
        ],
        [shape(H, shard_len, span), shape(shard_len, width, kind=F32)],
        [heads_of(4, shard_len, span), lanes_of(shard_len, 2)],
        [pltpu.VMEM((shard_len, span), F32)],
        (
            tied(place, up_side), seq_lengths, queries, keys, values, bias, row(key_mask), mate_live,
        ),
        8 * shard_len * span * width,
        grid=(pairs // 2,),
        name="attend",
    )
    up_other, up_across, mixed, down_z = joined(up_other, up_across, mixed, down_z)
    up_pieces = twins((up_own, up_side, up_other, up_across))
    down_own = jnp.stack([down_unit] + down_z)
    down_side = shift(down_own, SIDE, "down_1")
    down_other = shift(down_own, OTHER_SIDE, "down_2")
    middle, second, context, active, slope = call(
        expand_kernel,
        [SMEM] + [VMEM] * 12,
        [
            shape(shard_len, width, kind=F32), shape(shard_len, width), shape(shard_len, width),
            shape(shard_len, ff), shape(shard_len, ff, kind=F32),
        ],
        [VMEM] * 5,
        [
            pltpu.VMEM((ff, width), LOW), pltpu.VMEM((units, out_rows, width), LOW),
            pltpu.VMEM((width, width), LOW),
        ],
        (tied(place, down_own), frames, mixed, vectors, up_bias_all) + up_pieces,
        2 * shard_len * width * (width + ff),
        name="expand", limit=36,
    )
    down_side, down_other, active = joined(down_side, down_other, active)
    down_across = shift(down_side, OTHER_SIDE, "down_3")
    active_twin, context_twin, second_twin = twin(active), twin(context), twin(second)
    first_twin = twin(first)
    down_parts = call(
        down_grad_kernel,
        [SMEM] + [VMEM] * 4,
        part_shapes(down_rows, width) + [shape(8, width, kind=F32)],
        [VMEM] * 5,
        [
            pltpu.VMEM((span, width // 2), LOW), pltpu.VMEM((units // 2, down_rows, width), F32),
        ],
        (tied(place, down_side), active, active_twin, cotangent, cotangent_twin),
        2 * shard_len * width * ff,
        name="down_grad", limit=24,
    )
    down_across, down_parts = joined(down_across, down_parts)
    down_bias_grad = down_parts[4]
    down_pieces = twins((down_own, down_side, down_other, down_across))
    turned = shift(down_parts[3], OTHER_SIDE, "rs_down_3")
    down_two = shift(down_parts[2], OTHER_SIDE, "rs_down_2")
    middle_grad, context_grad, vector_grads, branch_grad, up_bias_grad, hidden_grad = call(
        back_kernel,
        [SMEM] + [VMEM] * 20,
        [
            shape(shard_len, width, kind=F32), shape(shard_len, width), shape(8, width, kind=F32),
            shape(shard_len, width), shape(8, ff, kind=F32), shape(shard_len, ff),
        ],
        [VMEM] * 6,
        [
            pltpu.VMEM((units, down_rows, width), LOW), pltpu.VMEM((width, ff), LOW),
            pltpu.VMEM((ff, width), LOW), pltpu.VMEM((units, out_rows, width), LOW),
            pltpu.VMEM((width, width), LOW),
        ],
        (tied(place, down_parts[0]), cotangent, slope, middle, vectors) + down_pieces + up_pieces,
        2 * shard_len * width * (2 * ff + width),
        name="back", limit=48,
    )
    turned, down_two, hidden_grad, context_twin, second_twin, first_twin = joined(
        turned, down_two, hidden_grad, context_twin, second_twin, first_twin
    )
    side = (down_parts[1].astype(F32) + turned.astype(F32)).astype(LOW)
    down_one = shift(side, SIDE, "rs_down_1")
    hidden_twin = twin(hidden_grad)
    branch_twin = twin(branch_grad)
    down_sum = down_parts[0].astype(F32) + down_two.astype(F32)
    up_parts = call(
        up_grad_kernel,
        [SMEM] + [VMEM] * 8,
        [shape(n, up_rows + out_rows, width) for n in (4, 4, 2, 2, 4)],
        [VMEM] * 5,
        [
            pltpu.VMEM((span, ff // 2), LOW), pltpu.VMEM((span, width // 2), LOW),
            pltpu.VMEM((units // 2, up_rows + out_rows, width), LOW),
        ],
        (
            tied(place, down_sum, side), hidden_grad, hidden_twin, second, second_twin, branch_grad, branch_twin,
            context, context_twin,
        ),
        2 * shard_len * width * (ff + width),
        name="up_grad", limit=28,
    )
    down_one = tied(down_one, up_parts[0])
    turned = shift(up_parts[4], OTHER_SIDE, "rs_up_3")
    up_two = shift(up_parts[2], OTHER_SIDE, "rs_up_2a")
    down_sum = down_sum + down_one.astype(F32)
    down_low = down_sum.astype(LOW)
    down_z = [shift(down_low[n + 1], ALONG_Z[n], "rs_down_z") for n in range(2)]
    grads, diagonals = call(
        attend_back_kernel,
        [
            SMEM, lanes_of(shard_len, 2), lanes_of(span, 2), lanes_of(span, 2), lanes_of(shard_len, 2), lanes_of(shard_len, 2),
            heads_of(4, shard_len, span),
        ],
        [shape(3, span, width), shape(H, span + shard_len, kind=F32)],
        [pl.BlockSpec((3, span, 2 * pair_lanes), lambda n: (0, 0, n)), whole(H, span + shard_len)],
        [],
        (place, queries, keys, values, tied(context_grad, up_parts[0], down_sum), mixed, probs),
        16 * shard_len * span * width,
        grid=(pairs // 2,),
        name="attend_back", limit=24,
    )
    turned, up_two, down_z, grads = joined(turned, up_two, down_z, grads)
    up_rest = shift(up_parts[3], OTHER_SIDE, "rs_up_2b")
    grads_twin = twin(grads)
    side = (up_parts[1].astype(F32) + turned.astype(F32)).astype(LOW)
    up_one = shift(side, SIDE, "rs_up_1")
    own_grad, mate_grad, small = call(
        first_grad_kernel,
        [SMEM] + [VMEM] * 3 + [HBM] + [VMEM] * 4,
        [
            shape(shard_len, width, kind=F32), shape(shard_len, width, kind=F32),
            shape(12 + H, width, kind=F32),
        ],
        [VMEM] * 3,
        [pltpu.VMEM((3 * width, width), LOW), pltpu.SemaphoreType.DMA((1,))],
        (
            tied(place, side), frames, mate_frames, grads, weight, diagonals, vector_grads,
            down_bias_grad, up_bias_grad,
        ),
        2 * shard_len * width * 5 * width,
        name="first_grad", limit=24,
    )
    grads_twin, small = joined(grads_twin, small)
    down_z.append(shift(tied(down_low[3], small), ALONG_Z[2], "rs_down_z"))
    small_twin = twin(small)
    qkv_parts = call(
        qkv_grad_kernel,
        [SMEM] + [VMEM] * 9,
        part_shapes(qkv_rows + PAD, width),
        [VMEM] * 4,
        [
            pltpu.VMEM((2 * span, 3 * width // 2), LOW), pltpu.VMEM((3 * width // 2, width), F32),
            pltpu.VMEM((2, units, width), F32), pltpu.VMEM((H // 2, width), F32),
            pltpu.VMEM((units // 2, qkv_rows + PAD, width), LOW),
        ],
        (place, grads, grads_twin, first, first_twin, small, small_twin) + tuple(spreads),
        2 * shard_len * width * 6 * width,
        name="qkv_grad", limit=28,
    )
    up_one, up_rest, down_z = tied((up_one, up_rest, down_z), qkv_parts[0])
    turned = shift(qkv_parts[3], OTHER_SIDE, "rs_qkv_3")
    qkv_two = shift(qkv_parts[2], OTHER_SIDE, "rs_qkv_2")
    up_sum = [
        up_parts[0][n].astype(F32) + up_one[n].astype(F32) + (up_two, up_rest)[n // 2][n % 2].astype(F32)
        for n in range(4)
    ]
    up_low = [part.astype(LOW) for part in up_sum]
    up_z = [shift(up_low[n + 1], ALONG_Z[n], "rs_up_z") for n in range(2)]
    down_sum = z_sum(down_sum, down_z)
    own_part, mate_part = call(
        input_grad_kernel,
        [VMEM] * 6,
        [shape(shard_len, width, kind=F32), shape(shard_len, width)],
        [VMEM] * 2,
        [],
        (frames, mate_frames, own_grad, tied(mate_grad, *up_low), middle_grad, vectors),
        0,
        name="input_grad", limit=12,
    )
    turned, mate_part = joined(turned, mate_part)
    side = (qkv_parts[1].astype(F32) + turned.astype(F32)).astype(LOW)
    qkv_one = shift(side, SIDE, "rs_qkv_1")
    up_z, side_after = joined(up_z, side)
    up_z.append(shift(tied(up_low[3], side_after), ALONG_Z[2], "rs_up_z"))
    layer_out = call(
        finish_kernel,
        [SMEM] + [VMEM] * 11,
        [shape(shard_len, width, kind=F32)],
        [VMEM],
        [pltpu.VMEM((units, down_rows, width), LOW), pltpu.VMEM((width, ff), LOW)],
        (tied(place, side_after), active, middle, vectors) + down_pieces,
        2 * shard_len * width * ff,
        name="finish",
    )[0]
    qkv_one, qkv_two, up_z, layer_out = joined(qkv_one, qkv_two, up_z, layer_out)
    qkv_sum = qkv_parts[0].astype(F32) + qkv_one.astype(F32) + qkv_two.astype(F32)
    qkv_z = z_sends(qkv_sum, "rs_qkv")
    up_sum = z_sum(tied(up_sum[:1], qkv_sum), up_z)
    mate_part = shift(tied(mate_part, up_sum), PACK, "grad_pack")
    last = call(
        last_kernel,
        [VMEM] * 6,
        [
            shape(qkv_rows, width, kind=F32), shape(1, 2 * each, kind=F32), shape(1, up_rows, kind=F32),
            shape(H, BUCKETS, kind=F32), shape(shard_len, width, kind=F32),
        ]
        + [shape(1, each, kind=F32)] * NARROW,
        [VMEM] * (5 + NARROW),
        [],
        (qkv_sum[0],) + tuple(qkv_z) + (own_part, mate_part),
        0,
        name="last", limit=8,
    )
    qkv_grad, qv_bias_grad, up_bias_sum, table, frames_grad = last[:5]
    pieces = [piece.reshape(each) for piece in last[5:]]

    down_grad = jnp.concatenate(
        [down_sum[fold * each : (fold + 1) * each] for fold in range(folds)], axis=1
    )
    return (
        layer_out, frames_grad, qkv_grad.T, qv_bias_grad.reshape(2 * each),
        up_sum[up_rows : up_rows + each].T, pieces[4], up_sum[:up_rows].T, up_bias_sum.reshape(up_rows),
        down_grad.T, pieces[5], pieces[0], pieces[1], pieces[2], pieces[3], table.T,
    )


def paired(mesh):
    return mesh.shape["blk"] == 2 and mesh.shape["dp"] == 16


def solution(mesh):
    placed = (
        P(("dp", "blk"), None),
        P(("dp", "blk"), None),
        P("dp", None),
        P(("dp", "blk")),
        P(None, ("dp", "blk")),
        P(("dp", "blk")),
        P(None, ("dp", "blk")),
        P(("dp", "blk")),
        P(None, ("dp", "blk")),
        P(("dp", "blk")),
        P(None, ("dp", "blk")),
        P(("dp", "blk")),
        P(("dp", "blk")),
        P(("dp", "blk")),
        P(("dp", "blk")),
        P(("dp", "blk")),
        P(),
    )
    return jax.shard_map(
        paired_body if paired(mesh) else body,
        mesh=mesh,
        in_specs=placed,
        out_specs=(
            P(("dp", "blk"), None),
            P(("dp", "blk"), None),
            P(None, ("dp", "blk")),
            P(("dp", "blk")),
            P(None, ("dp", "blk")),
            P(("dp", "blk")),
            P(None, ("dp", "blk")),
            P(("dp", "blk")),
            P(None, ("dp", "blk")),
            P(("dp", "blk")),
            P(("dp", "blk")),
            P(("dp", "blk")),
            P(("dp", "blk")),
            P(("dp", "blk")),
            P(),
        ),
        check_vma=False,
    )
```
